32 devices in a mesh: dp: 8 (over z, core), tensor: 4 (over y, x).
Axes of the slice: x: 2, y: 2, z: 4, core: 2. Of those that a mesh axis runs over, the one named last changes fastest.
Arguments:
- tokens: bfloat16 [16384, 2048], P(('dp', 'tensor')), may hold values from -6 to 6
- segments: int32 [16384], P('dp'), may hold values from 0 to 287, as said below
- positions: int32 [16384], P('dp'), may hold values from 0 to 2397, as said below
- w_query: bfloat16 [2048, 2048], P('dp', 'tensor'), may hold values from -0.125 to 0.125
- w_key: bfloat16 [2048, 512], P('dp', 'tensor'), may hold values from -0.125 to 0.125
- w_value: bfloat16 [2048, 512], P('dp', 'tensor'), may hold values from -0.125 to 0.125
- w_out: bfloat16 [2048, 2048], P('dp', 'tensor'), may hold values from -1 to 1
- w_gate: bfloat16 [2048, 8192], P('dp', 'tensor'), may hold values from -0.125 to 0.125
- w_up: bfloat16 [2048, 8192], P('dp', 'tensor'), may hold values from -0.125 to 0.125
- w_down: bfloat16 [2048, 8192], P('dp', 'tensor'), may hold values from -0.0625 to 0.0625
- norm_attn: float32 [2048], replicated, may hold values from 0.1 to 1.9
- norm_mlp: float32 [2048], replicated, may hold values from 0.1 to 1.9
- query_gain: float32 [64], replicated, may hold values from 0.1 to 1.9
- key_gain: float32 [64], replicated, may hold values from 0.1 to 1.9
- out_grad: bfloat16 [16384, 2048], P(('dp', 'tensor')), may hold values from -6 to 6
Outputs:
- output: bfloat16 [16384, 2048], P(('dp', 'tensor'))
- grad_tokens: float32 [16384, 2048], P(('dp', 'tensor'))
- grad_w_query: float32 [2048, 2048], P('dp', 'tensor')
- grad_w_key: float32 [2048, 512], P('dp', 'tensor')
- grad_w_value: float32 [2048, 512], P('dp', 'tensor')
- grad_w_out: float32 [2048, 2048], P('dp', 'tensor')
- grad_w_gate: float32 [2048, 8192], P('dp', 'tensor')
- grad_w_up: float32 [2048, 8192], P('dp', 'tensor')
- grad_w_down: float32 [2048, 8192], P('dp', 'tensor')
- grad_norm_attn: float32 [2048], replicated
- grad_norm_mlp: float32 [2048], replicated
- grad_query_gain: float32 [64], replicated
- grad_key_gain: float32 [64], replicated
The draws below stay inside these ranges and needn't reach their ends.
Inputs may be any that keep to these rules, and one draw needn't show every extreme that they name: `segments`: document numbers never fall along a sequence of 1024 tokens, and no number stands in two sequences; every document has 60 to 800 tokens, except that the last one of a sequence may be cut short. `positions`: 0 at a document's first token, then rising by 1 to 3 from each token of the document to the next.
All inputs are finite; a program needn't handle non-finite values.
Results may differ from the reference program's by a relative error of at most 0.019.
Values may be sent and summed in bfloat16 or wider, within the bound.
A program may use at most 224 MiB of HBM per device.

```python
import jax
import jax.numpy as jnp
from jax import lax

D = 2048
HQ = 32
HK = 8
HD = 64
FF = 8192
L = 1024
SEQ_DP = 2
DOC_MIN = 60
DOC_MAX = 800
TOKENS = 16384


def doc_layout(key):
    seq_count = TOKENS // L
    most_docs = L // DOC_MIN + 1
    lengths = jax.random.randint(jax.random.fold_in(key, 11), (seq_count, most_docs), DOC_MIN, DOC_MAX + 1)
    lengths = lengths.at[0, 0].set(DOC_MAX)
    doc_ends = jnp.cumsum(lengths, axis=1)
    doc_starts = doc_ends - lengths
    indices = jnp.arange(L, dtype=jnp.int32)
    local_doc = jnp.sum((doc_ends[:, None, :] <= indices[None, :, None]).astype(jnp.int32), axis=2)
    pos_steps = jax.random.randint(jax.random.fold_in(key, 12), (seq_count, L), 1, 4)
    first_rows = (jnp.arange(seq_count, dtype=jnp.int32)[:, None] == 0) & (indices[None, :] < DOC_MAX)
    pos_steps = jnp.where(first_rows, 3, pos_steps)
    pos_running = jnp.cumsum(pos_steps, axis=1)
    picked = (local_doc[:, :, None] == jnp.arange(most_docs, dtype=jnp.int32)[None, None, :]).astype(jnp.int32)
    first_index = jnp.sum(picked * doc_starts[:, None, :], axis=2)
    base_value = jnp.take_along_axis(pos_running, first_index, axis=1)
    places = pos_running - base_value
    last_doc = local_doc[:, L - 1:L]
    number = local_doc + (most_docs - 1 - last_doc) + jnp.arange(seq_count, dtype=jnp.int32)[:, None] * most_docs
    return (number.reshape(TOKENS), places.reshape(TOKENS))


def draw_segments(key, part):
    number, places = doc_layout(key)
    return number


def draw_positions(key, part):
    number, places = doc_layout(key)
    return places


def shard_levels(stream_key, extent, shards, least, top_value):
    def one(axis_at, parts):
        draws = jax.random.uniform(jax.random.fold_in(jax.random.fold_in(stream_key, 6), axis_at), (parts,), jnp.float32, least / len(shards), top_value / len(shards))
        return jnp.repeat(jnp.exp(draws), extent[axis_at] // parts).reshape((-1,) + (1,) * (len(extent) - axis_at - 1))

    gain = one(*shards[0])
    for cut in shards[1:]:
        gain = gain * one(*cut)
    return gain


def normal_values(key, extent, scale, most, cuts=(), held_as=jnp.bfloat16):
    drawn = jax.random.normal(key, extent, jnp.float32) * scale
    if len(cuts) > 0:
        drawn = shard_levels(key, extent, cuts, -0.22, 0.18) * drawn
    return jnp.clip(drawn, min=-most, max=most).astype(held_as)


def setup_inputs(seed: int = 0) -> dict:
    key_of = jax.random.split(jax.random.key(seed), 16)
    tokens = normal_values(key_of[0], (TOKENS, D), 1.0, 6.0, ((0, 32),))
    segments = draw_segments(jax.random.fold_in(key_of[15], 71), 0)
    positions = draw_positions(jax.random.fold_in(key_of[15], 71), 0)
    w_query = normal_values(key_of[3], (D, HQ * HD), D ** -0.5, 0.125, ((0, 8), (1, 4)))
    w_key = normal_values(key_of[4], (D, HK * HD), D ** -0.5, 0.125, ((0, 8), (1, 4)))
    w_value = normal_values(key_of[5], (D, HK * HD), D ** -0.5, 0.125, ((0, 8), (1, 4)))
    w_out = normal_values(key_of[6], (D, HQ * HD), (HQ * HD // 64) ** -0.5, 1.0, ((0, 8), (1, 4)))
    w_gate = normal_values(key_of[7], (D, FF), D ** -0.5, 0.125, ((0, 8), (1, 4)))
    w_up = normal_values(key_of[8], (D, FF), D ** -0.5, 0.125, ((0, 8), (1, 4)))
    w_down = normal_values(key_of[9], (D, FF), FF ** -0.5, 0.0625, ((0, 8), (1, 4)))
    norm_attn = jnp.clip(1.0 + 0.18 * jax.random.normal(key_of[10], (D,), jnp.float32), 0.1, 1.9)
    norm_mlp = jnp.clip(1.0 + 0.18 * jax.random.normal(key_of[11], (D,), jnp.float32), 0.1, 1.9)
    query_gain = jnp.clip(1.0 + 0.18 * jax.random.normal(key_of[12], (HD,), jnp.float32), 0.1, 1.9)
    key_gain = jnp.clip(1.0 + 0.18 * jax.random.normal(key_of[13], (HD,), jnp.float32), 0.1, 1.9)
    out_grad = normal_values(key_of[14], (TOKENS, D), 1.0, 6.0, ((0, 32),))
    return {"tokens": tokens, "segments": segments, "positions": positions, "w_query": w_query, "w_key": w_key, "w_value": w_value, "w_out": w_out, "w_gate": w_gate, "w_up": w_up, "w_down": w_down, "norm_attn": norm_attn, "norm_mlp": norm_mlp, "query_gain": query_gain, "key_gain": key_gain, "out_grad": out_grad}


EPS = 1e-05
THETA = 1000000.0

@jax.custom_vjp
def low(v):
    return lax.optimization_barrier(v.astype(jnp.bfloat16)).astype(jnp.float32)

@jax.custom_vjp
def low_back(v):
    return v

def low_keep(v):
    return (low(v), None)

def low_pass(kept, grad):
    return (grad,)

def back_keep(v):
    return (v, None)

def back_low(kept, grad):
    return (low(grad),)
low.defvjp(low_keep, low_pass)
low_back.defvjp(back_keep, back_low)

def matmul_high(left, right):
    return jnp.dot(left, right, precision=lax.Precision.HIGHEST)

def rms_normed(values):
    return values * lax.rsqrt(lax.optimization_barrier(jnp.mean(values * values, axis=-1, keepdims=True)) + EPS)

def rotary_tables(places, width):
    half_width = width // 2
    frequency = THETA ** (-jnp.arange(half_width, dtype=jnp.float32) * 2.0 / width)
    angles = places.astype(jnp.float32)[:, None] * frequency[None, :]
    cosine_table = jnp.concatenate([jnp.cos(angles), jnp.cos(angles)], axis=-1)[:, None, :]
    sine_table = jnp.concatenate([jnp.sin(angles), jnp.sin(angles)], axis=-1)[:, None, :]
    return (cosine_table, sine_table)

def rotate(values, cosine_table, sine_table):
    half_width = values.shape[-1] // 2
    turned = jnp.concatenate([-values[..., half_width:], values[..., :half_width]], axis=-1)
    return values * cosine_table + turned * sine_table

def attend(pieces):
    queries, keys, values, segment_ids = pieces
    row_count = queries.shape[0]
    repeat = HQ // HK
    grouped = queries.reshape(row_count, HK, repeat, HD)
    scores = jnp.einsum('bkrd,ckd->krbc', grouped, keys, precision=lax.Precision.HIGHEST) * HD ** (-0.5)
    scores = low_back(scores)
    indices = jnp.arange(row_count)
    allowed = (segment_ids[:, None] == segment_ids[None, :]) & (indices[None, :] <= indices[:, None])
    scores = jnp.where(allowed, scores, -jnp.inf)
    probabilities = low(jax.nn.softmax(scores, axis=-1))
    mixture = jnp.einsum('krbc,ckd->bkrd', probabilities, values, precision=lax.Precision.HIGHEST)
    return mixture.reshape(row_count, HQ * HD)

def forward(inputs, segment_ids, cosine_table, sine_table, params):
    w_query, w_key, w_value, w_out, w_gate, w_up, w_down, norm_attn, norm_mlp, query_gain, key_gain = params
    row_count = inputs.shape[0]
    hidden_one = low(rms_normed(inputs) * norm_attn)
    query_raw = low_back(matmul_high(hidden_one, w_query)).reshape(row_count, HQ, HD)
    key_raw = low_back(matmul_high(hidden_one, w_key)).reshape(row_count, HK, HD)
    values = low(low_back(matmul_high(hidden_one, w_value))).reshape(row_count, HK, HD)
    queries = low(rotate(rms_normed(query_raw) * query_gain, cosine_table, sine_table))
    keys = low(rotate(rms_normed(key_raw) * key_gain, cosine_table, sine_table))
    sequences = row_count // L
    attended = lax.map(jax.checkpoint(attend), (queries.reshape(sequences, L, HQ, HD), keys.reshape(sequences, L, HK, HD), values.reshape(sequences, L, HK, HD), segment_ids.reshape(sequences, L)))
    attended = low(low_back(attended.reshape(row_count, HQ * HD)))
    resid = inputs + low_back(matmul_high(attended, w_out.T))
    hidden_two = low(rms_normed(resid) * norm_mlp)
    gate_raw = low_back(matmul_high(hidden_two, w_gate))
    up_raw = low_back(matmul_high(hidden_two, w_up))
    act = low(jax.nn.silu(gate_raw) * up_raw)
    return resid + low_back(matmul_high(act, w_down.T))

def reference(tokens, segments, positions, w_query, w_key, w_value, w_out, w_gate, w_up, w_down, norm_attn, norm_mlp, query_gain, key_gain, out_grad):
    group_rows = SEQ_DP * L
    groups = TOKENS // group_rows
    params = tuple((item.astype(jnp.float32) for item in (w_query, w_key, w_value, w_out, w_gate, w_up, w_down, norm_attn, norm_mlp, query_gain, key_gain)))

    def one_group(sums, pieces):
        inputs, segment_ids, places, cotangent = pieces
        cosine_table, sine_table = rotary_tables(places, HD)

        def run_block(inputs, params):
            return forward(inputs, segment_ids, cosine_table, sine_table, params)
        result, pull_back = jax.vjp(run_block, inputs, params)
        grad_inputs, grad_params = pull_back(cotangent)
        sums = tuple((total + part_grad for total, part_grad in zip(sums, grad_params)))
        return (sums, (result.astype(jnp.bfloat16), grad_inputs))
    zero_grads = tuple((jnp.zeros_like(item) for item in params))
    sums, (outputs, grad_inputs) = lax.scan(one_group, zero_grads, (tokens.astype(jnp.float32).reshape(groups, group_rows, D), segments.reshape(groups, group_rows), positions.reshape(groups, group_rows), out_grad.astype(jnp.float32).reshape(groups, group_rows, D)))
    return (outputs.reshape(TOKENS, D), grad_inputs.reshape(TOKENS, D), sums[0], sums[1], sums[2], sums[3], sums[4], sums[5], sums[6], sums[7], sums[8], sums[9], sums[10])
```

```python
import functools

import jax
import jax.numpy as jnp
from jax import lax
from jax.experimental import pallas as pl
from jax.experimental.pallas import tpu as pltpu
from jax.sharding import PartitionSpec as P

EPS = 1e-05
THETA = 1000000.0
SEQ = 1024
TILE = 256
LOG2E = 1.4426950408889634
MASKED = -1e30
NT = (((1,), (1,)), ((), ()))
TN = (((0,), (0,)), ((), ()))


def rms_scale(values):
    return lax.rsqrt(jnp.mean(values * values, axis=-1, keepdims=True) + EPS)


def norm_back(grad_normed, normed, inverse):
    return inverse * (grad_normed - normed * jnp.mean(grad_normed * normed, axis=-1, keepdims=True))


def rotary_tables(places):
    lane = jnp.arange(128)
    frequency = THETA ** (-(lane % 32).astype(jnp.float32) * 2.0 / 64)
    angles = places.astype(jnp.float32)[:, None] * frequency[None, :]
    sine = jnp.sin(angles)
    upper = (lane % 64 >= 32)[None, :]
    return jnp.cos(angles), jnp.where(upper, 0.0, -sine), jnp.where(upper, sine, 0.0)


def contract_rows(left, right):
    return lax.dot_general(
        left, right, (((0,), (0,)), ((), ())), preferred_element_type=jnp.float32
    )


def half_lanes(rows):
    return lax.broadcasted_iota(jnp.int32, (rows, 128), 1) < 64


def ones_side(side, rows):
    low = half_lanes(rows)
    return jnp.where(low if side == 0 else ~low, 1.0, 0.0).astype(jnp.bfloat16)


def attend_kernel(q_ref, k_ref, v_ref, segc_ref, segr_ref, out_ref, inv_ref, bias_ref, total_ref):
    coef = LOG2E * 64 ** (-0.5)

    @pl.when(pl.program_id(1) == 0)
    def _():
        for at in range(0, SEQ, TILE):
            end = at + TILE
            rows = lax.broadcasted_iota(jnp.int32, (TILE, end), 0) + at
            cols = lax.broadcasted_iota(jnp.int32, (TILE, end), 1)
            allowed = (segc_ref[at:end, :] == segr_ref[0, :, :end]) & (cols <= rows)
            bias_ref[at:end, :end] = jnp.where(allowed, 0.0, MASKED)

    for side in range(2):
        lanes = slice(side * 128, side * 128 + 128)
        for key_at in range(0, SEQ, TILE):
            keys, rows = slice(key_at, key_at + TILE), slice(key_at, SEQ)
            scores = lax.dot_general(
                q_ref[rows, :], k_ref[keys, lanes], NT, preferred_element_type=jnp.float32
            )
            weights = jnp.exp2(scores * coef + bias_ref[rows, keys]).astype(jnp.bfloat16)
            mixed = jnp.concatenate([v_ref[keys, lanes], ones_side(side, TILE)], axis=1)
            part = jnp.dot(weights, mixed, preferred_element_type=jnp.float32)
            if side == 0 and key_at == 0:
                total_ref[...] = part
            else:
                total_ref[rows, :] += part
    inverse = 1.0 / total_ref[:, 128:]
    out_ref[...] = (total_ref[:, :128] * inverse).astype(jnp.bfloat16)
    inv_ref[...] = inverse


def unrotated(grads, raw, cosine, sine_low, sine_high, gain):
    grads = grads * 0.125
    turned = (
        grads * cosine
        - pltpu.roll(grads, 96, 1) * sine_low
        - pltpu.roll(grads, 32, 1) * sine_high
    )
    inverse = head_inverse(raw)
    normed = raw * inverse
    scaled = turned * gain
    change = inverse * (scaled - normed * head_mean(scaled * normed))
    return change, jnp.sum((turned * normed).reshape(-1, 8, 128), axis=0)


def attend_back_kernel(
    chunks, inner_ref, q_ref, k_ref, v_ref, segc_ref, segr_ref, out_ref, inv_ref,
    qraw_ref, kraw_ref, cos_ref, low_ref, high_ref, qgain_ref, kgain_ref, *refs,
):
    pieces, results = refs[:chunks], refs[chunks : 2 * chunks]
    (
        qsum_ref, ksum_ref, bias_ref, mix_ref, qside_ref, gside_ref,
        dq_ref, dk_ref, dv_ref, kpair_ref, vpair_ref, grad_ref,
    ) = refs[2 * chunks :]
    chunk_rows = SEQ // chunks
    q_width = 128 * pl.num_programs(1)
    kv_width = (results[0].shape[1] - q_width) // 2

    def rows_of(k):
        return pl.ds(pl.multiple_of((inner_ref[0] ^ k) * chunk_rows, chunk_rows), chunk_rows)

    def put(values, place):
        dq_ref[...] = values
        for k, result_ref in enumerate(results):
            lanes = pl.ds(pl.multiple_of(place, 128), 128)
            result_ref[:, lanes] = dq_ref[rows_of(k), :].astype(jnp.bfloat16)

    coef = LOG2E * 64 ** (-0.5)
    step = pl.program_id(1)

    @pl.when(step == 0)
    def _():
        for key_at in range(0, SEQ, TILE):
            key_end = key_at + TILE
            keys = lax.broadcasted_iota(jnp.int32, (TILE, SEQ - key_at), 0) + key_at
            rows = lax.broadcasted_iota(jnp.int32, (TILE, SEQ - key_at), 1) + key_at
            allowed = (segc_ref[key_at:key_end, :] == segr_ref[0, :, key_at:]) & (keys <= rows)
            bias_ref[key_at:key_end, key_at:] = jnp.where(allowed, 0.0, MASKED)

    @pl.when((step == 0) & (pl.program_id(0) == 0))
    def _():
        qsum_ref[...] = jnp.zeros_like(qsum_ref)
        ksum_ref[...] = jnp.zeros_like(ksum_ref)

    @pl.when(lax.rem(step, 4) == 0)
    def _():
        kpair_ref[...] = jnp.zeros_like(kpair_ref)
        vpair_ref[...] = jnp.zeros_like(vpair_ref)

    @pl.when(lax.rem(step, 2) == 0)
    def _():
        dk_ref[...] = jnp.zeros_like(dk_ref)
        dv_ref[...] = jnp.zeros_like(dv_ref)

    for k, piece_ref in enumerate(pieces):
        grad_ref[rows_of(k), :] = piece_ref[...].astype(jnp.float32)
    low = half_lanes(SEQ)
    scaled = grad_ref[...] * inv_ref[...]
    scaled_low = scaled.astype(jnp.bfloat16)
    mix_ref[:, :128] = scaled_low
    mix_ref[:, 128:] = -(scaled * out_ref[...].astype(jnp.float32)).astype(jnp.bfloat16)
    none = jnp.zeros_like(scaled_low)
    queries = q_ref[...]
    gside_ref[:, :128] = jnp.where(low, scaled_low, none)
    gside_ref[:, 128:] = jnp.where(low, none, scaled_low)
    qside_ref[:, :128] = jnp.where(low, queries, none)
    qside_ref[:, 128:] = jnp.where(low, none, queries)

    for key_at in range(0, SEQ, TILE):
        keys, rows = slice(key_at, key_at + TILE), slice(key_at, SEQ)
        for side in range(2):
            lanes = slice(side * 128, side * 128 + 128)
            key_side = k_ref[keys, lanes]
            value_side = jnp.concatenate([v_ref[keys, lanes], ones_side(side, TILE)], axis=1)
            scores = lax.dot_general(
                key_side, q_ref[rows, :], NT, preferred_element_type=jnp.float32
            )
            weights = jnp.exp2(scores * coef + bias_ref[keys, rows])
            change = lax.dot_general(
                value_side, mix_ref[rows, :], NT, preferred_element_type=jnp.float32
            )
            grads = (weights * change).astype(jnp.bfloat16)
            dv_ref[keys, :] += jnp.dot(
                weights.astype(jnp.bfloat16),
                gside_ref[rows, lanes],
                preferred_element_type=jnp.float32,
            )
            dk_ref[keys, :] += jnp.dot(
                grads, qside_ref[rows, lanes], preferred_element_type=jnp.float32
            )
            dq = lax.dot_general(grads, key_side, TN, preferred_element_type=jnp.float32)
            if key_at == 0 and side == 0:
                dq_ref[...] = dq
            else:
                dq_ref[rows, :] += dq

    cosine, sine_low, sine_high = cos_ref[...], low_ref[...], high_ref[...]
    change, sums = unrotated(
        dq_ref[...], qraw_ref[...], cosine, sine_low, sine_high, qgain_ref[...]
    )
    qsum_ref[...] += sums
    put(change, step * 128)

    @pl.when(lax.rem(step, 2) == 1)
    def _():
        mine = low == (lax.rem(step, 4) == 1)
        for sum_ref, pair_ref in ((dk_ref, kpair_ref), (dv_ref, vpair_ref)):
            sums = sum_ref[...]
            pair_ref[...] = jnp.where(mine, sums + pltpu.roll(sums, 64, 1), pair_ref[...])

    @pl.when((lax.rem(step, 4) == 3) | (step == pl.num_programs(1) - 1))
    def _():
        change, sums = unrotated(
            kpair_ref[...], kraw_ref[...], cosine, sine_low, sine_high, kgain_ref[...]
        )
        ksum_ref[...] += sums
        put(change, q_width + step // 4 * 128)
        put(vpair_ref[...], q_width + kv_width + step // 4 * 128)


def attention_specs():
    pair = pl.BlockSpec((SEQ, 128), lambda s, p, *_: (s, p))
    group = pl.BlockSpec((SEQ, 256), lambda s, p, *_: (s, p // 2))
    seg_col = pl.BlockSpec((SEQ, 1), lambda s, p, *_: (s, 0))
    seg_row = pl.BlockSpec((1, 1, SEQ), lambda s, p, *_: (s, 0, 0))
    return pair, group, seg_col, seg_row


def attend(queries, key_sides, value_sides, segments):
    rows, width = queries.shape
    sequences, pairs = rows // SEQ, width // 128
    pair, group, seg_col, seg_row = attention_specs()
    work = rows * SEQ * width
    return pl.pallas_call(
        attend_kernel,
        grid=(sequences, pairs),
        in_specs=[pair, group, group, seg_col, seg_row],
        out_specs=[pair, pair],
        out_shape=[
            jax.ShapeDtypeStruct((rows, width), jnp.bfloat16),
            jax.ShapeDtypeStruct((rows, width), jnp.float32),
        ],
        scratch_shapes=[pltpu.VMEM((SEQ, SEQ), jnp.float32), pltpu.VMEM((SEQ, 256), jnp.float32)],
        compiler_params=pltpu.CompilerParams(vmem_limit_bytes=60 * 2**20),
        cost_estimate=pl.CostEstimate(
            flops=42 * work // 10, bytes_accessed=rows * width * 12, transcendentals=work // 128
        ),
    )(queries, key_sides, value_sides, segments[:, None], segments.reshape(sequences, 1, SEQ))


def attend_back(
    inner, sequence, queries, key_sides, value_sides, segments, attended, inverse, pieces, raw, tables,
    query_gain, key_gain,
):
    width = queries.shape[1]
    pairs, chunks, chunk_rows = width // 128, len(pieces), pieces[0].shape[0]
    kv_width = key_sides.shape[1] // 4
    pair, group, seg_col, seg_row = attention_specs()
    kv_raw = pl.BlockSpec((SEQ, 128), lambda s, p, *_: (0, width // 128 + p // 4))
    table = pl.BlockSpec((SEQ, 128), lambda s, p, *_: (sequence, 0))
    gain = pl.BlockSpec((1, 128), lambda s, p, *_: (0, 0))
    total = pl.BlockSpec((8, 128), lambda s, p, *_: (0, 0))
    piece = pl.BlockSpec((chunk_rows, 128), lambda s, p, *_: (0, p))
    columns = width + 2 * kv_width
    work = SEQ * SEQ * width
    flat = pltpu.VMEM((SEQ, 128), jnp.float32)
    return pl.pallas_call(
        functools.partial(attend_back_kernel, chunks),
        grid_spec=pltpu.PrefetchScalarGridSpec(
            num_scalar_prefetch=1,
            grid=(1, pairs),
            in_specs=[pair, group, group, seg_col, seg_row, pair, pair]
            + [pair, kv_raw, table, table, table, gain, gain]
            + [piece] * chunks,
            out_specs=[pl.BlockSpec((chunk_rows, columns), lambda s, p, *_: (0, 0))] * chunks
            + [total, total],
            scratch_shapes=[
                pltpu.VMEM((SEQ, SEQ), jnp.float32),
                pltpu.VMEM((SEQ, 256), jnp.bfloat16),
                pltpu.VMEM((SEQ, 256), jnp.bfloat16),
                pltpu.VMEM((SEQ, 256), jnp.bfloat16),
                flat, flat, flat, flat, flat, flat,
            ],
        ),
        out_shape=[jax.ShapeDtypeStruct((chunk_rows, columns), jnp.bfloat16)] * chunks
        + [jax.ShapeDtypeStruct((8, 128), jnp.float32)] * 2,
        compiler_params=pltpu.CompilerParams(vmem_limit_bytes=60 * 2**20),
        cost_estimate=pl.CostEstimate(
            flops=110 * work // 10, bytes_accessed=SEQ * width * 20, transcendentals=work // 128
        ),
    )(
        inner, queries, key_sides, value_sides, segments[:, None], segments.reshape(-1, 1, SEQ),
        attended, inverse, raw, raw, *tables,
        jnp.tile(query_gain, 2)[None, :], jnp.tile(key_gain, 2)[None, :], *pieces,
    )


def cost(flops, moved, share):
    return pl.CostEstimate(
        flops=int(0.2 * flops / share), bytes_accessed=int(0.2 * moved), transcendentals=0
    )


def head_inverse(values):
    squares = values * values
    high = squares.astype(jnp.bfloat16)
    low = (squares - high.astype(jnp.float32)).astype(jnp.bfloat16)
    return lax.rsqrt(head_sum(high, low) * (1.0 / 64) + EPS)


def head_sum(high, low):
    from_head = lax.broadcasted_iota(jnp.int32, (128, 128), 0) // 64
    to_head = lax.broadcasted_iota(jnp.int32, (128, 128), 1) // 64
    same = jnp.where(from_head == to_head, 1.0, 0.0).astype(jnp.bfloat16)
    return jnp.dot(high, same, preferred_element_type=jnp.float32) + jnp.dot(
        low, same, preferred_element_type=jnp.float32
    )


def head_mean(values):
    high = values.astype(jnp.bfloat16)
    low = (values - high.astype(jnp.float32)).astype(jnp.bfloat16)
    return head_sum(high, low) * (1.0 / 64)


def project_kernel(
    pieces, inner_ref, *refs,
):
    norm_ref, w_ref, cos_ref, low_ref, high_ref, qgain_ref, kgain_ref = refs[pieces : pieces + 7]
    inv_ref, q_ref, k_ref, v_ref, raw_ref = refs[pieces + 7 :]
    inputs = refs[0][...].astype(jnp.float32)
    inverse = rms_scale(inputs)
    hidden = (inputs * inverse * norm_ref[...]).astype(jnp.bfloat16)
    inv_ref[...] = jnp.broadcast_to(inverse, inv_ref.shape)
    q_width, kv_width = q_ref.shape[1], k_ref.shape[1] // 4
    cosine, sine_low, sine_high = cos_ref[...], low_ref[...], high_ref[...]
    lower = lax.broadcasted_iota(jnp.int32, cosine.shape, 1) < 64
    none = jnp.zeros_like(cosine)

    def rotated(raw, gain):
        scaled = raw * head_inverse(raw) * gain
        return (
            scaled * cosine
            + pltpu.roll(scaled, 96, 1) * sine_low
            + pltpu.roll(scaled, 32, 1) * sine_high
        )

    def to_sides(pair, out_ref, at):
        first, second = jnp.where(lower, pair, none), jnp.where(lower, none, pair)
        sides = (first, pltpu.roll(first, 64, 1), pltpu.roll(second, 64, 1), second)
        for index, side in enumerate(sides):
            lanes = slice(at * 4 + index * 128, at * 4 + index * 128 + 128)
            out_ref[:, lanes] = side.astype(jnp.bfloat16)

    wide = jnp.dot(hidden, w_ref[:, q_width:], preferred_element_type=jnp.float32)
    raw_ref[...] = wide[:, : q_width + kv_width]
    for at in range(0, q_width, 128):
        q_ref[:, at : at + 128] = rotated(wide[:, at : at + 128], qgain_ref[...]).astype(
            jnp.bfloat16
        )
    for at in range(0, kv_width, 128):
        place = q_width + at
        to_sides(rotated(wide[:, place : place + 128], kgain_ref[...]), k_ref, at)
        place = q_width + kv_width + at
        to_sides(wide[:, place : place + 128], v_ref, at)


def placed(chunk_rows, block):
    per = chunk_rows // block
    here = lambda r, inner: (r, 0)
    there = lambda r, inner: ((r // per ^ inner[0]) * per + r % per, 0)
    return here, there


def project(inner, sequence, inputs, chunk_rows, norm, weights, tables, query_gain, key_gain, q_width, kv_width):
    rows, width = inputs.shape
    block = chunk_rows
    here, there = placed(block, block)
    fixed = lambda r, mine: (0, 0)
    used = q_width + 2 * kv_width
    table = pl.BlockSpec(
        (block, 128), lambda r, inner: (sequence * (rows // block) + there(r, inner)[0], 0)
    )
    gain = pl.BlockSpec((1, 128), fixed)
    return pl.pallas_call(
        functools.partial(project_kernel, 1),
        grid_spec=pltpu.PrefetchScalarGridSpec(
            num_scalar_prefetch=1,
            grid=(rows // block,),
            in_specs=[
                pl.BlockSpec((block, width), here),
                pl.BlockSpec((1, width), fixed),
                pl.BlockSpec(weights.shape, fixed, pipeline_mode=pl.Buffered(1)),
                table, table, table, gain, gain,
            ],
            out_specs=[
                pl.BlockSpec((block, 128), here),
                pl.BlockSpec((block, q_width), there),
                pl.BlockSpec((block, 4 * kv_width), there),
                pl.BlockSpec((block, 4 * kv_width), there),
                pl.BlockSpec((block, q_width + kv_width), there),
            ],
        ),
        out_shape=[
            jax.ShapeDtypeStruct((rows, 128), jnp.float32),
            jax.ShapeDtypeStruct((rows, q_width), jnp.bfloat16),
            jax.ShapeDtypeStruct((rows, 4 * kv_width), jnp.bfloat16),
            jax.ShapeDtypeStruct((rows, 4 * kv_width), jnp.bfloat16),
            jax.ShapeDtypeStruct((rows, q_width + kv_width), jnp.float32),
        ],
        compiler_params=pltpu.CompilerParams(vmem_limit_bytes=60 * 2**20),
        cost_estimate=cost(2 * rows * width * used, rows * width * 6, 0.22),
    )(
        inner, inputs, norm[None, :], weights, *tables,
        jnp.tile(query_gain, 2)[None, :], jnp.tile(key_gain, 2)[None, :],
    )


def heads_kernel(count, core_ref, grads_ref, *refs):
    rights, outs = refs[: 2 * count - 1], refs[2 * count - 1 :]
    outs[0][...] = jnp.dot(
        grads_ref[...], rights[0][...], preferred_element_type=jnp.float32
    ).astype(jnp.bfloat16)
    half = rights[1].shape[0]
    near = grads_ref[:, pl.ds(pl.multiple_of(core_ref[0] * half, half), half)]
    other = grads_ref[:, pl.ds(pl.multiple_of((1 - core_ref[0]) * half, half), half)]
    for k in range(1, count):
        outs[k][...] = (
            jnp.dot(near, rights[k][...], preferred_element_type=jnp.float32)
            + jnp.dot(other, rights[count - 1 + k][...], preferred_element_type=jnp.float32)
        ).astype(jnp.bfloat16)


def grad_heads(core, grads, own, others, q_width, count):
    rows, width = grads.shape
    fixed = lambda i, core: (0, 0)
    return pl.pallas_call(
        functools.partial(heads_kernel, count),
        grid_spec=pltpu.PrefetchScalarGridSpec(
            num_scalar_prefetch=1,
            grid=(1,),
            in_specs=[pl.BlockSpec(grads.shape, fixed), pl.BlockSpec((width, q_width), fixed)]
            + [pl.BlockSpec(piece.shape, fixed) for piece in others],
            out_specs=[pl.BlockSpec((rows, q_width), fixed)] * count,
        ),
        out_shape=[jax.ShapeDtypeStruct((rows, q_width), jnp.bfloat16)] * count,
        compiler_params=pltpu.CompilerParams(vmem_limit_bytes=60 * 2**20),
        cost_estimate=cost(2 * rows * width * q_width * count, rows * width, 2.67),
    )(core, grads, own, *others)


def peer(distance):
    mine = lax.axis_index("tensor")
    if distance == 1:
        return mine + 1 - 2 * (mine % 2)
    return (mine + 2) % 4 if distance == 2 else 3 - mine


def remote(distance):
    return dict(device_id={"tensor": peer(distance)}, device_id_type=pl.DeviceIdType.MESH)


def greet(distances):
    barrier = pltpu.get_barrier_semaphore()
    for distance in distances:
        pl.semaphore_signal(barrier, inc=1, **remote(distance))
    pl.semaphore_wait(barrier, len(distances))


def carry(distances, src_refs, dst_refs, send_sems=None, recv_sems=None):
    if not distances:
        return
    copies = [
        pltpu.make_async_remote_copy(
            src_ref=src_ref, dst_ref=dst_ref, send_sem=send_sems.at[i], recv_sem=recv_sems.at[i],
            **remote(distance),
        )
        for i, (distance, src_ref, dst_ref) in enumerate(zip(distances, src_refs, dst_refs))
    ]

    @pl.when(pl.program_id(0) == 0)
    def _():
        greet(sorted(set(distances)))
        for sent in copies:
            sent.start()

    @pl.when(pl.program_id(0) == pl.num_programs(0) - 1)
    def _():
        for sent in copies:
            sent.wait()


def carried(sends, collective_id):
    place = pl.BlockSpec(memory_space=pl.ANY)
    count = len(sends)
    if not count:
        return [], [], [], [], {}, []
    return (
        [place] * count,
        [place] * count,
        [jax.ShapeDtypeStruct(value.shape, value.dtype) for _, value in sends],
        [pltpu.SemaphoreType.DMA((count,)), pltpu.SemaphoreType.DMA((count,))],
        dict(collective_id=collective_id, has_side_effects=True),
        [value for _, value in sends],
    )


def hidden_kernel(filled, distances, x_ref, dy_ref, w_ref, *refs):
    refs, count = refs[filled:], len(distances)
    act_ref, grads_ref = refs[count : count + 2]
    carry(distances, refs[:count], refs[count + 2 : 2 * count + 2], *refs[2 * count + 2 :])
    units = act_ref.shape[1]
    inputs, cotangent = x_ref[...], dy_ref[...]
    for at in range(0, units, 256):
        lanes = slice(at, at + 256)
        gate = jnp.dot(inputs, w_ref[:, lanes], preferred_element_type=jnp.float32)
        up = jnp.dot(
            inputs, w_ref[:, units + at : units + at + 256], preferred_element_type=jnp.float32
        )
        change = jnp.dot(
            cotangent, w_ref[:, 2 * units + at : 2 * units + at + 256],
            preferred_element_type=jnp.float32,
        )
        sigmoid = 1.0 / (1.0 + jnp.exp(-gate))
        silu = gate * sigmoid
        act_ref[:, lanes] = (silu * up).astype(jnp.bfloat16)
        grads_ref[:, lanes] = (change * up * sigmoid * (1.0 + gate - silu)).astype(jnp.bfloat16)
        grads_ref[:, units + at : units + at + 256] = (change * silu).astype(jnp.bfloat16)


def hidden_units(inputs, cotangent, weights, filled, sends=(), collective_id=None):
    rows, width = inputs.shape
    units = weights.shape[1] // 3
    block = min(512, rows)
    row = lambda r: (r, 0)
    place = 0 if filled is None else 1
    in_more, out_more, shapes, scratch, params, operands = carried(sends, collective_id)
    act, grads, *received = pl.pallas_call(
        functools.partial(hidden_kernel, place, [distance for distance, _ in sends]),
        grid=(rows // block,),
        in_specs=[
            pl.BlockSpec((block, width), row),
            pl.BlockSpec((block, width), row),
            pl.BlockSpec(weights.shape, lambda r: (0, 0), pipeline_mode=pl.Buffered(1)),
        ]
        + [pl.BlockSpec(memory_space=pl.ANY)] * place
        + in_more,
        out_specs=[
            pl.BlockSpec((block, units), lambda r: (r, place)),
            pl.BlockSpec((block, 2 * units), row),
        ]
        + out_more,
        out_shape=[
            jax.ShapeDtypeStruct((rows, 2 * units), jnp.bfloat16),
            jax.ShapeDtypeStruct((rows, 2 * units), jnp.bfloat16),
        ]
        + shapes,
        scratch_shapes=scratch,
        input_output_aliases={3: 0} if place else {},
        compiler_params=pltpu.CompilerParams(vmem_limit_bytes=60 * 2**20, **params),
        cost_estimate=cost(6 * rows * width * units, (rows * width + width * units) * 6, 0.63),
    )(inputs, cotangent, weights, *([filled] * place), *operands)
    return act, grads, received


def half_types(distance):
    if distance == 0:
        return (jnp.float32, jnp.float32)
    if distance == 1:
        return (jnp.bfloat16, jnp.float32)
    if distance == 2:
        return (jnp.float32, jnp.bfloat16)
    return (jnp.bfloat16, jnp.bfloat16)


def rows_out_kernel(terms, halves, distances, *refs):
    count = len(distances)
    at = 2 * terms + count
    outs = refs[at : at + halves]
    carry(distances, refs[2 * terms : at], refs[at + halves : at + halves + count], *refs[at + halves + count :])
    total = None
    for left_ref, right_ref in zip(refs[:terms], refs[terms : 2 * terms]):
        product = lax.dot_general(
            left_ref[...], right_ref[...], NT, preferred_element_type=jnp.float32
        )
        total = product if total is None else total + product
    half = outs[0].shape[0]
    for index, out_ref in enumerate(outs):
        out_ref[...] = total[index * half : (index + 1) * half].astype(out_ref.dtype)


def rows_out(distances, lefts, rights, spans, chunk_rows, sends=(), collective_id=None):
    width, rows = rights[0].shape[0], len(distances) * chunk_rows
    first = distances[0] // len(distances)
    halves = [dtype for k in distances for dtype in half_types(k)]
    in_specs = [
        pl.BlockSpec(
            (rows, left[1]), lambda n, index=left[2]: (first, index), pipeline_mode=pl.Buffered(1)
        )
        for left in lefts
    ] + [
        pl.BlockSpec((256, columns), lambda n, index=index: (n, index)) for columns, index in spans
    ]
    depth = sum(left[1] for left in lefts)
    in_more, out_more, shapes, scratch, params, operands = carried(sends, collective_id)
    outs = pl.pallas_call(
        functools.partial(
            rows_out_kernel, len(lefts), len(halves), [distance for distance, _ in sends]
        ),
        grid=(width // 256,),
        in_specs=in_specs + in_more,
        out_specs=[pl.BlockSpec((chunk_rows // 2, 256), lambda n: (0, n))] * len(halves) + out_more,
        out_shape=[jax.ShapeDtypeStruct((chunk_rows // 2, width), dtype) for dtype in halves] + shapes,
        scratch_shapes=scratch,
        compiler_params=pltpu.CompilerParams(vmem_limit_bytes=60 * 2**20, **params),
        cost_estimate=cost(2 * rows * depth * width, depth * rows // 4, 4.07),
    )(*(left[0] for left in lefts), *rights, *operands)
    parts = {k: (outs[2 * i], outs[2 * i + 1]) for i, k in enumerate(distances)}
    return (parts, outs[len(halves) :]) if sends else parts


def resid_kernel(count, place_ref, *refs):
    inputs, lefts = refs[:2], (refs[2 : 2 + count], refs[2 + count : 2 + 2 * count])
    rights = refs[2 + 2 * count : 1 + 4 * count]
    norm_ref, hidden_ref, resid_ref, sums_ref = refs[1 + 4 * count :]
    half = sums_ref.shape[1] // 2
    blocks = pl.num_programs(0) // 2

    def block(x_ref, left_refs):
        for core, others in (
            (place_ref[1], rights[1:count]), (1 - place_ref[1], rights[count:])
        ):
            start = pl.multiple_of(core * half, half)
            total = lax.dot_general(
                left_refs[0][...], rights[0][pl.ds(start, half), :], NT,
                preferred_element_type=jnp.float32,
            )
            for left_ref, right_ref in zip(left_refs[1:], others):
                total = total + lax.dot_general(
                    left_ref[...], right_ref[...], NT, preferred_element_type=jnp.float32
                )
            sums_ref[:, pl.ds(start, half)] = total
        resid = x_ref[...].astype(jnp.float32) + sums_ref[...]
        hidden_ref[...] = (resid * rms_scale(resid) * norm_ref[...]).astype(jnp.bfloat16)

        @pl.when(pl.program_id(0) < resid_ref.shape[0])
        def _():
            resid_ref[pl.program_id(0)] = resid

    for sequence in range(2):

        @pl.when(pl.program_id(0) // blocks == sequence)
        def _():
            block(inputs[sequence], lefts[sequence])


def residual(place, inputs, heads, own, others, norm, chunk_rows):
    width, count = inputs[0].shape[1], len(heads[0])
    q_width = heads[0][0].shape[1]
    rows, block = 2 * SEQ, min(512, chunk_rows)
    here, there = placed(chunk_rows, block)
    blocks = SEQ // block
    fixed = lambda r, place: (0, 0)
    once = pl.Buffered(1)
    steps = (
        lambda r: jnp.minimum(r, blocks - 1),
        lambda r: jnp.maximum(r - blocks, 0),
    )
    return pl.pallas_call(
        functools.partial(resid_kernel, count),
        grid_spec=pltpu.PrefetchScalarGridSpec(
            num_scalar_prefetch=1,
            grid=(rows // block,),
            in_specs=[
                pl.BlockSpec((block, width), lambda r, place, step=step: here(step(r), place))
                for step in steps
            ]
            + [
                pl.BlockSpec((block, q_width), lambda r, place, step=step: there(step(r), place))
                for step in steps
                for _ in range(count)
            ]
            + [pl.BlockSpec((width, q_width), fixed, pipeline_mode=once)]
            + [pl.BlockSpec(piece.shape, fixed, pipeline_mode=once) for piece in others]
            + [pl.BlockSpec((1, width), fixed)],
            out_specs=[
                pl.BlockSpec((block, width), here),
                pl.BlockSpec((chunk_rows // block, block, width), lambda r, place: (0, 0, 0)),
            ],
            scratch_shapes=[pltpu.VMEM((block, width), jnp.float32)],
        ),
        out_shape=[
            jax.ShapeDtypeStruct((rows, width), jnp.bfloat16),
            jax.ShapeDtypeStruct((chunk_rows // block, block, width), jnp.float32),
        ],
        compiler_params=pltpu.CompilerParams(vmem_limit_bytes=60 * 2**20),
        cost_estimate=cost(2 * rows * width * width, rows * width * 8, 0.46),
    )(place, *inputs, *heads[0], *heads[1], own, *others, norm[None, :])


def input_kernel(count, core_ref, *refs):
    lefts, rights = refs[:count], refs[count : 3 * count - 1]
    x_ref, grad_ref, norm_ref, out_ref, gains_ref, sums_ref = refs[3 * count - 1 :]
    used = lefts[0].shape[1]
    step, steps = pl.program_id(0), pl.num_programs(0)

    def block(others):
        own = rights[0][:, rights[0].shape[1] - used :]
        total = lax.dot_general(lefts[0][...], own, NT, preferred_element_type=jnp.float32)
        for left_ref, right_ref in zip(lefts[1:], others):
            total = total + lax.dot_general(
                left_ref[...], right_ref[...], NT, preferred_element_type=jnp.float32
            )
        sums_ref[:, pl.ds(pl.multiple_of(step * 256, 256), 256)] = total

    for half in range(2):

        @pl.when(step // (steps // 2) == (core_ref[0] if half == 0 else 1 - core_ref[0]))
        def _():
            block(rights[1 + half * (count - 1) : 1 + (half + 1) * (count - 1)])

    @pl.when(step == steps - 1)
    def _():
        gains_ref[...] = jnp.zeros_like(gains_ref)
        for at in range(0, sums_ref.shape[0], 64):
            rows = slice(at, at + 64)
            grads = sums_ref[rows, :]
            inputs = x_ref[rows, :].astype(jnp.float32)
            inverse = rms_scale(inputs)
            normed = inputs * inverse
            gains_ref[...] += jnp.sum((grads * normed).reshape(-1, 8, grads.shape[1]), axis=0)
            out_ref[rows, :] = grad_ref[rows, :] + norm_back(
                grads * norm_ref[...], normed, inverse
            )


def input_back(core, grads, own, others, inputs, grad_resid, norm):
    rows, width = inputs.shape
    count, used = len(grads), grads[0].shape[1]
    steps = width // 256
    whole = lambda n, core: (0, 0)
    near = lambda n, core: (jnp.clip(n - core[0] * (steps // 2), 0, steps // 2 - 1), 0)
    other = lambda n, core: (jnp.clip(n - (1 - core[0]) * (steps // 2), 0, steps // 2 - 1), 0)
    once = pl.Buffered(1)
    return pl.pallas_call(
        functools.partial(input_kernel, count),
        grid_spec=pltpu.PrefetchScalarGridSpec(
            num_scalar_prefetch=1,
            grid=(steps,),
            in_specs=[pl.BlockSpec((rows, used), whole, pipeline_mode=once)] * count
            + [pl.BlockSpec((256, own.shape[1]), lambda n, core: (n, 0))]
            + [pl.BlockSpec((256, used), near)] * (count - 1)
            + [pl.BlockSpec((256, used), other)] * (count - 1)
            + [pl.BlockSpec((rows, width), whole, pipeline_mode=once)] * 2
            + [pl.BlockSpec((1, width), whole)],
            out_specs=[pl.BlockSpec((rows, width), whole), pl.BlockSpec((8, width), whole)],
            scratch_shapes=[pltpu.VMEM((rows, width), jnp.float32)],
        ),
        out_shape=[
            jax.ShapeDtypeStruct((rows, width), jnp.float32),
            jax.ShapeDtypeStruct((8, width), jnp.float32),
        ],
        compiler_params=pltpu.CompilerParams(vmem_limit_bytes=60 * 2**20),
        cost_estimate=cost(2 * rows * used * width * count, rows * width * 20, 0.28),
    )(core, *grads, own, *others, inputs, grad_resid, norm[None, :])


def attention_weights_kernel(inner_ref, *refs):
    out_ref = refs[-1]
    total = jnp.zeros(out_ref.shape, jnp.float32)
    pieces, at = [], 0
    chunk_rows = refs[0].shape[0]
    for ref in refs[:-1]:
        if ref.shape[0] < SEQ:
            pieces.append(ref)
            continue
        at = 0
        for piece in pieces:
            rows = piece.shape[0]
            start = (at // chunk_rows ^ inner_ref[0]) * chunk_rows + at % chunk_rows
            total = total + lax.dot_general(
                piece[...], ref[pl.ds(pl.multiple_of(start, rows), rows), :], TN,
                preferred_element_type=jnp.float32,
            )
            at += rows
        pieces = []
    out_ref[...] = total.astype(jnp.bfloat16)


def out_weights(inner, pieces, attended):
    width, q_width = pieces[0][0].shape[1], attended[0].shape[1]
    whole = lambda n, inner: (0, 0)
    in_specs = []
    for rows in range(2):
        in_specs += [pl.BlockSpec((piece.shape[0], 256), lambda n, inner: (0, n)) for piece in pieces[rows]]
        in_specs.append(pl.BlockSpec((SEQ, q_width), whole))
    return pl.pallas_call(
        attention_weights_kernel,
        grid_spec=pltpu.PrefetchScalarGridSpec(
            num_scalar_prefetch=1,
            grid=(width // 256,),
            in_specs=in_specs,
            out_specs=pl.BlockSpec((256, q_width), lambda n, inner: (n, 0)),
        ),
        out_shape=jax.ShapeDtypeStruct((width, q_width), jnp.bfloat16),
        compiler_params=pltpu.CompilerParams(vmem_limit_bytes=60 * 2**20),
        cost_estimate=cost(4 * SEQ * q_width * width, SEQ * width * 4, 0.35),
    )(inner, *pieces[0], attended[0], *pieces[1], attended[1])


def projection_weights_kernel(norm_ref, *refs):
    inputs, inverses, grads, out_ref = refs[:2], refs[2:4], refs[4:-1], refs[-1]
    total = jnp.zeros(out_ref.shape, jnp.float32)
    chunk_rows = grads[0].shape[0]
    for k, grad_ref in enumerate(grads):
        at = k * chunk_rows
        rows = slice(at % SEQ, at % SEQ + chunk_rows)
        inverse = inverses[at // SEQ][rows, :]
        normed = inputs[at // SEQ][rows, :].astype(jnp.float32) * jnp.concatenate([inverse] * 2, axis=1)
        total = total + lax.dot_general(
            (normed * norm_ref[...]).astype(jnp.bfloat16), grad_ref[...], TN,
            preferred_element_type=jnp.float32,
        )
    out_ref[...] = total.astype(jnp.bfloat16)


def projection_weights(inputs, inverse, norm, grads):
    width, columns = inputs[0].shape[1], grads[0].shape[1]
    whole = lambda n: (0, 0)
    column = lambda n: (0, n)
    return pl.pallas_call(
        projection_weights_kernel,
        grid=(width // 256,),
        in_specs=[pl.BlockSpec((1, 256), column)]
        + [pl.BlockSpec((SEQ, 256), column)] * 2
        + [pl.BlockSpec((SEQ, 128), whole)] * 2
        + [pl.BlockSpec(part.shape, whole) for part in grads],
        out_specs=pl.BlockSpec((256, columns), lambda n: (n, 0)),
        out_shape=jax.ShapeDtypeStruct((width, columns), jnp.bfloat16),
        compiler_params=pltpu.CompilerParams(vmem_limit_bytes=60 * 2**20),
        cost_estimate=cost(4 * SEQ * columns * width, SEQ * width * 4, 0.43),
    )(norm[None, :], *inputs, *inverse, *grads)


def shift(values, distance, count, axis="tensor"):
    return lax.ppermute(values, axis, [(i, i ^ distance) for i in range(count)])


def gather_kernel(src_ref, own_ref, other_ref, send_sems, recv_sems, local_sem):
    rows = src_ref.shape[0]
    half = rows // 2
    x_top, x_bottom = own_ref.at[pl.ds(rows, half)], own_ref.at[pl.ds(rows + half, half)]
    y_top, y_bottom = other_ref.at[pl.ds(0, half)], other_ref.at[pl.ds(half, half)]
    far_top, far_bottom = other_ref.at[pl.ds(rows, half)], other_ref.at[pl.ds(rows + half, half)]
    top, bottom = src_ref.at[pl.ds(0, half)], src_ref.at[pl.ds(half, half)]
    greet([1, 2])

    def copy(index, from_ref, to_ref, distance):
        return pltpu.make_async_remote_copy(
            src_ref=from_ref, dst_ref=to_ref, send_sem=send_sems.at[index],
            recv_sem=recv_sems.at[index], **remote(distance),
        )

    first = [
        copy(0, bottom, x_bottom, 1), copy(1, top, y_top, 2),
        copy(2, top, x_top, 1), copy(3, bottom, y_bottom, 2),
    ]
    for sent in first:
        sent.start()
    local = pltpu.make_async_copy(src_ref, own_ref.at[pl.ds(0, rows)], local_sem.at[0])
    local.start()
    first[1].wait_recv()
    relay_top = copy(4, y_top, far_top, 1)
    relay_top.start()
    first[0].wait_recv()
    relay_bottom = copy(5, x_bottom, far_bottom, 2)
    relay_bottom.start()
    first[2].wait_recv()
    first[3].wait_recv()
    relay_top.wait_recv()
    relay_bottom.wait_recv()
    for sent in first + [relay_top, relay_bottom]:
        sent.wait_send()
    local.wait()


def gather_rows(values, count):
    if count != 4:
        near = gather_near(values, count)
        return [jnp.concatenate(near[i : i + count // 2], axis=0) for i in (0, count // 2)]
    place = pl.BlockSpec(memory_space=pl.ANY)
    rows, width = values.shape
    wide = jax.ShapeDtypeStruct((2 * rows, width), values.dtype)
    return pl.pallas_call(
        gather_kernel,
        in_specs=[place],
        out_specs=[place] * 2,
        out_shape=[wide, wide],
        scratch_shapes=[
            pltpu.SemaphoreType.DMA((6,)), pltpu.SemaphoreType.DMA((6,)),
            pltpu.SemaphoreType.DMA((1,)),
        ],
        compiler_params=pltpu.CompilerParams(collective_id=1, has_side_effects=True),
        cost_estimate=pl.CostEstimate(
            flops=0, bytes_accessed=values.size * 12, transcendentals=0,
            remote_bytes_transferred=values.size * 6,
        ),
    )(values)


def gather_near(values, count):
    if count == 4:
        return [values, shift(values, 1, count), shift(values, 2, count)]
    whole = lax.all_gather(values, "tensor", axis=0)
    mine = lax.axis_index("tensor")
    return [lax.dynamic_index_in_dim(whole, mine ^ k, 0, False) for k in range(count)]


def gather_far(near, count):
    if count != 4:
        return []
    half = near[0].shape[0] // 2
    return [shift(near[2][:half], 1, count), shift(near[1][half:], 2, count)]


def gather_chunks(values, count):
    near = gather_near(values, count)
    far = gather_far(near, count)
    return near + [jnp.concatenate(far, axis=0)] if far else near


def exchange(parts, distances, count):
    return [part if k == 0 else shift(part, k, count) for k, part in zip(distances, parts)]


def column_piece(weights, columns, core):
    half = weights.shape[0] // 2
    return lax.dynamic_slice(
        weights, (core[0] * half, columns[0]), (half, columns[1] - columns[0])
    )


def gather_others(weights, columns, core, sizes):
    piece = column_piece(weights, columns, core)
    pieces = [shift(piece, k, sizes["tensor"]) for k in range(1, sizes["tensor"])]
    return pieces + [shift(piece, 1, sizes["dp"], "dp") for piece in pieces]


def sum_first(parts, count):
    if count != 4:
        return None
    return shift(parts[3][0], 1, count), shift(parts[3][1], 2, count)


def sum_rest(parts, first, count):
    if count != 4:
        mine = lax.axis_index("tensor")
        half, width = parts[0][0].shape
        stacked = jnp.zeros((count, 2 * half, width), jnp.bfloat16)
        for k in range(count):
            term = jnp.concatenate([side.astype(jnp.bfloat16) for side in parts[k]], axis=0)
            stacked = lax.dynamic_update_index_in_dim(stacked, term, mine ^ k, 0)
        total = lax.psum_scatter(
            stacked.reshape(-1, width), "tensor", scatter_dimension=0, tiled=True
        ).astype(jnp.float32)
        none = jnp.zeros((half, width), jnp.bfloat16)
        return [[total[:half], none, none], [total[half:], none, none]]
    far_top, far_bottom = first
    x_top = shift(parts[1][0], 1, count)
    y_bottom = shift(parts[2][1], 2, count)
    y_top = shift((parts[2][0] + far_top.astype(jnp.float32)).astype(jnp.bfloat16), 2, count)
    x_bottom = shift((parts[1][1] + far_bottom.astype(jnp.float32)).astype(jnp.bfloat16), 1, count)
    return [[None, x_top, y_top], [None, x_bottom, y_bottom]]


def added(own_ref, x_ref, y_ref):
    return own_ref[...] + x_ref[...].astype(jnp.float32) + y_ref[...].astype(jnp.float32)


def own_rows_call(kernel, sums, twos, ones, out_shapes, gains):
    half, width = sums[0][0].shape
    block = min(64, half)
    term = pl.BlockSpec((block, width), lambda i: (i, 0))
    both = pl.BlockSpec((2, block, width), lambda i: (0, i, 0))
    out_specs = [both] * len(out_shapes)
    if gains:
        out_specs.append(pl.BlockSpec((8, width), lambda i: (0, 0)))
        out_shapes = out_shapes + [jax.ShapeDtypeStruct((8, width), jnp.float32)]
    return pl.pallas_call(
        kernel,
        grid=(half // block,),
        in_specs=[term] * 6 + [both] * len(twos) + [pl.BlockSpec((1, width), lambda i: (0, 0))] * len(ones),
        out_specs=out_specs,
        out_shape=out_shapes,
        compiler_params=pltpu.CompilerParams(vmem_limit_bytes=60 * 2**20),
        cost_estimate=cost(half * width * 10, half * width * 10, 1.0),
    )(*sums[0], *sums[1], *twos, *ones)


def resid_back_kernel(*refs):
    dy_ref, resid_ref, norm_ref, grad_ref, low_ref, gains_ref = refs[6:]

    @pl.when(pl.program_id(0) == 0)
    def _():
        gains_ref[...] = jnp.zeros_like(gains_ref)

    for side in range(2):
        grads = added(*refs[3 * side : 3 * side + 3])
        resid = resid_ref[side]
        inverse = rms_scale(resid)
        normed = resid * inverse
        gains_ref[...] += jnp.sum((grads * normed).reshape(-1, 8, grads.shape[1]), axis=0)
        total = dy_ref[side].astype(jnp.float32) + norm_back(grads * norm_ref[...], normed, inverse)
        grad_ref[side] = total
        low_ref[side] = total.astype(jnp.bfloat16)


def output_kernel(*refs):
    resid_ref, out_ref = refs[6:]
    for side in range(2):
        out_ref[side] = (resid_ref[side] + added(*refs[3 * side : 3 * side + 3])).astype(jnp.bfloat16)


def total_everywhere(values, sizes):
    for axis, size in sizes.items():
        distance = 1
        while distance < size:
            values = values + shift(values, distance, size, axis)
            distance *= 2
    return values


def after(value, *others):
    return lax.optimization_barrier((value, others))[0]


def pad_columns(values, width):
    return jnp.pad(values, ((0, 0), (0, width - values.shape[1])))


def gather_weights(*parts):
    return lax.all_gather(jnp.concatenate(parts, axis=1), "dp", axis=0, tiled=True)


def scatter_weights(grads):
    return lax.psum_scatter(grads, "dp", scatter_dimension=0, tiled=True)


def per_device(
    sizes,
    tokens,
    segments,
    positions,
    w_query,
    w_key,
    w_value,
    w_out,
    w_gate,
    w_up,
    w_down,
    norm_attn,
    norm_mlp,
    query_gain,
    key_gain,
    out_grad,
):
    count = sizes["tensor"]
    chunk_rows = tokens.shape[0]
    q_width, key_width = w_query.shape[1], w_key.shape[1]
    kv_width = -(-key_width // 128) * 128
    units = w_gate.shape[1] // 2
    mine = lax.axis_index("tensor").astype(jnp.int32).reshape(1)

    half, width = chunk_rows // 2, tokens.shape[1]
    inner_count = count // 2
    inner, flip = mine % inner_count, mine // inner_count
    core = lax.axis_index("dp").astype(jnp.int32).reshape(1) % 2

    def own_first(values):
        pair = values.reshape(2, SEQ)
        return jnp.where(flip == 0, pair, pair[::-1])

    w_attn = gather_weights(
        w_out, w_query, pad_columns(w_key, kv_width), pad_columns(w_value, kv_width)
    )
    rows_in = gather_rows(tokens, count)
    w_mlp = [
        gather_weights(w_gate[:, part], w_up[:, part], w_down[:, part])
        for part in (slice(0, units), slice(units, 2 * units))
    ]
    segments, positions = own_first(segments), own_first(positions)
    out_others = gather_others(after(w_attn, rows_in), (0, q_width), core, sizes)
    inv_rows, queries, key_sides, value_sides, raw = [], [], [], [], []
    tables = rotary_tables(positions.reshape(-1))
    attended, inv_total, heads = [], [], []
    for sequence in range(2):
        rows = rows_in[sequence]
        if sequence == 1:
            rows = after(rows, attended, out_others[: count - 1])
        results = project(
            inner, sequence, rows, chunk_rows, norm_attn, w_attn, tables, query_gain, key_gain, q_width, kv_width
        )
        for kept, result in zip((inv_rows, queries, key_sides, value_sides, raw), results):
            kept.append(result)
        result, inverse = attend(
            queries[sequence], key_sides[sequence], value_sides[sequence], segments[sequence]
        )
        attended.append(result)
        inv_total.append(inverse)
        heads.append(gather_chunks(result, count))
    grad_near = gather_near(after(out_grad, heads), count)
    crossed = [
        heads[sequence][:inner_count] + heads[1 - sequence][inner_count:] for sequence in range(2)
    ]
    rows_two, resid = residual(
        jnp.concatenate([inner, core]), rows_in, crossed, w_attn, out_others, norm_mlp, chunk_rows
    )
    resid = resid.reshape(2, half, width)
    grad_near = after(grad_near, rows_two)
    grad_rows = jnp.concatenate(grad_near + gather_far(grad_near, count), axis=0)

    half_columns = column_piece(after(w_attn, grad_rows), (q_width, w_attn.shape[1]), core)
    in_near = [shift(half_columns, k, count) for k in range(1, count - 1)]
    act_a, grads_a, _ = hidden_units(rows_two, grad_rows, w_mlp[0], None)
    in_near = after(in_near, grads_a)
    grad_a = contract_rows(after(rows_two, in_near), grads_a).astype(jnp.bfloat16)
    if count == 4:
        in_far = [jnp.concatenate(gather_far([half_columns, *in_near], count), axis=0)]
    else:
        in_far = [shift(in_near[0], count - 2, count)]
    act, grads_b, _ = hidden_units(after(rows_two, grad_a, in_far), grad_rows, w_mlp[1], act_a)
    in_others = in_near + in_far
    in_others = in_others + [shift(part, 1, sizes["dp"], "dp") for part in in_others]
    spans = [(2 * units, 0), (2 * units, 0)]

    def two_parts(distances, grads):
        lefts = [(grads, 2 * units, 0), (grads_b, 2 * units, 0)]
        return rows_out(distances, lefts, w_mlp, spans, chunk_rows)

    grad_b = contract_rows(rows_two, grads_b).astype(jnp.bfloat16)
    two = two_parts(list(range(inner_count, count)), after(grads_a, grad_b))
    two_first = sum_first(two, count)
    for k in range(1, inner_count):
        two.update(two_parts([k], after(grads_a, two[count - 1])))
    if count == 4:
        two_rest = sum_rest(two, two_first, count)
        sent = (two_rest[0][1], two_rest[1][2])
        two.update(two_parts([0], after(grads_a, two[1], sent)))
        two_rest[0][0], two_rest[1][0] = two[0]
    else:
        sent = ()
        two.update(two_parts([0], after(grads_a, two[1])))
        two_rest = sum_rest(two, None, count)
    grad_resid, branch_low, gain_mlp = own_rows_call(
        resid_back_kernel,
        two_rest,
        [out_grad.reshape(2, half, width), resid],
        [norm_mlp[None, :]],
        [
            jax.ShapeDtypeStruct((2, half, width), jnp.float32),
            jax.ShapeDtypeStruct((2, half, width), jnp.bfloat16),
        ],
        True,
    )
    branch_low = branch_low.reshape(chunk_rows, width)
    distances = list(range(count))
    heads_out = grad_heads(core, branch_low, w_attn, out_others, q_width, count)
    heads_in = exchange(heads_out, distances, count)
    scattered_a = scatter_weights(after(grad_a, in_far))
    scattered_b = scatter_weights(after(grad_b, scattered_a, two[count - 1]))
    out_act = after(act, heads_out[0])
    out = rows_out(
        distances, [(out_act, units, 0), (out_act, units, 1)], w_mlp, [(units, 2), (units, 2)], chunk_rows
    )
    grad_down = contract_rows(after(grad_rows, out[0], scattered_b, heads_in), act).astype(jnp.bfloat16)
    tops = bottoms = relays = []
    if count == 4:
        top, bottom = after((branch_low[:half], branch_low[half:]), heads_in, out[0])
        tops = [shift(top, 1, count), shift(top, 2, count)]
    sums, raw_grads = [], []
    for sequence in range(2):
        pieces = heads_in[sequence * inner_count : (sequence + 1) * inner_count]
        if sequence == 0:
            pieces = after(pieces, heads_in, grad_down, tops)
            if count == 4:
                bottom = after(bottom, tops)
                bottoms = [shift(bottom, 1, count), shift(bottom, 2, count)]
        else:
            pieces = after(pieces, bottoms, raw_grads)
            if count == 4:
                near_bottom, near_top = after((bottoms[0], tops[1]), bottoms, raw_grads)
                relays = [shift(near_top, 1, count), shift(near_bottom, 2, count)]
        results = attend_back(
            inner, sequence, queries[sequence], key_sides[sequence], value_sides[sequence],
            segments[sequence], attended[sequence], inv_total[sequence], pieces, raw[sequence], tables,
            query_gain, key_gain,
        )
        raw_grads += results[:inner_count]
        sums.append(results[inner_count:])
    raw_in = exchange(raw_grads, distances, count)
    if count == 4:
        branch = (
            [branch_low, tops[0], bottoms[0]],
            [tops[1], bottoms[1], *relays],
        )
    else:
        branch_near = gather_near(branch_low, count)
        branch = (branch_near[:inner_count], branch_near[inner_count:])
    out_first = sum_first(out, count)
    out_rest = sum_rest(out, out_first, count)
    if count == 4:
        out_rest[0][0], out_rest[1][0] = out[0]
    (output,) = own_rows_call(
        output_kernel, out_rest, [resid], [], [jax.ShapeDtypeStruct((2, half, width), jnp.bfloat16)],
        False,
    )
    distances = list(range(count))
    grad_tokens, gain_attn = input_back(
        core, raw_in, w_attn, in_others, tokens, grad_resid.reshape(chunk_rows, width), norm_attn
    )
    grad_w_out = out_weights(inner, after(branch, raw_grads), attended)
    grad_qkv = projection_weights(after(rows_in, raw_grads, relays), inv_rows, norm_attn, raw_grads)

    scattered_down = scatter_weights(after(grad_down, scattered_b, tops))
    scattered_attn = scatter_weights(
        after(
            jnp.concatenate([grad_w_out, grad_qkv], axis=1),
            scattered_down, raw_in,
        )
    )

    gains = [
        jnp.sum(gain_attn, axis=0),
        jnp.sum(gain_mlp, axis=0),
        jnp.sum((sums[0][0] + sums[1][0]).reshape(-1, 64), axis=0),
        jnp.sum((sums[0][1] + sums[1][1]).reshape(-1, 64), axis=0),
    ]
    gains = jnp.concatenate(gains).reshape(-1, 128)
    gains = total_everywhere(gains, sizes).reshape(-1)
    key_at = 2 * q_width
    value_at = key_at + kv_width
    return (
        output.reshape(chunk_rows, width),
        grad_tokens.reshape(chunk_rows, width),
        scattered_attn[:, q_width:key_at].astype(jnp.float32),
        scattered_attn[:, key_at : key_at + key_width].astype(jnp.float32),
        scattered_attn[:, value_at : value_at + key_width].astype(jnp.float32),
        scattered_attn[:, :q_width].astype(jnp.float32),
        jnp.concatenate([scattered_a[:, :units], scattered_b[:, :units]], axis=1).astype(jnp.float32),
        jnp.concatenate([scattered_a[:, units:], scattered_b[:, units:]], axis=1).astype(jnp.float32),
        scattered_down.astype(jnp.float32),
        gains[:width],
        gains[width : 2 * width],
        gains[2 * width : 2 * width + 64],
        gains[2 * width + 64 : 2 * width + 128],
    )


def solution(mesh):
    return jax.shard_map(
        functools.partial(per_device, dict(mesh.shape)),
        mesh=mesh,
        in_specs=(
            P(("dp", "tensor"), None),
            P("dp"),
            P("dp"),
            P("dp", "tensor"),
            P("dp", "tensor"),
            P("dp", "tensor"),
            P("dp", "tensor"),
            P("dp", "tensor"),
            P("dp", "tensor"),
            P("dp", "tensor"),
            P(),
            P(),
            P(),
            P(),
            P(("dp", "tensor"), None),
        ),
        out_specs=(
            P(("dp", "tensor"), None),
            P(("dp", "tensor"), None),
            P("dp", "tensor"),
            P("dp", "tensor"),
            P("dp", "tensor"),
            P("dp", "tensor"),
            P("dp", "tensor"),
            P("dp", "tensor"),
            P("dp", "tensor"),
            P(),
            P(),
            P(),
            P(),
        ),
        check_vma=False,
    )
```

```python
import functools

import jax
import jax.numpy as jnp
from jax import lax
from jax.experimental import pallas as pl
from jax.experimental.pallas import tpu as pltpu
from jax.sharding import PartitionSpec as P

EPS = 1e-05
THETA = 1000000.0
SEQ = 1024
TILE = 256
LOG2E = 1.4426950408889634
MASKED = -1e30
NT = (((1,), (1,)), ((), ()))
TN = (((0,), (0,)), ((), ()))


def rms_scale(values):
    return lax.rsqrt(jnp.mean(values * values, axis=-1, keepdims=True) + EPS)


def norm_back(grad_normed, normed, inverse):
    return inverse * (grad_normed - normed * jnp.mean(grad_normed * normed, axis=-1, keepdims=True))


def rotary_tables(places):
    lane = jnp.arange(128)
    frequency = THETA ** (-(lane % 32).astype(jnp.float32) * 2.0 / 64)
    angles = places.astype(jnp.float32)[:, None] * frequency[None, :]
    sine = jnp.sin(angles)
    upper = (lane % 64 >= 32)[None, :]
    return jnp.cos(angles), jnp.where(upper, 0.0, -sine), jnp.where(upper, sine, 0.0)


def contract_rows(left, right):
    return lax.dot_general(
        left, right, (((0,), (0,)), ((), ())), preferred_element_type=jnp.float32
    )


def half_lanes(rows):
    return lax.broadcasted_iota(jnp.int32, (rows, 128), 1) < 64


def ones_side(side, rows):
    low = half_lanes(rows)
    return jnp.where(low if side == 0 else ~low, 1.0, 0.0).astype(jnp.bfloat16)


def attend_kernel(q_ref, k_ref, v_ref, segc_ref, segr_ref, out_ref, inv_ref, bias_ref, total_ref):
    coef = LOG2E * 64 ** (-0.5)

    @pl.when(pl.program_id(1) == 0)
    def _():
        for at in range(0, SEQ, TILE):
            end = at + TILE
            rows = lax.broadcasted_iota(jnp.int32, (TILE, end), 0) + at
            cols = lax.broadcasted_iota(jnp.int32, (TILE, end), 1)
            allowed = (segc_ref[at:end, :] == segr_ref[0, :, :end]) & (cols <= rows)
            bias_ref[at:end, :end] = jnp.where(allowed, 0.0, MASKED)

    for side in range(2):
        lanes = slice(side * 128, side * 128 + 128)
        for key_at in range(0, SEQ, TILE):
            keys, rows = slice(key_at, key_at + TILE), slice(key_at, SEQ)
            scores = lax.dot_general(
                q_ref[rows, :], k_ref[keys, lanes], NT, preferred_element_type=jnp.float32
            )
            weights = jnp.exp2(scores * coef + bias_ref[rows, keys]).astype(jnp.bfloat16)
            mixed = jnp.concatenate([v_ref[keys, lanes], ones_side(side, TILE)], axis=1)
            part = jnp.dot(weights, mixed, preferred_element_type=jnp.float32)
            if side == 0 and key_at == 0:
                total_ref[...] = part
            else:
                total_ref[rows, :] += part
    inverse = 1.0 / total_ref[:, 128:]
    out_ref[...] = (total_ref[:, :128] * inverse).astype(jnp.bfloat16)
    inv_ref[...] = inverse


def unrotated(grads, raw, cosine, sine_low, sine_high, gain):
    grads = grads * 0.125
    turned = (
        grads * cosine
        - pltpu.roll(grads, 96, 1) * sine_low
        - pltpu.roll(grads, 32, 1) * sine_high
    )
    inverse = head_inverse(raw)
    normed = raw * inverse
    scaled = turned * gain
    change = inverse * (scaled - normed * head_mean(scaled * normed))
    return change, jnp.sum((turned * normed).reshape(-1, 8, 128), axis=0)


def attend_back_kernel(
    chunks, inner_ref, q_ref, k_ref, v_ref, segc_ref, segr_ref, out_ref, inv_ref,
    qraw_ref, kraw_ref, cos_ref, low_ref, high_ref, qgain_ref, kgain_ref, *refs,
):
    pieces, results = refs[:chunks], refs[chunks : 2 * chunks]
    (
        qsum_ref, ksum_ref, bias_ref, mix_ref, qside_ref, gside_ref,
        dq_ref, dk_ref, dv_ref, kpair_ref, vpair_ref, grad_ref,
    ) = refs[2 * chunks :]
    chunk_rows = SEQ // chunks
    q_width = 128 * pl.num_programs(1)
    kv_width = (results[0].shape[1] - q_width) // 2

    def rows_of(k):
        return pl.ds(pl.multiple_of((inner_ref[0] ^ k) * chunk_rows, chunk_rows), chunk_rows)

    def put(values, place):
        dq_ref[...] = values
        for k, result_ref in enumerate(results):
            lanes = pl.ds(pl.multiple_of(place, 128), 128)
            result_ref[:, lanes] = dq_ref[rows_of(k), :].astype(jnp.bfloat16)

    coef = LOG2E * 64 ** (-0.5)
    step = pl.program_id(1)

    @pl.when(step == 0)
    def _():
        for key_at in range(0, SEQ, TILE):
            key_end = key_at + TILE
            keys = lax.broadcasted_iota(jnp.int32, (TILE, SEQ - key_at), 0) + key_at
            rows = lax.broadcasted_iota(jnp.int32, (TILE, SEQ - key_at), 1) + key_at
            allowed = (segc_ref[key_at:key_end, :] == segr_ref[0, :, key_at:]) & (keys <= rows)
            bias_ref[key_at:key_end, key_at:] = jnp.where(allowed, 0.0, MASKED)

    @pl.when((step == 0) & (pl.program_id(0) == 0))
    def _():
        qsum_ref[...] = jnp.zeros_like(qsum_ref)
        ksum_ref[...] = jnp.zeros_like(ksum_ref)

    @pl.when(lax.rem(step, 4) == 0)
    def _():
        kpair_ref[...] = jnp.zeros_like(kpair_ref)
        vpair_ref[...] = jnp.zeros_like(vpair_ref)

    @pl.when(lax.rem(step, 2) == 0)
    def _():
        dk_ref[...] = jnp.zeros_like(dk_ref)
        dv_ref[...] = jnp.zeros_like(dv_ref)

    for k, piece_ref in enumerate(pieces):
        grad_ref[rows_of(k), :] = piece_ref[...].astype(jnp.float32)
    low = half_lanes(SEQ)
    scaled = grad_ref[...] * inv_ref[...]
    scaled_low = scaled.astype(jnp.bfloat16)
    mix_ref[:, :128] = scaled_low
    mix_ref[:, 128:] = -(scaled * out_ref[...].astype(jnp.float32)).astype(jnp.bfloat16)
    none = jnp.zeros_like(scaled_low)
    queries = q_ref[...]
    gside_ref[:, :128] = jnp.where(low, scaled_low, none)
    gside_ref[:, 128:] = jnp.where(low, none, scaled_low)
    qside_ref[:, :128] = jnp.where(low, queries, none)
    qside_ref[:, 128:] = jnp.where(low, none, queries)

    for key_at in range(0, SEQ, TILE):
        keys, rows = slice(key_at, key_at + TILE), slice(key_at, SEQ)
        for side in range(2):
            lanes = slice(side * 128, side * 128 + 128)
            key_side = k_ref[keys, lanes]
            value_side = jnp.concatenate([v_ref[keys, lanes], ones_side(side, TILE)], axis=1)
            scores = lax.dot_general(
                key_side, q_ref[rows, :], NT, preferred_element_type=jnp.float32
            )
            weights = jnp.exp2(scores * coef + bias_ref[keys, rows])
            change = lax.dot_general(
                value_side, mix_ref[rows, :], NT, preferred_element_type=jnp.float32
            )
            grads = (weights * change).astype(jnp.bfloat16)
            dv_ref[keys, :] += jnp.dot(
                weights.astype(jnp.bfloat16),
                gside_ref[rows, lanes],
                preferred_element_type=jnp.float32,
            )
            dk_ref[keys, :] += jnp.dot(
                grads, qside_ref[rows, lanes], preferred_element_type=jnp.float32
            )
            dq = lax.dot_general(grads, key_side, TN, preferred_element_type=jnp.float32)
            if key_at == 0 and side == 0:
                dq_ref[...] = dq
            else:
                dq_ref[rows, :] += dq

    cosine, sine_low, sine_high = cos_ref[...], low_ref[...], high_ref[...]
    change, sums = unrotated(
        dq_ref[...], qraw_ref[...], cosine, sine_low, sine_high, qgain_ref[...]
    )
    qsum_ref[...] += sums
    put(change, step * 128)

    @pl.when(lax.rem(step, 2) == 1)
    def _():
        mine = low == (lax.rem(step, 4) == 1)
        for sum_ref, pair_ref in ((dk_ref, kpair_ref), (dv_ref, vpair_ref)):
            sums = sum_ref[...]
            pair_ref[...] = jnp.where(mine, sums + pltpu.roll(sums, 64, 1), pair_ref[...])

    @pl.when((lax.rem(step, 4) == 3) | (step == pl.num_programs(1) - 1))
    def _():
        change, sums = unrotated(
            kpair_ref[...], kraw_ref[...], cosine, sine_low, sine_high, kgain_ref[...]
        )
        ksum_ref[...] += sums
        put(change, q_width + step // 4 * 128)
        put(vpair_ref[...], q_width + kv_width + step // 4 * 128)


def attention_specs():
    pair = pl.BlockSpec((SEQ, 128), lambda s, p, *_: (s, p))
    group = pl.BlockSpec((SEQ, 256), lambda s, p, *_: (s, p // 2))
    seg_col = pl.BlockSpec((SEQ, 1), lambda s, p, *_: (s, 0))
    seg_row = pl.BlockSpec((1, 1, SEQ), lambda s, p, *_: (s, 0, 0))
    return pair, group, seg_col, seg_row


def attend(queries, key_sides, value_sides, segments):
    rows, width = queries.shape
    sequences, pairs = rows // SEQ, width // 128
    pair, group, seg_col, seg_row = attention_specs()
    work = rows * SEQ * width
    return pl.pallas_call(
        attend_kernel,
        grid=(sequences, pairs),
        in_specs=[pair, group, group, seg_col, seg_row],
        out_specs=[pair, pair],
        out_shape=[
            jax.ShapeDtypeStruct((rows, width), jnp.bfloat16),
            jax.ShapeDtypeStruct((rows, width), jnp.float32),
        ],
        scratch_shapes=[pltpu.VMEM((SEQ, SEQ), jnp.float32), pltpu.VMEM((SEQ, 256), jnp.float32)],
        compiler_params=pltpu.CompilerParams(vmem_limit_bytes=60 * 2**20),
        cost_estimate=pl.CostEstimate(
            flops=42 * work // 10, bytes_accessed=rows * width * 12, transcendentals=work // 128
        ),
    )(queries, key_sides, value_sides, segments[:, None], segments.reshape(sequences, 1, SEQ))


def attend_back(
    inner, sequence, queries, key_sides, value_sides, segments, attended, inverse, pieces, raw, tables,
    query_gain, key_gain,
):
    width = queries.shape[1]
    pairs, chunks, chunk_rows = width // 128, len(pieces), pieces[0].shape[0]
    kv_width = key_sides.shape[1] // 4
    pair, group, seg_col, seg_row = attention_specs()
    kv_raw = pl.BlockSpec((SEQ, 128), lambda s, p, *_: (0, width // 128 + p // 4))
    table = pl.BlockSpec((SEQ, 128), lambda s, p, *_: (sequence, 0))
    gain = pl.BlockSpec((1, 128), lambda s, p, *_: (0, 0))
    total = pl.BlockSpec((8, 128), lambda s, p, *_: (0, 0))
    piece = pl.BlockSpec((chunk_rows, 128), lambda s, p, *_: (0, p))
    columns = width + 2 * kv_width
    work = SEQ * SEQ * width
    flat = pltpu.VMEM((SEQ, 128), jnp.float32)
    return pl.pallas_call(
        functools.partial(attend_back_kernel, chunks),
        grid_spec=pltpu.PrefetchScalarGridSpec(
            num_scalar_prefetch=1,
            grid=(1, pairs),
            in_specs=[pair, group, group, seg_col, seg_row, pair, pair]
            + [pair, kv_raw, table, table, table, gain, gain]
            + [piece] * chunks,
            out_specs=[pl.BlockSpec((chunk_rows, columns), lambda s, p, *_: (0, 0))] * chunks
            + [total, total],
            scratch_shapes=[
                pltpu.VMEM((SEQ, SEQ), jnp.float32),
                pltpu.VMEM((SEQ, 256), jnp.bfloat16),
                pltpu.VMEM((SEQ, 256), jnp.bfloat16),
                pltpu.VMEM((SEQ, 256), jnp.bfloat16),
                flat, flat, flat, flat, flat, flat,
            ],
        ),
        out_shape=[jax.ShapeDtypeStruct((chunk_rows, columns), jnp.bfloat16)] * chunks
        + [jax.ShapeDtypeStruct((8, 128), jnp.float32)] * 2,
        compiler_params=pltpu.CompilerParams(vmem_limit_bytes=60 * 2**20),
        cost_estimate=pl.CostEstimate(
            flops=110 * work // 10, bytes_accessed=SEQ * width * 20, transcendentals=work // 128
        ),
    )(
        inner, queries, key_sides, value_sides, segments[:, None], segments.reshape(-1, 1, SEQ),
        attended, inverse, raw, raw, *tables,
        jnp.tile(query_gain, 2)[None, :], jnp.tile(key_gain, 2)[None, :], *pieces,
    )


def cost(flops, moved, share):
    return pl.CostEstimate(
        flops=int(0.2 * flops / share), bytes_accessed=int(0.2 * moved), transcendentals=0
    )


def head_inverse(values):
    squares = values * values
    high = squares.astype(jnp.bfloat16)
    low = (squares - high.astype(jnp.float32)).astype(jnp.bfloat16)
    return lax.rsqrt(head_sum(high, low) * (1.0 / 64) + EPS)


def head_sum(high, low):
    from_head = lax.broadcasted_iota(jnp.int32, (128, 128), 0) // 64
    to_head = lax.broadcasted_iota(jnp.int32, (128, 128), 1) // 64
    same = jnp.where(from_head == to_head, 1.0, 0.0).astype(jnp.bfloat16)
    return jnp.dot(high, same, preferred_element_type=jnp.float32) + jnp.dot(
        low, same, preferred_element_type=jnp.float32
    )


def head_mean(values):
    high = values.astype(jnp.bfloat16)
    low = (values - high.astype(jnp.float32)).astype(jnp.bfloat16)
    return head_sum(high, low) * (1.0 / 64)


def project_kernel(
    pieces, inner_ref, *refs,
):
    norm_ref, w_ref, cos_ref, low_ref, high_ref, qgain_ref, kgain_ref = refs[pieces : pieces + 7]
    inv_ref, q_ref, k_ref, v_ref, raw_ref = refs[pieces + 7 :]
    inputs = refs[0][...].astype(jnp.float32)
    inverse = rms_scale(inputs)
    hidden = (inputs * inverse * norm_ref[...]).astype(jnp.bfloat16)
    inv_ref[...] = jnp.broadcast_to(inverse, inv_ref.shape)
    q_width, kv_width = q_ref.shape[1], k_ref.shape[1] // 4
    cosine, sine_low, sine_high = cos_ref[...], low_ref[...], high_ref[...]
    lower = lax.broadcasted_iota(jnp.int32, cosine.shape, 1) < 64
    none = jnp.zeros_like(cosine)

    def rotated(raw, gain):
        scaled = raw * head_inverse(raw) * gain
        return (
            scaled * cosine
            + pltpu.roll(scaled, 96, 1) * sine_low
            + pltpu.roll(scaled, 32, 1) * sine_high
        )

    def to_sides(pair, out_ref, at):
        first, second = jnp.where(lower, pair, none), jnp.where(lower, none, pair)
        sides = (first, pltpu.roll(first, 64, 1), pltpu.roll(second, 64, 1), second)
        for index, side in enumerate(sides):
            lanes = slice(at * 4 + index * 128, at * 4 + index * 128 + 128)
            out_ref[:, lanes] = side.astype(jnp.bfloat16)

    wide = jnp.dot(hidden, w_ref[:, q_width:], preferred_element_type=jnp.float32)
    raw_ref[...] = wide[:, : q_width + kv_width]
    for at in range(0, q_width, 128):
        q_ref[:, at : at + 128] = rotated(wide[:, at : at + 128], qgain_ref[...]).astype(
            jnp.bfloat16
        )
    for at in range(0, kv_width, 128):
        place = q_width + at
        to_sides(rotated(wide[:, place : place + 128], kgain_ref[...]), k_ref, at)
        place = q_width + kv_width + at
        to_sides(wide[:, place : place + 128], v_ref, at)


def placed(chunk_rows, block):
    per = chunk_rows // block
    here = lambda r, inner: (r, 0)
    there = lambda r, inner: ((r // per ^ inner[0]) * per + r % per, 0)
    return here, there


def project(inner, sequence, inputs, chunk_rows, norm, weights, tables, query_gain, key_gain, q_width, kv_width):
    rows, width = inputs.shape
    block = chunk_rows
    here, there = placed(block, block)
    fixed = lambda r, mine: (0, 0)
    used = q_width + 2 * kv_width
    table = pl.BlockSpec(
        (block, 128), lambda r, inner: (sequence * (rows // block) + there(r, inner)[0], 0)
    )
    gain = pl.BlockSpec((1, 128), fixed)
    return pl.pallas_call(
        functools.partial(project_kernel, 1),
        grid_spec=pltpu.PrefetchScalarGridSpec(
            num_scalar_prefetch=1,
            grid=(rows // block,),
            in_specs=[
                pl.BlockSpec((block, width), here),
                pl.BlockSpec((1, width), fixed),
                pl.BlockSpec(weights.shape, fixed, pipeline_mode=pl.Buffered(1)),
                table, table, table, gain, gain,
            ],
            out_specs=[
                pl.BlockSpec((block, 128), here),
                pl.BlockSpec((block, q_width), there),
                pl.BlockSpec((block, 4 * kv_width), there),
                pl.BlockSpec((block, 4 * kv_width), there),
                pl.BlockSpec((block, q_width + kv_width), there),
            ],
        ),
        out_shape=[
            jax.ShapeDtypeStruct((rows, 128), jnp.float32),
            jax.ShapeDtypeStruct((rows, q_width), jnp.bfloat16),
            jax.ShapeDtypeStruct((rows, 4 * kv_width), jnp.bfloat16),
            jax.ShapeDtypeStruct((rows, 4 * kv_width), jnp.bfloat16),
            jax.ShapeDtypeStruct((rows, q_width + kv_width), jnp.float32),
        ],
        compiler_params=pltpu.CompilerParams(vmem_limit_bytes=60 * 2**20),
        cost_estimate=cost(2 * rows * width * used, rows * width * 6, 0.22),
    )(
        inner, inputs, norm[None, :], weights, *tables,
        jnp.tile(query_gain, 2)[None, :], jnp.tile(key_gain, 2)[None, :],
    )


def heads_kernel(count, core_ref, grads_ref, *refs):
    rights, outs = refs[: 2 * count - 1], refs[2 * count - 1 :]
    outs[0][...] = jnp.dot(
        grads_ref[...], rights[0][...], preferred_element_type=jnp.float32
    ).astype(jnp.bfloat16)
    half = rights[1].shape[0]
    near = grads_ref[:, pl.ds(pl.multiple_of(core_ref[0] * half, half), half)]
    other = grads_ref[:, pl.ds(pl.multiple_of((1 - core_ref[0]) * half, half), half)]
    for k in range(1, count):
        outs[k][...] = (
            jnp.dot(near, rights[k][...], preferred_element_type=jnp.float32)
            + jnp.dot(other, rights[count - 1 + k][...], preferred_element_type=jnp.float32)
        ).astype(jnp.bfloat16)


def grad_heads(core, grads, own, others, q_width, count):
    rows, width = grads.shape
    fixed = lambda i, core: (0, 0)
    return pl.pallas_call(
        functools.partial(heads_kernel, count),
        grid_spec=pltpu.PrefetchScalarGridSpec(
            num_scalar_prefetch=1,
            grid=(1,),
            in_specs=[pl.BlockSpec(grads.shape, fixed), pl.BlockSpec((width, q_width), fixed)]
            + [pl.BlockSpec(piece.shape, fixed) for piece in others],
            out_specs=[pl.BlockSpec((rows, q_width), fixed)] * count,
        ),
        out_shape=[jax.ShapeDtypeStruct((rows, q_width), jnp.bfloat16)] * count,
        compiler_params=pltpu.CompilerParams(vmem_limit_bytes=60 * 2**20),
        cost_estimate=cost(2 * rows * width * q_width * count, rows * width, 2.67),
    )(core, grads, own, *others)


def peer(distance):
    mine = lax.axis_index("tensor")
    if distance == 1:
        return mine + 1 - 2 * (mine % 2)
    return (mine + 2) % 4 if distance == 2 else 3 - mine


def remote(distance):
    return dict(device_id={"tensor": peer(distance)}, device_id_type=pl.DeviceIdType.MESH)


def greet(distances):
    barrier = pltpu.get_barrier_semaphore()
    for distance in distances:
        pl.semaphore_signal(barrier, inc=1, **remote(distance))
    pl.semaphore_wait(barrier, len(distances))


def hidden_kernel(x_ref, dy_ref, w_ref, filled_ref, act_ref, grads_ref):
    units = act_ref.shape[1]
    inputs, cotangent = x_ref[...], dy_ref[...]
    for at in range(0, units, 256):
        lanes = slice(at, at + 256)
        gate = jnp.dot(inputs, w_ref[:, lanes], preferred_element_type=jnp.float32)
        up = jnp.dot(
            inputs, w_ref[:, units + at : units + at + 256], preferred_element_type=jnp.float32
        )
        change = jnp.dot(
            cotangent, w_ref[:, 2 * units + at : 2 * units + at + 256],
            preferred_element_type=jnp.float32,
        )
        sigmoid = 1.0 / (1.0 + jnp.exp(-gate))
        silu = gate * sigmoid
        act_ref[:, lanes] = (silu * up).astype(jnp.bfloat16)
        grads_ref[:, lanes] = (change * up * sigmoid * (1.0 + gate - silu)).astype(jnp.bfloat16)
        grads_ref[:, units + at : units + at + 256] = (change * silu).astype(jnp.bfloat16)


def hidden_units(inputs, cotangent, weights, filled):
    rows, width = inputs.shape
    units = weights.shape[1] // 3
    block = min(512, rows)
    row = lambda r: (r, 0)
    return pl.pallas_call(
        hidden_kernel,
        grid=(rows // block,),
        in_specs=[
            pl.BlockSpec((block, width), row),
            pl.BlockSpec((block, width), row),
            pl.BlockSpec(weights.shape, lambda r: (0, 0), pipeline_mode=pl.Buffered(1)),
            pl.BlockSpec(memory_space=pl.ANY),
        ],
        out_specs=[
            pl.BlockSpec((block, units), lambda r: (r, 1)),
            pl.BlockSpec((block, 2 * units), row),
        ],
        out_shape=[jax.ShapeDtypeStruct((rows, 2 * units), jnp.bfloat16)] * 2,
        input_output_aliases={3: 0},
        compiler_params=pltpu.CompilerParams(vmem_limit_bytes=60 * 2**20),
        cost_estimate=cost(6 * rows * width * units, (rows * width + width * units) * 6, 0.63),
    )(inputs, cotangent, weights, filled)


def hidden_forward_kernel(x_ref, w_ref, act_ref, factors_ref):
    units = act_ref.shape[1]
    inputs = x_ref[...]
    for at in range(0, units, 256):
        lanes, beside = slice(at, at + 256), slice(units + at, units + at + 256)
        gate = jnp.dot(inputs, w_ref[:, lanes], preferred_element_type=jnp.float32)
        up = jnp.dot(inputs, w_ref[:, beside], preferred_element_type=jnp.float32)
        sigmoid = 1.0 / (1.0 + jnp.exp(-gate))
        silu = gate * sigmoid
        act_ref[:, lanes] = (silu * up).astype(jnp.bfloat16)
        factors_ref[:, lanes] = (up * sigmoid * (1.0 + gate - silu)).astype(jnp.bfloat16)
        factors_ref[:, beside] = silu.astype(jnp.bfloat16)


def hidden_forward(inputs, weights):
    rows, width = inputs.shape
    units = weights.shape[1] // 3
    block = min(512, rows)
    row = lambda r: (r, 0)
    return pl.pallas_call(
        hidden_forward_kernel,
        grid=(rows // block,),
        in_specs=[
            pl.BlockSpec((block, width), row),
            pl.BlockSpec((width, 2 * units), lambda r: (0, 0), pipeline_mode=pl.Buffered(1)),
        ],
        out_specs=[pl.BlockSpec((block, units), row), pl.BlockSpec((block, 2 * units), row)],
        out_shape=[jax.ShapeDtypeStruct((rows, 2 * units), jnp.bfloat16)] * 2,
        compiler_params=pltpu.CompilerParams(vmem_limit_bytes=60 * 2**20),
        cost_estimate=cost(4 * rows * width * units, (rows * width + width * units) * 4, 0.63),
    )(inputs, weights)


def hidden_backward_kernel(dy_ref, factors_ref, w_ref, grads_ref):
    units = w_ref.shape[1]
    cotangent = dy_ref[...]
    for at in range(0, units, 256):
        change = jnp.dot(
            cotangent, w_ref[:, at : at + 256], preferred_element_type=jnp.float32
        )
        for lanes in (slice(at, at + 256), slice(units + at, units + at + 256)):
            grads_ref[:, lanes] = (change * factors_ref[:, lanes].astype(jnp.float32)).astype(
                jnp.bfloat16
            )


def hidden_backward(cotangent, factors, weights):
    rows, width = cotangent.shape
    units = weights.shape[1] // 3
    block = min(512, rows)
    row = lambda r: (r, 0)
    return pl.pallas_call(
        hidden_backward_kernel,
        grid=(rows // block,),
        in_specs=[
            pl.BlockSpec((block, width), row),
            pl.BlockSpec((block, 2 * units), row),
            pl.BlockSpec((width, units), lambda r: (0, 2), pipeline_mode=pl.Buffered(1)),
        ],
        out_specs=pl.BlockSpec((block, 2 * units), row),
        out_shape=jax.ShapeDtypeStruct((rows, 2 * units), jnp.bfloat16),
        compiler_params=pltpu.CompilerParams(vmem_limit_bytes=60 * 2**20),
        cost_estimate=cost(2 * rows * width * units, (rows * width + width * units) * 4, 0.63),
    )(cotangent, factors, weights)


def half_types(distance):
    if distance == 0:
        return (jnp.float32, jnp.float32)
    if distance == 1:
        return (jnp.bfloat16, jnp.float32)
    if distance == 2:
        return (jnp.float32, jnp.bfloat16)
    return (jnp.bfloat16, jnp.bfloat16)


def rows_out_kernel(terms, *refs):
    outs = refs[2 * terms :]
    total = None
    for left_ref, right_ref in zip(refs[:terms], refs[terms : 2 * terms]):
        product = lax.dot_general(
            left_ref[...], right_ref[...], NT, preferred_element_type=jnp.float32
        )
        total = product if total is None else total + product
    half = outs[0].shape[0]
    for index, out_ref in enumerate(outs):
        out_ref[...] = total[index * half : (index + 1) * half].astype(out_ref.dtype)


def rows_out(distances, lefts, rights, spans, chunk_rows):
    width, rows = rights[0].shape[0], len(distances) * chunk_rows
    first = distances[0] // len(distances)
    halves = [dtype for k in distances for dtype in half_types(k)]
    in_specs = [
        pl.BlockSpec(
            (rows, left[1]), lambda n, index=left[2]: (first, index), pipeline_mode=pl.Buffered(1)
        )
        for left in lefts
    ] + [
        pl.BlockSpec((256, columns), lambda n, index=index: (n, index)) for columns, index in spans
    ]
    depth = sum(left[1] for left in lefts)
    outs = pl.pallas_call(
        functools.partial(rows_out_kernel, len(lefts)),
        grid=(width // 256,),
        in_specs=in_specs,
        out_specs=[pl.BlockSpec((chunk_rows // 2, 256), lambda n: (0, n))] * len(halves),
        out_shape=[jax.ShapeDtypeStruct((chunk_rows // 2, width), dtype) for dtype in halves],
        compiler_params=pltpu.CompilerParams(vmem_limit_bytes=60 * 2**20),
        cost_estimate=cost(2 * rows * depth * width, depth * rows // 4, 4.07),
    )(*(left[0] for left in lefts), *rights)
    return {k: (outs[2 * i], outs[2 * i + 1]) for i, k in enumerate(distances)}


def resid_kernel(count, place_ref, *refs):
    inputs, lefts = refs[:2], (refs[2 : 2 + count], refs[2 + count : 2 + 2 * count])
    rights = refs[2 + 2 * count : 1 + 4 * count]
    norm_ref, hidden_ref, resid_ref, sums_ref = refs[1 + 4 * count :]
    half = sums_ref.shape[1] // 2
    blocks = pl.num_programs(0) // 2

    def block(x_ref, left_refs):
        for core, others in (
            (place_ref[1], rights[1:count]), (1 - place_ref[1], rights[count:])
        ):
            start = pl.multiple_of(core * half, half)
            total = lax.dot_general(
                left_refs[0][...], rights[0][pl.ds(start, half), :], NT,
                preferred_element_type=jnp.float32,
            )
            for left_ref, right_ref in zip(left_refs[1:], others):
                total = total + lax.dot_general(
                    left_ref[...], right_ref[...], NT, preferred_element_type=jnp.float32
                )
            sums_ref[:, pl.ds(start, half)] = total
        resid = x_ref[...].astype(jnp.float32) + sums_ref[...]
        hidden_ref[...] = (resid * rms_scale(resid) * norm_ref[...]).astype(jnp.bfloat16)

        @pl.when(pl.program_id(0) < resid_ref.shape[0])
        def _():
            resid_ref[pl.program_id(0)] = resid

    for sequence in range(2):

        @pl.when(pl.program_id(0) // blocks == sequence)
        def _():
            block(inputs[sequence], lefts[sequence])


def residual(place, inputs, heads, own, others, norm, chunk_rows):
    width, count = inputs[0].shape[1], len(heads[0])
    q_width = heads[0][0].shape[1]
    rows, block = 2 * SEQ, min(512, chunk_rows)
    here, there = placed(chunk_rows, block)
    blocks = SEQ // block
    fixed = lambda r, place: (0, 0)
    once = pl.Buffered(1)
    steps = (
        lambda r: jnp.minimum(r, blocks - 1),
        lambda r: jnp.maximum(r - blocks, 0),
    )
    return pl.pallas_call(
        functools.partial(resid_kernel, count),
        grid_spec=pltpu.PrefetchScalarGridSpec(
            num_scalar_prefetch=1,
            grid=(rows // block,),
            in_specs=[
                pl.BlockSpec((block, width), lambda r, place, step=step: here(step(r), place))
                for step in steps
            ]
            + [
                pl.BlockSpec((block, q_width), lambda r, place, step=step: there(step(r), place))
                for step in steps
                for _ in range(count)
            ]
            + [pl.BlockSpec((width, q_width), fixed, pipeline_mode=once)]
            + [pl.BlockSpec(piece.shape, fixed, pipeline_mode=once) for piece in others]
            + [pl.BlockSpec((1, width), fixed)],
            out_specs=[
                pl.BlockSpec((block, width), here),
                pl.BlockSpec((chunk_rows // block, block, width), lambda r, place: (0, 0, 0)),
            ],
            scratch_shapes=[pltpu.VMEM((block, width), jnp.float32)],
        ),
        out_shape=[
            jax.ShapeDtypeStruct((rows, width), jnp.bfloat16),
            jax.ShapeDtypeStruct((chunk_rows // block, block, width), jnp.float32),
        ],
        compiler_params=pltpu.CompilerParams(vmem_limit_bytes=60 * 2**20),
        cost_estimate=cost(2 * rows * width * width, rows * width * 8, 0.46),
    )(place, *inputs, *heads[0], *heads[1], own, *others, norm[None, :])


def input_kernel(count, core_ref, *refs):
    lefts, rights = refs[:count], refs[count : 3 * count - 1]
    x_ref, grad_ref, norm_ref, out_ref, gains_ref, sums_ref = refs[3 * count - 1 :]
    used = lefts[0].shape[1]
    step, steps = pl.program_id(0), pl.num_programs(0)

    def block(others):
        own = rights[0][:, rights[0].shape[1] - used :]
        total = lax.dot_general(lefts[0][...], own, NT, preferred_element_type=jnp.float32)
        for left_ref, right_ref in zip(lefts[1:], others):
            total = total + lax.dot_general(
                left_ref[...], right_ref[...], NT, preferred_element_type=jnp.float32
            )
        sums_ref[:, pl.ds(pl.multiple_of(step * 256, 256), 256)] = total

    for half in range(2):

        @pl.when(step // (steps // 2) == (core_ref[0] if half == 0 else 1 - core_ref[0]))
        def _():
            block(rights[1 + half * (count - 1) : 1 + (half + 1) * (count - 1)])

    @pl.when(step == steps - 1)
    def _():
        gains_ref[...] = jnp.zeros_like(gains_ref)
        for at in range(0, sums_ref.shape[0], 64):
            rows = slice(at, at + 64)
            grads = sums_ref[rows, :]
            inputs = x_ref[rows, :].astype(jnp.float32)
            inverse = rms_scale(inputs)
            normed = inputs * inverse
            gains_ref[...] += jnp.sum((grads * normed).reshape(-1, 8, grads.shape[1]), axis=0)
            out_ref[rows, :] = grad_ref[rows, :] + norm_back(
                grads * norm_ref[...], normed, inverse
            )


def input_back(core, grads, own, others, inputs, grad_resid, norm):
    rows, width = inputs.shape
    count, used = len(grads), grads[0].shape[1]
    steps = width // 256
    whole = lambda n, core: (0, 0)
    near = lambda n, core: (jnp.clip(n - core[0] * (steps // 2), 0, steps // 2 - 1), 0)
    other = lambda n, core: (jnp.clip(n - (1 - core[0]) * (steps // 2), 0, steps // 2 - 1), 0)
    once = pl.Buffered(1)
    return pl.pallas_call(
        functools.partial(input_kernel, count),
        grid_spec=pltpu.PrefetchScalarGridSpec(
            num_scalar_prefetch=1,
            grid=(steps,),
            in_specs=[pl.BlockSpec((rows, used), whole, pipeline_mode=once)] * count
            + [pl.BlockSpec((256, own.shape[1]), lambda n, core: (n, 0))]
            + [pl.BlockSpec((256, used), near)] * (count - 1)
            + [pl.BlockSpec((256, used), other)] * (count - 1)
            + [pl.BlockSpec((rows, width), whole, pipeline_mode=once)] * 2
            + [pl.BlockSpec((1, width), whole)],
            out_specs=[pl.BlockSpec((rows, width), whole), pl.BlockSpec((8, width), whole)],
            scratch_shapes=[pltpu.VMEM((rows, width), jnp.float32)],
        ),
        out_shape=[
            jax.ShapeDtypeStruct((rows, width), jnp.float32),
            jax.ShapeDtypeStruct((8, width), jnp.float32),
        ],
        compiler_params=pltpu.CompilerParams(vmem_limit_bytes=60 * 2**20),
        cost_estimate=cost(2 * rows * used * width * count, rows * width * 20, 0.28),
    )(core, *grads, own, *others, inputs, grad_resid, norm[None, :])


def attention_weights_kernel(inner_ref, *refs):
    out_ref = refs[-1]
    total = jnp.zeros(out_ref.shape, jnp.float32)
    pieces, at = [], 0
    chunk_rows = refs[0].shape[0]
    for ref in refs[:-1]:
        if ref.shape[0] < SEQ:
            pieces.append(ref)
            continue
        at = 0
        for piece in pieces:
            rows = piece.shape[0]
            start = (at // chunk_rows ^ inner_ref[0]) * chunk_rows + at % chunk_rows
            total = total + lax.dot_general(
                piece[...], ref[pl.ds(pl.multiple_of(start, rows), rows), :], TN,
                preferred_element_type=jnp.float32,
            )
            at += rows
        pieces = []
    out_ref[...] = total.astype(jnp.bfloat16)


def out_weights(inner, pieces, attended):
    width, q_width = pieces[0][0].shape[1], attended[0].shape[1]
    whole = lambda n, inner: (0, 0)
    in_specs = []
    for rows in range(2):
        in_specs += [pl.BlockSpec((piece.shape[0], 256), lambda n, inner: (0, n)) for piece in pieces[rows]]
        in_specs.append(pl.BlockSpec((SEQ, q_width), whole))
    return pl.pallas_call(
        attention_weights_kernel,
        grid_spec=pltpu.PrefetchScalarGridSpec(
            num_scalar_prefetch=1,
            grid=(width // 256,),
            in_specs=in_specs,
            out_specs=pl.BlockSpec((256, q_width), lambda n, inner: (n, 0)),
        ),
        out_shape=jax.ShapeDtypeStruct((width, q_width), jnp.bfloat16),
        compiler_params=pltpu.CompilerParams(vmem_limit_bytes=60 * 2**20),
        cost_estimate=cost(4 * SEQ * q_width * width, SEQ * width * 4, 0.35),
    )(inner, *pieces[0], attended[0], *pieces[1], attended[1])


def projection_weights_kernel(norm_ref, *refs):
    inputs, inverses, grads, out_ref = refs[:2], refs[2:4], refs[4:-1], refs[-1]
    total = jnp.zeros(out_ref.shape, jnp.float32)
    chunk_rows = grads[0].shape[0]
    for k, grad_ref in enumerate(grads):
        at = k * chunk_rows
        rows = slice(at % SEQ, at % SEQ + chunk_rows)
        inverse = inverses[at // SEQ][rows, :]
        normed = inputs[at // SEQ][rows, :].astype(jnp.float32) * jnp.concatenate([inverse] * 2, axis=1)
        total = total + lax.dot_general(
            (normed * norm_ref[...]).astype(jnp.bfloat16), grad_ref[...], TN,
            preferred_element_type=jnp.float32,
        )
    out_ref[...] = total.astype(jnp.bfloat16)


def projection_weights(inputs, inverse, norm, grads):
    width, columns = inputs[0].shape[1], grads[0].shape[1]
    whole = lambda n: (0, 0)
    column = lambda n: (0, n)
    return pl.pallas_call(
        projection_weights_kernel,
        grid=(width // 256,),
        in_specs=[pl.BlockSpec((1, 256), column)]
        + [pl.BlockSpec((SEQ, 256), column)] * 2
        + [pl.BlockSpec((SEQ, 128), whole)] * 2
        + [pl.BlockSpec(part.shape, whole) for part in grads],
        out_specs=pl.BlockSpec((256, columns), lambda n: (n, 0)),
        out_shape=jax.ShapeDtypeStruct((width, columns), jnp.bfloat16),
        compiler_params=pltpu.CompilerParams(vmem_limit_bytes=60 * 2**20),
        cost_estimate=cost(4 * SEQ * columns * width, SEQ * width * 4, 0.43),
    )(norm[None, :], *inputs, *inverse, *grads)


def shift(values, distance, count, axis="tensor"):
    return lax.ppermute(values, axis, [(i, i ^ distance) for i in range(count)])


def gather_kernel(src_ref, own_ref, other_ref, send_sems, recv_sems, local_sem):
    rows = src_ref.shape[0]
    half = rows // 2
    x_top, x_bottom = own_ref.at[pl.ds(rows, half)], own_ref.at[pl.ds(rows + half, half)]
    y_top, y_bottom = other_ref.at[pl.ds(0, half)], other_ref.at[pl.ds(half, half)]
    far_top, far_bottom = other_ref.at[pl.ds(rows, half)], other_ref.at[pl.ds(rows + half, half)]
    top, bottom = src_ref.at[pl.ds(0, half)], src_ref.at[pl.ds(half, half)]
    greet([1, 2])

    def copy(index, from_ref, to_ref, distance):
        return pltpu.make_async_remote_copy(
            src_ref=from_ref, dst_ref=to_ref, send_sem=send_sems.at[index],
            recv_sem=recv_sems.at[index], **remote(distance),
        )

    first = [
        copy(0, bottom, x_bottom, 1), copy(1, top, y_top, 2),
        copy(2, top, x_top, 1), copy(3, bottom, y_bottom, 2),
    ]
    for sent in first:
        sent.start()
    local = pltpu.make_async_copy(src_ref, own_ref.at[pl.ds(0, rows)], local_sem.at[0])
    local.start()
    first[1].wait_recv()
    relay_top = copy(4, y_top, far_top, 1)
    relay_top.start()
    first[0].wait_recv()
    relay_bottom = copy(5, x_bottom, far_bottom, 2)
    relay_bottom.start()
    first[2].wait_recv()
    first[3].wait_recv()
    relay_top.wait_recv()
    relay_bottom.wait_recv()
    for sent in first + [relay_top, relay_bottom]:
        sent.wait_send()
    local.wait()


def gather_rows(values, count):
    if count != 4:
        near = gather_near(values, count)
        return [jnp.concatenate(near[i : i + count // 2], axis=0) for i in (0, count // 2)]
    place = pl.BlockSpec(memory_space=pl.ANY)
    rows, width = values.shape
    wide = jax.ShapeDtypeStruct((2 * rows, width), values.dtype)
    return pl.pallas_call(
        gather_kernel,
        in_specs=[place],
        out_specs=[place] * 2,
        out_shape=[wide, wide],
        scratch_shapes=[
            pltpu.SemaphoreType.DMA((6,)), pltpu.SemaphoreType.DMA((6,)),
            pltpu.SemaphoreType.DMA((1,)),
        ],
        compiler_params=pltpu.CompilerParams(collective_id=1, has_side_effects=True),
        cost_estimate=pl.CostEstimate(
            flops=0, bytes_accessed=values.size * 12, transcendentals=0,
            remote_bytes_transferred=values.size * 6,
        ),
    )(values)


def gather_near(values, count):
    if count == 4:
        return [values, shift(values, 1, count), shift(values, 2, count)]
    whole = lax.all_gather(values, "tensor", axis=0)
    mine = lax.axis_index("tensor")
    return [lax.dynamic_index_in_dim(whole, mine ^ k, 0, False) for k in range(count)]


def gather_far(near, count):
    if count != 4:
        return []
    half = near[0].shape[0] // 2
    return [shift(near[2][:half], 1, count), shift(near[1][half:], 2, count)]


def gather_chunks(values, count):
    near = gather_near(values, count)
    far = gather_far(near, count)
    return near + [jnp.concatenate(far, axis=0)] if far else near


def exchange(parts, distances, count):
    return [part if k == 0 else shift(part, k, count) for k, part in zip(distances, parts)]


def column_piece(weights, columns, core):
    half = weights.shape[0] // 2
    return lax.dynamic_slice(
        weights, (core[0] * half, columns[0]), (half, columns[1] - columns[0])
    )


def sum_first(parts, count):
    if count != 4:
        return None
    return shift(parts[3][0], 1, count), shift(parts[3][1], 2, count)


def sum_rest(parts, first, count):
    if count != 4:
        mine = lax.axis_index("tensor")
        half, width = parts[0][0].shape
        stacked = jnp.zeros((count, 2 * half, width), jnp.bfloat16)
        for k in range(count):
            term = jnp.concatenate([side.astype(jnp.bfloat16) for side in parts[k]], axis=0)
            stacked = lax.dynamic_update_index_in_dim(stacked, term, mine ^ k, 0)
        total = lax.psum_scatter(
            stacked.reshape(-1, width), "tensor", scatter_dimension=0, tiled=True
        ).astype(jnp.float32)
        none = jnp.zeros((half, width), jnp.bfloat16)
        return [[total[:half], none, none], [total[half:], none, none]]
    far_top, far_bottom = first
    x_top = shift(parts[1][0], 1, count)
    y_bottom = shift(parts[2][1], 2, count)
    y_top = shift((parts[2][0] + far_top.astype(jnp.float32)).astype(jnp.bfloat16), 2, count)
    x_bottom = shift((parts[1][1] + far_bottom.astype(jnp.float32)).astype(jnp.bfloat16), 1, count)
    return [[None, x_top, y_top], [None, x_bottom, y_bottom]]


def added(own_ref, x_ref, y_ref):
    return own_ref[...] + x_ref[...].astype(jnp.float32) + y_ref[...].astype(jnp.float32)


def own_rows_call(kernel, sums, twos, ones, out_shapes, gains):
    half, width = sums[0][0].shape
    block = min(64, half)
    term = pl.BlockSpec((block, width), lambda i: (i, 0))
    both = pl.BlockSpec((2, block, width), lambda i: (0, i, 0))
    out_specs = [both] * len(out_shapes)
    if gains:
        out_specs.append(pl.BlockSpec((8, width), lambda i: (0, 0)))
        out_shapes = out_shapes + [jax.ShapeDtypeStruct((8, width), jnp.float32)]
    return pl.pallas_call(
        kernel,
        grid=(half // block,),
        in_specs=[term] * 6 + [both] * len(twos) + [pl.BlockSpec((1, width), lambda i: (0, 0))] * len(ones),
        out_specs=out_specs,
        out_shape=out_shapes,
        compiler_params=pltpu.CompilerParams(vmem_limit_bytes=60 * 2**20),
        cost_estimate=cost(half * width * 10, half * width * 10, 1.0),
    )(*sums[0], *sums[1], *twos, *ones)


def resid_back_kernel(*refs):
    dy_ref, resid_ref, norm_ref, grad_ref, low_ref, gains_ref = refs[6:]

    @pl.when(pl.program_id(0) == 0)
    def _():
        gains_ref[...] = jnp.zeros_like(gains_ref)

    for side in range(2):
        grads = added(*refs[3 * side : 3 * side + 3])
        resid = resid_ref[side]
        inverse = rms_scale(resid)
        normed = resid * inverse
        gains_ref[...] += jnp.sum((grads * normed).reshape(-1, 8, grads.shape[1]), axis=0)
        total = dy_ref[side].astype(jnp.float32) + norm_back(grads * norm_ref[...], normed, inverse)
        grad_ref[side] = total
        low_ref[side] = total.astype(jnp.bfloat16)


def output_kernel(*refs):
    resid_ref, out_ref = refs[6:]
    for side in range(2):
        out_ref[side] = (resid_ref[side] + added(*refs[3 * side : 3 * side + 3])).astype(jnp.bfloat16)


def total_everywhere(values, sizes):
    for axis, size in sizes.items():
        distance = 1
        while distance < size:
            values = values + shift(values, distance, size, axis)
            distance *= 2
    return values


def after(value, *others):
    return lax.optimization_barrier((value, others))[0]


def pad_columns(values, width):
    return jnp.pad(values, ((0, 0), (0, width - values.shape[1])))


def gather_weights(*parts):
    return lax.all_gather(jnp.concatenate(parts, axis=1), "dp", axis=0, tiled=True)


def scatter_weights(grads):
    return lax.psum_scatter(grads, "dp", scatter_dimension=0, tiled=True)


def per_device(
    sizes,
    tokens,
    segments,
    positions,
    w_query,
    w_key,
    w_value,
    w_out,
    w_gate,
    w_up,
    w_down,
    norm_attn,
    norm_mlp,
    query_gain,
    key_gain,
    out_grad,
):
    count = sizes["tensor"]
    chunk_rows = tokens.shape[0]
    q_width, key_width = w_query.shape[1], w_key.shape[1]
    kv_width = -(-key_width // 128) * 128
    units = w_gate.shape[1] // 2
    mine = lax.axis_index("tensor").astype(jnp.int32).reshape(1)

    half, width = chunk_rows // 2, tokens.shape[1]
    inner_count = count // 2
    inner, flip = mine % inner_count, mine // inner_count
    core = lax.axis_index("dp").astype(jnp.int32).reshape(1) % 2

    def own_first(values):
        pair = values.reshape(2, SEQ)
        return jnp.where(flip == 0, pair, pair[::-1])

    w_attn = gather_weights(
        w_out, w_query, pad_columns(w_key, kv_width), pad_columns(w_value, kv_width)
    )
    rows_in = gather_rows(tokens, count)
    w_mlp = [
        gather_weights(w_gate[:, part], w_up[:, part], w_down[:, part])
        for part in (slice(0, units), slice(units, 2 * units))
    ]
    segments, positions = own_first(segments), own_first(positions)
    out_near = gather_near(column_piece(after(w_attn, rows_in), (0, q_width), core), count)
    inv_rows, queries, key_sides, value_sides, raw = [], [], [], [], []
    tables = rotary_tables(positions.reshape(-1))
    attended, inv_total, heads = [], [], []
    for sequence in range(2):
        rows = rows_in[sequence]
        if sequence == 1:
            rows = after(rows, attended, out_near)
            out_near = after(out_near, attended)
            out_far = gather_far(out_near, count)
            out_others = out_near[1:] + ([jnp.concatenate(out_far, axis=0)] if out_far else [])
            out_others = out_others + [shift(part, 1, sizes["dp"], "dp") for part in out_others]
        results = project(
            inner, sequence, rows, chunk_rows, norm_attn, w_attn, tables, query_gain, key_gain, q_width, kv_width
        )
        for kept, result in zip((inv_rows, queries, key_sides, value_sides, raw), results):
            kept.append(result)
        result, inverse = attend(
            queries[sequence], key_sides[sequence], value_sides[sequence], segments[sequence]
        )
        attended.append(result)
        inv_total.append(inverse)
        heads.append(gather_chunks(result, count))
    grad_near = gather_near(after(out_grad, heads), count)
    crossed = [
        heads[sequence][:inner_count] + heads[1 - sequence][inner_count:] for sequence in range(2)
    ]
    rows_two, resid = residual(
        jnp.concatenate([inner, core]), rows_in, crossed, w_attn, out_others, norm_mlp, chunk_rows
    )
    resid = resid.reshape(2, half, width)
    grad_near = after(grad_near, rows_two)
    grad_far = gather_far(grad_near, count)
    act_a, factors = hidden_forward(rows_two, w_mlp[0])
    grad_rows = jnp.concatenate(grad_near + after(grad_far, act_a), axis=0)

    grads_a = hidden_backward(grad_rows, factors, w_mlp[0])
    grad_a = contract_rows(rows_two, grads_a).astype(jnp.bfloat16)
    half_columns = column_piece(after(w_attn, grads_a), (q_width, w_attn.shape[1]), core)
    in_near = [shift(half_columns, k, count) for k in range(1, count - 1)]
    if count == 4:
        far_halves = gather_far([half_columns, *in_near], count)
        in_far = [jnp.concatenate(far_halves, axis=0)]
    else:
        far_halves = in_far = [shift(half_columns, count - 1, count)]
    act, grads_b = hidden_units(after(rows_two, grad_a), grad_rows, w_mlp[1], act_a)
    in_others = in_near + in_far
    in_others = in_others + [shift(part, 1, sizes["dp"], "dp") for part in in_others]
    spans = [(2 * units, 0), (2 * units, 0)]

    def two_parts(distances, grads):
        lefts = [(grads, 2 * units, 0), (grads_b, 2 * units, 0)]
        return rows_out(distances, lefts, w_mlp, spans, chunk_rows)

    grad_b = contract_rows(after(rows_two, in_near), grads_b).astype(jnp.bfloat16)
    two = two_parts(list(range(inner_count, count)), after(grads_a, grad_b, far_halves))
    two_first = sum_first(two, count)
    for k in range(1, inner_count):
        two.update(two_parts([k], after(grads_a, two[count - 1])))
    if count == 4:
        two_rest = sum_rest(two, two_first, count)
        sent = (two_rest[0][1], two_rest[1][2])
        two.update(two_parts([0], after(grads_a, two[1])))
        two_rest[0][0], two_rest[1][0] = two[0]
    else:
        sent = ()
        two.update(two_parts([0], after(grads_a, two[1])))
        two_rest = sum_rest(two, None, count)
    grad_resid, branch_low, gain_mlp = own_rows_call(
        resid_back_kernel,
        two_rest,
        [out_grad.reshape(2, half, width), resid],
        [norm_mlp[None, :]],
        [
            jax.ShapeDtypeStruct((2, half, width), jnp.float32),
            jax.ShapeDtypeStruct((2, half, width), jnp.bfloat16),
        ],
        True,
    )
    branch_low = branch_low.reshape(chunk_rows, width)
    distances = list(range(count))
    heads_out = grad_heads(core, branch_low, w_attn, out_others, q_width, count)
    heads_in = exchange(heads_out, distances, count)
    scattered_a = scatter_weights(grad_a)
    scattered_b = scatter_weights(after(grad_b, scattered_a, two[count - 1]))
    out_act = after(act, heads_out[0])
    out = rows_out(
        distances, [(out_act, units, 0), (out_act, units, 1)], w_mlp, [(units, 2), (units, 2)], chunk_rows
    )
    grad_down = contract_rows(after(grad_rows, out[0], scattered_b, heads_in), act).astype(jnp.bfloat16)
    tops = bottoms = relays = []
    if count == 4:
        top, bottom = after((branch_low[:half], branch_low[half:]), heads_in, out[0])
        tops = [shift(top, 1, count), shift(top, 2, count)]
    sums, raw_grads = [], []
    for sequence in range(2):
        pieces = heads_in[sequence * inner_count : (sequence + 1) * inner_count]
        if sequence == 0:
            pieces = after(pieces, heads_in, grad_down, tops)
            if count == 4:
                bottom = after(bottom, tops)
                bottoms = [shift(bottom, 1, count), shift(bottom, 2, count)]
        else:
            pieces = after(pieces, bottoms, raw_grads)
            if count == 4:
                near_bottom, near_top = after((bottoms[0], tops[1]), bottoms, raw_grads)
                relays = [shift(near_top, 1, count), shift(near_bottom, 2, count)]
        results = attend_back(
            inner, sequence, queries[sequence], key_sides[sequence], value_sides[sequence],
            segments[sequence], attended[sequence], inv_total[sequence], pieces, raw[sequence], tables,
            query_gain, key_gain,
        )
        raw_grads += results[:inner_count]
        sums.append(results[inner_count:])
    raw_in = exchange(raw_grads, distances, count)
    if count == 4:
        branch = (
            [branch_low, tops[0], bottoms[0]],
            [tops[1], bottoms[1], *relays],
        )
    else:
        branch_near = gather_near(branch_low, count)
        branch = (branch_near[:inner_count], branch_near[inner_count:])
    out_first = sum_first(out, count)
    grad_w_out = out_weights(inner, after(branch, raw_grads), attended)
    grad_qkv = projection_weights(after(rows_in, raw_grads, relays), inv_rows, norm_attn, raw_grads)

    scattered_down = scatter_weights(after(grad_down, scattered_b, tops))
    scattered_attn = scatter_weights(
        after(
            jnp.concatenate([grad_w_out, grad_qkv], axis=1),
            scattered_down, raw_in,
        )
    )

    grad_w_gate = jnp.concatenate(
        [scattered_a[:, :units], scattered_b[:, :units]], axis=1
    ).astype(jnp.float32)
    grad_w_up = jnp.concatenate(
        [scattered_a[:, units:], scattered_b[:, units:]], axis=1
    ).astype(jnp.float32)
    grad_w_down = scattered_down.astype(jnp.float32)
    grad_tokens, gain_attn = input_back(
        core, after(raw_in, grad_w_gate, grad_w_up), w_attn, in_others, tokens, grad_resid.reshape(chunk_rows, width), norm_attn
    )
    out_rest = sum_rest(out, after(out_first, gain_attn) if count == 4 else None, count)
    if count == 4:
        out_rest[0][0], out_rest[1][0] = out[0]
    gains = [
        jnp.sum(gain_attn, axis=0),
        jnp.sum(gain_mlp, axis=0),
        jnp.sum((sums[0][0] + sums[1][0]).reshape(-1, 64), axis=0),
        jnp.sum((sums[0][1] + sums[1][1]).reshape(-1, 64), axis=0),
    ]
    gains = jnp.concatenate(gains).reshape(-1, 128)
    gains = total_everywhere(gains, sizes).reshape(-1)
    (output,) = own_rows_call(
        output_kernel, after(out_rest, gains), [resid], [], [jax.ShapeDtypeStruct((2, half, width), jnp.bfloat16)],
        False,
    )
    distances = list(range(count))
    key_at = 2 * q_width
    value_at = key_at + kv_width
    return (
        output.reshape(chunk_rows, width),
        grad_tokens.reshape(chunk_rows, width),
        scattered_attn[:, q_width:key_at].astype(jnp.float32),
        scattered_attn[:, key_at : key_at + key_width].astype(jnp.float32),
        scattered_attn[:, value_at : value_at + key_width].astype(jnp.float32),
        scattered_attn[:, :q_width].astype(jnp.float32),
        grad_w_gate,
        grad_w_up,
        grad_w_down,
        gains[:width],
        gains[width : 2 * width],
        gains[2 * width : 2 * width + 64],
        gains[2 * width + 64 : 2 * width + 128],
    )


def solution(mesh):
    return jax.shard_map(
        functools.partial(per_device, dict(mesh.shape)),
        mesh=mesh,
        in_specs=(
            P(("dp", "tensor"), None),
            P("dp"),
            P("dp"),
            P("dp", "tensor"),
            P("dp", "tensor"),
            P("dp", "tensor"),
            P("dp", "tensor"),
            P("dp", "tensor"),
            P("dp", "tensor"),
            P("dp", "tensor"),
            P(),
            P(),
            P(),
            P(),
            P(("dp", "tensor"), None),
        ),
        out_specs=(
            P(("dp", "tensor"), None),
            P(("dp", "tensor"), None),
            P("dp", "tensor"),
            P("dp", "tensor"),
            P("dp", "tensor"),
            P("dp", "tensor"),
            P("dp", "tensor"),
            P("dp", "tensor"),
            P("dp", "tensor"),
            P(),
            P(),
            P(),
            P(),
        ),
        check_vma=False,
    )
```

```python
import functools

import jax
import jax.numpy as jnp
from jax import lax
from jax.experimental import pallas as pl
from jax.experimental.pallas import tpu as pltpu
from jax.sharding import PartitionSpec as P

EPS = 1e-05
THETA = 1000000.0
SEQ = 1024
TILE = 256
LOG2E = 1.4426950408889634
MASKED = -1e30
NT = (((1,), (1,)), ((), ()))
TN = (((0,), (0,)), ((), ()))


def rms_scale(values):
    return lax.rsqrt(jnp.mean(values * values, axis=-1, keepdims=True) + EPS)


def norm_back(grad_normed, normed, inverse):
    return inverse * (grad_normed - normed * jnp.mean(grad_normed * normed, axis=-1, keepdims=True))


def rotary_tables(places):
    lane = jnp.arange(128)
    frequency = THETA ** (-(lane % 32).astype(jnp.float32) * 2.0 / 64)
    angles = places.astype(jnp.float32)[:, None] * frequency[None, :]
    sine = jnp.sin(angles)
    upper = (lane % 64 >= 32)[None, :]
    return jnp.cos(angles), jnp.where(upper, 0.0, -sine), jnp.where(upper, sine, 0.0)


def contract_rows(left, right):
    return lax.dot_general(
        left, right, (((0,), (0,)), ((), ())), preferred_element_type=jnp.float32
    )


def half_lanes(rows):
    return lax.broadcasted_iota(jnp.int32, (rows, 128), 1) < 64


def ones_side(side, rows):
    low = half_lanes(rows)
    return jnp.where(low if side == 0 else ~low, 1.0, 0.0).astype(jnp.bfloat16)


def attend_kernel(q_ref, k_ref, v_ref, segc_ref, segr_ref, out_ref, inv_ref, bias_ref, total_ref):
    coef = LOG2E * 64 ** (-0.5)

    @pl.when(pl.program_id(1) == 0)
    def _():
        for at in range(0, SEQ, TILE):
            end = at + TILE
            rows = lax.broadcasted_iota(jnp.int32, (TILE, end), 0) + at
            cols = lax.broadcasted_iota(jnp.int32, (TILE, end), 1)
            allowed = (segc_ref[at:end, :] == segr_ref[0, :, :end]) & (cols <= rows)
            bias_ref[at:end, :end] = jnp.where(allowed, 0.0, MASKED)

    for side in range(2):
        lanes = slice(side * 128, side * 128 + 128)
        for key_at in range(0, SEQ, TILE):
            keys, rows = slice(key_at, key_at + TILE), slice(key_at, SEQ)
            scores = lax.dot_general(
                q_ref[rows, :], k_ref[keys, lanes], NT, preferred_element_type=jnp.float32
            )
            weights = jnp.exp2(scores * coef + bias_ref[rows, keys]).astype(jnp.bfloat16)
            mixed = jnp.concatenate([v_ref[keys, lanes], ones_side(side, TILE)], axis=1)
            part = jnp.dot(weights, mixed, preferred_element_type=jnp.float32)
            if side == 0 and key_at == 0:
                total_ref[...] = part
            else:
                total_ref[rows, :] += part
    inverse = 1.0 / total_ref[:, 128:]
    out_ref[...] = (total_ref[:, :128] * inverse).astype(jnp.bfloat16)
    inv_ref[...] = inverse


def unrotated(grads, raw, cosine, sine_low, sine_high, gain):
    grads = grads * 0.125
    turned = (
        grads * cosine
        - pltpu.roll(grads, 96, 1) * sine_low
        - pltpu.roll(grads, 32, 1) * sine_high
    )
    inverse = head_inverse(raw)
    normed = raw * inverse
    scaled = turned * gain
    change = inverse * (scaled - normed * head_mean(scaled * normed))
    return change, jnp.sum((turned * normed).reshape(-1, 8, 128), axis=0)


def attend_back_kernel(
    chunks, inner_ref, q_ref, k_ref, v_ref, segc_ref, segr_ref, out_ref, inv_ref,
    qraw_ref, kraw_ref, cos_ref, low_ref, high_ref, qgain_ref, kgain_ref, *refs,
):
    pieces, results = refs[:chunks], refs[chunks : 2 * chunks]
    (
        qsum_ref, ksum_ref, bias_ref, mix_ref, qside_ref, gside_ref,
        dq_ref, dk_ref, dv_ref, kpair_ref, vpair_ref, grad_ref,
    ) = refs[2 * chunks :]
    chunk_rows = SEQ // chunks
    q_width = 128 * pl.num_programs(1)
    kv_width = (results[0].shape[1] - q_width) // 2

    def rows_of(k):
        return pl.ds(pl.multiple_of((inner_ref[0] ^ k) * chunk_rows, chunk_rows), chunk_rows)

    def put(values, place):
        dq_ref[...] = values
        for k, result_ref in enumerate(results):
            lanes = pl.ds(pl.multiple_of(place, 128), 128)
            result_ref[:, lanes] = dq_ref[rows_of(k), :].astype(jnp.bfloat16)

    coef = LOG2E * 64 ** (-0.5)
    step = pl.program_id(1)

    @pl.when(step == 0)
    def _():
        for key_at in range(0, SEQ, TILE):
            key_end = key_at + TILE
            keys = lax.broadcasted_iota(jnp.int32, (TILE, SEQ - key_at), 0) + key_at
            rows = lax.broadcasted_iota(jnp.int32, (TILE, SEQ - key_at), 1) + key_at
            allowed = (segc_ref[key_at:key_end, :] == segr_ref[0, :, key_at:]) & (keys <= rows)
            bias_ref[key_at:key_end, key_at:] = jnp.where(allowed, 0.0, MASKED)

    @pl.when((step == 0) & (pl.program_id(0) == 0))
    def _():
        qsum_ref[...] = jnp.zeros_like(qsum_ref)
        ksum_ref[...] = jnp.zeros_like(ksum_ref)

    @pl.when(lax.rem(step, 4) == 0)
    def _():
        kpair_ref[...] = jnp.zeros_like(kpair_ref)
        vpair_ref[...] = jnp.zeros_like(vpair_ref)

    @pl.when(lax.rem(step, 2) == 0)
    def _():
        dk_ref[...] = jnp.zeros_like(dk_ref)
        dv_ref[...] = jnp.zeros_like(dv_ref)

    for k, piece_ref in enumerate(pieces):
        grad_ref[rows_of(k), :] = piece_ref[...].astype(jnp.float32)
    low = half_lanes(SEQ)
    scaled = grad_ref[...] * inv_ref[...]
    scaled_low = scaled.astype(jnp.bfloat16)
    mix_ref[:, :128] = scaled_low
    mix_ref[:, 128:] = -(scaled * out_ref[...].astype(jnp.float32)).astype(jnp.bfloat16)
    none = jnp.zeros_like(scaled_low)
    queries = q_ref[...]
    gside_ref[:, :128] = jnp.where(low, scaled_low, none)
    gside_ref[:, 128:] = jnp.where(low, none, scaled_low)
    qside_ref[:, :128] = jnp.where(low, queries, none)
    qside_ref[:, 128:] = jnp.where(low, none, queries)

    for key_at in range(0, SEQ, TILE):
        keys, rows = slice(key_at, key_at + TILE), slice(key_at, SEQ)
        for side in range(2):
            lanes = slice(side * 128, side * 128 + 128)
            key_side = k_ref[keys, lanes]
            value_side = jnp.concatenate([v_ref[keys, lanes], ones_side(side, TILE)], axis=1)
            scores = lax.dot_general(
                key_side, q_ref[rows, :], NT, preferred_element_type=jnp.float32
            )
            weights = jnp.exp2(scores * coef + bias_ref[keys, rows])
            change = lax.dot_general(
                value_side, mix_ref[rows, :], NT, preferred_element_type=jnp.float32
            )
            grads = (weights * change).astype(jnp.bfloat16)
            dv_ref[keys, :] += jnp.dot(
                weights.astype(jnp.bfloat16),
                gside_ref[rows, lanes],
                preferred_element_type=jnp.float32,
            )
            dk_ref[keys, :] += jnp.dot(
                grads, qside_ref[rows, lanes], preferred_element_type=jnp.float32
            )
            dq = lax.dot_general(grads, key_side, TN, preferred_element_type=jnp.float32)
            if key_at == 0 and side == 0:
                dq_ref[...] = dq
            else:
                dq_ref[rows, :] += dq

    cosine, sine_low, sine_high = cos_ref[...], low_ref[...], high_ref[...]
    change, sums = unrotated(
        dq_ref[...], qraw_ref[...], cosine, sine_low, sine_high, qgain_ref[...]
    )
    qsum_ref[...] += sums
    put(change, step * 128)

    @pl.when(lax.rem(step, 2) == 1)
    def _():
        mine = low == (lax.rem(step, 4) == 1)
        for sum_ref, pair_ref in ((dk_ref, kpair_ref), (dv_ref, vpair_ref)):
            sums = sum_ref[...]
            pair_ref[...] = jnp.where(mine, sums + pltpu.roll(sums, 64, 1), pair_ref[...])

    @pl.when((lax.rem(step, 4) == 3) | (step == pl.num_programs(1) - 1))
    def _():
        change, sums = unrotated(
            kpair_ref[...], kraw_ref[...], cosine, sine_low, sine_high, kgain_ref[...]
        )
        ksum_ref[...] += sums
        put(change, q_width + step // 4 * 128)
        put(vpair_ref[...], q_width + kv_width + step // 4 * 128)


def attention_specs():
    pair = pl.BlockSpec((SEQ, 128), lambda s, p, *_: (s, p))
    group = pl.BlockSpec((SEQ, 256), lambda s, p, *_: (s, p // 2))
    seg_col = pl.BlockSpec((SEQ, 1), lambda s, p, *_: (s, 0))
    seg_row = pl.BlockSpec((1, 1, SEQ), lambda s, p, *_: (s, 0, 0))
    return pair, group, seg_col, seg_row


def attend(queries, key_sides, value_sides, segments):
    rows, width = queries.shape
    sequences, pairs = rows // SEQ, width // 128
    pair, group, seg_col, seg_row = attention_specs()
    work = rows * SEQ * width
    return pl.pallas_call(
        attend_kernel,
        grid=(sequences, pairs),
        in_specs=[pair, group, group, seg_col, seg_row],
        out_specs=[pair, pair],
        out_shape=[
            jax.ShapeDtypeStruct((rows, width), jnp.bfloat16),
            jax.ShapeDtypeStruct((rows, width), jnp.float32),
        ],
        scratch_shapes=[pltpu.VMEM((SEQ, SEQ), jnp.float32), pltpu.VMEM((SEQ, 256), jnp.float32)],
        compiler_params=pltpu.CompilerParams(vmem_limit_bytes=60 * 2**20),
        cost_estimate=pl.CostEstimate(
            flops=42 * work // 10, bytes_accessed=rows * width * 12, transcendentals=work // 128
        ),
    )(queries, key_sides, value_sides, segments[:, None], segments.reshape(sequences, 1, SEQ))


def attend_back(
    inner, sequence, queries, key_sides, value_sides, segments, attended, inverse, pieces, raw, tables,
    query_gain, key_gain,
):
    width = queries.shape[1]
    pairs, chunks, chunk_rows = width // 128, len(pieces), pieces[0].shape[0]
    kv_width = key_sides.shape[1] // 4
    pair, group, seg_col, seg_row = attention_specs()
    kv_raw = pl.BlockSpec((SEQ, 128), lambda s, p, *_: (0, width // 128 + p // 4))
    table = pl.BlockSpec((SEQ, 128), lambda s, p, *_: (sequence, 0))
    gain = pl.BlockSpec((1, 128), lambda s, p, *_: (0, 0))
    total = pl.BlockSpec((8, 128), lambda s, p, *_: (0, 0))
    piece = pl.BlockSpec((chunk_rows, 128), lambda s, p, *_: (0, p))
    columns = width + 2 * kv_width
    work = SEQ * SEQ * width
    flat = pltpu.VMEM((SEQ, 128), jnp.float32)
    return pl.pallas_call(
        functools.partial(attend_back_kernel, chunks),
        grid_spec=pltpu.PrefetchScalarGridSpec(
            num_scalar_prefetch=1,
            grid=(1, pairs),
            in_specs=[pair, group, group, seg_col, seg_row, pair, pair]
            + [pair, kv_raw, table, table, table, gain, gain]
            + [piece] * chunks,
            out_specs=[pl.BlockSpec((chunk_rows, columns), lambda s, p, *_: (0, 0))] * chunks
            + [total, total],
            scratch_shapes=[
                pltpu.VMEM((SEQ, SEQ), jnp.float32),
                pltpu.VMEM((SEQ, 256), jnp.bfloat16),
                pltpu.VMEM((SEQ, 256), jnp.bfloat16),
                pltpu.VMEM((SEQ, 256), jnp.bfloat16),
                flat, flat, flat, flat, flat, flat,
            ],
        ),
        out_shape=[jax.ShapeDtypeStruct((chunk_rows, columns), jnp.bfloat16)] * chunks
        + [jax.ShapeDtypeStruct((8, 128), jnp.float32)] * 2,
        compiler_params=pltpu.CompilerParams(vmem_limit_bytes=60 * 2**20),
        cost_estimate=pl.CostEstimate(
            flops=110 * work // 10, bytes_accessed=SEQ * width * 20, transcendentals=work // 128
        ),
    )(
        inner, queries, key_sides, value_sides, segments[:, None], segments.reshape(-1, 1, SEQ),
        attended, inverse, raw, raw, *tables,
        jnp.tile(query_gain, 2)[None, :], jnp.tile(key_gain, 2)[None, :], *pieces,
    )


def cost(flops, moved, share):
    return pl.CostEstimate(
        flops=int(0.2 * flops / share), bytes_accessed=int(0.2 * moved), transcendentals=0
    )


def head_inverse(values):
    squares = values * values
    high = squares.astype(jnp.bfloat16)
    low = (squares - high.astype(jnp.float32)).astype(jnp.bfloat16)
    return lax.rsqrt(head_sum(high, low) * (1.0 / 64) + EPS)


def head_sum(high, low):
    from_head = lax.broadcasted_iota(jnp.int32, (128, 128), 0) // 64
    to_head = lax.broadcasted_iota(jnp.int32, (128, 128), 1) // 64
    same = jnp.where(from_head == to_head, 1.0, 0.0).astype(jnp.bfloat16)
    return jnp.dot(high, same, preferred_element_type=jnp.float32) + jnp.dot(
        low, same, preferred_element_type=jnp.float32
    )


def head_mean(values):
    high = values.astype(jnp.bfloat16)
    low = (values - high.astype(jnp.float32)).astype(jnp.bfloat16)
    return head_sum(high, low) * (1.0 / 64)


def project_kernel(
    pieces, inner_ref, *refs,
):
    norm_ref, w_ref, cos_ref, low_ref, high_ref, qgain_ref, kgain_ref = refs[pieces : pieces + 7]
    inv_ref, q_ref, k_ref, v_ref, raw_ref = refs[pieces + 7 :]
    inputs = refs[0][...].astype(jnp.float32)
    inverse = rms_scale(inputs)
    hidden = (inputs * inverse * norm_ref[...]).astype(jnp.bfloat16)
    inv_ref[...] = jnp.broadcast_to(inverse, inv_ref.shape)
    q_width, kv_width = q_ref.shape[1], k_ref.shape[1] // 4
    cosine, sine_low, sine_high = cos_ref[...], low_ref[...], high_ref[...]
    lower = lax.broadcasted_iota(jnp.int32, cosine.shape, 1) < 64
    none = jnp.zeros_like(cosine)

    def rotated(raw, gain):
        scaled = raw * head_inverse(raw) * gain
        return (
            scaled * cosine
            + pltpu.roll(scaled, 96, 1) * sine_low
            + pltpu.roll(scaled, 32, 1) * sine_high
        )

    def to_sides(pair, out_ref, at):
        first, second = jnp.where(lower, pair, none), jnp.where(lower, none, pair)
        sides = (first, pltpu.roll(first, 64, 1), pltpu.roll(second, 64, 1), second)
        for index, side in enumerate(sides):
            lanes = slice(at * 4 + index * 128, at * 4 + index * 128 + 128)
            out_ref[:, lanes] = side.astype(jnp.bfloat16)

    wide = jnp.dot(hidden, w_ref[:, q_width:], preferred_element_type=jnp.float32)
    raw_ref[...] = wide[:, : q_width + kv_width]
    for at in range(0, q_width, 128):
        q_ref[:, at : at + 128] = rotated(wide[:, at : at + 128], qgain_ref[...]).astype(
            jnp.bfloat16
        )
    for at in range(0, kv_width, 128):
        place = q_width + at
        to_sides(rotated(wide[:, place : place + 128], kgain_ref[...]), k_ref, at)
        place = q_width + kv_width + at
        to_sides(wide[:, place : place + 128], v_ref, at)


def placed(chunk_rows, block):
    per = chunk_rows // block
    here = lambda r, inner: (r, 0)
    there = lambda r, inner: ((r // per ^ inner[0]) * per + r % per, 0)
    return here, there


def project(inner, sequence, inputs, chunk_rows, norm, weights, tables, query_gain, key_gain, q_width, kv_width):
    rows, width = inputs.shape
    block = chunk_rows
    here, there = placed(block, block)
    fixed = lambda r, mine: (0, 0)
    used = q_width + 2 * kv_width
    table = pl.BlockSpec(
        (block, 128), lambda r, inner: (sequence * (rows // block) + there(r, inner)[0], 0)
    )
    gain = pl.BlockSpec((1, 128), fixed)
    return pl.pallas_call(
        functools.partial(project_kernel, 1),
        grid_spec=pltpu.PrefetchScalarGridSpec(
            num_scalar_prefetch=1,
            grid=(rows // block,),
            in_specs=[
                pl.BlockSpec((block, width), here),
                pl.BlockSpec((1, width), fixed),
                pl.BlockSpec(weights.shape, fixed, pipeline_mode=pl.Buffered(1)),
                table, table, table, gain, gain,
            ],
            out_specs=[
                pl.BlockSpec((block, 128), here),
                pl.BlockSpec((block, q_width), there),
                pl.BlockSpec((block, 4 * kv_width), there),
                pl.BlockSpec((block, 4 * kv_width), there),
                pl.BlockSpec((block, q_width + kv_width), there),
            ],
        ),
        out_shape=[
            jax.ShapeDtypeStruct((rows, 128), jnp.float32),
            jax.ShapeDtypeStruct((rows, q_width), jnp.bfloat16),
            jax.ShapeDtypeStruct((rows, 4 * kv_width), jnp.bfloat16),
            jax.ShapeDtypeStruct((rows, 4 * kv_width), jnp.bfloat16),
            jax.ShapeDtypeStruct((rows, q_width + kv_width), jnp.float32),
        ],
        compiler_params=pltpu.CompilerParams(vmem_limit_bytes=60 * 2**20),
        cost_estimate=cost(2 * rows * width * used, rows * width * 6, 0.22),
    )(
        inner, inputs, norm[None, :], weights, *tables,
        jnp.tile(query_gain, 2)[None, :], jnp.tile(key_gain, 2)[None, :],
    )


def heads_kernel(count, core_ref, grads_ref, *refs):
    rights, outs = refs[: 2 * count - 1], refs[2 * count - 1 :]
    outs[0][...] = jnp.dot(
        grads_ref[...], rights[0][...], preferred_element_type=jnp.float32
    ).astype(jnp.bfloat16)
    half = rights[1].shape[0]
    near = grads_ref[:, pl.ds(pl.multiple_of(core_ref[0] * half, half), half)]
    other = grads_ref[:, pl.ds(pl.multiple_of((1 - core_ref[0]) * half, half), half)]
    for k in range(1, count):
        outs[k][...] = (
            jnp.dot(near, rights[k][...], preferred_element_type=jnp.float32)
            + jnp.dot(other, rights[count - 1 + k][...], preferred_element_type=jnp.float32)
        ).astype(jnp.bfloat16)


def grad_heads(core, grads, own, others, q_width, count):
    rows, width = grads.shape
    fixed = lambda i, core: (0, 0)
    return pl.pallas_call(
        functools.partial(heads_kernel, count),
        grid_spec=pltpu.PrefetchScalarGridSpec(
            num_scalar_prefetch=1,
            grid=(1,),
            in_specs=[pl.BlockSpec(grads.shape, fixed), pl.BlockSpec((width, q_width), fixed)]
            + [pl.BlockSpec(piece.shape, fixed) for piece in others],
            out_specs=[pl.BlockSpec((rows, q_width), fixed)] * count,
        ),
        out_shape=[jax.ShapeDtypeStruct((rows, q_width), jnp.bfloat16)] * count,
        compiler_params=pltpu.CompilerParams(vmem_limit_bytes=60 * 2**20),
        cost_estimate=cost(2 * rows * width * q_width * count, rows * width, 2.67),
    )(core, grads, own, *others)


def peer(distance):
    mine = lax.axis_index("tensor")
    if distance == 1:
        return mine + 1 - 2 * (mine % 2)
    return (mine + 2) % 4 if distance == 2 else 3 - mine


def remote(distance):
    return dict(device_id={"tensor": peer(distance)}, device_id_type=pl.DeviceIdType.MESH)


def greet(distances):
    barrier = pltpu.get_barrier_semaphore()
    for distance in distances:
        pl.semaphore_signal(barrier, inc=1, **remote(distance))
    pl.semaphore_wait(barrier, len(distances))


def hidden_kernel(x_ref, dy_ref, w_ref, filled_ref, act_ref, grads_ref):
    units = act_ref.shape[1]
    inputs, cotangent = x_ref[...], dy_ref[...]
    for at in range(0, units, 256):
        lanes = slice(at, at + 256)
        gate = jnp.dot(inputs, w_ref[:, lanes], preferred_element_type=jnp.float32)
        up = jnp.dot(
            inputs, w_ref[:, units + at : units + at + 256], preferred_element_type=jnp.float32
        )
        change = jnp.dot(
            cotangent, w_ref[:, 2 * units + at : 2 * units + at + 256],
            preferred_element_type=jnp.float32,
        )
        sigmoid = 1.0 / (1.0 + jnp.exp(-gate))
        silu = gate * sigmoid
        act_ref[:, lanes] = (silu * up).astype(jnp.bfloat16)
        grads_ref[:, lanes] = (change * up * sigmoid * (1.0 + gate - silu)).astype(jnp.bfloat16)
        grads_ref[:, units + at : units + at + 256] = (change * silu).astype(jnp.bfloat16)


def hidden_units(inputs, cotangent, weights, filled):
    rows, width = inputs.shape
    units = weights.shape[1] // 3
    block = min(512, rows)
    row = lambda r: (r, 0)
    return pl.pallas_call(
        hidden_kernel,
        grid=(rows // block,),
        in_specs=[
            pl.BlockSpec((block, width), row),
            pl.BlockSpec((block, width), row),
            pl.BlockSpec(weights.shape, lambda r: (0, 0), pipeline_mode=pl.Buffered(1)),
            pl.BlockSpec(memory_space=pl.ANY),
        ],
        out_specs=[
            pl.BlockSpec((block, units), lambda r: (r, 1)),
            pl.BlockSpec((block, 2 * units), row),
        ],
        out_shape=[jax.ShapeDtypeStruct((rows, 2 * units), jnp.bfloat16)] * 2,
        input_output_aliases={3: 0},
        compiler_params=pltpu.CompilerParams(vmem_limit_bytes=60 * 2**20),
        cost_estimate=cost(6 * rows * width * units, (rows * width + width * units) * 6, 0.63),
    )(inputs, cotangent, weights, filled)


def hidden_forward_kernel(x_ref, w_ref, act_ref, factors_ref):
    units = act_ref.shape[1]
    inputs = x_ref[...]
    for at in range(0, units, 256):
        lanes, beside = slice(at, at + 256), slice(units + at, units + at + 256)
        gate = jnp.dot(inputs, w_ref[:, lanes], preferred_element_type=jnp.float32)
        up = jnp.dot(inputs, w_ref[:, beside], preferred_element_type=jnp.float32)
        sigmoid = 1.0 / (1.0 + jnp.exp(-gate))
        silu = gate * sigmoid
        act_ref[:, lanes] = (silu * up).astype(jnp.bfloat16)
        factors_ref[:, lanes] = (up * sigmoid * (1.0 + gate - silu)).astype(jnp.bfloat16)
        factors_ref[:, beside] = silu.astype(jnp.bfloat16)


def hidden_forward(inputs, weights):
    rows, width = inputs.shape
    units = weights.shape[1] // 3
    block = min(512, rows)
    row = lambda r: (r, 0)
    return pl.pallas_call(
        hidden_forward_kernel,
        grid=(rows // block,),
        in_specs=[
            pl.BlockSpec((block, width), row),
            pl.BlockSpec((width, 2 * units), lambda r: (0, 0), pipeline_mode=pl.Buffered(1)),
        ],
        out_specs=[pl.BlockSpec((block, units), row), pl.BlockSpec((block, 2 * units), row)],
        out_shape=[jax.ShapeDtypeStruct((rows, 2 * units), jnp.bfloat16)] * 2,
        compiler_params=pltpu.CompilerParams(vmem_limit_bytes=60 * 2**20),
        cost_estimate=cost(4 * rows * width * units, (rows * width + width * units) * 4, 0.63),
    )(inputs, weights)


def hidden_backward_kernel(dy_ref, factors_ref, w_ref, grads_ref):
    units = w_ref.shape[1]
    cotangent = dy_ref[...]
    for at in range(0, units, 256):
        change = jnp.dot(
            cotangent, w_ref[:, at : at + 256], preferred_element_type=jnp.float32
        )
        for lanes in (slice(at, at + 256), slice(units + at, units + at + 256)):
            grads_ref[:, lanes] = (change * factors_ref[:, lanes].astype(jnp.float32)).astype(
                jnp.bfloat16
            )


def hidden_backward(cotangent, factors, weights):
    rows, width = cotangent.shape
    units = weights.shape[1] // 3
    block = min(512, rows)
    row = lambda r: (r, 0)
    return pl.pallas_call(
        hidden_backward_kernel,
        grid=(rows // block,),
        in_specs=[
            pl.BlockSpec((block, width), row),
            pl.BlockSpec((block, 2 * units), row),
            pl.BlockSpec((width, units), lambda r: (0, 2), pipeline_mode=pl.Buffered(1)),
        ],
        out_specs=pl.BlockSpec((block, 2 * units), row),
        out_shape=jax.ShapeDtypeStruct((rows, 2 * units), jnp.bfloat16),
        compiler_params=pltpu.CompilerParams(vmem_limit_bytes=60 * 2**20),
        cost_estimate=cost(2 * rows * width * units, (rows * width + width * units) * 4, 0.63),
    )(cotangent, factors, weights)


def half_types(distance):
    if distance == 0:
        return (jnp.float32, jnp.float32)
    if distance == 1:
        return (jnp.bfloat16, jnp.float32)
    if distance == 2:
        return (jnp.float32, jnp.bfloat16)
    return (jnp.bfloat16, jnp.bfloat16)


def rows_out_kernel(terms, *refs):
    outs = refs[2 * terms :]
    total = None
    for left_ref, right_ref in zip(refs[:terms], refs[terms : 2 * terms]):
        product = lax.dot_general(
            left_ref[...], right_ref[...], NT, preferred_element_type=jnp.float32
        )
        total = product if total is None else total + product
    half = outs[0].shape[0]
    for index, out_ref in enumerate(outs):
        out_ref[...] = total[index * half : (index + 1) * half].astype(out_ref.dtype)


def rows_out(distances, lefts, rights, spans, chunk_rows):
    width, rows = rights[0].shape[0], len(distances) * chunk_rows
    first = distances[0] // len(distances)
    halves = [dtype for k in distances for dtype in half_types(k)]
    in_specs = [
        pl.BlockSpec(
            (rows, left[1]), lambda n, index=left[2]: (first, index), pipeline_mode=pl.Buffered(1)
        )
        for left in lefts
    ] + [
        pl.BlockSpec((256, columns), lambda n, index=index: (n, index)) for columns, index in spans
    ]
    depth = sum(left[1] for left in lefts)
    outs = pl.pallas_call(
        functools.partial(rows_out_kernel, len(lefts)),
        grid=(width // 256,),
        in_specs=in_specs,
        out_specs=[pl.BlockSpec((chunk_rows // 2, 256), lambda n: (0, n))] * len(halves),
        out_shape=[jax.ShapeDtypeStruct((chunk_rows // 2, width), dtype) for dtype in halves],
        compiler_params=pltpu.CompilerParams(vmem_limit_bytes=60 * 2**20),
        cost_estimate=cost(2 * rows * depth * width, depth * rows // 4, 4.07),
    )(*(left[0] for left in lefts), *rights)
    return {k: (outs[2 * i], outs[2 * i + 1]) for i, k in enumerate(distances)}


def resid_kernel(count, place_ref, *refs):
    inputs, lefts = refs[:2], (refs[2 : 2 + count], refs[2 + count : 2 + 2 * count])
    rights = refs[2 + 2 * count : 1 + 4 * count]
    norm_ref, hidden_ref, resid_ref, sums_ref = refs[1 + 4 * count :]
    half = sums_ref.shape[1] // 2
    blocks = pl.num_programs(0) // 2

    def block(x_ref, left_refs):
        for core, others in (
            (place_ref[1], rights[1:count]), (1 - place_ref[1], rights[count:])
        ):
            start = pl.multiple_of(core * half, half)
            total = lax.dot_general(
                left_refs[0][...], rights[0][pl.ds(start, half), :], NT,
                preferred_element_type=jnp.float32,
            )
            for left_ref, right_ref in zip(left_refs[1:], others):
                total = total + lax.dot_general(
                    left_ref[...], right_ref[...], NT, preferred_element_type=jnp.float32
                )
            sums_ref[:, pl.ds(start, half)] = total
        resid = x_ref[...].astype(jnp.float32) + sums_ref[...]
        hidden_ref[...] = (resid * rms_scale(resid) * norm_ref[...]).astype(jnp.bfloat16)

        @pl.when(pl.program_id(0) < resid_ref.shape[0])
        def _():
            resid_ref[pl.program_id(0)] = resid

    for sequence in range(2):

        @pl.when(pl.program_id(0) // blocks == sequence)
        def _():
            block(inputs[sequence], lefts[sequence])


def residual(place, inputs, heads, own, others, norm, chunk_rows):
    width, count = inputs[0].shape[1], len(heads[0])
    q_width = heads[0][0].shape[1]
    rows, block = 2 * SEQ, min(512, chunk_rows)
    here, there = placed(chunk_rows, block)
    blocks = SEQ // block
    fixed = lambda r, place: (0, 0)
    once = pl.Buffered(1)
    steps = (
        lambda r: jnp.minimum(r, blocks - 1),
        lambda r: jnp.maximum(r - blocks, 0),
    )
    return pl.pallas_call(
        functools.partial(resid_kernel, count),
        grid_spec=pltpu.PrefetchScalarGridSpec(
            num_scalar_prefetch=1,
            grid=(rows // block,),
            in_specs=[
                pl.BlockSpec((block, width), lambda r, place, step=step: here(step(r), place))
                for step in steps
            ]
            + [
                pl.BlockSpec((block, q_width), lambda r, place, step=step: there(step(r), place))
                for step in steps
                for _ in range(count)
            ]
            + [pl.BlockSpec((width, q_width), fixed, pipeline_mode=once)]
            + [pl.BlockSpec(piece.shape, fixed, pipeline_mode=once) for piece in others]
            + [pl.BlockSpec((1, width), fixed)],
            out_specs=[
                pl.BlockSpec((block, width), here),
                pl.BlockSpec((chunk_rows // block, block, width), lambda r, place: (0, 0, 0)),
            ],
            scratch_shapes=[pltpu.VMEM((block, width), jnp.float32)],
        ),
        out_shape=[
            jax.ShapeDtypeStruct((rows, width), jnp.bfloat16),
            jax.ShapeDtypeStruct((chunk_rows // block, block, width), jnp.float32),
        ],
        compiler_params=pltpu.CompilerParams(vmem_limit_bytes=60 * 2**20),
        cost_estimate=cost(2 * rows * width * width, rows * width * 8, 0.46),
    )(place, *inputs, *heads[0], *heads[1], own, *others, norm[None, :])


def input_kernel(count, core_ref, *refs):
    lefts, rights = refs[:count], refs[count : 3 * count - 1]
    x_ref, grad_ref, norm_ref, out_ref, gains_ref, sums_ref = refs[3 * count - 1 :]
    used = lefts[0].shape[1]
    step, steps = pl.program_id(0), pl.num_programs(0)

    def block(others):
        own = rights[0][:, rights[0].shape[1] - used :]
        total = lax.dot_general(lefts[0][...], own, NT, preferred_element_type=jnp.float32)
        for left_ref, right_ref in zip(lefts[1:], others):
            total = total + lax.dot_general(
                left_ref[...], right_ref[...], NT, preferred_element_type=jnp.float32
            )
        sums_ref[:, pl.ds(pl.multiple_of(step * 256, 256), 256)] = total

    for half in range(2):

        @pl.when(step // (steps // 2) == (core_ref[0] if half == 0 else 1 - core_ref[0]))
        def _():
            block(rights[1 + half * (count - 1) : 1 + (half + 1) * (count - 1)])

    @pl.when(step == steps - 1)
    def _():
        gains_ref[...] = jnp.zeros_like(gains_ref)
        for at in range(0, sums_ref.shape[0], 64):
            rows = slice(at, at + 64)
            grads = sums_ref[rows, :]
            inputs = x_ref[rows, :].astype(jnp.float32)
            inverse = rms_scale(inputs)
            normed = inputs * inverse
            gains_ref[...] += jnp.sum((grads * normed).reshape(-1, 8, grads.shape[1]), axis=0)
            out_ref[rows, :] = grad_ref[rows, :] + norm_back(
                grads * norm_ref[...], normed, inverse
            )


def input_back(core, grads, own, others, inputs, grad_resid, norm):
    rows, width = inputs.shape
    count, used = len(grads), grads[0].shape[1]
    steps = width // 256
    whole = lambda n, core: (0, 0)
    near = lambda n, core: (jnp.clip(n - core[0] * (steps // 2), 0, steps // 2 - 1), 0)
    other = lambda n, core: (jnp.clip(n - (1 - core[0]) * (steps // 2), 0, steps // 2 - 1), 0)
    once = pl.Buffered(1)
    return pl.pallas_call(
        functools.partial(input_kernel, count),
        grid_spec=pltpu.PrefetchScalarGridSpec(
            num_scalar_prefetch=1,
            grid=(steps,),
            in_specs=[pl.BlockSpec((rows, used), whole, pipeline_mode=once)] * count
            + [pl.BlockSpec((256, own.shape[1]), lambda n, core: (n, 0))]
            + [pl.BlockSpec((256, used), near)] * (count - 1)
            + [pl.BlockSpec((256, used), other)] * (count - 1)
            + [pl.BlockSpec((rows, width), whole, pipeline_mode=once)] * 2
            + [pl.BlockSpec((1, width), whole)],
            out_specs=[pl.BlockSpec((rows, width), whole), pl.BlockSpec((8, width), whole)],
            scratch_shapes=[pltpu.VMEM((rows, width), jnp.float32)],
        ),
        out_shape=[
            jax.ShapeDtypeStruct((rows, width), jnp.float32),
            jax.ShapeDtypeStruct((8, width), jnp.float32),
        ],
        compiler_params=pltpu.CompilerParams(vmem_limit_bytes=60 * 2**20),
        cost_estimate=cost(2 * rows * used * width * count, rows * width * 20, 0.28),
    )(core, *grads, own, *others, inputs, grad_resid, norm[None, :])


def attention_weights_kernel(inner_ref, *refs):
    out_ref = refs[-1]
    total = jnp.zeros(out_ref.shape, jnp.float32)
    pieces, at = [], 0
    chunk_rows = refs[0].shape[0]
    for ref in refs[:-1]:
        if ref.shape[0] < SEQ:
            pieces.append(ref)
            continue
        at = 0
        for piece in pieces:
            rows = piece.shape[0]
            start = (at // chunk_rows ^ inner_ref[0]) * chunk_rows + at % chunk_rows
            total = total + lax.dot_general(
                piece[...], ref[pl.ds(pl.multiple_of(start, rows), rows), :], TN,
                preferred_element_type=jnp.float32,
            )
            at += rows
        pieces = []
    out_ref[...] = total.astype(jnp.bfloat16)


def out_weights(inner, pieces, attended):
    width, q_width = pieces[0][0].shape[1], attended[0].shape[1]
    whole = lambda n, inner: (0, 0)
    in_specs = []
    for rows in range(2):
        in_specs += [pl.BlockSpec((piece.shape[0], 256), lambda n, inner: (0, n)) for piece in pieces[rows]]
        in_specs.append(pl.BlockSpec((SEQ, q_width), whole))
    return pl.pallas_call(
        attention_weights_kernel,
        grid_spec=pltpu.PrefetchScalarGridSpec(
            num_scalar_prefetch=1,
            grid=(width // 256,),
            in_specs=in_specs,
            out_specs=pl.BlockSpec((256, q_width), lambda n, inner: (n, 0)),
        ),
        out_shape=jax.ShapeDtypeStruct((width, q_width), jnp.bfloat16),
        compiler_params=pltpu.CompilerParams(vmem_limit_bytes=60 * 2**20),
        cost_estimate=cost(4 * SEQ * q_width * width, SEQ * width * 4, 0.35),
    )(inner, *pieces[0], attended[0], *pieces[1], attended[1])


def projection_weights_kernel(norm_ref, *refs):
    inputs, inverses, grads, out_ref = refs[:2], refs[2:4], refs[4:-1], refs[-1]
    total = jnp.zeros(out_ref.shape, jnp.float32)
    chunk_rows = grads[0].shape[0]
    for k, grad_ref in enumerate(grads):
        at = k * chunk_rows
        rows = slice(at % SEQ, at % SEQ + chunk_rows)
        inverse = inverses[at // SEQ][rows, :]
        normed = inputs[at // SEQ][rows, :].astype(jnp.float32) * jnp.concatenate([inverse] * 2, axis=1)
        total = total + lax.dot_general(
            (normed * norm_ref[...]).astype(jnp.bfloat16), grad_ref[...], TN,
            preferred_element_type=jnp.float32,
        )
    out_ref[...] = total.astype(jnp.bfloat16)


def projection_weights(inputs, inverse, norm, grads):
    width, columns = inputs[0].shape[1], grads[0].shape[1]
    whole = lambda n: (0, 0)
    column = lambda n: (0, n)
    return pl.pallas_call(
        projection_weights_kernel,
        grid=(width // 256,),
        in_specs=[pl.BlockSpec((1, 256), column)]
        + [pl.BlockSpec((SEQ, 256), column)] * 2
        + [pl.BlockSpec((SEQ, 128), whole)] * 2
        + [pl.BlockSpec(part.shape, whole) for part in grads],
        out_specs=pl.BlockSpec((256, columns), lambda n: (n, 0)),
        out_shape=jax.ShapeDtypeStruct((width, columns), jnp.bfloat16),
        compiler_params=pltpu.CompilerParams(vmem_limit_bytes=60 * 2**20),
        cost_estimate=cost(4 * SEQ * columns * width, SEQ * width * 4, 0.43),
    )(norm[None, :], *inputs, *inverse, *grads)


def shift(values, distance, count, axis="tensor"):
    return lax.ppermute(values, axis, [(i, i ^ distance) for i in range(count)])


def gather_kernel(src_ref, own_ref, other_ref, send_sems, recv_sems, local_sem):
    rows = src_ref.shape[0]
    half = rows // 2
    x_top, x_bottom = own_ref.at[pl.ds(rows, half)], own_ref.at[pl.ds(rows + half, half)]
    y_top, y_bottom = other_ref.at[pl.ds(0, half)], other_ref.at[pl.ds(half, half)]
    far_top, far_bottom = other_ref.at[pl.ds(rows, half)], other_ref.at[pl.ds(rows + half, half)]
    top, bottom = src_ref.at[pl.ds(0, half)], src_ref.at[pl.ds(half, half)]
    greet([1, 2])

    def copy(index, from_ref, to_ref, distance):
        return pltpu.make_async_remote_copy(
            src_ref=from_ref, dst_ref=to_ref, send_sem=send_sems.at[index],
            recv_sem=recv_sems.at[index], **remote(distance),
        )

    first = [
        copy(0, bottom, x_bottom, 1), copy(1, top, y_top, 2),
        copy(2, top, x_top, 1), copy(3, bottom, y_bottom, 2),
    ]
    for sent in first:
        sent.start()
    local = pltpu.make_async_copy(src_ref, own_ref.at[pl.ds(0, rows)], local_sem.at[0])
    local.start()
    first[1].wait_recv()
    relay_top = copy(4, y_top, far_top, 1)
    relay_top.start()
    first[0].wait_recv()
    relay_bottom = copy(5, x_bottom, far_bottom, 2)
    relay_bottom.start()
    first[2].wait_recv()
    first[3].wait_recv()
    relay_top.wait_recv()
    relay_bottom.wait_recv()
    for sent in first + [relay_top, relay_bottom]:
        sent.wait_send()
    local.wait()


def gather_rows(values, count):
    if count != 4:
        near = gather_near(values, count)
        return [jnp.concatenate(near[i : i + count // 2], axis=0) for i in (0, count // 2)]
    place = pl.BlockSpec(memory_space=pl.ANY)
    rows, width = values.shape
    wide = jax.ShapeDtypeStruct((2 * rows, width), values.dtype)
    return pl.pallas_call(
        gather_kernel,
        in_specs=[place],
        out_specs=[place] * 2,
        out_shape=[wide, wide],
        scratch_shapes=[
            pltpu.SemaphoreType.DMA((6,)), pltpu.SemaphoreType.DMA((6,)),
            pltpu.SemaphoreType.DMA((1,)),
        ],
        compiler_params=pltpu.CompilerParams(collective_id=1, has_side_effects=True),
        cost_estimate=pl.CostEstimate(
            flops=0, bytes_accessed=values.size * 12, transcendentals=0,
            remote_bytes_transferred=values.size * 6,
        ),
    )(values)


def gather_near(values, count):
    if count == 4:
        return [values, shift(values, 1, count), shift(values, 2, count)]
    whole = lax.all_gather(values, "tensor", axis=0)
    mine = lax.axis_index("tensor")
    return [lax.dynamic_index_in_dim(whole, mine ^ k, 0, False) for k in range(count)]


def gather_far(near, count):
    if count != 4:
        return []
    half = near[0].shape[0] // 2
    return [shift(near[2][:half], 1, count), shift(near[1][half:], 2, count)]


def gather_chunks(values, count):
    near = gather_near(values, count)
    far = gather_far(near, count)
    return near + [jnp.concatenate(far, axis=0)] if far else near


def exchange(parts, distances, count):
    return [part if k == 0 else shift(part, k, count) for k, part in zip(distances, parts)]


def column_piece(weights, columns, core):
    half = weights.shape[0] // 2
    return lax.dynamic_slice(
        weights, (core[0] * half, columns[0]), (half, columns[1] - columns[0])
    )


def sum_first(parts, count):
    if count != 4:
        return None
    return shift(parts[3][0], 1, count), shift(parts[3][1], 2, count)


def sum_rest(parts, first, count):
    if count != 4:
        mine = lax.axis_index("tensor")
        half, width = parts[0][0].shape
        stacked = jnp.zeros((count, 2 * half, width), jnp.bfloat16)
        for k in range(count):
            term = jnp.concatenate([side.astype(jnp.bfloat16) for side in parts[k]], axis=0)
            stacked = lax.dynamic_update_index_in_dim(stacked, term, mine ^ k, 0)
        total = lax.psum_scatter(
            stacked.reshape(-1, width), "tensor", scatter_dimension=0, tiled=True
        ).astype(jnp.float32)
        none = jnp.zeros((half, width), jnp.bfloat16)
        return [[total[:half], none, none], [total[half:], none, none]]
    far_top, far_bottom = first
    x_top = shift(parts[1][0], 1, count)
    y_bottom = shift(parts[2][1], 2, count)
    y_top = shift((parts[2][0] + far_top.astype(jnp.float32)).astype(jnp.bfloat16), 2, count)
    x_bottom = shift((parts[1][1] + far_bottom.astype(jnp.float32)).astype(jnp.bfloat16), 1, count)
    return [[None, x_top, y_top], [None, x_bottom, y_bottom]]


def added(own_ref, x_ref, y_ref):
    return own_ref[...] + x_ref[...].astype(jnp.float32) + y_ref[...].astype(jnp.float32)


def own_rows_call(kernel, sums, twos, ones, out_shapes, gains):
    half, width = sums[0][0].shape
    block = min(64, half)
    term = pl.BlockSpec((block, width), lambda i: (i, 0))
    both = pl.BlockSpec((2, block, width), lambda i: (0, i, 0))
    out_specs = [both] * len(out_shapes)
    if gains:
        out_specs.append(pl.BlockSpec((8, width), lambda i: (0, 0)))
        out_shapes = out_shapes + [jax.ShapeDtypeStruct((8, width), jnp.float32)]
    return pl.pallas_call(
        kernel,
        grid=(half // block,),
        in_specs=[term] * 6 + [both] * len(twos) + [pl.BlockSpec((1, width), lambda i: (0, 0))] * len(ones),
        out_specs=out_specs,
        out_shape=out_shapes,
        compiler_params=pltpu.CompilerParams(vmem_limit_bytes=60 * 2**20),
        cost_estimate=cost(half * width * 10, half * width * 10, 1.0),
    )(*sums[0], *sums[1], *twos, *ones)


def resid_back_kernel(*refs):
    dy_ref, resid_ref, norm_ref, grad_ref, low_ref, gains_ref = refs[6:]

    @pl.when(pl.program_id(0) == 0)
    def _():
        gains_ref[...] = jnp.zeros_like(gains_ref)

    for side in range(2):
        grads = added(*refs[3 * side : 3 * side + 3])
        resid = resid_ref[side]
        inverse = rms_scale(resid)
        normed = resid * inverse
        gains_ref[...] += jnp.sum((grads * normed).reshape(-1, 8, grads.shape[1]), axis=0)
        total = dy_ref[side].astype(jnp.float32) + norm_back(grads * norm_ref[...], normed, inverse)
        grad_ref[side] = total
        low_ref[side] = total.astype(jnp.bfloat16)


def output_kernel(*refs):
    resid_ref, out_ref = refs[6:]
    for side in range(2):
        out_ref[side] = (resid_ref[side] + added(*refs[3 * side : 3 * side + 3])).astype(jnp.bfloat16)


def total_everywhere(values, sizes):
    for axis, size in sizes.items():
        distance = 1
        while distance < size:
            values = values + shift(values, distance, size, axis)
            distance *= 2
    return values


def after(value, *others):
    return lax.optimization_barrier((value, others))[0]


def pad_columns(values, width):
    return jnp.pad(values, ((0, 0), (0, width - values.shape[1])))


def gather_weights(*parts):
    return lax.all_gather(jnp.concatenate(parts, axis=1), "dp", axis=0, tiled=True)


def scatter_weights(grads):
    return lax.psum_scatter(grads, "dp", scatter_dimension=0, tiled=True)


def per_device(
    sizes,
    tokens,
    segments,
    positions,
    w_query,
    w_key,
    w_value,
    w_out,
    w_gate,
    w_up,
    w_down,
    norm_attn,
    norm_mlp,
    query_gain,
    key_gain,
    out_grad,
):
    count = sizes["tensor"]
    chunk_rows = tokens.shape[0]
    q_width, key_width = w_query.shape[1], w_key.shape[1]
    kv_width = -(-key_width // 128) * 128
    units = w_gate.shape[1] // 2
    mine = lax.axis_index("tensor").astype(jnp.int32).reshape(1)

    half, width = chunk_rows // 2, tokens.shape[1]
    inner_count = count // 2
    inner, flip = mine % inner_count, mine // inner_count
    core = lax.axis_index("dp").astype(jnp.int32).reshape(1) % 2

    def own_first(values):
        pair = values.reshape(2, SEQ)
        return jnp.where(flip == 0, pair, pair[::-1])

    w_attn = gather_weights(
        w_out, w_query, pad_columns(w_key, kv_width), pad_columns(w_value, kv_width)
    )
    rows_in = gather_rows(tokens, count)
    w_mlp = [
        gather_weights(w_gate[:, part], w_up[:, part], w_down[:, part])
        for part in (slice(0, units), slice(units, 2 * units))
    ]
    segments, positions = own_first(segments), own_first(positions)
    out_near = gather_near(column_piece(after(w_attn, rows_in), (0, q_width), core), count)
    inv_rows, queries, key_sides, value_sides, raw = [], [], [], [], []
    tables = rotary_tables(positions.reshape(-1))
    attended, inv_total, heads = [], [], []
    for sequence in range(2):
        rows = rows_in[sequence]
        if sequence == 1:
            rows = after(rows, attended, out_near)
            out_near = after(out_near, attended)
            out_far = gather_far(out_near, count)
            out_others = out_near[1:] + ([jnp.concatenate(out_far, axis=0)] if out_far else [])
            out_others = out_others + [shift(part, 1, sizes["dp"], "dp") for part in out_others]
        results = project(
            inner, sequence, rows, chunk_rows, norm_attn, w_attn, tables, query_gain, key_gain, q_width, kv_width
        )
        for kept, result in zip((inv_rows, queries, key_sides, value_sides, raw), results):
            kept.append(result)
        result, inverse = attend(
            queries[sequence], key_sides[sequence], value_sides[sequence], segments[sequence]
        )
        attended.append(result)
        inv_total.append(inverse)
        heads.append(gather_chunks(result, count))
    grad_near = gather_near(after(out_grad, heads), count)
    crossed = [
        heads[sequence][:inner_count] + heads[1 - sequence][inner_count:] for sequence in range(2)
    ]
    rows_two, resid = residual(
        jnp.concatenate([inner, core]), rows_in, crossed, w_attn, out_others, norm_mlp, chunk_rows
    )
    resid = resid.reshape(2, half, width)
    grad_near = after(grad_near, rows_two)
    grad_far = gather_far(grad_near, count)
    act_a, factors = hidden_forward(rows_two, w_mlp[0])
    grad_rows = jnp.concatenate(grad_near + after(grad_far, act_a), axis=0)

    grads_a = hidden_backward(grad_rows, factors, w_mlp[0])
    grad_a = contract_rows(rows_two, grads_a).astype(jnp.bfloat16)
    half_columns = column_piece(after(w_attn, grads_a), (q_width, w_attn.shape[1]), core)
    in_near = [shift(half_columns, k, count) for k in range(1, count - 1)]
    if count == 4:
        far_halves = gather_far([half_columns, *in_near], count)
        in_far = [jnp.concatenate(far_halves, axis=0)]
    else:
        far_halves = in_far = [shift(half_columns, count - 1, count)]
    act, grads_b = hidden_units(after(rows_two, grad_a), grad_rows, w_mlp[1], act_a)
    in_others = in_near + in_far
    in_others = in_others + [shift(part, 1, sizes["dp"], "dp") for part in in_others]
    spans = [(2 * units, 0), (2 * units, 0)]

    def two_parts(distances, grads):
        lefts = [(grads, 2 * units, 0), (grads_b, 2 * units, 0)]
        return rows_out(distances, lefts, w_mlp, spans, chunk_rows)

    grad_b = contract_rows(after(rows_two, in_near), grads_b).astype(jnp.bfloat16)
    two = two_parts(list(range(inner_count, count)), after(grads_a, grad_b, far_halves))
    two_first = sum_first(two, count)
    for k in range(1, inner_count):
        two.update(two_parts([k], after(grads_a, two[count - 1])))
    if count == 4:
        two_rest = sum_rest(two, two_first, count)
        sent = (two_rest[0][1], two_rest[1][2])
        two.update(two_parts([0], after(grads_a, two[1])))
        two_rest[0][0], two_rest[1][0] = two[0]
    else:
        sent = ()
        two.update(two_parts([0], after(grads_a, two[1])))
        two_rest = sum_rest(two, None, count)
    distances = list(range(count))
    out_act = after(act, two[0])
    out = rows_out(
        distances, [(out_act, units, 0), (out_act, units, 1)], w_mlp, [(units, 2), (units, 2)], chunk_rows
    )
    out_first = sum_first(out, count)
    grad_resid, branch_low, gain_mlp = own_rows_call(
        resid_back_kernel,
        after(two_rest, out[0]),
        [out_grad.reshape(2, half, width), resid],
        [norm_mlp[None, :]],
        [
            jax.ShapeDtypeStruct((2, half, width), jnp.float32),
            jax.ShapeDtypeStruct((2, half, width), jnp.bfloat16),
        ],
        True,
    )
    branch_low = branch_low.reshape(chunk_rows, width)
    heads_out = grad_heads(core, branch_low, w_attn, out_others, q_width, count)
    heads_in = exchange(heads_out, distances, count)
    scattered_a = scatter_weights(grad_a)
    scattered_b = scatter_weights(after(grad_b, scattered_a, two[count - 1]))
    grad_down = contract_rows(
        after(grad_rows, heads_out[0], scattered_b, out_first), act
    ).astype(jnp.bfloat16)
    tops = bottoms = relays = []
    if count == 4:
        top, bottom = after((branch_low[:half], branch_low[half:]), heads_in, grad_down)
        tops = [shift(top, 1, count), shift(top, 2, count)]
    sums, raw_grads = [], []
    for sequence in range(2):
        pieces = heads_in[sequence * inner_count : (sequence + 1) * inner_count]
        if sequence == 0:
            pieces = after(pieces, heads_in, grad_down)
        else:
            pieces = after(pieces, tops, raw_grads)
            if count == 4:
                bottom = after(bottom, tops, raw_grads)
                bottoms = [shift(bottom, 1, count), shift(bottom, 2, count)]
        results = attend_back(
            inner, sequence, queries[sequence], key_sides[sequence], value_sides[sequence],
            segments[sequence], attended[sequence], inv_total[sequence], pieces, raw[sequence], tables,
            query_gain, key_gain,
        )
        raw_grads += results[:inner_count]
        sums.append(results[inner_count:])
    raw_in = exchange(raw_grads, distances, count)
    if count == 4:
        near_bottom, near_top = after((bottoms[0], tops[1]), bottoms, raw_grads)
        relays = [shift(near_top, 1, count), shift(near_bottom, 2, count)]
        branch = (
            [branch_low, tops[0], bottoms[0]],
            [tops[1], bottoms[1], *relays],
        )
    else:
        branch_near = gather_near(branch_low, count)
        branch = (branch_near[:inner_count], branch_near[inner_count:])
    grad_qkv = projection_weights(after(rows_in, raw_grads, bottoms), inv_rows, norm_attn, raw_grads)
    grad_w_out = out_weights(inner, after(branch, raw_grads, grad_qkv), attended)

    scattered_down = scatter_weights(after(grad_down, scattered_b, heads_in))
    scattered_attn = scatter_weights(
        after(
            jnp.concatenate([grad_w_out, grad_qkv], axis=1),
            scattered_down, raw_in,
        )
    )

    grad_w_gate = jnp.concatenate(
        [scattered_a[:, :units], scattered_b[:, :units]], axis=1
    ).astype(jnp.float32)
    grad_w_up = jnp.concatenate(
        [scattered_a[:, units:], scattered_b[:, units:]], axis=1
    ).astype(jnp.float32)
    grad_w_down = scattered_down.astype(jnp.float32)
    grad_tokens, gain_attn = input_back(
        core, after(raw_in, grad_w_gate, grad_w_up, grad_w_down), w_attn, in_others, tokens, grad_resid.reshape(chunk_rows, width), norm_attn
    )
    out_rest = sum_rest(out, after(out_first, gain_attn) if count == 4 else None, count)
    if count == 4:
        out_rest[0][0], out_rest[1][0] = out[0]
    gains = [
        jnp.sum(gain_attn, axis=0),
        jnp.sum(gain_mlp, axis=0),
        jnp.sum((sums[0][0] + sums[1][0]).reshape(-1, 64), axis=0),
        jnp.sum((sums[0][1] + sums[1][1]).reshape(-1, 64), axis=0),
    ]
    gains = jnp.concatenate(gains).reshape(-1, 128)
    gains = total_everywhere(gains, sizes).reshape(-1)
    (output,) = own_rows_call(
        output_kernel, after(out_rest, gains), [resid], [], [jax.ShapeDtypeStruct((2, half, width), jnp.bfloat16)],
        False,
    )
    distances = list(range(count))
    key_at = 2 * q_width
    value_at = key_at + kv_width
    return (
        output.reshape(chunk_rows, width),
        grad_tokens.reshape(chunk_rows, width),
        scattered_attn[:, q_width:key_at].astype(jnp.float32),
        scattered_attn[:, key_at : key_at + key_width].astype(jnp.float32),
        scattered_attn[:, value_at : value_at + key_width].astype(jnp.float32),
        scattered_attn[:, :q_width].astype(jnp.float32),
        grad_w_gate,
        grad_w_up,
        grad_w_down,
        gains[:width],
        gains[width : 2 * width],
        gains[2 * width : 2 * width + 64],
        gains[2 * width + 64 : 2 * width + 128],
    )


def solution(mesh):
    return jax.shard_map(
        functools.partial(per_device, dict(mesh.shape)),
        mesh=mesh,
        in_specs=(
            P(("dp", "tensor"), None),
            P("dp"),
            P("dp"),
            P("dp", "tensor"),
            P("dp", "tensor"),
            P("dp", "tensor"),
            P("dp", "tensor"),
            P("dp", "tensor"),
            P("dp", "tensor"),
            P("dp", "tensor"),
            P(),
            P(),
            P(),
            P(),
            P(("dp", "tensor"), None),
        ),
        out_specs=(
            P(("dp", "tensor"), None),
            P(("dp", "tensor"), None),
            P("dp", "tensor"),
            P("dp", "tensor"),
            P("dp", "tensor"),
            P("dp", "tensor"),
            P("dp", "tensor"),
            P("dp", "tensor"),
            P("dp", "tensor"),
            P(),
            P(),
            P(),
            P(),
        ),
        check_vma=False,
    )
```

```python
import functools

import jax
import jax.numpy as jnp
from jax import lax
from jax.experimental import pallas as pl
from jax.experimental.pallas import tpu as pltpu
from jax.sharding import PartitionSpec as P

EPS = 1e-05
THETA = 1000000.0
SEQ = 1024
TILE = 256
LOG2E = 1.4426950408889634
MASKED = -1e30
NT = (((1,), (1,)), ((), ()))
TN = (((0,), (0,)), ((), ()))


def rms_scale(values):
    return lax.rsqrt(jnp.mean(values * values, axis=-1, keepdims=True) + EPS)


def norm_back(grad_normed, normed, inverse):
    return inverse * (grad_normed - normed * jnp.mean(grad_normed * normed, axis=-1, keepdims=True))


def rotary_tables(places):
    lane = jnp.arange(128)
    frequency = THETA ** (-(lane % 32).astype(jnp.float32) * 2.0 / 64)
    angles = places.astype(jnp.float32)[:, None] * frequency[None, :]
    sine = jnp.sin(angles)
    upper = (lane % 64 >= 32)[None, :]
    return jnp.cos(angles), jnp.where(upper, 0.0, -sine), jnp.where(upper, sine, 0.0)


def contract_rows(left, right):
    return lax.dot_general(
        left, right, (((0,), (0,)), ((), ())), preferred_element_type=jnp.float32
    )


def half_lanes(rows):
    return lax.broadcasted_iota(jnp.int32, (rows, 128), 1) < 64


def ones_side(side, rows):
    low = half_lanes(rows)
    return jnp.where(low if side == 0 else ~low, 1.0, 0.0).astype(jnp.bfloat16)


def attend_kernel(q_ref, k_ref, v_ref, segc_ref, segr_ref, out_ref, inv_ref, bias_ref, total_ref):
    coef = LOG2E * 64 ** (-0.5)

    @pl.when(pl.program_id(1) == 0)
    def _():
        for at in range(0, SEQ, TILE):
            end = at + TILE
            rows = lax.broadcasted_iota(jnp.int32, (TILE, end), 0) + at
            cols = lax.broadcasted_iota(jnp.int32, (TILE, end), 1)
            allowed = (segc_ref[at:end, :] == segr_ref[0, :, :end]) & (cols <= rows)
            bias_ref[at:end, :end] = jnp.where(allowed, 0.0, MASKED)

    for side in range(2):
        lanes = slice(side * 128, side * 128 + 128)
        for key_at in range(0, SEQ, TILE):
            keys, rows = slice(key_at, key_at + TILE), slice(key_at, SEQ)
            scores = lax.dot_general(
                q_ref[rows, :], k_ref[keys, lanes], NT, preferred_element_type=jnp.float32
            )
            weights = jnp.exp2(scores * coef + bias_ref[rows, keys]).astype(jnp.bfloat16)
            mixed = jnp.concatenate([v_ref[keys, lanes], ones_side(side, TILE)], axis=1)
            part = jnp.dot(weights, mixed, preferred_element_type=jnp.float32)
            if side == 0 and key_at == 0:
                total_ref[...] = part
            else:
                total_ref[rows, :] += part
    inverse = 1.0 / total_ref[:, 128:]
    out_ref[...] = (total_ref[:, :128] * inverse).astype(jnp.bfloat16)
    inv_ref[...] = inverse


def unrotated(grads, raw, cosine, sine_low, sine_high, gain):
    grads = grads * 0.125
    turned = (
        grads * cosine
        - pltpu.roll(grads, 96, 1) * sine_low
        - pltpu.roll(grads, 32, 1) * sine_high
    )
    inverse = head_inverse(raw)
    normed = raw * inverse
    scaled = turned * gain
    change = inverse * (scaled - normed * head_mean(scaled * normed))
    return change, jnp.sum((turned * normed).reshape(-1, 8, 128), axis=0)


def attend_back_kernel(
    chunks, inner_ref, q_ref, k_ref, v_ref, segc_ref, segr_ref, out_ref, inv_ref,
    qraw_ref, kraw_ref, cos_ref, low_ref, high_ref, qgain_ref, kgain_ref, *refs,
):
    pieces, results = refs[:chunks], refs[chunks : 2 * chunks]
    (
        qsum_ref, ksum_ref, bias_ref, mix_ref, qside_ref, gside_ref,
        dq_ref, dk_ref, dv_ref, kpair_ref, vpair_ref, grad_ref,
    ) = refs[2 * chunks :]
    chunk_rows = SEQ // chunks
    q_width = 128 * pl.num_programs(1)
    kv_width = (results[0].shape[1] - q_width) // 2

    def rows_of(k):
        return pl.ds(pl.multiple_of((inner_ref[0] ^ k) * chunk_rows, chunk_rows), chunk_rows)

    def put(values, place):
        dq_ref[...] = values
        for k, result_ref in enumerate(results):
            lanes = pl.ds(pl.multiple_of(place, 128), 128)
            result_ref[:, lanes] = dq_ref[rows_of(k), :].astype(jnp.bfloat16)

    coef = LOG2E * 64 ** (-0.5)
    step = pl.program_id(1)

    @pl.when(step == 0)
    def _():
        for key_at in range(0, SEQ, TILE):
            key_end = key_at + TILE
            keys = lax.broadcasted_iota(jnp.int32, (TILE, SEQ - key_at), 0) + key_at
            rows = lax.broadcasted_iota(jnp.int32, (TILE, SEQ - key_at), 1) + key_at
            allowed = (segc_ref[key_at:key_end, :] == segr_ref[0, :, key_at:]) & (keys <= rows)
            bias_ref[key_at:key_end, key_at:] = jnp.where(allowed, 0.0, MASKED)

    @pl.when((step == 0) & (pl.program_id(0) == 0))
    def _():
        qsum_ref[...] = jnp.zeros_like(qsum_ref)
        ksum_ref[...] = jnp.zeros_like(ksum_ref)

    @pl.when(lax.rem(step, 4) == 0)
    def _():
        kpair_ref[...] = jnp.zeros_like(kpair_ref)
        vpair_ref[...] = jnp.zeros_like(vpair_ref)

    @pl.when(lax.rem(step, 2) == 0)
    def _():
        dk_ref[...] = jnp.zeros_like(dk_ref)
        dv_ref[...] = jnp.zeros_like(dv_ref)

    for k, piece_ref in enumerate(pieces):
        grad_ref[rows_of(k), :] = piece_ref[...].astype(jnp.float32)
    low = half_lanes(SEQ)
    scaled = grad_ref[...] * inv_ref[...]
    scaled_low = scaled.astype(jnp.bfloat16)
    mix_ref[:, :128] = scaled_low
    mix_ref[:, 128:] = -(scaled * out_ref[...].astype(jnp.float32)).astype(jnp.bfloat16)
    none = jnp.zeros_like(scaled_low)
    queries = q_ref[...]
    gside_ref[:, :128] = jnp.where(low, scaled_low, none)
    gside_ref[:, 128:] = jnp.where(low, none, scaled_low)
    qside_ref[:, :128] = jnp.where(low, queries, none)
    qside_ref[:, 128:] = jnp.where(low, none, queries)

    for key_at in range(0, SEQ, TILE):
        keys, rows = slice(key_at, key_at + TILE), slice(key_at, SEQ)
        for side in range(2):
            lanes = slice(side * 128, side * 128 + 128)
            key_side = k_ref[keys, lanes]
            value_side = jnp.concatenate([v_ref[keys, lanes], ones_side(side, TILE)], axis=1)
            scores = lax.dot_general(
                key_side, q_ref[rows, :], NT, preferred_element_type=jnp.float32
            )
            weights = jnp.exp2(scores * coef + bias_ref[keys, rows])
            change = lax.dot_general(
                value_side, mix_ref[rows, :], NT, preferred_element_type=jnp.float32
            )
            grads = (weights * change).astype(jnp.bfloat16)
            dv_ref[keys, :] += jnp.dot(
                weights.astype(jnp.bfloat16),
                gside_ref[rows, lanes],
                preferred_element_type=jnp.float32,
            )
            dk_ref[keys, :] += jnp.dot(
                grads, qside_ref[rows, lanes], preferred_element_type=jnp.float32
            )
            dq = lax.dot_general(grads, key_side, TN, preferred_element_type=jnp.float32)
            if key_at == 0 and side == 0:
                dq_ref[...] = dq
            else:
                dq_ref[rows, :] += dq

    cosine, sine_low, sine_high = cos_ref[...], low_ref[...], high_ref[...]
    change, sums = unrotated(
        dq_ref[...], qraw_ref[...], cosine, sine_low, sine_high, qgain_ref[...]
    )
    qsum_ref[...] += sums
    put(change, step * 128)

    @pl.when(lax.rem(step, 2) == 1)
    def _():
        mine = low == (lax.rem(step, 4) == 1)
        for sum_ref, pair_ref in ((dk_ref, kpair_ref), (dv_ref, vpair_ref)):
            sums = sum_ref[...]
            pair_ref[...] = jnp.where(mine, sums + pltpu.roll(sums, 64, 1), pair_ref[...])

    @pl.when((lax.rem(step, 4) == 3) | (step == pl.num_programs(1) - 1))
    def _():
        change, sums = unrotated(
            kpair_ref[...], kraw_ref[...], cosine, sine_low, sine_high, kgain_ref[...]
        )
        ksum_ref[...] += sums
        put(change, q_width + step // 4 * 128)
        put(vpair_ref[...], q_width + kv_width + step // 4 * 128)


def attention_specs():
    pair = pl.BlockSpec((SEQ, 128), lambda s, p, *_: (s, p))
    group = pl.BlockSpec((SEQ, 256), lambda s, p, *_: (s, p // 2))
    seg_col = pl.BlockSpec((SEQ, 1), lambda s, p, *_: (s, 0))
    seg_row = pl.BlockSpec((1, 1, SEQ), lambda s, p, *_: (s, 0, 0))
    return pair, group, seg_col, seg_row


def attend(queries, key_sides, value_sides, segments):
    rows, width = queries.shape
    sequences, pairs = rows // SEQ, width // 128
    pair, group, seg_col, seg_row = attention_specs()
    work = rows * SEQ * width
    return pl.pallas_call(
        attend_kernel,
        grid=(sequences, pairs),
        in_specs=[pair, group, group, seg_col, seg_row],
        out_specs=[pair, pair],
        out_shape=[
            jax.ShapeDtypeStruct((rows, width), jnp.bfloat16),
            jax.ShapeDtypeStruct((rows, width), jnp.float32),
        ],
        scratch_shapes=[pltpu.VMEM((SEQ, SEQ), jnp.float32), pltpu.VMEM((SEQ, 256), jnp.float32)],
        compiler_params=pltpu.CompilerParams(vmem_limit_bytes=60 * 2**20),
        cost_estimate=pl.CostEstimate(
            flops=42 * work // 10, bytes_accessed=rows * width * 12, transcendentals=work // 128
        ),
    )(queries, key_sides, value_sides, segments[:, None], segments.reshape(sequences, 1, SEQ))


def attend_back(
    inner, sequence, queries, key_sides, value_sides, segments, attended, inverse, pieces, raw, tables,
    query_gain, key_gain,
):
    width = queries.shape[1]
    pairs, chunks, chunk_rows = width // 128, len(pieces), pieces[0].shape[0]
    kv_width = key_sides.shape[1] // 4
    pair, group, seg_col, seg_row = attention_specs()
    kv_raw = pl.BlockSpec((SEQ, 128), lambda s, p, *_: (0, width // 128 + p // 4))
    table = pl.BlockSpec((SEQ, 128), lambda s, p, *_: (sequence, 0))
    gain = pl.BlockSpec((1, 128), lambda s, p, *_: (0, 0))
    total = pl.BlockSpec((8, 128), lambda s, p, *_: (0, 0))
    piece = pl.BlockSpec((chunk_rows, 128), lambda s, p, *_: (0, p))
    columns = width + 2 * kv_width
    work = SEQ * SEQ * width
    flat = pltpu.VMEM((SEQ, 128), jnp.float32)
    return pl.pallas_call(
        functools.partial(attend_back_kernel, chunks),
        grid_spec=pltpu.PrefetchScalarGridSpec(
            num_scalar_prefetch=1,
            grid=(1, pairs),
            in_specs=[pair, group, group, seg_col, seg_row, pair, pair]
            + [pair, kv_raw, table, table, table, gain, gain]
            + [piece] * chunks,
            out_specs=[pl.BlockSpec((chunk_rows, columns), lambda s, p, *_: (0, 0))] * chunks
            + [total, total],
            scratch_shapes=[
                pltpu.VMEM((SEQ, SEQ), jnp.float32),
                pltpu.VMEM((SEQ, 256), jnp.bfloat16),
                pltpu.VMEM((SEQ, 256), jnp.bfloat16),
                pltpu.VMEM((SEQ, 256), jnp.bfloat16),
                flat, flat, flat, flat, flat, flat,
            ],
        ),
        out_shape=[jax.ShapeDtypeStruct((chunk_rows, columns), jnp.bfloat16)] * chunks
        + [jax.ShapeDtypeStruct((8, 128), jnp.float32)] * 2,
        compiler_params=pltpu.CompilerParams(vmem_limit_bytes=60 * 2**20),
        cost_estimate=pl.CostEstimate(
            flops=110 * work // 10, bytes_accessed=SEQ * width * 20, transcendentals=work // 128
        ),
    )(
        inner, queries, key_sides, value_sides, segments[:, None], segments.reshape(-1, 1, SEQ),
        attended, inverse, raw, raw, *tables,
        jnp.tile(query_gain, 2)[None, :], jnp.tile(key_gain, 2)[None, :], *pieces,
    )


def cost(flops, moved, share):
    return pl.CostEstimate(
        flops=int(0.2 * flops / share), bytes_accessed=int(0.2 * moved), transcendentals=0
    )


def head_inverse(values):
    squares = values * values
    high = squares.astype(jnp.bfloat16)
    low = (squares - high.astype(jnp.float32)).astype(jnp.bfloat16)
    return lax.rsqrt(head_sum(high, low) * (1.0 / 64) + EPS)


def head_sum(high, low):
    from_head = lax.broadcasted_iota(jnp.int32, (128, 128), 0) // 64
    to_head = lax.broadcasted_iota(jnp.int32, (128, 128), 1) // 64
    same = jnp.where(from_head == to_head, 1.0, 0.0).astype(jnp.bfloat16)
    return jnp.dot(high, same, preferred_element_type=jnp.float32) + jnp.dot(
        low, same, preferred_element_type=jnp.float32
    )


def head_mean(values):
    high = values.astype(jnp.bfloat16)
    low = (values - high.astype(jnp.float32)).astype(jnp.bfloat16)
    return head_sum(high, low) * (1.0 / 64)


def project_kernel(
    pieces, inner_ref, *refs,
):
    norm_ref, w_ref, cos_ref, low_ref, high_ref, qgain_ref, kgain_ref = refs[pieces : pieces + 7]
    inv_ref, q_ref, k_ref, v_ref, raw_ref = refs[pieces + 7 :]
    inputs = refs[0][...].astype(jnp.float32)
    inverse = rms_scale(inputs)
    hidden = (inputs * inverse * norm_ref[...]).astype(jnp.bfloat16)
    inv_ref[...] = jnp.broadcast_to(inverse, inv_ref.shape)
    q_width, kv_width = q_ref.shape[1], k_ref.shape[1] // 4
    cosine, sine_low, sine_high = cos_ref[...], low_ref[...], high_ref[...]
    lower = lax.broadcasted_iota(jnp.int32, cosine.shape, 1) < 64
    none = jnp.zeros_like(cosine)

    def rotated(raw, gain):
        scaled = raw * head_inverse(raw) * gain
        return (
            scaled * cosine
            + pltpu.roll(scaled, 96, 1) * sine_low
            + pltpu.roll(scaled, 32, 1) * sine_high
        )

    def to_sides(pair, out_ref, at):
        first, second = jnp.where(lower, pair, none), jnp.where(lower, none, pair)
        sides = (first, pltpu.roll(first, 64, 1), pltpu.roll(second, 64, 1), second)
        for index, side in enumerate(sides):
            lanes = slice(at * 4 + index * 128, at * 4 + index * 128 + 128)
            out_ref[:, lanes] = side.astype(jnp.bfloat16)

    wide = jnp.dot(hidden, w_ref[:, q_width:], preferred_element_type=jnp.float32)
    raw_ref[...] = wide[:, : q_width + kv_width]
    for at in range(0, q_width, 128):
        q_ref[:, at : at + 128] = rotated(wide[:, at : at + 128], qgain_ref[...]).astype(
            jnp.bfloat16
        )
    for at in range(0, kv_width, 128):
        place = q_width + at
        to_sides(rotated(wide[:, place : place + 128], kgain_ref[...]), k_ref, at)
        place = q_width + kv_width + at
        to_sides(wide[:, place : place + 128], v_ref, at)


def placed(chunk_rows, block):
    per = chunk_rows // block
    here = lambda r, inner: (r, 0)
    there = lambda r, inner: ((r // per ^ inner[0]) * per + r % per, 0)
    return here, there


def project(inner, sequence, inputs, chunk_rows, norm, weights, tables, query_gain, key_gain, q_width, kv_width):
    rows, width = inputs.shape
    block = chunk_rows
    here, there = placed(block, block)
    fixed = lambda r, mine: (0, 0)
    used = q_width + 2 * kv_width
    table = pl.BlockSpec(
        (block, 128), lambda r, inner: (sequence * (rows // block) + there(r, inner)[0], 0)
    )
    gain = pl.BlockSpec((1, 128), fixed)
    return pl.pallas_call(
        functools.partial(project_kernel, 1),
        grid_spec=pltpu.PrefetchScalarGridSpec(
            num_scalar_prefetch=1,
            grid=(rows // block,),
            in_specs=[
                pl.BlockSpec((block, width), here),
                pl.BlockSpec((1, width), fixed),
                pl.BlockSpec(weights.shape, fixed, pipeline_mode=pl.Buffered(1)),
                table, table, table, gain, gain,
            ],
            out_specs=[
                pl.BlockSpec((block, 128), here),
                pl.BlockSpec((block, q_width), there),
                pl.BlockSpec((block, 4 * kv_width), there),
                pl.BlockSpec((block, 4 * kv_width), there),
                pl.BlockSpec((block, q_width + kv_width), there),
            ],
        ),
        out_shape=[
            jax.ShapeDtypeStruct((rows, 128), jnp.float32),
            jax.ShapeDtypeStruct((rows, q_width), jnp.bfloat16),
            jax.ShapeDtypeStruct((rows, 4 * kv_width), jnp.bfloat16),
            jax.ShapeDtypeStruct((rows, 4 * kv_width), jnp.bfloat16),
            jax.ShapeDtypeStruct((rows, q_width + kv_width), jnp.float32),
        ],
        compiler_params=pltpu.CompilerParams(vmem_limit_bytes=60 * 2**20),
        cost_estimate=cost(2 * rows * width * used, rows * width * 6, 0.22),
    )(
        inner, inputs, norm[None, :], weights, *tables,
        jnp.tile(query_gain, 2)[None, :], jnp.tile(key_gain, 2)[None, :],
    )


def heads_kernel(count, core_ref, grads_ref, *refs):
    rights, outs = refs[: 2 * count - 1], refs[2 * count - 1 :]
    outs[0][...] = jnp.dot(
        grads_ref[...], rights[0][...], preferred_element_type=jnp.float32
    ).astype(jnp.bfloat16)
    half = rights[1].shape[0]
    near = grads_ref[:, pl.ds(pl.multiple_of(core_ref[0] * half, half), half)]
    other = grads_ref[:, pl.ds(pl.multiple_of((1 - core_ref[0]) * half, half), half)]
    for k in range(1, count):
        outs[k][...] = (
            jnp.dot(near, rights[k][...], preferred_element_type=jnp.float32)
            + jnp.dot(other, rights[count - 1 + k][...], preferred_element_type=jnp.float32)
        ).astype(jnp.bfloat16)


def grad_heads(core, grads, own, others, q_width, count):
    rows, width = grads.shape
    fixed = lambda i, core: (0, 0)
    return pl.pallas_call(
        functools.partial(heads_kernel, count),
        grid_spec=pltpu.PrefetchScalarGridSpec(
            num_scalar_prefetch=1,
            grid=(1,),
            in_specs=[pl.BlockSpec(grads.shape, fixed), pl.BlockSpec((width, q_width), fixed)]
            + [pl.BlockSpec(piece.shape, fixed) for piece in others],
            out_specs=[pl.BlockSpec((rows, q_width), fixed)] * count,
        ),
        out_shape=[jax.ShapeDtypeStruct((rows, q_width), jnp.bfloat16)] * count,
        compiler_params=pltpu.CompilerParams(vmem_limit_bytes=60 * 2**20),
        cost_estimate=cost(2 * rows * width * q_width * count, rows * width, 2.67),
    )(core, grads, own, *others)


def peer(distance):
    mine = lax.axis_index("tensor")
    if distance == 1:
        return mine + 1 - 2 * (mine % 2)
    return (mine + 2) % 4 if distance == 2 else 3 - mine


def remote(distance):
    return dict(device_id={"tensor": peer(distance)}, device_id_type=pl.DeviceIdType.MESH)


def greet(distances):
    barrier = pltpu.get_barrier_semaphore()
    for distance in distances:
        pl.semaphore_signal(barrier, inc=1, **remote(distance))
    pl.semaphore_wait(barrier, len(distances))


def hidden_kernel(x_ref, dy_ref, w_ref, filled_ref, act_ref, grads_ref):
    units = act_ref.shape[1]
    inputs, cotangent = x_ref[...], dy_ref[...]
    for at in range(0, units, 256):
        lanes = slice(at, at + 256)
        gate = jnp.dot(inputs, w_ref[:, lanes], preferred_element_type=jnp.float32)
        up = jnp.dot(
            inputs, w_ref[:, units + at : units + at + 256], preferred_element_type=jnp.float32
        )
        change = jnp.dot(
            cotangent, w_ref[:, 2 * units + at : 2 * units + at + 256],
            preferred_element_type=jnp.float32,
        )
        sigmoid = 1.0 / (1.0 + jnp.exp(-gate))
        silu = gate * sigmoid
        act_ref[:, lanes] = (silu * up).astype(jnp.bfloat16)
        grads_ref[:, lanes] = (change * up * sigmoid * (1.0 + gate - silu)).astype(jnp.bfloat16)
        grads_ref[:, units + at : units + at + 256] = (change * silu).astype(jnp.bfloat16)


def hidden_units(inputs, cotangent, weights, filled):
    rows, width = inputs.shape
    units = weights.shape[1] // 3
    block = min(512, rows)
    row = lambda r: (r, 0)
    return pl.pallas_call(
        hidden_kernel,
        grid=(rows // block,),
        in_specs=[
            pl.BlockSpec((block, width), row),
            pl.BlockSpec((block, width), row),
            pl.BlockSpec(weights.shape, lambda r: (0, 0), pipeline_mode=pl.Buffered(1)),
            pl.BlockSpec(memory_space=pl.ANY),
        ],
        out_specs=[
            pl.BlockSpec((block, units), lambda r: (r, 1)),
            pl.BlockSpec((block, 2 * units), row),
        ],
        out_shape=[jax.ShapeDtypeStruct((rows, 2 * units), jnp.bfloat16)] * 2,
        input_output_aliases={3: 0},
        compiler_params=pltpu.CompilerParams(vmem_limit_bytes=60 * 2**20),
        cost_estimate=cost(6 * rows * width * units, (rows * width + width * units) * 6, 0.63),
    )(inputs, cotangent, weights, filled)


def hidden_forward_kernel(x_ref, w_ref, act_ref, factors_ref):
    units = act_ref.shape[1]
    inputs = x_ref[...]
    for at in range(0, units, 256):
        lanes, beside = slice(at, at + 256), slice(units + at, units + at + 256)
        gate = jnp.dot(inputs, w_ref[:, lanes], preferred_element_type=jnp.float32)
        up = jnp.dot(inputs, w_ref[:, beside], preferred_element_type=jnp.float32)
        sigmoid = 1.0 / (1.0 + jnp.exp(-gate))
        silu = gate * sigmoid
        act_ref[:, lanes] = (silu * up).astype(jnp.bfloat16)
        factors_ref[:, lanes] = (up * sigmoid * (1.0 + gate - silu)).astype(jnp.bfloat16)
        factors_ref[:, beside] = silu.astype(jnp.bfloat16)


def hidden_forward(inputs, weights):
    rows, width = inputs.shape
    units = weights.shape[1] // 3
    block = min(512, rows)
    row = lambda r: (r, 0)
    return pl.pallas_call(
        hidden_forward_kernel,
        grid=(rows // block,),
        in_specs=[
            pl.BlockSpec((block, width), row),
            pl.BlockSpec((width, 2 * units), lambda r: (0, 0), pipeline_mode=pl.Buffered(1)),
        ],
        out_specs=[pl.BlockSpec((block, units), row), pl.BlockSpec((block, 2 * units), row)],
        out_shape=[jax.ShapeDtypeStruct((rows, 2 * units), jnp.bfloat16)] * 2,
        compiler_params=pltpu.CompilerParams(vmem_limit_bytes=60 * 2**20),
        cost_estimate=cost(4 * rows * width * units, (rows * width + width * units) * 4, 0.63),
    )(inputs, weights)


def hidden_backward_kernel(dy_ref, factors_ref, w_ref, grads_ref):
    units = w_ref.shape[1]
    cotangent = dy_ref[...]
    for at in range(0, units, 256):
        change = jnp.dot(
            cotangent, w_ref[:, at : at + 256], preferred_element_type=jnp.float32
        )
        for lanes in (slice(at, at + 256), slice(units + at, units + at + 256)):
            grads_ref[:, lanes] = (change * factors_ref[:, lanes].astype(jnp.float32)).astype(
                jnp.bfloat16
            )


def hidden_backward(cotangent, factors, weights):
    rows, width = cotangent.shape
    units = weights.shape[1] // 3
    block = min(512, rows)
    row = lambda r: (r, 0)
    return pl.pallas_call(
        hidden_backward_kernel,
        grid=(rows // block,),
        in_specs=[
            pl.BlockSpec((block, width), row),
            pl.BlockSpec((block, 2 * units), row),
            pl.BlockSpec((width, units), lambda r: (0, 2), pipeline_mode=pl.Buffered(1)),
        ],
        out_specs=pl.BlockSpec((block, 2 * units), row),
        out_shape=jax.ShapeDtypeStruct((rows, 2 * units), jnp.bfloat16),
        compiler_params=pltpu.CompilerParams(vmem_limit_bytes=60 * 2**20),
        cost_estimate=cost(2 * rows * width * units, (rows * width + width * units) * 4, 0.63),
    )(cotangent, factors, weights)


def half_types(distance):
    if distance == 0:
        return (jnp.float32, jnp.float32)
    if distance == 1:
        return (jnp.bfloat16, jnp.float32)
    if distance == 2:
        return (jnp.float32, jnp.bfloat16)
    return (jnp.bfloat16, jnp.bfloat16)


def rows_out_kernel(terms, *refs):
    outs = refs[2 * terms :]
    total = None
    for left_ref, right_ref in zip(refs[:terms], refs[terms : 2 * terms]):
        product = lax.dot_general(
            left_ref[...], right_ref[...], NT, preferred_element_type=jnp.float32
        )
        total = product if total is None else total + product
    half = outs[0].shape[0]
    for index, out_ref in enumerate(outs):
        out_ref[...] = total[index * half : (index + 1) * half].astype(out_ref.dtype)


def rows_out(distances, lefts, rights, spans, chunk_rows):
    width, rows = rights[0].shape[0], len(distances) * chunk_rows
    first = distances[0] // len(distances)
    halves = [dtype for k in distances for dtype in half_types(k)]
    in_specs = [
        pl.BlockSpec(
            (rows, left[1]), lambda n, index=left[2]: (first, index), pipeline_mode=pl.Buffered(1)
        )
        for left in lefts
    ] + [
        pl.BlockSpec((256, columns), lambda n, index=index: (n, index)) for columns, index in spans
    ]
    depth = sum(left[1] for left in lefts)
    outs = pl.pallas_call(
        functools.partial(rows_out_kernel, len(lefts)),
        grid=(width // 256,),
        in_specs=in_specs,
        out_specs=[pl.BlockSpec((chunk_rows // 2, 256), lambda n: (0, n))] * len(halves),
        out_shape=[jax.ShapeDtypeStruct((chunk_rows // 2, width), dtype) for dtype in halves],
        compiler_params=pltpu.CompilerParams(vmem_limit_bytes=60 * 2**20),
        cost_estimate=cost(2 * rows * depth * width, depth * rows // 4, 4.07),
    )(*(left[0] for left in lefts), *rights)
    return {k: (outs[2 * i], outs[2 * i + 1]) for i, k in enumerate(distances)}


def resid_kernel(count, place_ref, *refs):
    inputs, lefts = refs[:2], (refs[2 : 2 + count], refs[2 + count : 2 + 2 * count])
    rights = refs[2 + 2 * count : 1 + 4 * count]
    norm_ref, hidden_ref, resid_ref, sums_ref = refs[1 + 4 * count :]
    half = sums_ref.shape[1] // 2
    blocks = pl.num_programs(0) // 2

    def block(x_ref, left_refs):
        for core, others in (
            (place_ref[1], rights[1:count]), (1 - place_ref[1], rights[count:])
        ):
            start = pl.multiple_of(core * half, half)
            total = lax.dot_general(
                left_refs[0][...], rights[0][pl.ds(start, half), :], NT,
                preferred_element_type=jnp.float32,
            )
            for left_ref, right_ref in zip(left_refs[1:], others):
                total = total + lax.dot_general(
                    left_ref[...], right_ref[...], NT, preferred_element_type=jnp.float32
                )
            sums_ref[:, pl.ds(start, half)] = total
        resid = x_ref[...].astype(jnp.float32) + sums_ref[...]
        hidden_ref[...] = (resid * rms_scale(resid) * norm_ref[...]).astype(jnp.bfloat16)

        @pl.when(pl.program_id(0) < resid_ref.shape[0])
        def _():
            resid_ref[pl.program_id(0)] = resid

    for sequence in range(2):

        @pl.when(pl.program_id(0) // blocks == sequence)
        def _():
            block(inputs[sequence], lefts[sequence])


def residual(place, inputs, heads, own, others, norm, chunk_rows):
    width, count = inputs[0].shape[1], len(heads[0])
    q_width = heads[0][0].shape[1]
    rows, block = 2 * SEQ, min(512, chunk_rows)
    here, there = placed(chunk_rows, block)
    blocks = SEQ // block
    fixed = lambda r, place: (0, 0)
    once = pl.Buffered(1)
    steps = (
        lambda r: jnp.minimum(r, blocks - 1),
        lambda r: jnp.maximum(r - blocks, 0),
    )
    return pl.pallas_call(
        functools.partial(resid_kernel, count),
        grid_spec=pltpu.PrefetchScalarGridSpec(
            num_scalar_prefetch=1,
            grid=(rows // block,),
            in_specs=[
                pl.BlockSpec((block, width), lambda r, place, step=step: here(step(r), place))
                for step in steps
            ]
            + [
                pl.BlockSpec((block, q_width), lambda r, place, step=step: there(step(r), place))
                for step in steps
                for _ in range(count)
            ]
            + [pl.BlockSpec((width, q_width), fixed, pipeline_mode=once)]
            + [pl.BlockSpec(piece.shape, fixed, pipeline_mode=once) for piece in others]
            + [pl.BlockSpec((1, width), fixed)],
            out_specs=[
                pl.BlockSpec((block, width), here),
                pl.BlockSpec((chunk_rows // block, block, width), lambda r, place: (0, 0, 0)),
            ],
            scratch_shapes=[pltpu.VMEM((block, width), jnp.float32)],
        ),
        out_shape=[
            jax.ShapeDtypeStruct((rows, width), jnp.bfloat16),
            jax.ShapeDtypeStruct((chunk_rows // block, block, width), jnp.float32),
        ],
        compiler_params=pltpu.CompilerParams(vmem_limit_bytes=60 * 2**20),
        cost_estimate=cost(2 * rows * width * width, rows * width * 8, 0.46),
    )(place, *inputs, *heads[0], *heads[1], own, *others, norm[None, :])


def input_kernel(count, core_ref, *refs):
    lefts, rights = refs[:count], refs[count : 3 * count - 1]
    x_ref, grad_ref, norm_ref, out_ref, gains_ref, sums_ref = refs[3 * count - 1 :]
    used = lefts[0].shape[1]
    step, steps = pl.program_id(0), pl.num_programs(0)

    def block(others):
        own = rights[0][:, rights[0].shape[1] - used :]
        total = lax.dot_general(lefts[0][...], own, NT, preferred_element_type=jnp.float32)
        for left_ref, right_ref in zip(lefts[1:], others):
            total = total + lax.dot_general(
                left_ref[...], right_ref[...], NT, preferred_element_type=jnp.float32
            )
        sums_ref[:, pl.ds(pl.multiple_of(step * 256, 256), 256)] = total

    for half in range(2):

        @pl.when(step // (steps // 2) == (core_ref[0] if half == 0 else 1 - core_ref[0]))
        def _():
            block(rights[1 + half * (count - 1) : 1 + (half + 1) * (count - 1)])

    @pl.when(step == steps - 1)
    def _():
        gains_ref[...] = jnp.zeros_like(gains_ref)
        for at in range(0, sums_ref.shape[0], 64):
            rows = slice(at, at + 64)
            grads = sums_ref[rows, :]
            inputs = x_ref[rows, :].astype(jnp.float32)
            inverse = rms_scale(inputs)
            normed = inputs * inverse
            gains_ref[...] += jnp.sum((grads * normed).reshape(-1, 8, grads.shape[1]), axis=0)
            out_ref[rows, :] = grad_ref[rows, :] + norm_back(
                grads * norm_ref[...], normed, inverse
            )


def input_back(core, grads, own, others, inputs, grad_resid, norm):
    rows, width = inputs.shape
    count, used = len(grads), grads[0].shape[1]
    steps = width // 256
    whole = lambda n, core: (0, 0)
    near = lambda n, core: (jnp.clip(n - core[0] * (steps // 2), 0, steps // 2 - 1), 0)
    other = lambda n, core: (jnp.clip(n - (1 - core[0]) * (steps // 2), 0, steps // 2 - 1), 0)
    once = pl.Buffered(1)
    return pl.pallas_call(
        functools.partial(input_kernel, count),
        grid_spec=pltpu.PrefetchScalarGridSpec(
            num_scalar_prefetch=1,
            grid=(steps,),
            in_specs=[pl.BlockSpec((rows, used), whole, pipeline_mode=once)] * count
            + [pl.BlockSpec((256, own.shape[1]), lambda n, core: (n, 0))]
            + [pl.BlockSpec((256, used), near)] * (count - 1)
            + [pl.BlockSpec((256, used), other)] * (count - 1)
            + [pl.BlockSpec((rows, width), whole, pipeline_mode=once)] * 2
            + [pl.BlockSpec((1, width), whole)],
            out_specs=[pl.BlockSpec((rows, width), whole), pl.BlockSpec((8, width), whole)],
            scratch_shapes=[pltpu.VMEM((rows, width), jnp.float32)],
        ),
        out_shape=[
            jax.ShapeDtypeStruct((rows, width), jnp.float32),
            jax.ShapeDtypeStruct((8, width), jnp.float32),
        ],
        compiler_params=pltpu.CompilerParams(vmem_limit_bytes=60 * 2**20),
        cost_estimate=cost(2 * rows * used * width * count, rows * width * 20, 0.28),
    )(core, *grads, own, *others, inputs, grad_resid, norm[None, :])


def attention_weights_kernel(inner_ref, beside_ref, *refs):
    out_ref = refs[-1]
    q_width = refs[-2].shape[1]
    total = jnp.zeros((out_ref.shape[0], q_width), jnp.float32)
    pieces, at = [], 0
    chunk_rows = refs[0].shape[0]
    for ref in refs[:-1]:
        if ref.shape[0] < SEQ:
            pieces.append(ref)
            continue
        at = 0
        for piece in pieces:
            rows = piece.shape[0]
            start = (at // chunk_rows ^ inner_ref[0]) * chunk_rows + at % chunk_rows
            total = total + lax.dot_general(
                piece[...], ref[pl.ds(pl.multiple_of(start, rows), rows), :], TN,
                preferred_element_type=jnp.float32,
            )
            at += rows
        pieces = []
    out_ref[:, :q_width] = total.astype(jnp.bfloat16)
    out_ref[:, q_width:] = beside_ref[...]


def out_weights(inner, beside, pieces, attended):
    width, q_width = pieces[0][0].shape[1], attended[0].shape[1]
    whole = lambda n, inner: (0, 0)
    columns = q_width + beside.shape[1]
    in_specs = [pl.BlockSpec((256, beside.shape[1]), lambda n, inner: (n, 0))]
    for rows in range(2):
        in_specs += [pl.BlockSpec((piece.shape[0], 256), lambda n, inner: (0, n)) for piece in pieces[rows]]
        in_specs.append(pl.BlockSpec((SEQ, q_width), whole))
    return pl.pallas_call(
        attention_weights_kernel,
        grid_spec=pltpu.PrefetchScalarGridSpec(
            num_scalar_prefetch=1,
            grid=(width // 256,),
            in_specs=in_specs,
            out_specs=pl.BlockSpec((256, columns), lambda n, inner: (n, 0)),
        ),
        out_shape=jax.ShapeDtypeStruct((width, columns), jnp.bfloat16),
        compiler_params=pltpu.CompilerParams(vmem_limit_bytes=60 * 2**20),
        cost_estimate=cost(4 * SEQ * q_width * width, SEQ * width * 4, 0.35),
    )(inner, beside, *pieces[0], attended[0], *pieces[1], attended[1])


def projection_weights_kernel(norm_ref, *refs):
    inputs, inverses, grads, out_ref = refs[:2], refs[2:4], refs[4:-1], refs[-1]
    total = jnp.zeros(out_ref.shape, jnp.float32)
    chunk_rows = grads[0].shape[0]
    for k, grad_ref in enumerate(grads):
        at = k * chunk_rows
        rows = slice(at % SEQ, at % SEQ + chunk_rows)
        inverse = inverses[at // SEQ][rows, :]
        normed = inputs[at // SEQ][rows, :].astype(jnp.float32) * jnp.concatenate([inverse] * 2, axis=1)
        total = total + lax.dot_general(
            (normed * norm_ref[...]).astype(jnp.bfloat16), grad_ref[...], TN,
            preferred_element_type=jnp.float32,
        )
    out_ref[...] = total.astype(jnp.bfloat16)


def projection_weights(inputs, inverse, norm, grads):
    width, columns = inputs[0].shape[1], grads[0].shape[1]
    whole = lambda n: (0, 0)
    column = lambda n: (0, n)
    return pl.pallas_call(
        projection_weights_kernel,
        grid=(width // 256,),
        in_specs=[pl.BlockSpec((1, 256), column)]
        + [pl.BlockSpec((SEQ, 256), column)] * 2
        + [pl.BlockSpec((SEQ, 128), whole)] * 2
        + [pl.BlockSpec(part.shape, whole) for part in grads],
        out_specs=pl.BlockSpec((256, columns), lambda n: (n, 0)),
        out_shape=jax.ShapeDtypeStruct((width, columns), jnp.bfloat16),
        compiler_params=pltpu.CompilerParams(vmem_limit_bytes=60 * 2**20),
        cost_estimate=cost(4 * SEQ * columns * width, SEQ * width * 4, 0.43),
    )(norm[None, :], *inputs, *inverse, *grads)


def shift(values, distance, count, axis="tensor"):
    return lax.ppermute(values, axis, [(i, i ^ distance) for i in range(count)])


def gather_kernel(src_ref, own_ref, other_ref, send_sems, recv_sems, local_sem):
    rows = src_ref.shape[0]
    half = rows // 2
    x_top, x_bottom = own_ref.at[pl.ds(rows, half)], own_ref.at[pl.ds(rows + half, half)]
    y_top, y_bottom = other_ref.at[pl.ds(0, half)], other_ref.at[pl.ds(half, half)]
    far_top, far_bottom = other_ref.at[pl.ds(rows, half)], other_ref.at[pl.ds(rows + half, half)]
    top, bottom = src_ref.at[pl.ds(0, half)], src_ref.at[pl.ds(half, half)]
    greet([1, 2])

    def copy(index, from_ref, to_ref, distance):
        return pltpu.make_async_remote_copy(
            src_ref=from_ref, dst_ref=to_ref, send_sem=send_sems.at[index],
            recv_sem=recv_sems.at[index], **remote(distance),
        )

    first = [
        copy(0, bottom, x_bottom, 1), copy(1, top, y_top, 2),
        copy(2, top, x_top, 1), copy(3, bottom, y_bottom, 2),
    ]
    for sent in first:
        sent.start()
    local = pltpu.make_async_copy(src_ref, own_ref.at[pl.ds(0, rows)], local_sem.at[0])
    local.start()
    first[1].wait_recv()
    relay_top = copy(4, y_top, far_top, 1)
    relay_top.start()
    first[0].wait_recv()
    relay_bottom = copy(5, x_bottom, far_bottom, 2)
    relay_bottom.start()
    first[2].wait_recv()
    first[3].wait_recv()
    relay_top.wait_recv()
    relay_bottom.wait_recv()
    for sent in first + [relay_top, relay_bottom]:
        sent.wait_send()
    local.wait()


def gather_rows(values, count):
    if count != 4:
        near = gather_near(values, count)
        return [jnp.concatenate(near[i : i + count // 2], axis=0) for i in (0, count // 2)]
    place = pl.BlockSpec(memory_space=pl.ANY)
    rows, width = values.shape
    wide = jax.ShapeDtypeStruct((2 * rows, width), values.dtype)
    return pl.pallas_call(
        gather_kernel,
        in_specs=[place],
        out_specs=[place] * 2,
        out_shape=[wide, wide],
        scratch_shapes=[
            pltpu.SemaphoreType.DMA((6,)), pltpu.SemaphoreType.DMA((6,)),
            pltpu.SemaphoreType.DMA((1,)),
        ],
        compiler_params=pltpu.CompilerParams(collective_id=1, has_side_effects=True),
        cost_estimate=pl.CostEstimate(
            flops=0, bytes_accessed=values.size * 12, transcendentals=0,
            remote_bytes_transferred=values.size * 6,
        ),
    )(values)


def gather_near(values, count):
    if count == 4:
        return [values, shift(values, 1, count), shift(values, 2, count)]
    whole = lax.all_gather(values, "tensor", axis=0)
    mine = lax.axis_index("tensor")
    return [lax.dynamic_index_in_dim(whole, mine ^ k, 0, False) for k in range(count)]


def gather_far(near, count):
    if count != 4:
        return []
    half = near[0].shape[0] // 2
    return [shift(near[2][:half], 1, count), shift(near[1][half:], 2, count)]


def gather_chunks(values, count):
    near = gather_near(values, count)
    far = gather_far(near, count)
    return near + [jnp.concatenate(far, axis=0)] if far else near


def exchange(parts, distances, count):
    return [part if k == 0 else shift(part, k, count) for k, part in zip(distances, parts)]


def column_piece(weights, columns, core):
    half = weights.shape[0] // 2
    return lax.dynamic_slice(
        weights, (core[0] * half, columns[0]), (half, columns[1] - columns[0])
    )


def sum_first(parts, count):
    if count != 4:
        return None
    return shift(parts[3][0], 1, count), shift(parts[3][1], 2, count)


def sum_adds(parts, first):
    far_top, far_bottom = first
    return (
        (parts[2][0] + far_top.astype(jnp.float32)).astype(jnp.bfloat16),
        (parts[1][1] + far_bottom.astype(jnp.float32)).astype(jnp.bfloat16),
    )


def sum_rest(parts, near, adds, count):
    if count != 4:
        mine = lax.axis_index("tensor")
        half, width = parts[0][0].shape
        stacked = jnp.zeros((count, 2 * half, width), jnp.bfloat16)
        for k in range(count):
            term = jnp.concatenate([side.astype(jnp.bfloat16) for side in parts[k]], axis=0)
            stacked = lax.dynamic_update_index_in_dim(stacked, term, mine ^ k, 0)
        total = lax.psum_scatter(
            stacked.reshape(-1, width), "tensor", scatter_dimension=0, tiled=True
        ).astype(jnp.float32)
        none = jnp.zeros((half, width), jnp.bfloat16)
        return [[total[:half], none, none], [total[half:], none, none]]
    x_top, y_bottom = near
    y_top, x_bottom = shift(adds[0], 2, count), shift(adds[1], 1, count)
    return [[parts[0][0], x_top, y_top], [parts[0][1], x_bottom, y_bottom]]


def sum_near(parts, count):
    if count != 4:
        return ()
    return shift(parts[1][0], 1, count), shift(parts[2][1], 2, count)


def added(own_ref, x_ref, y_ref):
    return own_ref[...] + x_ref[...].astype(jnp.float32) + y_ref[...].astype(jnp.float32)


def own_rows_call(kernel, sums, twos, ones, out_shapes, gains):
    half, width = sums[0][0].shape
    block = min(64, half)
    term = pl.BlockSpec((block, width), lambda i: (i, 0))
    both = pl.BlockSpec((2, block, width), lambda i: (0, i, 0))
    out_specs = [both] * len(out_shapes)
    if gains:
        out_specs.append(pl.BlockSpec((8, width), lambda i: (0, 0)))
        out_shapes = out_shapes + [jax.ShapeDtypeStruct((8, width), jnp.float32)]
    return pl.pallas_call(
        kernel,
        grid=(half // block,),
        in_specs=[term] * 6 + [both] * len(twos) + [pl.BlockSpec((1, width), lambda i: (0, 0))] * len(ones),
        out_specs=out_specs,
        out_shape=out_shapes,
        compiler_params=pltpu.CompilerParams(vmem_limit_bytes=60 * 2**20),
        cost_estimate=cost(half * width * 10, half * width * 10, 1.0),
    )(*sums[0], *sums[1], *twos, *ones)


def resid_back_kernel(*refs):
    dy_ref, resid_ref, norm_ref, grad_ref, low_ref, gains_ref = refs[6:]

    @pl.when(pl.program_id(0) == 0)
    def _():
        gains_ref[...] = jnp.zeros_like(gains_ref)

    for side in range(2):
        grads = added(*refs[3 * side : 3 * side + 3])
        resid = resid_ref[side]
        inverse = rms_scale(resid)
        normed = resid * inverse
        gains_ref[...] += jnp.sum((grads * normed).reshape(-1, 8, grads.shape[1]), axis=0)
        total = dy_ref[side].astype(jnp.float32) + norm_back(grads * norm_ref[...], normed, inverse)
        grad_ref[side] = total
        low_ref[side] = total.astype(jnp.bfloat16)


def output_kernel(*refs):
    resid_ref, out_ref = refs[6:]
    for side in range(2):
        out_ref[side] = (resid_ref[side] + added(*refs[3 * side : 3 * side + 3])).astype(jnp.bfloat16)


def total_everywhere(values, sizes):
    for axis, size in sizes.items():
        distance = 1
        while distance < size:
            values = values + shift(values, distance, size, axis)
            distance *= 2
    return values


def after(value, *others):
    return lax.optimization_barrier((value, others))[0]


def pad_columns(values, width):
    return jnp.pad(values, ((0, 0), (0, width - values.shape[1])))


def gather_weights(*parts):
    return lax.all_gather(jnp.concatenate(parts, axis=1), "dp", axis=0, tiled=True)


def scatter_weights(grads):
    return lax.psum_scatter(grads, "dp", scatter_dimension=0, tiled=True)


def per_device(
    sizes,
    tokens,
    segments,
    positions,
    w_query,
    w_key,
    w_value,
    w_out,
    w_gate,
    w_up,
    w_down,
    norm_attn,
    norm_mlp,
    query_gain,
    key_gain,
    out_grad,
):
    count = sizes["tensor"]
    chunk_rows = tokens.shape[0]
    q_width, key_width = w_query.shape[1], w_key.shape[1]
    kv_width = -(-key_width // 128) * 128
    units = w_gate.shape[1] // 2
    mine = lax.axis_index("tensor").astype(jnp.int32).reshape(1)

    half, width = chunk_rows // 2, tokens.shape[1]
    inner_count = count // 2
    inner, flip = mine % inner_count, mine // inner_count
    core = lax.axis_index("dp").astype(jnp.int32).reshape(1) % 2

    def own_first(values):
        pair = values.reshape(2, SEQ)
        return jnp.where(flip == 0, pair, pair[::-1])

    w_attn = gather_weights(
        w_out, w_query, pad_columns(w_key, kv_width), pad_columns(w_value, kv_width)
    )
    rows_in = gather_rows(tokens, count)
    w_mlp = [
        gather_weights(w_gate[:, part], w_up[:, part], w_down[:, part])
        for part in (slice(0, units), slice(units, 2 * units))
    ]
    segments, positions = own_first(segments), own_first(positions)
    out_near = gather_near(column_piece(after(w_attn, rows_in), (0, q_width), core), count)
    inv_rows, queries, key_sides, value_sides, raw = [], [], [], [], []
    tables = rotary_tables(positions.reshape(-1))
    attended, inv_total, heads = [], [], []
    for sequence in range(2):
        rows = rows_in[sequence]
        if sequence == 1:
            rows = after(rows, attended, out_near)
            out_near = after(out_near, attended)
            out_far = gather_far(out_near, count)
            out_others = out_near[1:] + ([jnp.concatenate(out_far, axis=0)] if out_far else [])
            out_others = out_others + [shift(part, 1, sizes["dp"], "dp") for part in out_others]
        results = project(
            inner, sequence, rows, chunk_rows, norm_attn, w_attn, tables, query_gain, key_gain, q_width, kv_width
        )
        for kept, result in zip((inv_rows, queries, key_sides, value_sides, raw), results):
            kept.append(result)
        result, inverse = attend(
            queries[sequence], key_sides[sequence], value_sides[sequence], segments[sequence]
        )
        attended.append(result)
        inv_total.append(inverse)
        heads.append(gather_chunks(result, count))
    grad_near = gather_near(after(out_grad, heads), count)
    crossed = [
        heads[sequence][:inner_count] + heads[1 - sequence][inner_count:] for sequence in range(2)
    ]
    rows_two, resid = residual(
        jnp.concatenate([inner, core]), rows_in, crossed, w_attn, out_others, norm_mlp, chunk_rows
    )
    resid = resid.reshape(2, half, width)
    grad_near = after(grad_near, rows_two)
    grad_far = gather_far(grad_near, count)
    act_a, factors = hidden_forward(rows_two, w_mlp[0])
    grad_rows = jnp.concatenate(grad_near + after(grad_far, act_a), axis=0)

    grads_a = hidden_backward(grad_rows, factors, w_mlp[0])
    grad_a = contract_rows(rows_two, grads_a).astype(jnp.bfloat16)
    half_columns = column_piece(after(w_attn, grads_a), (q_width, w_attn.shape[1]), core)
    in_near = [shift(half_columns, k, count) for k in range(1, count - 1)]
    if count == 4:
        far_halves = gather_far([half_columns, *in_near], count)
        in_far = [jnp.concatenate(far_halves, axis=0)]
    else:
        far_halves = in_far = [shift(half_columns, count - 1, count)]
    act, grads_b = hidden_units(after(rows_two, grad_a), grad_rows, w_mlp[1], act_a)
    in_others = in_near + in_far
    in_others = in_others + [shift(part, 1, sizes["dp"], "dp") for part in in_others]
    spans = [(2 * units, 0), (2 * units, 0)]

    def two_parts(distances, grads):
        lefts = [(grads, 2 * units, 0), (grads_b, 2 * units, 0)]
        return rows_out(distances, lefts, w_mlp, spans, chunk_rows)

    grad_b = contract_rows(after(rows_two, in_near), grads_b).astype(jnp.bfloat16)
    two = two_parts(list(range(inner_count, count)), after(grads_a, grad_b, far_halves))
    two_first = sum_first(two, count)
    for k in range(1, inner_count):
        two.update(two_parts([k], after(grads_a, two[count - 1])))
    two_near = sum_near(two, count)
    two_adds = sum_adds(two, two_first) if count == 4 else ()
    two.update(two_parts([0], after(grads_a, two[1], two_adds)))
    two_rest = sum_rest(two, two_near, two_adds, count)
    distances = list(range(count))
    out_act = after(act, two[0])
    out = rows_out(
        distances, [(out_act, units, 0), (out_act, units, 1)], w_mlp, [(units, 2), (units, 2)], chunk_rows
    )
    out_first = sum_first(out, count)
    out_near = sum_near(out, count)
    grad_resid, branch_low, gain_mlp = own_rows_call(
        resid_back_kernel,
        after(two_rest, out[0], in_others),
        [out_grad.reshape(2, half, width), resid],
        [norm_mlp[None, :]],
        [
            jax.ShapeDtypeStruct((2, half, width), jnp.float32),
            jax.ShapeDtypeStruct((2, half, width), jnp.bfloat16),
        ],
        True,
    )
    branch_low = branch_low.reshape(chunk_rows, width)
    heads_out = grad_heads(core, branch_low, w_attn, out_others, q_width, count)
    heads_in = exchange(heads_out, distances, count)
    scattered_a = scatter_weights(grad_a)
    scattered_b = scatter_weights(after(grad_b, scattered_a, two[count - 1]))
    grad_down = contract_rows(
        after(grad_rows, heads_out[0], scattered_b, out_first, out_near), act
    ).astype(jnp.bfloat16)
    tops = bottoms = relays = []
    if count == 4:
        top, bottom = after((branch_low[:half], branch_low[half:]), heads_in, grad_down)
        tops = [shift(top, 1, count), shift(top, 2, count)]
    sums, raw_grads = [], []
    for sequence in range(2):
        pieces = heads_in[sequence * inner_count : (sequence + 1) * inner_count]
        if sequence == 0:
            pieces = after(pieces, heads_in, grad_down)
        else:
            pieces = after(pieces, tops, raw_grads)
            if count == 4:
                bottom = after(bottom, tops, raw_grads)
                bottoms = [shift(bottom, 1, count), shift(bottom, 2, count)]
        results = attend_back(
            inner, sequence, queries[sequence], key_sides[sequence], value_sides[sequence],
            segments[sequence], attended[sequence], inv_total[sequence], pieces, raw[sequence], tables,
            query_gain, key_gain,
        )
        raw_grads += results[:inner_count]
        sums.append(results[inner_count:])
    raw_in = exchange(raw_grads, distances, count)
    if count == 4:
        near_bottom, near_top = after((bottoms[0], tops[1]), bottoms, raw_grads)
        relays = [shift(near_top, 1, count), shift(near_bottom, 2, count)]
        branch = (
            [branch_low, tops[0], bottoms[0]],
            [tops[1], bottoms[1], *relays],
        )
    else:
        branch_near = gather_near(branch_low, count)
        branch = (branch_near[:inner_count], branch_near[inner_count:])
    grad_qkv = projection_weights(after(rows_in, raw_grads, bottoms), inv_rows, norm_attn, raw_grads)
    grad_w_gate = jnp.concatenate(
        [scattered_a[:, :units], scattered_b[:, :units]], axis=1
    ).astype(jnp.float32)
    grad_w_up = jnp.concatenate(
        [scattered_a[:, units:], scattered_b[:, units:]], axis=1
    ).astype(jnp.float32)
    grad_attn = out_weights(inner, grad_qkv, after(branch, raw_grads, grad_w_gate, grad_w_up), attended)

    out_adds = sum_adds(out, after(out_first, grad_attn)) if count == 4 else ()
    scattered_down = scatter_weights(after(grad_down, scattered_b, heads_in))
    scattered_attn = scatter_weights(
        after(
            grad_attn, scattered_down, raw_in,
        )
    )

    grad_w_down = scattered_down.astype(jnp.float32)
    grad_tokens, gain_attn = input_back(
        core, after(raw_in, grad_w_down, out_adds), w_attn, in_others, tokens, grad_resid.reshape(chunk_rows, width), norm_attn
    )
    out_rest = sum_rest(out, out_near, out_adds, count)
    gains = [
        jnp.sum(gain_attn, axis=0),
        jnp.sum(gain_mlp, axis=0),
        jnp.sum((sums[0][0] + sums[1][0]).reshape(-1, 64), axis=0),
        jnp.sum((sums[0][1] + sums[1][1]).reshape(-1, 64), axis=0),
    ]
    gains = jnp.concatenate(gains).reshape(-1, 128)
    gains = total_everywhere(gains, sizes).reshape(-1)
    (output,) = own_rows_call(
        output_kernel, after(out_rest, gains), [resid], [], [jax.ShapeDtypeStruct((2, half, width), jnp.bfloat16)],
        False,
    )
    distances = list(range(count))
    key_at = 2 * q_width
    value_at = key_at + kv_width
    return (
        output.reshape(chunk_rows, width),
        grad_tokens.reshape(chunk_rows, width),
        scattered_attn[:, q_width:key_at].astype(jnp.float32),
        scattered_attn[:, key_at : key_at + key_width].astype(jnp.float32),
        scattered_attn[:, value_at : value_at + key_width].astype(jnp.float32),
        scattered_attn[:, :q_width].astype(jnp.float32),
        grad_w_gate,
        grad_w_up,
        grad_w_down,
        gains[:width],
        gains[width : 2 * width],
        gains[2 * width : 2 * width + 64],
        gains[2 * width + 64 : 2 * width + 128],
    )


def solution(mesh):
    return jax.shard_map(
        functools.partial(per_device, dict(mesh.shape)),
        mesh=mesh,
        in_specs=(
            P(("dp", "tensor"), None),
            P("dp"),
            P("dp"),
            P("dp", "tensor"),
            P("dp", "tensor"),
            P("dp", "tensor"),
            P("dp", "tensor"),
            P("dp", "tensor"),
            P("dp", "tensor"),
            P("dp", "tensor"),
            P(),
            P(),
            P(),
            P(),
            P(("dp", "tensor"), None),
        ),
        out_specs=(
            P(("dp", "tensor"), None),
            P(("dp", "tensor"), None),
            P("dp", "tensor"),
            P("dp", "tensor"),
            P("dp", "tensor"),
            P("dp", "tensor"),
            P("dp", "tensor"),
            P("dp", "tensor"),
            P("dp", "tensor"),
            P(),
            P(),
            P(),
            P(),
        ),
        check_vma=False,
    )
```

```python
import functools

import jax
import jax.numpy as jnp
from jax import lax
from jax.experimental import pallas as pl
from jax.experimental.pallas import tpu as pltpu
from jax.sharding import PartitionSpec as P

EPS = 1e-05
THETA = 1000000.0
SEQ = 1024
TILE = 256
LOG2E = 1.4426950408889634
MASKED = -1e30
NT = (((1,), (1,)), ((), ()))
TN = (((0,), (0,)), ((), ()))


def rms_scale(values):
    return lax.rsqrt(jnp.mean(values * values, axis=-1, keepdims=True) + EPS)


def norm_back(grad_normed, normed, inverse):
    return inverse * (grad_normed - normed * jnp.mean(grad_normed * normed, axis=-1, keepdims=True))


def rotary_tables(places):
    lane = jnp.arange(128)
    frequency = THETA ** (-(lane % 32).astype(jnp.float32) * 2.0 / 64)
    angles = places.astype(jnp.float32)[:, None] * frequency[None, :]
    sine = jnp.sin(angles)
    upper = (lane % 64 >= 32)[None, :]
    return jnp.cos(angles), jnp.where(upper, 0.0, -sine), jnp.where(upper, sine, 0.0)


def contract_rows(left, right):
    return lax.dot_general(
        left, right, (((0,), (0,)), ((), ())), preferred_element_type=jnp.float32
    )


def half_lanes(rows):
    return lax.broadcasted_iota(jnp.int32, (rows, 128), 1) < 64


def ones_side(side, rows):
    low = half_lanes(rows)
    return jnp.where(low if side == 0 else ~low, 1.0, 0.0).astype(jnp.bfloat16)


def attend_kernel(q_ref, k_ref, v_ref, segc_ref, segr_ref, out_ref, inv_ref, bias_ref, total_ref):
    coef = LOG2E * 64 ** (-0.5)

    @pl.when(pl.program_id(1) == 0)
    def _():
        for at in range(0, SEQ, TILE):
            end = at + TILE
            rows = lax.broadcasted_iota(jnp.int32, (TILE, end), 0) + at
            cols = lax.broadcasted_iota(jnp.int32, (TILE, end), 1)
            allowed = (segc_ref[at:end, :] == segr_ref[0, :, :end]) & (cols <= rows)
            bias_ref[at:end, :end] = jnp.where(allowed, 0.0, MASKED)

    for side in range(2):
        lanes = slice(side * 128, side * 128 + 128)
        for key_at in range(0, SEQ, TILE):
            keys, rows = slice(key_at, key_at + TILE), slice(key_at, SEQ)
            scores = lax.dot_general(
                q_ref[rows, :], k_ref[keys, lanes], NT, preferred_element_type=jnp.float32
            )
            weights = jnp.exp2(scores * coef + bias_ref[rows, keys]).astype(jnp.bfloat16)
            mixed = jnp.concatenate([v_ref[keys, lanes], ones_side(side, TILE)], axis=1)
            part = jnp.dot(weights, mixed, preferred_element_type=jnp.float32)
            if side == 0 and key_at == 0:
                total_ref[...] = part
            else:
                total_ref[rows, :] += part
    inverse = 1.0 / total_ref[:, 128:]
    out_ref[...] = (total_ref[:, :128] * inverse).astype(jnp.bfloat16)
    inv_ref[...] = inverse


def unrotated(grads, raw, cosine, sine_low, sine_high, gain):
    grads = grads * 0.125
    turned = (
        grads * cosine
        - pltpu.roll(grads, 96, 1) * sine_low
        - pltpu.roll(grads, 32, 1) * sine_high
    )
    inverse = head_inverse(raw)
    normed = raw * inverse
    scaled = turned * gain
    change = inverse * (scaled - normed * head_mean(scaled * normed))
    return change, jnp.sum((turned * normed).reshape(-1, 8, 128), axis=0)


def attend_back_kernel(
    chunks, inner_ref, q_ref, k_ref, v_ref, segc_ref, segr_ref, out_ref, inv_ref,
    qraw_ref, kraw_ref, cos_ref, low_ref, high_ref, qgain_ref, kgain_ref, *refs,
):
    pieces, results = refs[:chunks], refs[chunks : 2 * chunks]
    (
        qsum_ref, ksum_ref, bias_ref, mix_ref, qside_ref, gside_ref,
        dq_ref, dk_ref, dv_ref, kpair_ref, vpair_ref, grad_ref,
    ) = refs[2 * chunks :]
    chunk_rows = SEQ // chunks
    q_width = 128 * pl.num_programs(1)
    kv_width = (results[0].shape[1] - q_width) // 2

    def rows_of(k):
        return pl.ds(pl.multiple_of((inner_ref[0] ^ k) * chunk_rows, chunk_rows), chunk_rows)

    def put(values, place):
        dq_ref[...] = values
        for k, result_ref in enumerate(results):
            lanes = pl.ds(pl.multiple_of(place, 128), 128)
            result_ref[:, lanes] = dq_ref[rows_of(k), :].astype(jnp.bfloat16)

    coef = LOG2E * 64 ** (-0.5)
    step = pl.program_id(1)

    @pl.when(step == 0)
    def _():
        for key_at in range(0, SEQ, TILE):
            key_end = key_at + TILE
            keys = lax.broadcasted_iota(jnp.int32, (TILE, SEQ - key_at), 0) + key_at
            rows = lax.broadcasted_iota(jnp.int32, (TILE, SEQ - key_at), 1) + key_at
            allowed = (segc_ref[key_at:key_end, :] == segr_ref[0, :, key_at:]) & (keys <= rows)
            bias_ref[key_at:key_end, key_at:] = jnp.where(allowed, 0.0, MASKED)

    @pl.when((step == 0) & (pl.program_id(0) == 0))
    def _():
        qsum_ref[...] = jnp.zeros_like(qsum_ref)
        ksum_ref[...] = jnp.zeros_like(ksum_ref)

    @pl.when(lax.rem(step, 4) == 0)
    def _():
        kpair_ref[...] = jnp.zeros_like(kpair_ref)
        vpair_ref[...] = jnp.zeros_like(vpair_ref)

    @pl.when(lax.rem(step, 2) == 0)
    def _():
        dk_ref[...] = jnp.zeros_like(dk_ref)
        dv_ref[...] = jnp.zeros_like(dv_ref)

    for k, piece_ref in enumerate(pieces):
        grad_ref[rows_of(k), :] = piece_ref[...].astype(jnp.float32)
    low = half_lanes(SEQ)
    scaled = grad_ref[...] * inv_ref[...]
    scaled_low = scaled.astype(jnp.bfloat16)
    mix_ref[:, :128] = scaled_low
    mix_ref[:, 128:] = -(scaled * out_ref[...].astype(jnp.float32)).astype(jnp.bfloat16)
    none = jnp.zeros_like(scaled_low)
    queries = q_ref[...]
    gside_ref[:, :128] = jnp.where(low, scaled_low, none)
    gside_ref[:, 128:] = jnp.where(low, none, scaled_low)
    qside_ref[:, :128] = jnp.where(low, queries, none)
    qside_ref[:, 128:] = jnp.where(low, none, queries)

    for key_at in range(0, SEQ, TILE):
        keys, rows = slice(key_at, key_at + TILE), slice(key_at, SEQ)
        for side in range(2):
            lanes = slice(side * 128, side * 128 + 128)
            key_side = k_ref[keys, lanes]
            value_side = jnp.concatenate([v_ref[keys, lanes], ones_side(side, TILE)], axis=1)
            scores = lax.dot_general(
                key_side, q_ref[rows, :], NT, preferred_element_type=jnp.float32
            )
            weights = jnp.exp2(scores * coef + bias_ref[keys, rows])
            change = lax.dot_general(
                value_side, mix_ref[rows, :], NT, preferred_element_type=jnp.float32
            )
            grads = (weights * change).astype(jnp.bfloat16)
            dv_ref[keys, :] += jnp.dot(
                weights.astype(jnp.bfloat16),
                gside_ref[rows, lanes],
                preferred_element_type=jnp.float32,
            )
            dk_ref[keys, :] += jnp.dot(
                grads, qside_ref[rows, lanes], preferred_element_type=jnp.float32
            )
            dq = lax.dot_general(grads, key_side, TN, preferred_element_type=jnp.float32)
            if key_at == 0 and side == 0:
                dq_ref[...] = dq
            else:
                dq_ref[rows, :] += dq

    cosine, sine_low, sine_high = cos_ref[...], low_ref[...], high_ref[...]
    change, sums = unrotated(
        dq_ref[...], qraw_ref[...], cosine, sine_low, sine_high, qgain_ref[...]
    )
    qsum_ref[...] += sums
    put(change, step * 128)

    @pl.when(lax.rem(step, 2) == 1)
    def _():
        mine = low == (lax.rem(step, 4) == 1)
        for sum_ref, pair_ref in ((dk_ref, kpair_ref), (dv_ref, vpair_ref)):
            sums = sum_ref[...]
            pair_ref[...] = jnp.where(mine, sums + pltpu.roll(sums, 64, 1), pair_ref[...])

    @pl.when((lax.rem(step, 4) == 3) | (step == pl.num_programs(1) - 1))
    def _():
        change, sums = unrotated(
            kpair_ref[...], kraw_ref[...], cosine, sine_low, sine_high, kgain_ref[...]
        )
        ksum_ref[...] += sums
        put(change, q_width + step // 4 * 128)
        put(vpair_ref[...], q_width + kv_width + step // 4 * 128)


def attention_specs():
    pair = pl.BlockSpec((SEQ, 128), lambda s, p, *_: (s, p))
    group = pl.BlockSpec((SEQ, 256), lambda s, p, *_: (s, p // 2))
    seg_col = pl.BlockSpec((SEQ, 1), lambda s, p, *_: (s, 0))
    seg_row = pl.BlockSpec((1, 1, SEQ), lambda s, p, *_: (s, 0, 0))
    return pair, group, seg_col, seg_row


def attend(queries, key_sides, value_sides, segments):
    rows, width = queries.shape
    sequences, pairs = rows // SEQ, width // 128
    pair, group, seg_col, seg_row = attention_specs()
    work = rows * SEQ * width
    return pl.pallas_call(
        attend_kernel,
        grid=(sequences, pairs),
        in_specs=[pair, group, group, seg_col, seg_row],
        out_specs=[pair, pair],
        out_shape=[
            jax.ShapeDtypeStruct((rows, width), jnp.bfloat16),
            jax.ShapeDtypeStruct((rows, width), jnp.float32),
        ],
        scratch_shapes=[pltpu.VMEM((SEQ, SEQ), jnp.float32), pltpu.VMEM((SEQ, 256), jnp.float32)],
        compiler_params=pltpu.CompilerParams(vmem_limit_bytes=60 * 2**20),
        cost_estimate=pl.CostEstimate(
            flops=42 * work // 10, bytes_accessed=rows * width * 12, transcendentals=work // 128
        ),
    )(queries, key_sides, value_sides, segments[:, None], segments.reshape(sequences, 1, SEQ))


def attend_back(
    inner, sequence, queries, key_sides, value_sides, segments, attended, inverse, pieces, raw, tables,
    query_gain, key_gain,
):
    width = queries.shape[1]
    pairs, chunks, chunk_rows = width // 128, len(pieces), pieces[0].shape[0]
    kv_width = key_sides.shape[1] // 4
    pair, group, seg_col, seg_row = attention_specs()
    kv_raw = pl.BlockSpec((SEQ, 128), lambda s, p, *_: (0, width // 128 + p // 4))
    table = pl.BlockSpec((SEQ, 128), lambda s, p, *_: (sequence, 0))
    gain = pl.BlockSpec((1, 128), lambda s, p, *_: (0, 0))
    total = pl.BlockSpec((8, 128), lambda s, p, *_: (0, 0))
    piece = pl.BlockSpec((chunk_rows, 128), lambda s, p, *_: (0, p))
    columns = width + 2 * kv_width
    work = SEQ * SEQ * width
    flat = pltpu.VMEM((SEQ, 128), jnp.float32)
    return pl.pallas_call(
        functools.partial(attend_back_kernel, chunks),
        grid_spec=pltpu.PrefetchScalarGridSpec(
            num_scalar_prefetch=1,
            grid=(1, pairs),
            in_specs=[pair, group, group, seg_col, seg_row, pair, pair]
            + [pair, kv_raw, table, table, table, gain, gain]
            + [piece] * chunks,
            out_specs=[pl.BlockSpec((chunk_rows, columns), lambda s, p, *_: (0, 0))] * chunks
            + [total, total],
            scratch_shapes=[
                pltpu.VMEM((SEQ, SEQ), jnp.float32),
                pltpu.VMEM((SEQ, 256), jnp.bfloat16),
                pltpu.VMEM((SEQ, 256), jnp.bfloat16),
                pltpu.VMEM((SEQ, 256), jnp.bfloat16),
                flat, flat, flat, flat, flat, flat,
            ],
        ),
        out_shape=[jax.ShapeDtypeStruct((chunk_rows, columns), jnp.bfloat16)] * chunks
        + [jax.ShapeDtypeStruct((8, 128), jnp.float32)] * 2,
        compiler_params=pltpu.CompilerParams(vmem_limit_bytes=60 * 2**20),
        cost_estimate=pl.CostEstimate(
            flops=110 * work // 10, bytes_accessed=SEQ * width * 20, transcendentals=work // 128
        ),
    )(
        inner, queries, key_sides, value_sides, segments[:, None], segments.reshape(-1, 1, SEQ),
        attended, inverse, raw, raw, *tables,
        jnp.tile(query_gain, 2)[None, :], jnp.tile(key_gain, 2)[None, :], *pieces,
    )


def cost(flops, moved, share):
    return pl.CostEstimate(
        flops=int(0.2 * flops / share), bytes_accessed=int(0.2 * moved), transcendentals=0
    )


def head_inverse(values):
    squares = values * values
    high = squares.astype(jnp.bfloat16)
    low = (squares - high.astype(jnp.float32)).astype(jnp.bfloat16)
    return lax.rsqrt(head_sum(high, low) * (1.0 / 64) + EPS)


def head_sum(high, low):
    from_head = lax.broadcasted_iota(jnp.int32, (128, 128), 0) // 64
    to_head = lax.broadcasted_iota(jnp.int32, (128, 128), 1) // 64
    same = jnp.where(from_head == to_head, 1.0, 0.0).astype(jnp.bfloat16)
    return jnp.dot(high, same, preferred_element_type=jnp.float32) + jnp.dot(
        low, same, preferred_element_type=jnp.float32
    )


def head_mean(values):
    high = values.astype(jnp.bfloat16)
    low = (values - high.astype(jnp.float32)).astype(jnp.bfloat16)
    return head_sum(high, low) * (1.0 / 64)


def project_kernel(
    pieces, inner_ref, *refs,
):
    norm_ref, w_ref, cos_ref, low_ref, high_ref, qgain_ref, kgain_ref = refs[pieces : pieces + 7]
    inv_ref, q_ref, k_ref, v_ref, raw_ref = refs[pieces + 7 :]
    inputs = refs[0][...].astype(jnp.float32)
    inverse = rms_scale(inputs)
    hidden = (inputs * inverse * norm_ref[...]).astype(jnp.bfloat16)
    inv_ref[...] = jnp.broadcast_to(inverse, inv_ref.shape)
    q_width, kv_width = q_ref.shape[1], k_ref.shape[1] // 4
    cosine, sine_low, sine_high = cos_ref[...], low_ref[...], high_ref[...]
    lower = lax.broadcasted_iota(jnp.int32, cosine.shape, 1) < 64
    none = jnp.zeros_like(cosine)

    def rotated(raw, gain):
        scaled = raw * head_inverse(raw) * gain
        return (
            scaled * cosine
            + pltpu.roll(scaled, 96, 1) * sine_low
            + pltpu.roll(scaled, 32, 1) * sine_high
        )

    def to_sides(pair, out_ref, at):
        first, second = jnp.where(lower, pair, none), jnp.where(lower, none, pair)
        sides = (first, pltpu.roll(first, 64, 1), pltpu.roll(second, 64, 1), second)
        for index, side in enumerate(sides):
            lanes = slice(at * 4 + index * 128, at * 4 + index * 128 + 128)
            out_ref[:, lanes] = side.astype(jnp.bfloat16)

    wide = jnp.dot(hidden, w_ref[:, q_width:], preferred_element_type=jnp.float32)
    raw_ref[...] = wide[:, : q_width + kv_width]
    for at in range(0, q_width, 128):
        q_ref[:, at : at + 128] = rotated(wide[:, at : at + 128], qgain_ref[...]).astype(
            jnp.bfloat16
        )
    for at in range(0, kv_width, 128):
        place = q_width + at
        to_sides(rotated(wide[:, place : place + 128], kgain_ref[...]), k_ref, at)
        place = q_width + kv_width + at
        to_sides(wide[:, place : place + 128], v_ref, at)


def placed(chunk_rows, block):
    per = chunk_rows // block
    here = lambda r, inner: (r, 0)
    there = lambda r, inner: ((r // per ^ inner[0]) * per + r % per, 0)
    return here, there


def project(inner, sequence, inputs, chunk_rows, norm, weights, tables, query_gain, key_gain, q_width, kv_width):
    rows, width = inputs.shape
    block = chunk_rows
    here, there = placed(block, block)
    fixed = lambda r, mine: (0, 0)
    used = q_width + 2 * kv_width
    table = pl.BlockSpec(
        (block, 128), lambda r, inner: (sequence * (rows // block) + there(r, inner)[0], 0)
    )
    gain = pl.BlockSpec((1, 128), fixed)
    return pl.pallas_call(
        functools.partial(project_kernel, 1),
        grid_spec=pltpu.PrefetchScalarGridSpec(
            num_scalar_prefetch=1,
            grid=(rows // block,),
            in_specs=[
                pl.BlockSpec((block, width), here),
                pl.BlockSpec((1, width), fixed),
                pl.BlockSpec(weights.shape, fixed, pipeline_mode=pl.Buffered(1)),
                table, table, table, gain, gain,
            ],
            out_specs=[
                pl.BlockSpec((block, 128), here),
                pl.BlockSpec((block, q_width), there),
                pl.BlockSpec((block, 4 * kv_width), there),
                pl.BlockSpec((block, 4 * kv_width), there),
                pl.BlockSpec((block, q_width + kv_width), there),
            ],
        ),
        out_shape=[
            jax.ShapeDtypeStruct((rows, 128), jnp.float32),
            jax.ShapeDtypeStruct((rows, q_width), jnp.bfloat16),
            jax.ShapeDtypeStruct((rows, 4 * kv_width), jnp.bfloat16),
            jax.ShapeDtypeStruct((rows, 4 * kv_width), jnp.bfloat16),
            jax.ShapeDtypeStruct((rows, q_width + kv_width), jnp.float32),
        ],
        compiler_params=pltpu.CompilerParams(vmem_limit_bytes=60 * 2**20),
        cost_estimate=cost(2 * rows * width * used, rows * width * 6, 0.22),
    )(
        inner, inputs, norm[None, :], weights, *tables,
        jnp.tile(query_gain, 2)[None, :], jnp.tile(key_gain, 2)[None, :],
    )


def heads_kernel(count, core_ref, grads_ref, *refs):
    rights, outs = refs[: 2 * count - 1], refs[2 * count - 1 :]
    outs[0][...] = jnp.dot(
        grads_ref[...], rights[0][...], preferred_element_type=jnp.float32
    ).astype(jnp.bfloat16)
    half = rights[1].shape[0]
    near = grads_ref[:, pl.ds(pl.multiple_of(core_ref[0] * half, half), half)]
    other = grads_ref[:, pl.ds(pl.multiple_of((1 - core_ref[0]) * half, half), half)]
    for k in range(1, count):
        outs[k][...] = (
            jnp.dot(near, rights[k][...], preferred_element_type=jnp.float32)
            + jnp.dot(other, rights[count - 1 + k][...], preferred_element_type=jnp.float32)
        ).astype(jnp.bfloat16)


def grad_heads(core, grads, own, others, q_width, count):
    rows, width = grads.shape
    fixed = lambda i, core: (0, 0)
    return pl.pallas_call(
        functools.partial(heads_kernel, count),
        grid_spec=pltpu.PrefetchScalarGridSpec(
            num_scalar_prefetch=1,
            grid=(1,),
            in_specs=[pl.BlockSpec(grads.shape, fixed), pl.BlockSpec((width, q_width), fixed)]
            + [pl.BlockSpec(piece.shape, fixed) for piece in others],
            out_specs=[pl.BlockSpec((rows, q_width), fixed)] * count,
        ),
        out_shape=[jax.ShapeDtypeStruct((rows, q_width), jnp.bfloat16)] * count,
        compiler_params=pltpu.CompilerParams(vmem_limit_bytes=60 * 2**20),
        cost_estimate=cost(2 * rows * width * q_width * count, rows * width, 2.67),
    )(core, grads, own, *others)


def peer(distance):
    mine = lax.axis_index("tensor")
    if distance == 1:
        return mine + 1 - 2 * (mine % 2)
    return (mine + 2) % 4 if distance == 2 else 3 - mine


def remote(distance):
    return dict(device_id={"tensor": peer(distance)}, device_id_type=pl.DeviceIdType.MESH)


def greet(distances):
    barrier = pltpu.get_barrier_semaphore()
    for distance in distances:
        pl.semaphore_signal(barrier, inc=1, **remote(distance))
    pl.semaphore_wait(barrier, len(distances))


def hidden_kernel(x_ref, dy_ref, w_ref, filled_ref, act_ref, grads_ref):
    units = act_ref.shape[1]
    inputs, cotangent = x_ref[...], dy_ref[...]
    for at in range(0, units, 256):
        lanes = slice(at, at + 256)
        gate = jnp.dot(inputs, w_ref[:, lanes], preferred_element_type=jnp.float32)
        up = jnp.dot(
            inputs, w_ref[:, units + at : units + at + 256], preferred_element_type=jnp.float32
        )
        change = jnp.dot(
            cotangent, w_ref[:, 2 * units + at : 2 * units + at + 256],
            preferred_element_type=jnp.float32,
        )
        sigmoid = 1.0 / (1.0 + jnp.exp(-gate))
        silu = gate * sigmoid
        act_ref[:, lanes] = (silu * up).astype(jnp.bfloat16)
        grads_ref[:, lanes] = (change * up * sigmoid * (1.0 + gate - silu)).astype(jnp.bfloat16)
        grads_ref[:, units + at : units + at + 256] = (change * silu).astype(jnp.bfloat16)


def hidden_units(inputs, cotangent, weights, filled):
    rows, width = inputs.shape
    units = weights.shape[1] // 3
    block = min(512, rows)
    row = lambda r: (r, 0)
    return pl.pallas_call(
        hidden_kernel,
        grid=(rows // block,),
        in_specs=[
            pl.BlockSpec((block, width), row),
            pl.BlockSpec((block, width), row),
            pl.BlockSpec(weights.shape, lambda r: (0, 0), pipeline_mode=pl.Buffered(1)),
            pl.BlockSpec(memory_space=pl.ANY),
        ],
        out_specs=[
            pl.BlockSpec((block, units), lambda r: (r, 1)),
            pl.BlockSpec((block, 2 * units), row),
        ],
        out_shape=[jax.ShapeDtypeStruct((rows, 2 * units), jnp.bfloat16)] * 2,
        input_output_aliases={3: 0},
        compiler_params=pltpu.CompilerParams(vmem_limit_bytes=60 * 2**20),
        cost_estimate=cost(6 * rows * width * units, (rows * width + width * units) * 6, 0.63),
    )(inputs, cotangent, weights, filled)


def hidden_forward_kernel(x_ref, w_ref, act_ref, factors_ref):
    units = act_ref.shape[1]
    inputs = x_ref[...]
    for at in range(0, units, 256):
        lanes, beside = slice(at, at + 256), slice(units + at, units + at + 256)
        gate = jnp.dot(inputs, w_ref[:, lanes], preferred_element_type=jnp.float32)
        up = jnp.dot(inputs, w_ref[:, beside], preferred_element_type=jnp.float32)
        sigmoid = 1.0 / (1.0 + jnp.exp(-gate))
        silu = gate * sigmoid
        act_ref[:, lanes] = (silu * up).astype(jnp.bfloat16)
        factors_ref[:, lanes] = (up * sigmoid * (1.0 + gate - silu)).astype(jnp.bfloat16)
        factors_ref[:, beside] = silu.astype(jnp.bfloat16)


def hidden_forward(inputs, weights):
    rows, width = inputs.shape
    units = weights.shape[1] // 3
    block = min(512, rows)
    row = lambda r: (r, 0)
    return pl.pallas_call(
        hidden_forward_kernel,
        grid=(rows // block,),
        in_specs=[
            pl.BlockSpec((block, width), row),
            pl.BlockSpec((width, 2 * units), lambda r: (0, 0), pipeline_mode=pl.Buffered(1)),
        ],
        out_specs=[pl.BlockSpec((block, units), row), pl.BlockSpec((block, 2 * units), row)],
        out_shape=[jax.ShapeDtypeStruct((rows, 2 * units), jnp.bfloat16)] * 2,
        compiler_params=pltpu.CompilerParams(vmem_limit_bytes=60 * 2**20),
        cost_estimate=cost(4 * rows * width * units, (rows * width + width * units) * 4, 0.63),
    )(inputs, weights)


def hidden_backward_kernel(dy_ref, factors_ref, w_ref, grads_ref):
    units = w_ref.shape[1]
    cotangent = dy_ref[...]
    for at in range(0, units, 256):
        change = jnp.dot(
            cotangent, w_ref[:, at : at + 256], preferred_element_type=jnp.float32
        )
        for lanes in (slice(at, at + 256), slice(units + at, units + at + 256)):
            grads_ref[:, lanes] = (change * factors_ref[:, lanes].astype(jnp.float32)).astype(
                jnp.bfloat16
            )


def hidden_backward(cotangent, factors, weights):
    rows, width = cotangent.shape
    units = weights.shape[1] // 3
    block = min(512, rows)
    row = lambda r: (r, 0)
    return pl.pallas_call(
        hidden_backward_kernel,
        grid=(rows // block,),
        in_specs=[
            pl.BlockSpec((block, width), row),
            pl.BlockSpec((block, 2 * units), row),
            pl.BlockSpec((width, units), lambda r: (0, 2), pipeline_mode=pl.Buffered(1)),
        ],
        out_specs=pl.BlockSpec((block, 2 * units), row),
        out_shape=jax.ShapeDtypeStruct((rows, 2 * units), jnp.bfloat16),
        compiler_params=pltpu.CompilerParams(vmem_limit_bytes=60 * 2**20),
        cost_estimate=cost(2 * rows * width * units, (rows * width + width * units) * 4, 0.63),
    )(cotangent, factors, weights)


def half_types(distance):
    if distance == 0:
        return (jnp.float32, jnp.float32)
    if distance == 1:
        return (jnp.bfloat16, jnp.float32)
    if distance == 2:
        return (jnp.float32, jnp.bfloat16)
    return (jnp.bfloat16, jnp.bfloat16)


def rows_out_kernel(terms, *refs):
    outs = refs[2 * terms :]
    total = None
    for left_ref, right_ref in zip(refs[:terms], refs[terms : 2 * terms]):
        product = lax.dot_general(
            left_ref[...], right_ref[...], NT, preferred_element_type=jnp.float32
        )
        total = product if total is None else total + product
    half = outs[0].shape[0]
    for index, out_ref in enumerate(outs):
        out_ref[...] = total[index * half : (index + 1) * half].astype(out_ref.dtype)


def rows_out(distances, lefts, rights, spans, chunk_rows):
    width, rows = rights[0].shape[0], len(distances) * chunk_rows
    first = distances[0] // len(distances)
    halves = [dtype for k in distances for dtype in half_types(k)]
    in_specs = [
        pl.BlockSpec(
            (rows, left[1]), lambda n, index=left[2]: (first, index), pipeline_mode=pl.Buffered(1)
        )
        for left in lefts
    ] + [
        pl.BlockSpec((256, columns), lambda n, index=index: (n, index)) for columns, index in spans
    ]
    depth = sum(left[1] for left in lefts)
    outs = pl.pallas_call(
        functools.partial(rows_out_kernel, len(lefts)),
        grid=(width // 256,),
        in_specs=in_specs,
        out_specs=[pl.BlockSpec((chunk_rows // 2, 256), lambda n: (0, n))] * len(halves),
        out_shape=[jax.ShapeDtypeStruct((chunk_rows // 2, width), dtype) for dtype in halves],
        compiler_params=pltpu.CompilerParams(vmem_limit_bytes=60 * 2**20),
        cost_estimate=cost(2 * rows * depth * width, depth * rows // 4, 4.07),
    )(*(left[0] for left in lefts), *rights)
    return {k: (outs[2 * i], outs[2 * i + 1]) for i, k in enumerate(distances)}


def resid_kernel(count, place_ref, *refs):
    inputs, lefts = refs[:2], (refs[2 : 2 + count], refs[2 + count : 2 + 2 * count])
    rights = refs[2 + 2 * count : 1 + 4 * count]
    norm_ref, hidden_ref, resid_ref, sums_ref = refs[1 + 4 * count :]
    half = sums_ref.shape[1] // 2
    blocks = pl.num_programs(0) // 2

    def block(x_ref, left_refs):
        for core, others in (
            (place_ref[1], rights[1:count]), (1 - place_ref[1], rights[count:])
        ):
            start = pl.multiple_of(core * half, half)
            total = lax.dot_general(
                left_refs[0][...], rights[0][pl.ds(start, half), :], NT,
                preferred_element_type=jnp.float32,
            )
            for left_ref, right_ref in zip(left_refs[1:], others):
                total = total + lax.dot_general(
                    left_ref[...], right_ref[...], NT, preferred_element_type=jnp.float32
                )
            sums_ref[:, pl.ds(start, half)] = total
        resid = x_ref[...].astype(jnp.float32) + sums_ref[...]
        hidden_ref[...] = (resid * rms_scale(resid) * norm_ref[...]).astype(jnp.bfloat16)

        @pl.when(pl.program_id(0) < resid_ref.shape[0])
        def _():
            resid_ref[pl.program_id(0)] = resid

    for sequence in range(2):

        @pl.when(pl.program_id(0) // blocks == sequence)
        def _():
            block(inputs[sequence], lefts[sequence])


def residual(place, inputs, heads, own, others, norm, chunk_rows):
    width, count = inputs[0].shape[1], len(heads[0])
    q_width = heads[0][0].shape[1]
    rows, block = 2 * SEQ, min(512, chunk_rows)
    here, there = placed(chunk_rows, block)
    blocks = SEQ // block
    fixed = lambda r, place: (0, 0)
    once = pl.Buffered(1)
    steps = (
        lambda r: jnp.minimum(r, blocks - 1),
        lambda r: jnp.maximum(r - blocks, 0),
    )
    return pl.pallas_call(
        functools.partial(resid_kernel, count),
        grid_spec=pltpu.PrefetchScalarGridSpec(
            num_scalar_prefetch=1,
            grid=(rows // block,),
            in_specs=[
                pl.BlockSpec((block, width), lambda r, place, step=step: here(step(r), place))
                for step in steps
            ]
            + [
                pl.BlockSpec((block, q_width), lambda r, place, step=step: there(step(r), place))
                for step in steps
                for _ in range(count)
            ]
            + [pl.BlockSpec((width, q_width), fixed, pipeline_mode=once)]
            + [pl.BlockSpec(piece.shape, fixed, pipeline_mode=once) for piece in others]
            + [pl.BlockSpec((1, width), fixed)],
            out_specs=[
                pl.BlockSpec((block, width), here),
                pl.BlockSpec((chunk_rows // block, block, width), lambda r, place: (0, 0, 0)),
            ],
            scratch_shapes=[pltpu.VMEM((block, width), jnp.float32)],
        ),
        out_shape=[
            jax.ShapeDtypeStruct((rows, width), jnp.bfloat16),
            jax.ShapeDtypeStruct((chunk_rows // block, block, width), jnp.float32),
        ],
        compiler_params=pltpu.CompilerParams(vmem_limit_bytes=60 * 2**20),
        cost_estimate=cost(2 * rows * width * width, rows * width * 8, 0.46),
    )(place, *inputs, *heads[0], *heads[1], own, *others, norm[None, :])


def input_kernel(count, core_ref, *refs):
    lefts, rights = refs[:count], refs[count : 3 * count - 1]
    x_ref, grad_ref, norm_ref, out_ref, gains_ref, sums_ref = refs[3 * count - 1 :]
    used = lefts[0].shape[1]
    step, steps = pl.program_id(0), pl.num_programs(0)

    def block(others):
        own = rights[0][:, rights[0].shape[1] - used :]
        total = lax.dot_general(lefts[0][...], own, NT, preferred_element_type=jnp.float32)
        for left_ref, right_ref in zip(lefts[1:], others):
            total = total + lax.dot_general(
                left_ref[...], right_ref[...], NT, preferred_element_type=jnp.float32
            )
        sums_ref[:, pl.ds(pl.multiple_of(step * 256, 256), 256)] = total

    for half in range(2):

        @pl.when(step // (steps // 2) == (core_ref[0] if half == 0 else 1 - core_ref[0]))
        def _():
            block(rights[1 + half * (count - 1) : 1 + (half + 1) * (count - 1)])

    @pl.when(step == steps - 1)
    def _():
        gains_ref[...] = jnp.zeros_like(gains_ref)
        for at in range(0, sums_ref.shape[0], 64):
            rows = slice(at, at + 64)
            grads = sums_ref[rows, :]
            inputs = x_ref[rows, :].astype(jnp.float32)
            inverse = rms_scale(inputs)
            normed = inputs * inverse
            gains_ref[...] += jnp.sum((grads * normed).reshape(-1, 8, grads.shape[1]), axis=0)
            out_ref[rows, :] = grad_ref[rows, :] + norm_back(
                grads * norm_ref[...], normed, inverse
            )


def input_back(core, grads, own, others, inputs, grad_resid, norm):
    rows, width = inputs.shape
    count, used = len(grads), grads[0].shape[1]
    steps = width // 256
    whole = lambda n, core: (0, 0)
    near = lambda n, core: (jnp.clip(n - core[0] * (steps // 2), 0, steps // 2 - 1), 0)
    other = lambda n, core: (jnp.clip(n - (1 - core[0]) * (steps // 2), 0, steps // 2 - 1), 0)
    once = pl.Buffered(1)
    return pl.pallas_call(
        functools.partial(input_kernel, count),
        grid_spec=pltpu.PrefetchScalarGridSpec(
            num_scalar_prefetch=1,
            grid=(steps,),
            in_specs=[pl.BlockSpec((rows, used), whole, pipeline_mode=once)] * count
            + [pl.BlockSpec((256, own.shape[1]), lambda n, core: (n, 0))]
            + [pl.BlockSpec((256, used), near)] * (count - 1)
            + [pl.BlockSpec((256, used), other)] * (count - 1)
            + [pl.BlockSpec((rows, width), whole, pipeline_mode=once)] * 2
            + [pl.BlockSpec((1, width), whole)],
            out_specs=[pl.BlockSpec((rows, width), whole), pl.BlockSpec((8, width), whole)],
            scratch_shapes=[pltpu.VMEM((rows, width), jnp.float32)],
        ),
        out_shape=[
            jax.ShapeDtypeStruct((rows, width), jnp.float32),
            jax.ShapeDtypeStruct((8, width), jnp.float32),
        ],
        compiler_params=pltpu.CompilerParams(vmem_limit_bytes=60 * 2**20),
        cost_estimate=cost(2 * rows * used * width * count, rows * width * 20, 0.28),
    )(core, *grads, own, *others, inputs, grad_resid, norm[None, :])


def attention_weights_kernel(inner_ref, beside_ref, *refs):
    out_ref = refs[-1]
    q_width = refs[-2].shape[1]
    total = jnp.zeros((out_ref.shape[0], q_width), jnp.float32)
    pieces, at = [], 0
    chunk_rows = refs[0].shape[0]
    for ref in refs[:-1]:
        if ref.shape[0] < SEQ:
            pieces.append(ref)
            continue
        at = 0
        for piece in pieces:
            rows = piece.shape[0]
            start = (at // chunk_rows ^ inner_ref[0]) * chunk_rows + at % chunk_rows
            total = total + lax.dot_general(
                piece[...], ref[pl.ds(pl.multiple_of(start, rows), rows), :], TN,
                preferred_element_type=jnp.float32,
            )
            at += rows
        pieces = []
    out_ref[:, :q_width] = total.astype(jnp.bfloat16)
    out_ref[:, q_width:] = beside_ref[...]


def out_weights(inner, beside, pieces, attended):
    width, q_width = pieces[0][0].shape[1], attended[0].shape[1]
    whole = lambda n, inner: (0, 0)
    columns = q_width + beside.shape[1]
    in_specs = [pl.BlockSpec((256, beside.shape[1]), lambda n, inner: (n, 0))]
    for rows in range(2):
        in_specs += [pl.BlockSpec((piece.shape[0], 256), lambda n, inner: (0, n)) for piece in pieces[rows]]
        in_specs.append(pl.BlockSpec((SEQ, q_width), whole))
    return pl.pallas_call(
        attention_weights_kernel,
        grid_spec=pltpu.PrefetchScalarGridSpec(
            num_scalar_prefetch=1,
            grid=(width // 256,),
            in_specs=in_specs,
            out_specs=pl.BlockSpec((256, columns), lambda n, inner: (n, 0)),
        ),
        out_shape=jax.ShapeDtypeStruct((width, columns), jnp.bfloat16),
        compiler_params=pltpu.CompilerParams(vmem_limit_bytes=60 * 2**20),
        cost_estimate=cost(4 * SEQ * q_width * width, SEQ * width * 4, 0.35),
    )(inner, beside, *pieces[0], attended[0], *pieces[1], attended[1])


def projection_weights_kernel(norm_ref, *refs):
    inputs, inverses, grads, out_ref = refs[:2], refs[2:4], refs[4:-1], refs[-1]
    total = jnp.zeros(out_ref.shape, jnp.float32)
    chunk_rows = grads[0].shape[0]
    for k, grad_ref in enumerate(grads):
        at = k * chunk_rows
        rows = slice(at % SEQ, at % SEQ + chunk_rows)
        inverse = inverses[at // SEQ][rows, :]
        normed = inputs[at // SEQ][rows, :].astype(jnp.float32) * jnp.concatenate([inverse] * 2, axis=1)
        total = total + lax.dot_general(
            (normed * norm_ref[...]).astype(jnp.bfloat16), grad_ref[...], TN,
            preferred_element_type=jnp.float32,
        )
    out_ref[...] = total.astype(jnp.bfloat16)


def projection_weights(inputs, inverse, norm, grads):
    width, columns = inputs[0].shape[1], grads[0].shape[1]
    whole = lambda n: (0, 0)
    column = lambda n: (0, n)
    return pl.pallas_call(
        projection_weights_kernel,
        grid=(width // 256,),
        in_specs=[pl.BlockSpec((1, 256), column)]
        + [pl.BlockSpec((SEQ, 256), column)] * 2
        + [pl.BlockSpec((SEQ, 128), whole)] * 2
        + [pl.BlockSpec(part.shape, whole) for part in grads],
        out_specs=pl.BlockSpec((256, columns), lambda n: (n, 0)),
        out_shape=jax.ShapeDtypeStruct((width, columns), jnp.bfloat16),
        compiler_params=pltpu.CompilerParams(vmem_limit_bytes=60 * 2**20),
        cost_estimate=cost(4 * SEQ * columns * width, SEQ * width * 4, 0.43),
    )(norm[None, :], *inputs, *inverse, *grads)


def shift(values, distance, count, axis="tensor"):
    return lax.ppermute(values, axis, [(i, i ^ distance) for i in range(count)])


def gather_kernel(src_ref, own_ref, other_ref, send_sems, recv_sems, local_sem):
    rows = src_ref.shape[0]
    half = rows // 2
    x_top, x_bottom = own_ref.at[pl.ds(rows, half)], own_ref.at[pl.ds(rows + half, half)]
    y_top, y_bottom = other_ref.at[pl.ds(0, half)], other_ref.at[pl.ds(half, half)]
    far_top, far_bottom = other_ref.at[pl.ds(rows, half)], other_ref.at[pl.ds(rows + half, half)]
    top, bottom = src_ref.at[pl.ds(0, half)], src_ref.at[pl.ds(half, half)]
    greet([1, 2])

    def copy(index, from_ref, to_ref, distance):
        return pltpu.make_async_remote_copy(
            src_ref=from_ref, dst_ref=to_ref, send_sem=send_sems.at[index],
            recv_sem=recv_sems.at[index], **remote(distance),
        )

    first = [
        copy(0, bottom, x_bottom, 1), copy(1, top, y_top, 2),
        copy(2, top, x_top, 1), copy(3, bottom, y_bottom, 2),
    ]
    for sent in first:
        sent.start()
    local = pltpu.make_async_copy(src_ref, own_ref.at[pl.ds(0, rows)], local_sem.at[0])
    local.start()
    first[1].wait_recv()
    relay_top = copy(4, y_top, far_top, 1)
    relay_top.start()
    first[0].wait_recv()
    relay_bottom = copy(5, x_bottom, far_bottom, 2)
    relay_bottom.start()
    first[2].wait_recv()
    first[3].wait_recv()
    relay_top.wait_recv()
    relay_bottom.wait_recv()
    for sent in first + [relay_top, relay_bottom]:
        sent.wait_send()
    local.wait()


def gather_rows(values, count):
    if count != 4:
        near = gather_near(values, count)
        return [jnp.concatenate(near[i : i + count // 2], axis=0) for i in (0, count // 2)]
    place = pl.BlockSpec(memory_space=pl.ANY)
    rows, width = values.shape
    wide = jax.ShapeDtypeStruct((2 * rows, width), values.dtype)
    return pl.pallas_call(
        gather_kernel,
        in_specs=[place],
        out_specs=[place] * 2,
        out_shape=[wide, wide],
        scratch_shapes=[
            pltpu.SemaphoreType.DMA((6,)), pltpu.SemaphoreType.DMA((6,)),
            pltpu.SemaphoreType.DMA((1,)),
        ],
        compiler_params=pltpu.CompilerParams(collective_id=1, has_side_effects=True),
        cost_estimate=pl.CostEstimate(
            flops=0, bytes_accessed=values.size * 12, transcendentals=0,
            remote_bytes_transferred=values.size * 6,
        ),
    )(values)


def gather_near(values, count):
    if count == 4:
        return [values, shift(values, 1, count), shift(values, 2, count)]
    whole = lax.all_gather(values, "tensor", axis=0)
    mine = lax.axis_index("tensor")
    return [lax.dynamic_index_in_dim(whole, mine ^ k, 0, False) for k in range(count)]


def gather_far(near, count):
    if count != 4:
        return []
    half = near[0].shape[0] // 2
    return [shift(near[2][:half], 1, count), shift(near[1][half:], 2, count)]


def gather_chunks(values, count):
    near = gather_near(values, count)
    far = gather_far(near, count)
    return near + [jnp.concatenate(far, axis=0)] if far else near


def exchange(parts, distances, count):
    return [part if k == 0 else shift(part, k, count) for k, part in zip(distances, parts)]


def column_piece(weights, columns, core):
    half = weights.shape[0] // 2
    return lax.dynamic_slice(
        weights, (core[0] * half, columns[0]), (half, columns[1] - columns[0])
    )


def sum_first(parts, count):
    if count != 4:
        return None
    return shift(parts[3][0], 1, count), shift(parts[3][1], 2, count)


def sum_adds(parts, first):
    far_top, far_bottom = first
    return (
        (parts[2][0] + far_top.astype(jnp.float32)).astype(jnp.bfloat16),
        (parts[1][1] + far_bottom.astype(jnp.float32)).astype(jnp.bfloat16),
    )


def sum_rest(parts, near, adds, count):
    if count != 4:
        mine = lax.axis_index("tensor")
        half, width = parts[0][0].shape
        stacked = jnp.zeros((count, 2 * half, width), jnp.bfloat16)
        for k in range(count):
            term = jnp.concatenate([side.astype(jnp.bfloat16) for side in parts[k]], axis=0)
            stacked = lax.dynamic_update_index_in_dim(stacked, term, mine ^ k, 0)
        total = lax.psum_scatter(
            stacked.reshape(-1, width), "tensor", scatter_dimension=0, tiled=True
        ).astype(jnp.float32)
        none = jnp.zeros((half, width), jnp.bfloat16)
        return [[total[:half], none, none], [total[half:], none, none]]
    x_top, y_bottom = near
    y_top, x_bottom = shift(adds[0], 2, count), shift(adds[1], 1, count)
    return [[parts[0][0], x_top, y_top], [parts[0][1], x_bottom, y_bottom]]


def sum_near(parts, count):
    if count != 4:
        return ()
    return shift(parts[1][0], 1, count), shift(parts[2][1], 2, count)


def added(own_ref, x_ref, y_ref):
    return own_ref[...] + x_ref[...].astype(jnp.float32) + y_ref[...].astype(jnp.float32)


def own_rows_call(kernel, sums, twos, ones, out_shapes, gains):
    half, width = sums[0][0].shape
    block = min(64, half)
    term = pl.BlockSpec((block, width), lambda i: (i, 0))
    both = pl.BlockSpec((2, block, width), lambda i: (0, i, 0))
    out_specs = [both] * len(out_shapes)
    if gains:
        out_specs.append(pl.BlockSpec((8, width), lambda i: (0, 0)))
        out_shapes = out_shapes + [jax.ShapeDtypeStruct((8, width), jnp.float32)]
    return pl.pallas_call(
        kernel,
        grid=(half // block,),
        in_specs=[term] * 6 + [both] * len(twos) + [pl.BlockSpec((1, width), lambda i: (0, 0))] * len(ones),
        out_specs=out_specs,
        out_shape=out_shapes,
        compiler_params=pltpu.CompilerParams(vmem_limit_bytes=60 * 2**20),
        cost_estimate=cost(half * width * 10, half * width * 10, 1.0),
    )(*sums[0], *sums[1], *twos, *ones)


def resid_back_kernel(*refs):
    dy_ref, resid_ref, norm_ref, grad_ref, low_ref, gains_ref = refs[6:]

    @pl.when(pl.program_id(0) == 0)
    def _():
        gains_ref[...] = jnp.zeros_like(gains_ref)

    for side in range(2):
        grads = added(*refs[3 * side : 3 * side + 3])
        resid = resid_ref[side]
        inverse = rms_scale(resid)
        normed = resid * inverse
        gains_ref[...] += jnp.sum((grads * normed).reshape(-1, 8, grads.shape[1]), axis=0)
        total = dy_ref[side].astype(jnp.float32) + norm_back(grads * norm_ref[...], normed, inverse)
        grad_ref[side] = total
        low_ref[side] = total.astype(jnp.bfloat16)


def output_kernel(*refs):
    resid_ref, out_ref = refs[6:]
    for side in range(2):
        out_ref[side] = (resid_ref[side] + added(*refs[3 * side : 3 * side + 3])).astype(jnp.bfloat16)


def total_everywhere(values, sizes):
    for axis, size in sizes.items():
        distance = 1
        while distance < size:
            values = values + shift(values, distance, size, axis)
            distance *= 2
    return values


def after(value, *others):
    return lax.optimization_barrier((value, others))[0]


def pad_columns(values, width):
    return jnp.pad(values, ((0, 0), (0, width - values.shape[1])))


def gather_weights(*parts):
    return lax.all_gather(jnp.concatenate(parts, axis=1), "dp", axis=0, tiled=True)


def scatter_weights(grads):
    return lax.psum_scatter(grads, "dp", scatter_dimension=0, tiled=True)


def per_device(
    sizes,
    tokens,
    segments,
    positions,
    w_query,
    w_key,
    w_value,
    w_out,
    w_gate,
    w_up,
    w_down,
    norm_attn,
    norm_mlp,
    query_gain,
    key_gain,
    out_grad,
):
    count = sizes["tensor"]
    chunk_rows = tokens.shape[0]
    q_width, key_width = w_query.shape[1], w_key.shape[1]
    kv_width = -(-key_width // 128) * 128
    units = w_gate.shape[1] // 2
    mine = lax.axis_index("tensor").astype(jnp.int32).reshape(1)

    half, width = chunk_rows // 2, tokens.shape[1]
    inner_count = count // 2
    inner, flip = mine % inner_count, mine // inner_count
    core = lax.axis_index("dp").astype(jnp.int32).reshape(1) % 2

    def own_first(values):
        pair = values.reshape(2, SEQ)
        return jnp.where(flip == 0, pair, pair[::-1])

    w_attn = gather_weights(
        w_out, w_query, pad_columns(w_key, kv_width), pad_columns(w_value, kv_width)
    )
    rows_in = gather_rows(tokens, count)
    w_mlp = [
        gather_weights(w_gate[:, part], w_up[:, part], w_down[:, part])
        for part in (slice(0, units), slice(units, 2 * units))
    ]
    segments, positions = own_first(segments), own_first(positions)
    out_near = gather_near(column_piece(after(w_attn, rows_in), (0, q_width), core), count)
    inv_rows, queries, key_sides, value_sides, raw = [], [], [], [], []
    tables = rotary_tables(positions.reshape(-1))
    attended, inv_total, heads = [], [], []
    for sequence in range(2):
        rows = rows_in[sequence]
        if sequence == 1:
            rows = after(rows, attended, out_near)
            out_near = after(out_near, attended)
            out_far = gather_far(out_near, count)
            out_others = out_near[1:] + ([jnp.concatenate(out_far, axis=0)] if out_far else [])
            out_others = out_others + [shift(part, 1, sizes["dp"], "dp") for part in out_others]
        results = project(
            inner, sequence, rows, chunk_rows, norm_attn, w_attn, tables, query_gain, key_gain, q_width, kv_width
        )
        for kept, result in zip((inv_rows, queries, key_sides, value_sides, raw), results):
            kept.append(result)
        result, inverse = attend(
            queries[sequence], key_sides[sequence], value_sides[sequence], segments[sequence]
        )
        attended.append(result)
        inv_total.append(inverse)
        heads.append(gather_chunks(result, count))
    grad_near = gather_near(after(out_grad, heads), count)
    crossed = [
        heads[sequence][:inner_count] + heads[1 - sequence][inner_count:] for sequence in range(2)
    ]
    rows_two, resid = residual(
        jnp.concatenate([inner, core]), rows_in, crossed, w_attn, out_others, norm_mlp, chunk_rows
    )
    resid = resid.reshape(2, half, width)
    grad_near = after(grad_near, rows_two)
    grad_far = gather_far(grad_near, count)
    act_a, factors = hidden_forward(rows_two, w_mlp[0])
    grad_rows = jnp.concatenate(grad_near + after(grad_far, act_a), axis=0)

    grads_a = hidden_backward(grad_rows, factors, w_mlp[0])
    grad_a = contract_rows(rows_two, grads_a).astype(jnp.bfloat16)
    half_columns = column_piece(after(w_attn, grads_a), (q_width, w_attn.shape[1]), core)
    in_near = [shift(half_columns, k, count) for k in range(1, count - 1)]
    if count == 4:
        far_halves = gather_far([half_columns, *in_near], count)
        in_far = [jnp.concatenate(far_halves, axis=0)]
    else:
        far_halves = in_far = [shift(half_columns, count - 1, count)]
    act, grads_b = hidden_units(after(rows_two, grad_a), grad_rows, w_mlp[1], act_a)
    in_others = in_near + in_far
    in_others = in_others + [shift(part, 1, sizes["dp"], "dp") for part in in_others]
    spans = [(2 * units, 0), (2 * units, 0)]

    def two_parts(distances, grads):
        lefts = [(grads, 2 * units, 0), (grads_b, 2 * units, 0)]
        return rows_out(distances, lefts, w_mlp, spans, chunk_rows)

    grad_b = contract_rows(after(rows_two, in_near), grads_b).astype(jnp.bfloat16)
    two = two_parts(list(range(inner_count, count)), after(grads_a, grad_b, far_halves))
    two_first = sum_first(two, count)
    for k in range(1, inner_count):
        two.update(two_parts([k], after(grads_a, two[count - 1])))
    two_near = sum_near(two, count)
    two_adds = sum_adds(two, two_first) if count == 4 else ()
    two.update(two_parts([0], after(grads_a, two[1], two_adds)))
    two_rest = sum_rest(two, two_near, two_adds, count)
    distances = list(range(count))
    out_act = after(act, two[0])
    out = rows_out(
        distances, [(out_act, units, 0), (out_act, units, 1)], w_mlp, [(units, 2), (units, 2)], chunk_rows
    )
    out_first = sum_first(out, count)
    out_near = sum_near(out, count)
    grad_resid, branch_low, gain_mlp = own_rows_call(
        resid_back_kernel,
        after(two_rest, out[0]),
        [out_grad.reshape(2, half, width), resid],
        [norm_mlp[None, :]],
        [
            jax.ShapeDtypeStruct((2, half, width), jnp.float32),
            jax.ShapeDtypeStruct((2, half, width), jnp.bfloat16),
        ],
        True,
    )
    branch_low = branch_low.reshape(chunk_rows, width)
    heads_out = grad_heads(core, branch_low, w_attn, out_others, q_width, count)
    heads_in = exchange(heads_out, distances, count)
    scattered_a = scatter_weights(grad_a)
    scattered_b = scatter_weights(after(grad_b, scattered_a, two[count - 1]))
    grad_down = contract_rows(
        after(grad_rows, heads_out[0], scattered_b, out_first), act
    ).astype(jnp.bfloat16)
    tops = bottoms = relays = []
    if count == 4:
        top, bottom = after((branch_low[:half], branch_low[half:]), heads_in, grad_down)
        tops = [shift(top, 1, count), shift(top, 2, count)]
    sums, raw_grads = [], []
    for sequence in range(2):
        pieces = heads_in[sequence * inner_count : (sequence + 1) * inner_count]
        if sequence == 0:
            pieces = after(pieces, heads_in, grad_down)
        else:
            pieces = after(pieces, tops, raw_grads)
            if count == 4:
                bottom = after(bottom, tops, raw_grads)
                bottoms = [shift(bottom, 1, count), shift(bottom, 2, count)]
        results = attend_back(
            inner, sequence, queries[sequence], key_sides[sequence], value_sides[sequence],
            segments[sequence], attended[sequence], inv_total[sequence], pieces, raw[sequence], tables,
            query_gain, key_gain,
        )
        raw_grads += results[:inner_count]
        sums.append(results[inner_count:])
    raw_in = exchange(raw_grads, distances, count)
    if count == 4:
        near_bottom, near_top = after((bottoms[0], tops[1]), bottoms, raw_grads)
        relays = [shift(near_top, 1, count), shift(near_bottom, 2, count)]
        branch = (
            [branch_low, tops[0], bottoms[0]],
            [tops[1], bottoms[1], *relays],
        )
    else:
        branch_near = gather_near(branch_low, count)
        branch = (branch_near[:inner_count], branch_near[inner_count:])
    scattered_down = scatter_weights(after(grad_down, scattered_b, heads_in))
    grad_qkv = projection_weights(after(rows_in, raw_grads, bottoms), inv_rows, norm_attn, raw_grads)
    grad_w_gate = jnp.concatenate(
        [scattered_a[:, :units], scattered_b[:, :units]], axis=1
    ).astype(jnp.float32)
    grad_w_up = jnp.concatenate(
        [scattered_a[:, units:], scattered_b[:, units:]], axis=1
    ).astype(jnp.float32)
    grad_attn = out_weights(inner, grad_qkv, after(branch, raw_grads, grad_w_gate, grad_w_up, in_others), attended)

    out_adds = sum_adds(out, after(out_first, grad_attn)) if count == 4 else ()
    scattered_attn = scatter_weights(
        after(
            grad_attn, scattered_down, raw_in,
        )
    )

    grad_w_down = scattered_down.astype(jnp.float32)
    grad_tokens, gain_attn = input_back(
        core, after(raw_in, grad_w_down, out_adds), w_attn, in_others, tokens, grad_resid.reshape(chunk_rows, width), norm_attn
    )
    out_rest = sum_rest(out, out_near, out_adds, count)
    gains = [
        jnp.sum(gain_attn, axis=0),
        jnp.sum(gain_mlp, axis=0),
        jnp.sum((sums[0][0] + sums[1][0]).reshape(-1, 64), axis=0),
        jnp.sum((sums[0][1] + sums[1][1]).reshape(-1, 64), axis=0),
    ]
    gains = jnp.concatenate(gains).reshape(-1, 128)
    gains = total_everywhere(gains, sizes).reshape(-1)
    (output,) = own_rows_call(
        output_kernel, after(out_rest, gains), [resid], [], [jax.ShapeDtypeStruct((2, half, width), jnp.bfloat16)],
        False,
    )
    distances = list(range(count))
    key_at = 2 * q_width
    value_at = key_at + kv_width
    return (
        output.reshape(chunk_rows, width),
        grad_tokens.reshape(chunk_rows, width),
        scattered_attn[:, q_width:key_at].astype(jnp.float32),
        scattered_attn[:, key_at : key_at + key_width].astype(jnp.float32),
        scattered_attn[:, value_at : value_at + key_width].astype(jnp.float32),
        scattered_attn[:, :q_width].astype(jnp.float32),
        grad_w_gate,
        grad_w_up,
        grad_w_down,
        gains[:width],
        gains[width : 2 * width],
        gains[2 * width : 2 * width + 64],
        gains[2 * width + 64 : 2 * width + 128],
    )


def solution(mesh):
    return jax.shard_map(
        functools.partial(per_device, dict(mesh.shape)),
        mesh=mesh,
        in_specs=(
            P(("dp", "tensor"), None),
            P("dp"),
            P("dp"),
            P("dp", "tensor"),
            P("dp", "tensor"),
            P("dp", "tensor"),
            P("dp", "tensor"),
            P("dp", "tensor"),
            P("dp", "tensor"),
            P("dp", "tensor"),
            P(),
            P(),
            P(),
            P(),
            P(("dp", "tensor"), None),
        ),
        out_specs=(
            P(("dp", "tensor"), None),
            P(("dp", "tensor"), None),
            P("dp", "tensor"),
            P("dp", "tensor"),
            P("dp", "tensor"),
            P("dp", "tensor"),
            P("dp", "tensor"),
            P("dp", "tensor"),
            P("dp", "tensor"),
            P(),
            P(),
            P(),
            P(),
        ),
        check_vma=False,
    )
```

```python
import functools

import jax
import jax.numpy as jnp
from jax import lax
from jax.experimental import pallas as pl
from jax.experimental.pallas import tpu as pltpu
from jax.sharding import PartitionSpec as P

EPS = 1e-05
THETA = 1000000.0
SEQ = 1024
TILE = 256
LOG2E = 1.4426950408889634
MASKED = -1e30
NT = (((1,), (1,)), ((), ()))
TN = (((0,), (0,)), ((), ()))


def rms_scale(values):
    return lax.rsqrt(jnp.mean(values * values, axis=-1, keepdims=True) + EPS)


def norm_back(grad_normed, normed, inverse):
    return inverse * (grad_normed - normed * jnp.mean(grad_normed * normed, axis=-1, keepdims=True))


def rotary_tables(places):
    lane = jnp.arange(128)
    frequency = THETA ** (-(lane % 32).astype(jnp.float32) * 2.0 / 64)
    angles = places.astype(jnp.float32)[:, None] * frequency[None, :]
    sine = jnp.sin(angles)
    upper = (lane % 64 >= 32)[None, :]
    return jnp.cos(angles), jnp.where(upper, 0.0, -sine), jnp.where(upper, sine, 0.0)


def contract_rows(left, right):
    return lax.dot_general(
        left, right, (((0,), (0,)), ((), ())), preferred_element_type=jnp.float32
    )


def half_lanes(rows):
    return lax.broadcasted_iota(jnp.int32, (rows, 128), 1) < 64


def ones_side(side, rows):
    low = half_lanes(rows)
    return jnp.where(low if side == 0 else ~low, 1.0, 0.0).astype(jnp.bfloat16)


def attend_kernel(q_ref, k_ref, v_ref, segc_ref, segr_ref, out_ref, inv_ref, bias_ref, total_ref):
    coef = LOG2E * 64 ** (-0.5)

    @pl.when(pl.program_id(1) == 0)
    def _():
        for at in range(0, SEQ, TILE):
            end = at + TILE
            rows = lax.broadcasted_iota(jnp.int32, (TILE, end), 0) + at
            cols = lax.broadcasted_iota(jnp.int32, (TILE, end), 1)
            allowed = (segc_ref[at:end, :] == segr_ref[0, :, :end]) & (cols <= rows)
            bias_ref[at:end, :end] = jnp.where(allowed, 0.0, MASKED)

    for side in range(2):
        lanes = slice(side * 128, side * 128 + 128)
        for key_at in range(0, SEQ, TILE):
            keys, rows = slice(key_at, key_at + TILE), slice(key_at, SEQ)
            scores = lax.dot_general(
                q_ref[rows, :], k_ref[keys, lanes], NT, preferred_element_type=jnp.float32
            )
            weights = jnp.exp2(scores * coef + bias_ref[rows, keys]).astype(jnp.bfloat16)
            mixed = jnp.concatenate([v_ref[keys, lanes], ones_side(side, TILE)], axis=1)
            part = jnp.dot(weights, mixed, preferred_element_type=jnp.float32)
            if side == 0 and key_at == 0:
                total_ref[...] = part
            else:
                total_ref[rows, :] += part
    inverse = 1.0 / total_ref[:, 128:]
    out_ref[...] = (total_ref[:, :128] * inverse).astype(jnp.bfloat16)
    inv_ref[...] = inverse


def unrotated(grads, raw, cosine, sine_low, sine_high, gain):
    grads = grads * 0.125
    turned = (
        grads * cosine
        - pltpu.roll(grads, 96, 1) * sine_low
        - pltpu.roll(grads, 32, 1) * sine_high
    )
    inverse = head_inverse(raw)
    normed = raw * inverse
    scaled = turned * gain
    change = inverse * (scaled - normed * head_mean(scaled * normed))
    return change, jnp.sum((turned * normed).reshape(-1, 8, 128), axis=0)


def attend_back_kernel(
    chunks, inner_ref, q_ref, k_ref, v_ref, segc_ref, segr_ref, out_ref, inv_ref,
    qraw_ref, kraw_ref, cos_ref, low_ref, high_ref, qgain_ref, kgain_ref, *refs,
):
    pieces, results = refs[:chunks], refs[chunks : 2 * chunks]
    (
        qsum_ref, ksum_ref, bias_ref, mix_ref, qside_ref, gside_ref,
        dq_ref, dk_ref, dv_ref, kpair_ref, vpair_ref, grad_ref,
    ) = refs[2 * chunks :]
    chunk_rows = SEQ // chunks
    q_width = 128 * pl.num_programs(1)
    kv_width = (results[0].shape[1] - q_width) // 2

    def rows_of(k):
        return pl.ds(pl.multiple_of((inner_ref[0] ^ k) * chunk_rows, chunk_rows), chunk_rows)

    def put(values, place):
        dq_ref[...] = values
        for k, result_ref in enumerate(results):
            lanes = pl.ds(pl.multiple_of(place, 128), 128)
            result_ref[:, lanes] = dq_ref[rows_of(k), :].astype(jnp.bfloat16)

    coef = LOG2E * 64 ** (-0.5)
    step = pl.program_id(1)

    @pl.when(step == 0)
    def _():
        for key_at in range(0, SEQ, TILE):
            key_end = key_at + TILE
            keys = lax.broadcasted_iota(jnp.int32, (TILE, SEQ - key_at), 0) + key_at
            rows = lax.broadcasted_iota(jnp.int32, (TILE, SEQ - key_at), 1) + key_at
            allowed = (segc_ref[key_at:key_end, :] == segr_ref[0, :, key_at:]) & (keys <= rows)
            bias_ref[key_at:key_end, key_at:] = jnp.where(allowed, 0.0, MASKED)

    @pl.when((step == 0) & (pl.program_id(0) == 0))
    def _():
        qsum_ref[...] = jnp.zeros_like(qsum_ref)
        ksum_ref[...] = jnp.zeros_like(ksum_ref)

    @pl.when(lax.rem(step, 4) == 0)
    def _():
        kpair_ref[...] = jnp.zeros_like(kpair_ref)
        vpair_ref[...] = jnp.zeros_like(vpair_ref)

    @pl.when(lax.rem(step, 2) == 0)
    def _():
        dk_ref[...] = jnp.zeros_like(dk_ref)
        dv_ref[...] = jnp.zeros_like(dv_ref)

    for k, piece_ref in enumerate(pieces):
        grad_ref[rows_of(k), :] = piece_ref[...].astype(jnp.float32)
    low = half_lanes(SEQ)
    scaled = grad_ref[...] * inv_ref[...]
    scaled_low = scaled.astype(jnp.bfloat16)
    mix_ref[:, :128] = scaled_low
    mix_ref[:, 128:] = -(scaled * out_ref[...].astype(jnp.float32)).astype(jnp.bfloat16)
    none = jnp.zeros_like(scaled_low)
    queries = q_ref[...]
    gside_ref[:, :128] = jnp.where(low, scaled_low, none)
    gside_ref[:, 128:] = jnp.where(low, none, scaled_low)
    qside_ref[:, :128] = jnp.where(low, queries, none)
    qside_ref[:, 128:] = jnp.where(low, none, queries)

    for key_at in range(0, SEQ, TILE):
        keys, rows = slice(key_at, key_at + TILE), slice(key_at, SEQ)
        for side in range(2):
            lanes = slice(side * 128, side * 128 + 128)
            key_side = k_ref[keys, lanes]
            value_side = jnp.concatenate([v_ref[keys, lanes], ones_side(side, TILE)], axis=1)
            scores = lax.dot_general(
                key_side, q_ref[rows, :], NT, preferred_element_type=jnp.float32
            )
            weights = jnp.exp2(scores * coef + bias_ref[keys, rows])
            change = lax.dot_general(
                value_side, mix_ref[rows, :], NT, preferred_element_type=jnp.float32
            )
            grads = (weights * change).astype(jnp.bfloat16)
            dv_ref[keys, :] += jnp.dot(
                weights.astype(jnp.bfloat16),
                gside_ref[rows, lanes],
                preferred_element_type=jnp.float32,
            )
            dk_ref[keys, :] += jnp.dot(
                grads, qside_ref[rows, lanes], preferred_element_type=jnp.float32
            )
            dq = lax.dot_general(grads, key_side, TN, preferred_element_type=jnp.float32)
            if key_at == 0 and side == 0:
                dq_ref[...] = dq
            else:
                dq_ref[rows, :] += dq

    cosine, sine_low, sine_high = cos_ref[...], low_ref[...], high_ref[...]
    change, sums = unrotated(
        dq_ref[...], qraw_ref[...], cosine, sine_low, sine_high, qgain_ref[...]
    )
    qsum_ref[...] += sums
    put(change, step * 128)

    @pl.when(lax.rem(step, 2) == 1)
    def _():
        mine = low == (lax.rem(step, 4) == 1)
        for sum_ref, pair_ref in ((dk_ref, kpair_ref), (dv_ref, vpair_ref)):
            sums = sum_ref[...]
            pair_ref[...] = jnp.where(mine, sums + pltpu.roll(sums, 64, 1), pair_ref[...])

    @pl.when((lax.rem(step, 4) == 3) | (step == pl.num_programs(1) - 1))
    def _():
        change, sums = unrotated(
            kpair_ref[...], kraw_ref[...], cosine, sine_low, sine_high, kgain_ref[...]
        )
        ksum_ref[...] += sums
        put(change, q_width + step // 4 * 128)
        put(vpair_ref[...], q_width + kv_width + step // 4 * 128)


def attention_specs():
    pair = pl.BlockSpec((SEQ, 128), lambda s, p, *_: (s, p))
    group = pl.BlockSpec((SEQ, 256), lambda s, p, *_: (s, p // 2))
    seg_col = pl.BlockSpec((SEQ, 1), lambda s, p, *_: (s, 0))
    seg_row = pl.BlockSpec((1, 1, SEQ), lambda s, p, *_: (s, 0, 0))
    return pair, group, seg_col, seg_row


def attend(queries, key_sides, value_sides, segments):
    rows, width = queries.shape
    sequences, pairs = rows // SEQ, width // 128
    pair, group, seg_col, seg_row = attention_specs()
    work = rows * SEQ * width
    return pl.pallas_call(
        attend_kernel,
        grid=(sequences, pairs),
        in_specs=[pair, group, group, seg_col, seg_row],
        out_specs=[pair, pair],
        out_shape=[
            jax.ShapeDtypeStruct((rows, width), jnp.bfloat16),
            jax.ShapeDtypeStruct((rows, width), jnp.float32),
        ],
        scratch_shapes=[pltpu.VMEM((SEQ, SEQ), jnp.float32), pltpu.VMEM((SEQ, 256), jnp.float32)],
        compiler_params=pltpu.CompilerParams(vmem_limit_bytes=60 * 2**20),
        cost_estimate=pl.CostEstimate(
            flops=42 * work // 10, bytes_accessed=rows * width * 12, transcendentals=work // 128
        ),
    )(queries, key_sides, value_sides, segments[:, None], segments.reshape(sequences, 1, SEQ))


def attend_back(
    inner, sequence, queries, key_sides, value_sides, segments, attended, inverse, pieces, raw, tables,
    query_gain, key_gain,
):
    width = queries.shape[1]
    pairs, chunks, chunk_rows = width // 128, len(pieces), pieces[0].shape[0]
    kv_width = key_sides.shape[1] // 4
    pair, group, seg_col, seg_row = attention_specs()
    kv_raw = pl.BlockSpec((SEQ, 128), lambda s, p, *_: (0, width // 128 + p // 4))
    table = pl.BlockSpec((SEQ, 128), lambda s, p, *_: (sequence, 0))
    gain = pl.BlockSpec((1, 128), lambda s, p, *_: (0, 0))
    total = pl.BlockSpec((8, 128), lambda s, p, *_: (0, 0))
    piece = pl.BlockSpec((chunk_rows, 128), lambda s, p, *_: (0, p))
    columns = width + 2 * kv_width
    work = SEQ * SEQ * width
    flat = pltpu.VMEM((SEQ, 128), jnp.float32)
    return pl.pallas_call(
        functools.partial(attend_back_kernel, chunks),
        grid_spec=pltpu.PrefetchScalarGridSpec(
            num_scalar_prefetch=1,
            grid=(1, pairs),
            in_specs=[pair, group, group, seg_col, seg_row, pair, pair]
            + [pair, kv_raw, table, table, table, gain, gain]
            + [piece] * chunks,
            out_specs=[pl.BlockSpec((chunk_rows, columns), lambda s, p, *_: (0, 0))] * chunks
            + [total, total],
            scratch_shapes=[
                pltpu.VMEM((SEQ, SEQ), jnp.float32),
                pltpu.VMEM((SEQ, 256), jnp.bfloat16),
                pltpu.VMEM((SEQ, 256), jnp.bfloat16),
                pltpu.VMEM((SEQ, 256), jnp.bfloat16),
                flat, flat, flat, flat, flat, flat,
            ],
        ),
        out_shape=[jax.ShapeDtypeStruct((chunk_rows, columns), jnp.bfloat16)] * chunks
        + [jax.ShapeDtypeStruct((8, 128), jnp.float32)] * 2,
        compiler_params=pltpu.CompilerParams(vmem_limit_bytes=60 * 2**20),
        cost_estimate=pl.CostEstimate(
            flops=110 * work // 10, bytes_accessed=SEQ * width * 20, transcendentals=work // 128
        ),
    )(
        inner, queries, key_sides, value_sides, segments[:, None], segments.reshape(-1, 1, SEQ),
        attended, inverse, raw, raw, *tables,
        jnp.tile(query_gain, 2)[None, :], jnp.tile(key_gain, 2)[None, :], *pieces,
    )


def cost(flops, moved, share):
    return pl.CostEstimate(
        flops=int(0.2 * flops / share), bytes_accessed=int(0.2 * moved), transcendentals=0
    )


def head_inverse(values):
    squares = values * values
    high = squares.astype(jnp.bfloat16)
    low = (squares - high.astype(jnp.float32)).astype(jnp.bfloat16)
    return lax.rsqrt(head_sum(high, low) * (1.0 / 64) + EPS)


def head_sum(high, low):
    from_head = lax.broadcasted_iota(jnp.int32, (128, 128), 0) // 64
    to_head = lax.broadcasted_iota(jnp.int32, (128, 128), 1) // 64
    same = jnp.where(from_head == to_head, 1.0, 0.0).astype(jnp.bfloat16)
    return jnp.dot(high, same, preferred_element_type=jnp.float32) + jnp.dot(
        low, same, preferred_element_type=jnp.float32
    )


def head_mean(values):
    high = values.astype(jnp.bfloat16)
    low = (values - high.astype(jnp.float32)).astype(jnp.bfloat16)
    return head_sum(high, low) * (1.0 / 64)


def project_kernel(
    pieces, inner_ref, *refs,
):
    norm_ref, w_ref, cos_ref, low_ref, high_ref, qgain_ref, kgain_ref = refs[pieces : pieces + 7]
    inv_ref, q_ref, k_ref, v_ref, raw_ref = refs[pieces + 7 :]
    inputs = refs[0][...].astype(jnp.float32)
    inverse = rms_scale(inputs)
    hidden = (inputs * inverse * norm_ref[...]).astype(jnp.bfloat16)
    inv_ref[...] = jnp.broadcast_to(inverse, inv_ref.shape)
    q_width, kv_width = q_ref.shape[1], k_ref.shape[1] // 4
    cosine, sine_low, sine_high = cos_ref[...], low_ref[...], high_ref[...]
    lower = lax.broadcasted_iota(jnp.int32, cosine.shape, 1) < 64
    none = jnp.zeros_like(cosine)

    def rotated(raw, gain):
        scaled = raw * head_inverse(raw) * gain
        return (
            scaled * cosine
            + pltpu.roll(scaled, 96, 1) * sine_low
            + pltpu.roll(scaled, 32, 1) * sine_high
        )

    def to_sides(pair, out_ref, at):
        first, second = jnp.where(lower, pair, none), jnp.where(lower, none, pair)
        sides = (first, pltpu.roll(first, 64, 1), pltpu.roll(second, 64, 1), second)
        for index, side in enumerate(sides):
            lanes = slice(at * 4 + index * 128, at * 4 + index * 128 + 128)
            out_ref[:, lanes] = side.astype(jnp.bfloat16)

    wide = jnp.dot(hidden, w_ref[:, q_width:], preferred_element_type=jnp.float32)
    raw_ref[...] = wide[:, : q_width + kv_width]
    for at in range(0, q_width, 128):
        q_ref[:, at : at + 128] = rotated(wide[:, at : at + 128], qgain_ref[...]).astype(
            jnp.bfloat16
        )
    for at in range(0, kv_width, 128):
        place = q_width + at
        to_sides(rotated(wide[:, place : place + 128], kgain_ref[...]), k_ref, at)
        place = q_width + kv_width + at
        to_sides(wide[:, place : place + 128], v_ref, at)


def placed(chunk_rows, block):
    per = chunk_rows // block
    here = lambda r, inner: (r, 0)
    there = lambda r, inner: ((r // per ^ inner[0]) * per + r % per, 0)
    return here, there


def project(inner, sequence, inputs, chunk_rows, norm, weights, tables, query_gain, key_gain, q_width, kv_width):
    rows, width = inputs.shape
    block = chunk_rows
    here, there = placed(block, block)
    fixed = lambda r, mine: (0, 0)
    used = q_width + 2 * kv_width
    table = pl.BlockSpec(
        (block, 128), lambda r, inner: (sequence * (rows // block) + there(r, inner)[0], 0)
    )
    gain = pl.BlockSpec((1, 128), fixed)
    return pl.pallas_call(
        functools.partial(project_kernel, 1),
        grid_spec=pltpu.PrefetchScalarGridSpec(
            num_scalar_prefetch=1,
            grid=(rows // block,),
            in_specs=[
                pl.BlockSpec((block, width), here),
                pl.BlockSpec((1, width), fixed),
                pl.BlockSpec(weights.shape, fixed, pipeline_mode=pl.Buffered(1)),
                table, table, table, gain, gain,
            ],
            out_specs=[
                pl.BlockSpec((block, 128), here),
                pl.BlockSpec((block, q_width), there),
                pl.BlockSpec((block, 4 * kv_width), there),
                pl.BlockSpec((block, 4 * kv_width), there),
                pl.BlockSpec((block, q_width + kv_width), there),
            ],
        ),
        out_shape=[
            jax.ShapeDtypeStruct((rows, 128), jnp.float32),
            jax.ShapeDtypeStruct((rows, q_width), jnp.bfloat16),
            jax.ShapeDtypeStruct((rows, 4 * kv_width), jnp.bfloat16),
            jax.ShapeDtypeStruct((rows, 4 * kv_width), jnp.bfloat16),
            jax.ShapeDtypeStruct((rows, q_width + kv_width), jnp.float32),
        ],
        compiler_params=pltpu.CompilerParams(vmem_limit_bytes=60 * 2**20),
        cost_estimate=cost(2 * rows * width * used, rows * width * 6, 0.22),
    )(
        inner, inputs, norm[None, :], weights, *tables,
        jnp.tile(query_gain, 2)[None, :], jnp.tile(key_gain, 2)[None, :],
    )


def heads_kernel(count, core_ref, grads_ref, *refs):
    rights, outs = refs[: 2 * count - 1], refs[2 * count - 1 :]
    outs[0][...] = jnp.dot(
        grads_ref[...], rights[0][...], preferred_element_type=jnp.float32
    ).astype(jnp.bfloat16)
    half = rights[1].shape[0]
    near = grads_ref[:, pl.ds(pl.multiple_of(core_ref[0] * half, half), half)]
    other = grads_ref[:, pl.ds(pl.multiple_of((1 - core_ref[0]) * half, half), half)]
    for k in range(1, count):
        outs[k][...] = (
            jnp.dot(near, rights[k][...], preferred_element_type=jnp.float32)
            + jnp.dot(other, rights[count - 1 + k][...], preferred_element_type=jnp.float32)
        ).astype(jnp.bfloat16)


def grad_heads(core, grads, own, others, q_width, count):
    rows, width = grads.shape
    fixed = lambda i, core: (0, 0)
    return pl.pallas_call(
        functools.partial(heads_kernel, count),
        grid_spec=pltpu.PrefetchScalarGridSpec(
            num_scalar_prefetch=1,
            grid=(1,),
            in_specs=[pl.BlockSpec(grads.shape, fixed), pl.BlockSpec((width, q_width), fixed)]
            + [pl.BlockSpec(piece.shape, fixed) for piece in others],
            out_specs=[pl.BlockSpec((rows, q_width), fixed)] * count,
        ),
        out_shape=[jax.ShapeDtypeStruct((rows, q_width), jnp.bfloat16)] * count,
        compiler_params=pltpu.CompilerParams(vmem_limit_bytes=60 * 2**20),
        cost_estimate=cost(2 * rows * width * q_width * count, rows * width, 2.67),
    )(core, grads, own, *others)


def peer(distance):
    mine = lax.axis_index("tensor")
    if distance == 1:
        return mine + 1 - 2 * (mine % 2)
    return (mine + 2) % 4 if distance == 2 else 3 - mine


def remote(distance):
    return dict(device_id={"tensor": peer(distance)}, device_id_type=pl.DeviceIdType.MESH)


def greet(distances):
    barrier = pltpu.get_barrier_semaphore()
    for distance in distances:
        pl.semaphore_signal(barrier, inc=1, **remote(distance))
    pl.semaphore_wait(barrier, len(distances))


def hidden_kernel(x_ref, dy_ref, w_ref, filled_ref, act_ref, grads_ref):
    units = act_ref.shape[1]
    inputs, cotangent = x_ref[...], dy_ref[...]
    for at in range(0, units, 256):
        lanes = slice(at, at + 256)
        gate = jnp.dot(inputs, w_ref[:, lanes], preferred_element_type=jnp.float32)
        up = jnp.dot(
            inputs, w_ref[:, units + at : units + at + 256], preferred_element_type=jnp.float32
        )
        change = jnp.dot(
            cotangent, w_ref[:, 2 * units + at : 2 * units + at + 256],
            preferred_element_type=jnp.float32,
        )
        sigmoid = 1.0 / (1.0 + jnp.exp(-gate))
        silu = gate * sigmoid
        act_ref[:, lanes] = (silu * up).astype(jnp.bfloat16)
        grads_ref[:, lanes] = (change * up * sigmoid * (1.0 + gate - silu)).astype(jnp.bfloat16)
        grads_ref[:, units + at : units + at + 256] = (change * silu).astype(jnp.bfloat16)


def hidden_units(inputs, cotangent, weights, filled):
    rows, width = inputs.shape
    units = weights.shape[1] // 3
    block = min(512, rows)
    row = lambda r: (r, 0)
    return pl.pallas_call(
        hidden_kernel,
        grid=(rows // block,),
        in_specs=[
            pl.BlockSpec((block, width), row),
            pl.BlockSpec((block, width), row),
            pl.BlockSpec(weights.shape, lambda r: (0, 0), pipeline_mode=pl.Buffered(1)),
            pl.BlockSpec(memory_space=pl.ANY),
        ],
        out_specs=[
            pl.BlockSpec((block, units), lambda r: (r, 1)),
            pl.BlockSpec((block, 2 * units), row),
        ],
        out_shape=[jax.ShapeDtypeStruct((rows, 2 * units), jnp.bfloat16)] * 2,
        input_output_aliases={3: 0},
        compiler_params=pltpu.CompilerParams(vmem_limit_bytes=60 * 2**20),
        cost_estimate=cost(6 * rows * width * units, (rows * width + width * units) * 6, 0.63),
    )(inputs, cotangent, weights, filled)


def hidden_forward_kernel(x_ref, w_ref, act_ref, factors_ref):
    units = act_ref.shape[1]
    inputs = x_ref[...]
    for at in range(0, units, 256):
        lanes, beside = slice(at, at + 256), slice(units + at, units + at + 256)
        gate = jnp.dot(inputs, w_ref[:, lanes], preferred_element_type=jnp.float32)
        up = jnp.dot(inputs, w_ref[:, beside], preferred_element_type=jnp.float32)
        sigmoid = 1.0 / (1.0 + jnp.exp(-gate))
        silu = gate * sigmoid
        act_ref[:, lanes] = (silu * up).astype(jnp.bfloat16)
        factors_ref[:, lanes] = (up * sigmoid * (1.0 + gate - silu)).astype(jnp.bfloat16)
        factors_ref[:, beside] = silu.astype(jnp.bfloat16)


def hidden_forward(inputs, weights):
    rows, width = inputs.shape
    units = weights.shape[1] // 3
    block = min(512, rows)
    row = lambda r: (r, 0)
    return pl.pallas_call(
        hidden_forward_kernel,
        grid=(rows // block,),
        in_specs=[
            pl.BlockSpec((block, width), row),
            pl.BlockSpec((width, 2 * units), lambda r: (0, 0), pipeline_mode=pl.Buffered(1)),
        ],
        out_specs=[pl.BlockSpec((block, units), row), pl.BlockSpec((block, 2 * units), row)],
        out_shape=[jax.ShapeDtypeStruct((rows, 2 * units), jnp.bfloat16)] * 2,
        compiler_params=pltpu.CompilerParams(vmem_limit_bytes=60 * 2**20),
        cost_estimate=cost(4 * rows * width * units, (rows * width + width * units) * 4, 0.63),
    )(inputs, weights)


def hidden_backward_kernel(dy_ref, factors_ref, w_ref, grads_ref):
    units = w_ref.shape[1]
    cotangent = dy_ref[...]
    for at in range(0, units, 256):
        change = jnp.dot(
            cotangent, w_ref[:, at : at + 256], preferred_element_type=jnp.float32
        )
        for lanes in (slice(at, at + 256), slice(units + at, units + at + 256)):
            grads_ref[:, lanes] = (change * factors_ref[:, lanes].astype(jnp.float32)).astype(
                jnp.bfloat16
            )


def hidden_backward(cotangent, factors, weights):
    rows, width = cotangent.shape
    units = weights.shape[1] // 3
    block = min(512, rows)
    row = lambda r: (r, 0)
    return pl.pallas_call(
        hidden_backward_kernel,
        grid=(rows // block,),
        in_specs=[
            pl.BlockSpec((block, width), row),
            pl.BlockSpec((block, 2 * units), row),
            pl.BlockSpec((width, units), lambda r: (0, 2), pipeline_mode=pl.Buffered(1)),
        ],
        out_specs=pl.BlockSpec((block, 2 * units), row),
        out_shape=jax.ShapeDtypeStruct((rows, 2 * units), jnp.bfloat16),
        compiler_params=pltpu.CompilerParams(vmem_limit_bytes=60 * 2**20),
        cost_estimate=cost(2 * rows * width * units, (rows * width + width * units) * 4, 0.63),
    )(cotangent, factors, weights)


def half_types(distance):
    if distance == 0:
        return (jnp.float32, jnp.float32)
    if distance == 1:
        return (jnp.bfloat16, jnp.float32)
    if distance == 2:
        return (jnp.float32, jnp.bfloat16)
    return (jnp.bfloat16, jnp.bfloat16)


def rows_out_kernel(terms, *refs):
    outs = refs[2 * terms :]
    total = None
    for left_ref, right_ref in zip(refs[:terms], refs[terms : 2 * terms]):
        product = lax.dot_general(
            left_ref[...], right_ref[...], NT, preferred_element_type=jnp.float32
        )
        total = product if total is None else total + product
    half = outs[0].shape[0]
    for index, out_ref in enumerate(outs):
        out_ref[...] = total[index * half : (index + 1) * half].astype(out_ref.dtype)


def rows_out(distances, lefts, rights, spans, chunk_rows):
    width, rows = rights[0].shape[0], len(distances) * chunk_rows
    first = distances[0] // len(distances)
    halves = [dtype for k in distances for dtype in half_types(k)]
    in_specs = [
        pl.BlockSpec(
            (rows, left[1]), lambda n, index=left[2]: (first, index), pipeline_mode=pl.Buffered(1)
        )
        for left in lefts
    ] + [
        pl.BlockSpec((256, columns), lambda n, index=index: (n, index)) for columns, index in spans
    ]
    depth = sum(left[1] for left in lefts)
    outs = pl.pallas_call(
        functools.partial(rows_out_kernel, len(lefts)),
        grid=(width // 256,),
        in_specs=in_specs,
        out_specs=[pl.BlockSpec((chunk_rows // 2, 256), lambda n: (0, n))] * len(halves),
        out_shape=[jax.ShapeDtypeStruct((chunk_rows // 2, width), dtype) for dtype in halves],
        compiler_params=pltpu.CompilerParams(vmem_limit_bytes=60 * 2**20),
        cost_estimate=cost(2 * rows * depth * width, depth * rows // 4, 4.07),
    )(*(left[0] for left in lefts), *rights)
    return {k: (outs[2 * i], outs[2 * i + 1]) for i, k in enumerate(distances)}


def resid_kernel(count, place_ref, *refs):
    inputs, lefts = refs[:2], (refs[2 : 2 + count], refs[2 + count : 2 + 2 * count])
    rights = refs[2 + 2 * count : 1 + 4 * count]
    norm_ref, hidden_ref, resid_ref, sums_ref = refs[1 + 4 * count :]
    half = sums_ref.shape[1] // 2
    blocks = pl.num_programs(0) // 2

    def block(x_ref, left_refs):
        for core, others in (
            (place_ref[1], rights[1:count]), (1 - place_ref[1], rights[count:])
        ):
            start = pl.multiple_of(core * half, half)
            total = lax.dot_general(
                left_refs[0][...], rights[0][pl.ds(start, half), :], NT,
                preferred_element_type=jnp.float32,
            )
            for left_ref, right_ref in zip(left_refs[1:], others):
                total = total + lax.dot_general(
                    left_ref[...], right_ref[...], NT, preferred_element_type=jnp.float32
                )
            sums_ref[:, pl.ds(start, half)] = total
        resid = x_ref[...].astype(jnp.float32) + sums_ref[...]
        hidden_ref[...] = (resid * rms_scale(resid) * norm_ref[...]).astype(jnp.bfloat16)

        @pl.when(pl.program_id(0) < resid_ref.shape[0])
        def _():
            resid_ref[pl.program_id(0)] = resid

    for sequence in range(2):

        @pl.when(pl.program_id(0) // blocks == sequence)
        def _():
            block(inputs[sequence], lefts[sequence])


def residual(place, inputs, heads, own, others, norm, chunk_rows):
    width, count = inputs[0].shape[1], len(heads[0])
    q_width = heads[0][0].shape[1]
    rows, block = 2 * SEQ, min(512, chunk_rows)
    here, there = placed(chunk_rows, block)
    blocks = SEQ // block
    fixed = lambda r, place: (0, 0)
    once = pl.Buffered(1)
    steps = (
        lambda r: jnp.minimum(r, blocks - 1),
        lambda r: jnp.maximum(r - blocks, 0),
    )
    return pl.pallas_call(
        functools.partial(resid_kernel, count),
        grid_spec=pltpu.PrefetchScalarGridSpec(
            num_scalar_prefetch=1,
            grid=(rows // block,),
            in_specs=[
                pl.BlockSpec((block, width), lambda r, place, step=step: here(step(r), place))
                for step in steps
            ]
            + [
                pl.BlockSpec((block, q_width), lambda r, place, step=step: there(step(r), place))
                for step in steps
                for _ in range(count)
            ]
            + [pl.BlockSpec((width, q_width), fixed, pipeline_mode=once)]
            + [pl.BlockSpec(piece.shape, fixed, pipeline_mode=once) for piece in others]
            + [pl.BlockSpec((1, width), fixed)],
            out_specs=[
                pl.BlockSpec((block, width), here),
                pl.BlockSpec((chunk_rows // block, block, width), lambda r, place: (0, 0, 0)),
            ],
            scratch_shapes=[pltpu.VMEM((block, width), jnp.float32)],
        ),
        out_shape=[
            jax.ShapeDtypeStruct((rows, width), jnp.bfloat16),
            jax.ShapeDtypeStruct((chunk_rows // block, block, width), jnp.float32),
        ],
        compiler_params=pltpu.CompilerParams(vmem_limit_bytes=60 * 2**20),
        cost_estimate=cost(2 * rows * width * width, rows * width * 8, 0.46),
    )(place, *inputs, *heads[0], *heads[1], own, *others, norm[None, :])


def input_kernel(count, core_ref, *refs):
    lefts, rights = refs[:count], refs[count : 3 * count - 1]
    x_ref, grad_ref, norm_ref, out_ref, gains_ref, sums_ref = refs[3 * count - 1 :]
    used = lefts[0].shape[1]
    step, steps = pl.program_id(0), pl.num_programs(0)

    def block(others):
        own = rights[0][:, rights[0].shape[1] - used :]
        total = lax.dot_general(lefts[0][...], own, NT, preferred_element_type=jnp.float32)
        for left_ref, right_ref in zip(lefts[1:], others):
            total = total + lax.dot_general(
                left_ref[...], right_ref[...], NT, preferred_element_type=jnp.float32
            )
        sums_ref[:, pl.ds(pl.multiple_of(step * 256, 256), 256)] = total

    for half in range(2):

        @pl.when(step // (steps // 2) == (core_ref[0] if half == 0 else 1 - core_ref[0]))
        def _():
            block(rights[1 + half * (count - 1) : 1 + (half + 1) * (count - 1)])

    @pl.when(step == steps - 1)
    def _():
        gains_ref[...] = jnp.zeros_like(gains_ref)
        for at in range(0, sums_ref.shape[0], 64):
            rows = slice(at, at + 64)
            grads = sums_ref[rows, :]
            inputs = x_ref[rows, :].astype(jnp.float32)
            inverse = rms_scale(inputs)
            normed = inputs * inverse
            gains_ref[...] += jnp.sum((grads * normed).reshape(-1, 8, grads.shape[1]), axis=0)
            out_ref[rows, :] = grad_ref[rows, :] + norm_back(
                grads * norm_ref[...], normed, inverse
            )


def input_back(core, grads, own, others, inputs, grad_resid, norm):
    rows, width = inputs.shape
    count, used = len(grads), grads[0].shape[1]
    steps = width // 256
    whole = lambda n, core: (0, 0)
    near = lambda n, core: (jnp.clip(n - core[0] * (steps // 2), 0, steps // 2 - 1), 0)
    other = lambda n, core: (jnp.clip(n - (1 - core[0]) * (steps // 2), 0, steps // 2 - 1), 0)
    once = pl.Buffered(1)
    return pl.pallas_call(
        functools.partial(input_kernel, count),
        grid_spec=pltpu.PrefetchScalarGridSpec(
            num_scalar_prefetch=1,
            grid=(steps,),
            in_specs=[pl.BlockSpec((rows, used), whole, pipeline_mode=once)] * count
            + [pl.BlockSpec((256, own.shape[1]), lambda n, core: (n, 0))]
            + [pl.BlockSpec((256, used), near)] * (count - 1)
            + [pl.BlockSpec((256, used), other)] * (count - 1)
            + [pl.BlockSpec((rows, width), whole, pipeline_mode=once)] * 2
            + [pl.BlockSpec((1, width), whole)],
            out_specs=[pl.BlockSpec((rows, width), whole), pl.BlockSpec((8, width), whole)],
            scratch_shapes=[pltpu.VMEM((rows, width), jnp.float32)],
        ),
        out_shape=[
            jax.ShapeDtypeStruct((rows, width), jnp.float32),
            jax.ShapeDtypeStruct((8, width), jnp.float32),
        ],
        compiler_params=pltpu.CompilerParams(vmem_limit_bytes=60 * 2**20),
        cost_estimate=cost(2 * rows * used * width * count, rows * width * 20, 0.28),
    )(core, *grads, own, *others, inputs, grad_resid, norm[None, :])


def attention_weights_kernel(inner_ref, beside_ref, *refs):
    out_ref = refs[-1]
    q_width = refs[-2].shape[1]
    total = jnp.zeros((out_ref.shape[0], q_width), jnp.float32)
    pieces, at = [], 0
    chunk_rows = refs[0].shape[0]
    for ref in refs[:-1]:
        if ref.shape[0] < SEQ:
            pieces.append(ref)
            continue
        at = 0
        for piece in pieces:
            rows = piece.shape[0]
            start = (at // chunk_rows ^ inner_ref[0]) * chunk_rows + at % chunk_rows
            total = total + lax.dot_general(
                piece[...], ref[pl.ds(pl.multiple_of(start, rows), rows), :], TN,
                preferred_element_type=jnp.float32,
            )
            at += rows
        pieces = []
    out_ref[:, :q_width] = total.astype(jnp.bfloat16)
    out_ref[:, q_width:] = beside_ref[...]


def out_weights(inner, beside, pieces, attended):
    width, q_width = pieces[0][0].shape[1], attended[0].shape[1]
    whole = lambda n, inner: (0, 0)
    columns = q_width + beside.shape[1]
    in_specs = [pl.BlockSpec((256, beside.shape[1]), lambda n, inner: (n, 0))]
    for rows in range(2):
        in_specs += [pl.BlockSpec((piece.shape[0], 256), lambda n, inner: (0, n)) for piece in pieces[rows]]
        in_specs.append(pl.BlockSpec((SEQ, q_width), whole))
    return pl.pallas_call(
        attention_weights_kernel,
        grid_spec=pltpu.PrefetchScalarGridSpec(
            num_scalar_prefetch=1,
            grid=(width // 256,),
            in_specs=in_specs,
            out_specs=pl.BlockSpec((256, columns), lambda n, inner: (n, 0)),
        ),
        out_shape=jax.ShapeDtypeStruct((width, columns), jnp.bfloat16),
        compiler_params=pltpu.CompilerParams(vmem_limit_bytes=60 * 2**20),
        cost_estimate=cost(4 * SEQ * q_width * width, SEQ * width * 4, 0.35),
    )(inner, beside, *pieces[0], attended[0], *pieces[1], attended[1])


def projection_weights_kernel(norm_ref, *refs):
    inputs, inverses, grads, out_ref = refs[:2], refs[2:4], refs[4:-1], refs[-1]
    total = jnp.zeros(out_ref.shape, jnp.float32)
    chunk_rows = grads[0].shape[0]
    for k, grad_ref in enumerate(grads):
        at = k * chunk_rows
        rows = slice(at % SEQ, at % SEQ + chunk_rows)
        inverse = inverses[at // SEQ][rows, :]
        normed = inputs[at // SEQ][rows, :].astype(jnp.float32) * jnp.concatenate([inverse] * 2, axis=1)
        total = total + lax.dot_general(
            (normed * norm_ref[...]).astype(jnp.bfloat16), grad_ref[...], TN,
            preferred_element_type=jnp.float32,
        )
    out_ref[...] = total.astype(jnp.bfloat16)


def projection_weights(inputs, inverse, norm, grads):
    width, columns = inputs[0].shape[1], grads[0].shape[1]
    whole = lambda n: (0, 0)
    column = lambda n: (0, n)
    return pl.pallas_call(
        projection_weights_kernel,
        grid=(width // 256,),
        in_specs=[pl.BlockSpec((1, 256), column)]
        + [pl.BlockSpec((SEQ, 256), column)] * 2
        + [pl.BlockSpec((SEQ, 128), whole)] * 2
        + [pl.BlockSpec(part.shape, whole) for part in grads],
        out_specs=pl.BlockSpec((256, columns), lambda n: (n, 0)),
        out_shape=jax.ShapeDtypeStruct((width, columns), jnp.bfloat16),
        compiler_params=pltpu.CompilerParams(vmem_limit_bytes=60 * 2**20),
        cost_estimate=cost(4 * SEQ * columns * width, SEQ * width * 4, 0.43),
    )(norm[None, :], *inputs, *inverse, *grads)


def shift(values, distance, count, axis="tensor"):
    return lax.ppermute(values, axis, [(i, i ^ distance) for i in range(count)])


def gather_kernel(src_ref, own_ref, other_ref, send_sems, recv_sems, local_sem):
    rows = src_ref.shape[0]
    half = rows // 2
    x_top, x_bottom = own_ref.at[pl.ds(rows, half)], own_ref.at[pl.ds(rows + half, half)]
    y_top, y_bottom = other_ref.at[pl.ds(0, half)], other_ref.at[pl.ds(half, half)]
    far_top, far_bottom = other_ref.at[pl.ds(rows, half)], other_ref.at[pl.ds(rows + half, half)]
    top, bottom = src_ref.at[pl.ds(0, half)], src_ref.at[pl.ds(half, half)]
    greet([1, 2])

    def copy(index, from_ref, to_ref, distance):
        return pltpu.make_async_remote_copy(
            src_ref=from_ref, dst_ref=to_ref, send_sem=send_sems.at[index],
            recv_sem=recv_sems.at[index], **remote(distance),
        )

    first = [
        copy(0, bottom, x_bottom, 1), copy(1, top, y_top, 2),
        copy(2, top, x_top, 1), copy(3, bottom, y_bottom, 2),
    ]
    for sent in first:
        sent.start()
    local = pltpu.make_async_copy(src_ref, own_ref.at[pl.ds(0, rows)], local_sem.at[0])
    local.start()
    first[1].wait_recv()
    relay_top = copy(4, y_top, far_top, 1)
    relay_top.start()
    first[0].wait_recv()
    relay_bottom = copy(5, x_bottom, far_bottom, 2)
    relay_bottom.start()
    first[2].wait_recv()
    first[3].wait_recv()
    relay_top.wait_recv()
    relay_bottom.wait_recv()
    for sent in first + [relay_top, relay_bottom]:
        sent.wait_send()
    local.wait()


def gather_rows(values, count):
    if count != 4:
        near = gather_near(values, count)
        return [jnp.concatenate(near[i : i + count // 2], axis=0) for i in (0, count // 2)]
    place = pl.BlockSpec(memory_space=pl.ANY)
    rows, width = values.shape
    wide = jax.ShapeDtypeStruct((2 * rows, width), values.dtype)
    return pl.pallas_call(
        gather_kernel,
        in_specs=[place],
        out_specs=[place] * 2,
        out_shape=[wide, wide],
        scratch_shapes=[
            pltpu.SemaphoreType.DMA((6,)), pltpu.SemaphoreType.DMA((6,)),
            pltpu.SemaphoreType.DMA((1,)),
        ],
        compiler_params=pltpu.CompilerParams(collective_id=1, has_side_effects=True),
        cost_estimate=pl.CostEstimate(
            flops=0, bytes_accessed=values.size * 12, transcendentals=0,
            remote_bytes_transferred=values.size * 6,
        ),
    )(values)


def gather_near(values, count):
    if count == 4:
        return [values, shift(values, 1, count), shift(values, 2, count)]
    whole = lax.all_gather(values, "tensor", axis=0)
    mine = lax.axis_index("tensor")
    return [lax.dynamic_index_in_dim(whole, mine ^ k, 0, False) for k in range(count)]


def gather_far(near, count):
    if count != 4:
        return []
    half = near[0].shape[0] // 2
    return [shift(near[2][:half], 1, count), shift(near[1][half:], 2, count)]


def gather_chunks(values, count):
    near = gather_near(values, count)
    far = gather_far(near, count)
    return near + [jnp.concatenate(far, axis=0)] if far else near


def exchange(parts, distances, count):
    return [part if k == 0 else shift(part, k, count) for k, part in zip(distances, parts)]


def column_piece(weights, columns, core):
    half = weights.shape[0] // 2
    return lax.dynamic_slice(
        weights, (core[0] * half, columns[0]), (half, columns[1] - columns[0])
    )


def sum_first(parts, count):
    if count != 4:
        return None
    return shift(parts[3][0], 1, count), shift(parts[3][1], 2, count)


def sum_adds(parts, first):
    far_top, far_bottom = first
    return (
        (parts[2][0] + far_top.astype(jnp.float32)).astype(jnp.bfloat16),
        (parts[1][1] + far_bottom.astype(jnp.float32)).astype(jnp.bfloat16),
    )


def sum_rest(parts, near, adds, count):
    if count != 4:
        mine = lax.axis_index("tensor")
        half, width = parts[0][0].shape
        stacked = jnp.zeros((count, 2 * half, width), jnp.bfloat16)
        for k in range(count):
            term = jnp.concatenate([side.astype(jnp.bfloat16) for side in parts[k]], axis=0)
            stacked = lax.dynamic_update_index_in_dim(stacked, term, mine ^ k, 0)
        total = lax.psum_scatter(
            stacked.reshape(-1, width), "tensor", scatter_dimension=0, tiled=True
        ).astype(jnp.float32)
        none = jnp.zeros((half, width), jnp.bfloat16)
        return [[total[:half], none, none], [total[half:], none, none]]
    x_top, y_bottom = near
    y_top, x_bottom = shift(adds[0], 2, count), shift(adds[1], 1, count)
    return [[parts[0][0], x_top, y_top], [parts[0][1], x_bottom, y_bottom]]


def sum_near(parts, count):
    if count != 4:
        return ()
    return shift(parts[1][0], 1, count), shift(parts[2][1], 2, count)


def added(own_ref, x_ref, y_ref):
    return own_ref[...] + x_ref[...].astype(jnp.float32) + y_ref[...].astype(jnp.float32)


def own_rows_call(kernel, sums, twos, ones, out_shapes, gains):
    half, width = sums[0][0].shape
    block = min(64, half)
    term = pl.BlockSpec((block, width), lambda i: (i, 0))
    both = pl.BlockSpec((2, block, width), lambda i: (0, i, 0))
    out_specs = [both] * len(out_shapes)
    if gains:
        out_specs.append(pl.BlockSpec((8, width), lambda i: (0, 0)))
        out_shapes = out_shapes + [jax.ShapeDtypeStruct((8, width), jnp.float32)]
    return pl.pallas_call(
        kernel,
        grid=(half // block,),
        in_specs=[term] * 6 + [both] * len(twos) + [pl.BlockSpec((1, width), lambda i: (0, 0))] * len(ones),
        out_specs=out_specs,
        out_shape=out_shapes,
        compiler_params=pltpu.CompilerParams(vmem_limit_bytes=60 * 2**20),
        cost_estimate=cost(half * width * 10, half * width * 10, 1.0),
    )(*sums[0], *sums[1], *twos, *ones)


def resid_back_kernel(*refs):
    dy_ref, resid_ref, norm_ref, grad_ref, low_ref, gains_ref = refs[6:]

    @pl.when(pl.program_id(0) == 0)
    def _():
        gains_ref[...] = jnp.zeros_like(gains_ref)

    for side in range(2):
        grads = added(*refs[3 * side : 3 * side + 3])
        resid = resid_ref[side]
        inverse = rms_scale(resid)
        normed = resid * inverse
        gains_ref[...] += jnp.sum((grads * normed).reshape(-1, 8, grads.shape[1]), axis=0)
        total = dy_ref[side].astype(jnp.float32) + norm_back(grads * norm_ref[...], normed, inverse)
        grad_ref[side] = total
        low_ref[side] = total.astype(jnp.bfloat16)


def output_kernel(*refs):
    resid_ref, out_ref = refs[6:]
    for side in range(2):
        out_ref[side] = (resid_ref[side] + added(*refs[3 * side : 3 * side + 3])).astype(jnp.bfloat16)


def total_everywhere(values, sizes):
    for axis, size in sizes.items():
        distance = 1
        while distance < size:
            values = values + shift(values, distance, size, axis)
            distance *= 2
    return values


def after(value, *others):
    return lax.optimization_barrier((value, others))[0]


def pad_columns(values, width):
    return jnp.pad(values, ((0, 0), (0, width - values.shape[1])))


def gather_weights(*parts):
    return lax.all_gather(jnp.concatenate(parts, axis=1), "dp", axis=0, tiled=True)


def scatter_weights(grads):
    return lax.psum_scatter(grads, "dp", scatter_dimension=0, tiled=True)


def per_device(
    sizes,
    tokens,
    segments,
    positions,
    w_query,
    w_key,
    w_value,
    w_out,
    w_gate,
    w_up,
    w_down,
    norm_attn,
    norm_mlp,
    query_gain,
    key_gain,
    out_grad,
):
    count = sizes["tensor"]
    chunk_rows = tokens.shape[0]
    q_width, key_width = w_query.shape[1], w_key.shape[1]
    kv_width = -(-key_width // 128) * 128
    units = w_gate.shape[1] // 2
    mine = lax.axis_index("tensor").astype(jnp.int32).reshape(1)

    half, width = chunk_rows // 2, tokens.shape[1]
    inner_count = count // 2
    inner, flip = mine % inner_count, mine // inner_count
    core = lax.axis_index("dp").astype(jnp.int32).reshape(1) % 2

    def own_first(values):
        pair = values.reshape(2, SEQ)
        return jnp.where(flip == 0, pair, pair[::-1])

    w_attn = gather_weights(
        w_out, w_query, pad_columns(w_key, kv_width), pad_columns(w_value, kv_width)
    )
    rows_in = gather_rows(tokens, count)
    w_mlp = [
        gather_weights(w_gate[:, part], w_up[:, part], w_down[:, part])
        for part in (slice(0, units), slice(units, 2 * units))
    ]
    segments, positions = own_first(segments), own_first(positions)
    out_near = gather_near(column_piece(after(w_attn, rows_in), (0, q_width), core), count)
    inv_rows, queries, key_sides, value_sides, raw = [], [], [], [], []
    tables = rotary_tables(positions.reshape(-1))
    attended, inv_total, heads = [], [], []
    for sequence in range(2):
        rows = rows_in[sequence]
        if sequence == 1:
            rows = after(rows, attended, out_near)
            out_near = after(out_near, attended)
            out_far = gather_far(out_near, count)
            out_others = out_near[1:] + ([jnp.concatenate(out_far, axis=0)] if out_far else [])
            out_others = out_others + [shift(part, 1, sizes["dp"], "dp") for part in out_others]
        results = project(
            inner, sequence, rows, chunk_rows, norm_attn, w_attn, tables, query_gain, key_gain, q_width, kv_width
        )
        for kept, result in zip((inv_rows, queries, key_sides, value_sides, raw), results):
            kept.append(result)
        result, inverse = attend(
            queries[sequence], key_sides[sequence], value_sides[sequence], segments[sequence]
        )
        attended.append(result)
        inv_total.append(inverse)
        heads.append(gather_chunks(result, count))
    grad_near = gather_near(after(out_grad, heads), count)
    crossed = [
        heads[sequence][:inner_count] + heads[1 - sequence][inner_count:] for sequence in range(2)
    ]
    rows_two, resid = residual(
        jnp.concatenate([inner, core]), rows_in, crossed, w_attn, out_others, norm_mlp, chunk_rows
    )
    resid = resid.reshape(2, half, width)
    grad_near = after(grad_near, rows_two)
    grad_far = gather_far(grad_near, count)
    act_a, factors = hidden_forward(rows_two, w_mlp[0])
    grad_rows = jnp.concatenate(grad_near + after(grad_far, act_a), axis=0)

    grads_a = hidden_backward(grad_rows, factors, w_mlp[0])
    grad_a = contract_rows(rows_two, grads_a).astype(jnp.bfloat16)
    half_columns = column_piece(after(w_attn, grads_a), (q_width, w_attn.shape[1]), core)
    in_near = [shift(half_columns, k, count) for k in range(1, count - 1)]
    if count == 4:
        far_halves = gather_far([half_columns, *in_near], count)
        in_far = [jnp.concatenate(far_halves, axis=0)]
    else:
        far_halves = in_far = [shift(half_columns, count - 1, count)]
    act, grads_b = hidden_units(after(rows_two, grad_a), grad_rows, w_mlp[1], act_a)
    in_others = in_near + in_far
    in_others = in_others + [shift(part, 1, sizes["dp"], "dp") for part in in_others]
    spans = [(2 * units, 0), (2 * units, 0)]

    def two_parts(distances, grads):
        lefts = [(grads, 2 * units, 0), (grads_b, 2 * units, 0)]
        return rows_out(distances, lefts, w_mlp, spans, chunk_rows)

    grad_b = contract_rows(after(rows_two, in_near), grads_b).astype(jnp.bfloat16)
    two = two_parts(list(range(inner_count, count)), after(grads_a, grad_b, far_halves))
    two_first = sum_first(two, count)
    for k in range(1, inner_count):
        two.update(two_parts([k], after(grads_a, two[count - 1])))
    two_near = sum_near(two, count)
    two_adds = sum_adds(two, two_first) if count == 4 else ()
    two.update(two_parts([0], after(grads_a, two[1], two_adds)))
    two_rest = sum_rest(two, two_near, two_adds, count)
    distances = list(range(count))
    out_act = after(act, two[0])
    out = rows_out(
        distances, [(out_act, units, 0), (out_act, units, 1)], w_mlp, [(units, 2), (units, 2)], chunk_rows
    )
    out_first = sum_first(out, count)
    out_near = sum_near(out, count)
    grad_resid, branch_low, gain_mlp = own_rows_call(
        resid_back_kernel,
        after(two_rest, out[0]),
        [out_grad.reshape(2, half, width), resid],
        [norm_mlp[None, :]],
        [
            jax.ShapeDtypeStruct((2, half, width), jnp.float32),
            jax.ShapeDtypeStruct((2, half, width), jnp.bfloat16),
        ],
        True,
    )
    branch_low = branch_low.reshape(chunk_rows, width)
    heads_out = grad_heads(core, branch_low, w_attn, out_others, q_width, count)
    heads_in = exchange(heads_out, distances, count)
    scattered_a = scatter_weights(grad_a)
    scattered_b = scatter_weights(after(grad_b, scattered_a, two[count - 1]))
    grad_down = contract_rows(
        after(grad_rows, heads_out[0], scattered_b, out_first), act
    ).astype(jnp.bfloat16)
    tops = bottoms = relays = []
    if count == 4:
        top, bottom = after((branch_low[:half], branch_low[half:]), heads_in, grad_down)
        tops = [shift(top, 1, count), shift(top, 2, count)]
    sums, raw_grads = [], []
    for sequence in range(2):
        pieces = heads_in[sequence * inner_count : (sequence + 1) * inner_count]
        if sequence == 0:
            pieces = after(pieces, heads_in, grad_down)
        else:
            pieces = after(pieces, tops, raw_grads, in_others)
            if count == 4:
                bottom = after(bottom, tops, raw_grads)
                bottoms = [shift(bottom, 1, count), shift(bottom, 2, count)]
        results = attend_back(
            inner, sequence, queries[sequence], key_sides[sequence], value_sides[sequence],
            segments[sequence], attended[sequence], inv_total[sequence], pieces, raw[sequence], tables,
            query_gain, key_gain,
        )
        raw_grads += results[:inner_count]
        sums.append(results[inner_count:])
    raw_in = exchange(raw_grads, distances, count)
    if count == 4:
        near_bottom, near_top = after((bottoms[0], tops[1]), bottoms, raw_grads)
        relays = [shift(near_top, 1, count), shift(near_bottom, 2, count)]
        branch = (
            [branch_low, tops[0], bottoms[0]],
            [tops[1], bottoms[1], *relays],
        )
    else:
        branch_near = gather_near(branch_low, count)
        branch = (branch_near[:inner_count], branch_near[inner_count:])
    scattered_down = scatter_weights(after(grad_down, scattered_b, heads_in))
    out_adds = sum_adds(out, after(out_first, raw_grads)) if count == 4 else ()
    grad_qkv = projection_weights(after(rows_in, raw_grads, bottoms, out_adds), inv_rows, norm_attn, raw_grads)
    grad_w_gate = jnp.concatenate(
        [scattered_a[:, :units], scattered_b[:, :units]], axis=1
    ).astype(jnp.float32)
    grad_w_up = jnp.concatenate(
        [scattered_a[:, units:], scattered_b[:, units:]], axis=1
    ).astype(jnp.float32)
    grad_attn = out_weights(inner, grad_qkv, after(branch, raw_grads, grad_w_gate, grad_w_up, in_others), attended)

    scattered_attn = scatter_weights(
        after(
            grad_attn, scattered_down, raw_in,
        )
    )

    grad_w_down = scattered_down.astype(jnp.float32)
    grad_tokens, gain_attn = input_back(
        core, after(raw_in, grad_w_down), w_attn, in_others, tokens, grad_resid.reshape(chunk_rows, width), norm_attn
    )
    out_rest = sum_rest(out, out_near, out_adds, count)
    gains = [
        jnp.sum(gain_attn, axis=0),
        jnp.sum(gain_mlp, axis=0),
        jnp.sum((sums[0][0] + sums[1][0]).reshape(-1, 64), axis=0),
        jnp.sum((sums[0][1] + sums[1][1]).reshape(-1, 64), axis=0),
    ]
    gains = jnp.concatenate(gains).reshape(-1, 128)
    gains = total_everywhere(gains, sizes).reshape(-1)
    (output,) = own_rows_call(
        output_kernel, after(out_rest, gains), [resid], [], [jax.ShapeDtypeStruct((2, half, width), jnp.bfloat16)],
        False,
    )
    distances = list(range(count))
    key_at = 2 * q_width
    value_at = key_at + kv_width
    return (
        output.reshape(chunk_rows, width),
        grad_tokens.reshape(chunk_rows, width),
        scattered_attn[:, q_width:key_at].astype(jnp.float32),
        scattered_attn[:, key_at : key_at + key_width].astype(jnp.float32),
        scattered_attn[:, value_at : value_at + key_width].astype(jnp.float32),
        scattered_attn[:, :q_width].astype(jnp.float32),
        grad_w_gate,
        grad_w_up,
        grad_w_down,
        gains[:width],
        gains[width : 2 * width],
        gains[2 * width : 2 * width + 64],
        gains[2 * width + 64 : 2 * width + 128],
    )


def solution(mesh):
    return jax.shard_map(
        functools.partial(per_device, dict(mesh.shape)),
        mesh=mesh,
        in_specs=(
            P(("dp", "tensor"), None),
            P("dp"),
            P("dp"),
            P("dp", "tensor"),
            P("dp", "tensor"),
            P("dp", "tensor"),
            P("dp", "tensor"),
            P("dp", "tensor"),
            P("dp", "tensor"),
            P("dp", "tensor"),
            P(),
            P(),
            P(),
            P(),
            P(("dp", "tensor"), None),
        ),
        out_specs=(
            P(("dp", "tensor"), None),
            P(("dp", "tensor"), None),
            P("dp", "tensor"),
            P("dp", "tensor"),
            P("dp", "tensor"),
            P("dp", "tensor"),
            P("dp", "tensor"),
            P("dp", "tensor"),
            P("dp", "tensor"),
            P(),
            P(),
            P(),
            P(),
        ),
        check_vma=False,
    )
```

```python
import functools

import jax
import jax.numpy as jnp
from jax import lax
from jax.experimental import pallas as pl
from jax.experimental.pallas import tpu as pltpu
from jax.sharding import PartitionSpec as P

EPS = 1e-05
THETA = 1000000.0
SEQ = 1024
TILE = 256
LOG2E = 1.4426950408889634
MASKED = -1e30
NT = (((1,), (1,)), ((), ()))
TN = (((0,), (0,)), ((), ()))


def rms_scale(values):
    return lax.rsqrt(jnp.mean(values * values, axis=-1, keepdims=True) + EPS)


def norm_back(grad_normed, normed, inverse):
    return inverse * (grad_normed - normed * jnp.mean(grad_normed * normed, axis=-1, keepdims=True))


def rotary_tables(places):
    lane = jnp.arange(128)
    frequency = THETA ** (-(lane % 32).astype(jnp.float32) * 2.0 / 64)
    angles = places.astype(jnp.float32)[:, None] * frequency[None, :]
    sine = jnp.sin(angles)
    upper = (lane % 64 >= 32)[None, :]
    return jnp.cos(angles), jnp.where(upper, 0.0, -sine), jnp.where(upper, sine, 0.0)


def contract_rows(left, right):
    return lax.dot_general(
        left, right, (((0,), (0,)), ((), ())), preferred_element_type=jnp.float32
    )


def half_lanes(rows):
    return lax.broadcasted_iota(jnp.int32, (rows, 128), 1) < 64


def ones_side(side, rows):
    low = half_lanes(rows)
    return jnp.where(low if side == 0 else ~low, 1.0, 0.0).astype(jnp.bfloat16)


def attend_kernel(q_ref, k_ref, v_ref, segc_ref, segr_ref, out_ref, inv_ref, bias_ref, total_ref):
    coef = LOG2E * 64 ** (-0.5)

    @pl.when(pl.program_id(1) == 0)
    def _():
        for at in range(0, SEQ, TILE):
            end = at + TILE
            rows = lax.broadcasted_iota(jnp.int32, (TILE, end), 0) + at
            cols = lax.broadcasted_iota(jnp.int32, (TILE, end), 1)
            allowed = (segc_ref[at:end, :] == segr_ref[0, :, :end]) & (cols <= rows)
            bias_ref[at:end, :end] = jnp.where(allowed, 0.0, MASKED)

    for side in range(2):
        lanes = slice(side * 128, side * 128 + 128)
        for key_at in range(0, SEQ, TILE):
            keys, rows = slice(key_at, key_at + TILE), slice(key_at, SEQ)
            scores = lax.dot_general(
                q_ref[rows, :], k_ref[keys, lanes], NT, preferred_element_type=jnp.float32
            )
            weights = jnp.exp2(scores * coef + bias_ref[rows, keys]).astype(jnp.bfloat16)
            mixed = jnp.concatenate([v_ref[keys, lanes], ones_side(side, TILE)], axis=1)
            part = jnp.dot(weights, mixed, preferred_element_type=jnp.float32)
            if side == 0 and key_at == 0:
                total_ref[...] = part
            else:
                total_ref[rows, :] += part
    inverse = 1.0 / total_ref[:, 128:]
    out_ref[...] = (total_ref[:, :128] * inverse).astype(jnp.bfloat16)
    inv_ref[...] = inverse


def unrotated(grads, raw, cosine, sine_low, sine_high, gain):
    grads = grads * 0.125
    turned = (
        grads * cosine
        - pltpu.roll(grads, 96, 1) * sine_low
        - pltpu.roll(grads, 32, 1) * sine_high
    )
    inverse = head_inverse(raw)
    normed = raw * inverse
    scaled = turned * gain
    change = inverse * (scaled - normed * head_mean(scaled * normed))
    return change, jnp.sum((turned * normed).reshape(-1, 8, 128), axis=0)


def attend_back_kernel(
    chunks, inner_ref, q_ref, k_ref, v_ref, segc_ref, segr_ref, out_ref, inv_ref,
    qraw_ref, kraw_ref, cos_ref, low_ref, high_ref, qgain_ref, kgain_ref, *refs,
):
    pieces, results = refs[:chunks], refs[chunks : 2 * chunks]
    (
        qsum_ref, ksum_ref, bias_ref, mix_ref, qside_ref, gside_ref,
        dq_ref, dk_ref, dv_ref, kpair_ref, vpair_ref, grad_ref,
    ) = refs[2 * chunks :]
    chunk_rows = SEQ // chunks
    q_width = 128 * pl.num_programs(1)
    kv_width = (results[0].shape[1] - q_width) // 2

    def rows_of(k):
        return pl.ds(pl.multiple_of((inner_ref[0] ^ k) * chunk_rows, chunk_rows), chunk_rows)

    def put(values, place):
        dq_ref[...] = values
        for k, result_ref in enumerate(results):
            lanes = pl.ds(pl.multiple_of(place, 128), 128)
            result_ref[:, lanes] = dq_ref[rows_of(k), :].astype(jnp.bfloat16)

    coef = LOG2E * 64 ** (-0.5)
    step = pl.program_id(1)

    @pl.when(step == 0)
    def _():
        for key_at in range(0, SEQ, TILE):
            key_end = key_at + TILE
            keys = lax.broadcasted_iota(jnp.int32, (TILE, SEQ - key_at), 0) + key_at
            rows = lax.broadcasted_iota(jnp.int32, (TILE, SEQ - key_at), 1) + key_at
            allowed = (segc_ref[key_at:key_end, :] == segr_ref[0, :, key_at:]) & (keys <= rows)
            bias_ref[key_at:key_end, key_at:] = jnp.where(allowed, 0.0, MASKED)

    @pl.when((step == 0) & (pl.program_id(0) == 0))
    def _():
        qsum_ref[...] = jnp.zeros_like(qsum_ref)
        ksum_ref[...] = jnp.zeros_like(ksum_ref)

    @pl.when(lax.rem(step, 4) == 0)
    def _():
        kpair_ref[...] = jnp.zeros_like(kpair_ref)
        vpair_ref[...] = jnp.zeros_like(vpair_ref)

    @pl.when(lax.rem(step, 2) == 0)
    def _():
        dk_ref[...] = jnp.zeros_like(dk_ref)
        dv_ref[...] = jnp.zeros_like(dv_ref)

    for k, piece_ref in enumerate(pieces):
        grad_ref[rows_of(k), :] = piece_ref[...].astype(jnp.float32)
    low = half_lanes(SEQ)
    scaled = grad_ref[...] * inv_ref[...]
    scaled_low = scaled.astype(jnp.bfloat16)
    mix_ref[:, :128] = scaled_low
    mix_ref[:, 128:] = -(scaled * out_ref[...].astype(jnp.float32)).astype(jnp.bfloat16)
    none = jnp.zeros_like(scaled_low)
    queries = q_ref[...]
    gside_ref[:, :128] = jnp.where(low, scaled_low, none)
    gside_ref[:, 128:] = jnp.where(low, none, scaled_low)
    qside_ref[:, :128] = jnp.where(low, queries, none)
    qside_ref[:, 128:] = jnp.where(low, none, queries)

    for key_at in range(0, SEQ, TILE):
        keys, rows = slice(key_at, key_at + TILE), slice(key_at, SEQ)
        for side in range(2):
            lanes = slice(side * 128, side * 128 + 128)
            key_side = k_ref[keys, lanes]
            value_side = jnp.concatenate([v_ref[keys, lanes], ones_side(side, TILE)], axis=1)
            scores = lax.dot_general(
                key_side, q_ref[rows, :], NT, preferred_element_type=jnp.float32
            )
            weights = jnp.exp2(scores * coef + bias_ref[keys, rows])
            change = lax.dot_general(
                value_side, mix_ref[rows, :], NT, preferred_element_type=jnp.float32
            )
            grads = (weights * change).astype(jnp.bfloat16)
            dv_ref[keys, :] += jnp.dot(
                weights.astype(jnp.bfloat16),
                gside_ref[rows, lanes],
                preferred_element_type=jnp.float32,
            )
            dk_ref[keys, :] += jnp.dot(
                grads, qside_ref[rows, lanes], preferred_element_type=jnp.float32
            )
            dq = lax.dot_general(grads, key_side, TN, preferred_element_type=jnp.float32)
            if key_at == 0 and side == 0:
                dq_ref[...] = dq
            else:
                dq_ref[rows, :] += dq

    cosine, sine_low, sine_high = cos_ref[...], low_ref[...], high_ref[...]
    change, sums = unrotated(
        dq_ref[...], qraw_ref[...], cosine, sine_low, sine_high, qgain_ref[...]
    )
    qsum_ref[...] += sums
    put(change, step * 128)

    @pl.when(lax.rem(step, 2) == 1)
    def _():
        mine = low == (lax.rem(step, 4) == 1)
        for sum_ref, pair_ref in ((dk_ref, kpair_ref), (dv_ref, vpair_ref)):
            sums = sum_ref[...]
            pair_ref[...] = jnp.where(mine, sums + pltpu.roll(sums, 64, 1), pair_ref[...])

    @pl.when((lax.rem(step, 4) == 3) | (step == pl.num_programs(1) - 1))
    def _():
        change, sums = unrotated(
            kpair_ref[...], kraw_ref[...], cosine, sine_low, sine_high, kgain_ref[...]
        )
        ksum_ref[...] += sums
        put(change, q_width + step // 4 * 128)
        put(vpair_ref[...], q_width + kv_width + step // 4 * 128)


def attention_specs():
    pair = pl.BlockSpec((SEQ, 128), lambda s, p, *_: (s, p))
    group = pl.BlockSpec((SEQ, 256), lambda s, p, *_: (s, p // 2))
    seg_col = pl.BlockSpec((SEQ, 1), lambda s, p, *_: (s, 0))
    seg_row = pl.BlockSpec((1, 1, SEQ), lambda s, p, *_: (s, 0, 0))
    return pair, group, seg_col, seg_row


def attend(queries, key_sides, value_sides, segments):
    rows, width = queries.shape
    sequences, pairs = rows // SEQ, width // 128
    pair, group, seg_col, seg_row = attention_specs()
    work = rows * SEQ * width
    return pl.pallas_call(
        attend_kernel,
        grid=(sequences, pairs),
        in_specs=[pair, group, group, seg_col, seg_row],
        out_specs=[pair, pair],
        out_shape=[
            jax.ShapeDtypeStruct((rows, width), jnp.bfloat16),
            jax.ShapeDtypeStruct((rows, width), jnp.float32),
        ],
        scratch_shapes=[pltpu.VMEM((SEQ, SEQ), jnp.float32), pltpu.VMEM((SEQ, 256), jnp.float32)],
        compiler_params=pltpu.CompilerParams(vmem_limit_bytes=60 * 2**20),
        cost_estimate=pl.CostEstimate(
            flops=42 * work // 10, bytes_accessed=rows * width * 12, transcendentals=work // 128
        ),
    )(queries, key_sides, value_sides, segments[:, None], segments.reshape(sequences, 1, SEQ))


def attend_back(
    inner, sequence, queries, key_sides, value_sides, segments, attended, inverse, pieces, raw, tables,
    query_gain, key_gain,
):
    width = queries.shape[1]
    pairs, chunks, chunk_rows = width // 128, len(pieces), pieces[0].shape[0]
    kv_width = key_sides.shape[1] // 4
    pair, group, seg_col, seg_row = attention_specs()
    kv_raw = pl.BlockSpec((SEQ, 128), lambda s, p, *_: (0, width // 128 + p // 4))
    table = pl.BlockSpec((SEQ, 128), lambda s, p, *_: (sequence, 0))
    gain = pl.BlockSpec((1, 128), lambda s, p, *_: (0, 0))
    total = pl.BlockSpec((8, 128), lambda s, p, *_: (0, 0))
    piece = pl.BlockSpec((chunk_rows, 128), lambda s, p, *_: (0, p))
    columns = width + 2 * kv_width
    work = SEQ * SEQ * width
    flat = pltpu.VMEM((SEQ, 128), jnp.float32)
    return pl.pallas_call(
        functools.partial(attend_back_kernel, chunks),
        grid_spec=pltpu.PrefetchScalarGridSpec(
            num_scalar_prefetch=1,
            grid=(1, pairs),
            in_specs=[pair, group, group, seg_col, seg_row, pair, pair]
            + [pair, kv_raw, table, table, table, gain, gain]
            + [piece] * chunks,
            out_specs=[pl.BlockSpec((chunk_rows, columns), lambda s, p, *_: (0, 0))] * chunks
            + [total, total],
            scratch_shapes=[
                pltpu.VMEM((SEQ, SEQ), jnp.float32),
                pltpu.VMEM((SEQ, 256), jnp.bfloat16),
                pltpu.VMEM((SEQ, 256), jnp.bfloat16),
                pltpu.VMEM((SEQ, 256), jnp.bfloat16),
                flat, flat, flat, flat, flat, flat,
            ],
        ),
        out_shape=[jax.ShapeDtypeStruct((chunk_rows, columns), jnp.bfloat16)] * chunks
        + [jax.ShapeDtypeStruct((8, 128), jnp.float32)] * 2,
        compiler_params=pltpu.CompilerParams(vmem_limit_bytes=60 * 2**20),
        cost_estimate=pl.CostEstimate(
            flops=110 * work // 10, bytes_accessed=SEQ * width * 20, transcendentals=work // 128
        ),
    )(
        inner, queries, key_sides, value_sides, segments[:, None], segments.reshape(-1, 1, SEQ),
        attended, inverse, raw, raw, *tables,
        jnp.tile(query_gain, 2)[None, :], jnp.tile(key_gain, 2)[None, :], *pieces,
    )


def cost(flops, moved, share):
    return pl.CostEstimate(
        flops=int(0.2 * flops / share), bytes_accessed=int(0.2 * moved), transcendentals=0
    )


def head_inverse(values):
    squares = values * values
    high = squares.astype(jnp.bfloat16)
    low = (squares - high.astype(jnp.float32)).astype(jnp.bfloat16)
    return lax.rsqrt(head_sum(high, low) * (1.0 / 64) + EPS)


def head_sum(high, low):
    from_head = lax.broadcasted_iota(jnp.int32, (128, 128), 0) // 64
    to_head = lax.broadcasted_iota(jnp.int32, (128, 128), 1) // 64
    same = jnp.where(from_head == to_head, 1.0, 0.0).astype(jnp.bfloat16)
    return jnp.dot(high, same, preferred_element_type=jnp.float32) + jnp.dot(
        low, same, preferred_element_type=jnp.float32
    )


def head_mean(values):
    high = values.astype(jnp.bfloat16)
    low = (values - high.astype(jnp.float32)).astype(jnp.bfloat16)
    return head_sum(high, low) * (1.0 / 64)


def project_kernel(
    pieces, inner_ref, *refs,
):
    norm_ref, w_ref, cos_ref, low_ref, high_ref, qgain_ref, kgain_ref = refs[pieces : pieces + 7]
    inv_ref, q_ref, k_ref, v_ref, raw_ref = refs[pieces + 7 :]
    inputs = refs[0][...].astype(jnp.float32)
    inverse = rms_scale(inputs)
    hidden = (inputs * inverse * norm_ref[...]).astype(jnp.bfloat16)
    inv_ref[...] = jnp.broadcast_to(inverse, inv_ref.shape)
    q_width, kv_width = q_ref.shape[1], k_ref.shape[1] // 4
    cosine, sine_low, sine_high = cos_ref[...], low_ref[...], high_ref[...]
    lower = lax.broadcasted_iota(jnp.int32, cosine.shape, 1) < 64
    none = jnp.zeros_like(cosine)

    def rotated(raw, gain):
        scaled = raw * head_inverse(raw) * gain
        return (
            scaled * cosine
            + pltpu.roll(scaled, 96, 1) * sine_low
            + pltpu.roll(scaled, 32, 1) * sine_high
        )

    def to_sides(pair, out_ref, at):
        first, second = jnp.where(lower, pair, none), jnp.where(lower, none, pair)
        sides = (first, pltpu.roll(first, 64, 1), pltpu.roll(second, 64, 1), second)
        for index, side in enumerate(sides):
            lanes = slice(at * 4 + index * 128, at * 4 + index * 128 + 128)
            out_ref[:, lanes] = side.astype(jnp.bfloat16)

    wide = jnp.dot(hidden, w_ref[:, q_width:], preferred_element_type=jnp.float32)
    raw_ref[...] = wide[:, : q_width + kv_width]
    for at in range(0, q_width, 128):
        q_ref[:, at : at + 128] = rotated(wide[:, at : at + 128], qgain_ref[...]).astype(
            jnp.bfloat16
        )
    for at in range(0, kv_width, 128):
        place = q_width + at
        to_sides(rotated(wide[:, place : place + 128], kgain_ref[...]), k_ref, at)
        place = q_width + kv_width + at
        to_sides(wide[:, place : place + 128], v_ref, at)


def placed(chunk_rows, block):
    per = chunk_rows // block
    here = lambda r, inner: (r, 0)
    there = lambda r, inner: ((r // per ^ inner[0]) * per + r % per, 0)
    return here, there


def project(inner, sequence, inputs, chunk_rows, norm, weights, tables, query_gain, key_gain, q_width, kv_width):
    rows, width = inputs.shape
    block = chunk_rows
    here, there = placed(block, block)
    fixed = lambda r, mine: (0, 0)
    used = q_width + 2 * kv_width
    table = pl.BlockSpec(
        (block, 128), lambda r, inner: (sequence * (rows // block) + there(r, inner)[0], 0)
    )
    gain = pl.BlockSpec((1, 128), fixed)
    return pl.pallas_call(
        functools.partial(project_kernel, 1),
        grid_spec=pltpu.PrefetchScalarGridSpec(
            num_scalar_prefetch=1,
            grid=(rows // block,),
            in_specs=[
                pl.BlockSpec((block, width), here),
                pl.BlockSpec((1, width), fixed),
                pl.BlockSpec(weights.shape, fixed, pipeline_mode=pl.Buffered(1)),
                table, table, table, gain, gain,
            ],
            out_specs=[
                pl.BlockSpec((block, 128), here),
                pl.BlockSpec((block, q_width), there),
                pl.BlockSpec((block, 4 * kv_width), there),
                pl.BlockSpec((block, 4 * kv_width), there),
                pl.BlockSpec((block, q_width + kv_width), there),
            ],
        ),
        out_shape=[
            jax.ShapeDtypeStruct((rows, 128), jnp.float32),
            jax.ShapeDtypeStruct((rows, q_width), jnp.bfloat16),
            jax.ShapeDtypeStruct((rows, 4 * kv_width), jnp.bfloat16),
            jax.ShapeDtypeStruct((rows, 4 * kv_width), jnp.bfloat16),
            jax.ShapeDtypeStruct((rows, q_width + kv_width), jnp.float32),
        ],
        compiler_params=pltpu.CompilerParams(vmem_limit_bytes=60 * 2**20),
        cost_estimate=cost(2 * rows * width * used, rows * width * 6, 0.22),
    )(
        inner, inputs, norm[None, :], weights, *tables,
        jnp.tile(query_gain, 2)[None, :], jnp.tile(key_gain, 2)[None, :],
    )


def heads_kernel(count, core_ref, grads_ref, *refs):
    rights, outs = refs[: 2 * count - 1], refs[2 * count - 1 :]
    outs[0][...] = jnp.dot(
        grads_ref[...], rights[0][...], preferred_element_type=jnp.float32
    ).astype(jnp.bfloat16)
    half = rights[1].shape[0]
    near = grads_ref[:, pl.ds(pl.multiple_of(core_ref[0] * half, half), half)]
    other = grads_ref[:, pl.ds(pl.multiple_of((1 - core_ref[0]) * half, half), half)]
    for k in range(1, count):
        outs[k][...] = (
            jnp.dot(near, rights[k][...], preferred_element_type=jnp.float32)
            + jnp.dot(other, rights[count - 1 + k][...], preferred_element_type=jnp.float32)
        ).astype(jnp.bfloat16)


def grad_heads(core, grads, own, others, q_width, count):
    rows, width = grads.shape
    fixed = lambda i, core: (0, 0)
    return pl.pallas_call(
        functools.partial(heads_kernel, count),
        grid_spec=pltpu.PrefetchScalarGridSpec(
            num_scalar_prefetch=1,
            grid=(1,),
            in_specs=[pl.BlockSpec(grads.shape, fixed), pl.BlockSpec((width, q_width), fixed)]
            + [pl.BlockSpec(piece.shape, fixed) for piece in others],
            out_specs=[pl.BlockSpec((rows, q_width), fixed)] * count,
        ),
        out_shape=[jax.ShapeDtypeStruct((rows, q_width), jnp.bfloat16)] * count,
        compiler_params=pltpu.CompilerParams(vmem_limit_bytes=60 * 2**20),
        cost_estimate=cost(2 * rows * width * q_width * count, rows * width, 2.67),
    )(core, grads, own, *others)


def peer(distance):
    mine = lax.axis_index("tensor")
    if distance == 1:
        return mine + 1 - 2 * (mine % 2)
    return (mine + 2) % 4 if distance == 2 else 3 - mine


def remote(distance):
    return dict(device_id={"tensor": peer(distance)}, device_id_type=pl.DeviceIdType.MESH)


def greet(distances):
    barrier = pltpu.get_barrier_semaphore()
    for distance in distances:
        pl.semaphore_signal(barrier, inc=1, **remote(distance))
    pl.semaphore_wait(barrier, len(distances))


def hidden_kernel(x_ref, dy_ref, w_ref, filled_ref, act_ref, grads_ref):
    units = act_ref.shape[1]
    inputs, cotangent = x_ref[...], dy_ref[...]
    for at in range(0, units, 256):
        lanes = slice(at, at + 256)
        gate = jnp.dot(inputs, w_ref[:, lanes], preferred_element_type=jnp.float32)
        up = jnp.dot(
            inputs, w_ref[:, units + at : units + at + 256], preferred_element_type=jnp.float32
        )
        change = jnp.dot(
            cotangent, w_ref[:, 2 * units + at : 2 * units + at + 256],
            preferred_element_type=jnp.float32,
        )
        sigmoid = 1.0 / (1.0 + jnp.exp(-gate))
        silu = gate * sigmoid
        act_ref[:, lanes] = (silu * up).astype(jnp.bfloat16)
        grads_ref[:, lanes] = (change * up * sigmoid * (1.0 + gate - silu)).astype(jnp.bfloat16)
        grads_ref[:, units + at : units + at + 256] = (change * silu).astype(jnp.bfloat16)


def hidden_units(inputs, cotangent, weights, filled):
    rows, width = inputs.shape
    units = weights.shape[1] // 3
    block = min(512, rows)
    row = lambda r: (r, 0)
    return pl.pallas_call(
        hidden_kernel,
        grid=(rows // block,),
        in_specs=[
            pl.BlockSpec((block, width), row),
            pl.BlockSpec((block, width), row),
            pl.BlockSpec(weights.shape, lambda r: (0, 0), pipeline_mode=pl.Buffered(1)),
            pl.BlockSpec(memory_space=pl.ANY),
        ],
        out_specs=[
            pl.BlockSpec((block, units), lambda r: (r, 1)),
            pl.BlockSpec((block, 2 * units), row),
        ],
        out_shape=[jax.ShapeDtypeStruct((rows, 2 * units), jnp.bfloat16)] * 2,
        input_output_aliases={3: 0},
        compiler_params=pltpu.CompilerParams(vmem_limit_bytes=60 * 2**20),
        cost_estimate=cost(6 * rows * width * units, (rows * width + width * units) * 6, 0.63),
    )(inputs, cotangent, weights, filled)


def hidden_forward_kernel(x_ref, w_ref, act_ref, factors_ref):
    units = act_ref.shape[1]
    inputs = x_ref[...]
    for at in range(0, units, 256):
        lanes, beside = slice(at, at + 256), slice(units + at, units + at + 256)
        gate = jnp.dot(inputs, w_ref[:, lanes], preferred_element_type=jnp.float32)
        up = jnp.dot(inputs, w_ref[:, beside], preferred_element_type=jnp.float32)
        sigmoid = 1.0 / (1.0 + jnp.exp(-gate))
        silu = gate * sigmoid
        act_ref[:, lanes] = (silu * up).astype(jnp.bfloat16)
        factors_ref[:, lanes] = (up * sigmoid * (1.0 + gate - silu)).astype(jnp.bfloat16)
        factors_ref[:, beside] = silu.astype(jnp.bfloat16)


def hidden_forward(inputs, weights):
    rows, width = inputs.shape
    units = weights.shape[1] // 3
    block = min(512, rows)
    row = lambda r: (r, 0)
    return pl.pallas_call(
        hidden_forward_kernel,
        grid=(rows // block,),
        in_specs=[
            pl.BlockSpec((block, width), row),
            pl.BlockSpec((width, 2 * units), lambda r: (0, 0), pipeline_mode=pl.Buffered(1)),
        ],
        out_specs=[pl.BlockSpec((block, units), row), pl.BlockSpec((block, 2 * units), row)],
        out_shape=[jax.ShapeDtypeStruct((rows, 2 * units), jnp.bfloat16)] * 2,
        compiler_params=pltpu.CompilerParams(vmem_limit_bytes=60 * 2**20),
        cost_estimate=cost(4 * rows * width * units, (rows * width + width * units) * 4, 0.63),
    )(inputs, weights)


def hidden_backward_kernel(dy_ref, factors_ref, w_ref, grads_ref):
    units = w_ref.shape[1]
    cotangent = dy_ref[...]
    for at in range(0, units, 256):
        change = jnp.dot(
            cotangent, w_ref[:, at : at + 256], preferred_element_type=jnp.float32
        )
        for lanes in (slice(at, at + 256), slice(units + at, units + at + 256)):
            grads_ref[:, lanes] = (change * factors_ref[:, lanes].astype(jnp.float32)).astype(
                jnp.bfloat16
            )


def hidden_backward(cotangent, factors, weights):
    rows, width = cotangent.shape
    units = weights.shape[1] // 3
    block = min(512, rows)
    row = lambda r: (r, 0)
    return pl.pallas_call(
        hidden_backward_kernel,
        grid=(rows // block,),
        in_specs=[
            pl.BlockSpec((block, width), row),
            pl.BlockSpec((block, 2 * units), row),
            pl.BlockSpec((width, units), lambda r: (0, 2), pipeline_mode=pl.Buffered(1)),
        ],
        out_specs=pl.BlockSpec((block, 2 * units), row),
        out_shape=jax.ShapeDtypeStruct((rows, 2 * units), jnp.bfloat16),
        compiler_params=pltpu.CompilerParams(vmem_limit_bytes=60 * 2**20),
        cost_estimate=cost(2 * rows * width * units, (rows * width + width * units) * 4, 0.63),
    )(cotangent, factors, weights)


def half_types(distance):
    if distance == 0:
        return (jnp.float32, jnp.float32)
    if distance == 1:
        return (jnp.bfloat16, jnp.float32)
    if distance == 2:
        return (jnp.float32, jnp.bfloat16)
    return (jnp.bfloat16, jnp.bfloat16)


def rows_out_kernel(terms, *refs):
    outs = refs[2 * terms :]
    total = None
    for left_ref, right_ref in zip(refs[:terms], refs[terms : 2 * terms]):
        product = lax.dot_general(
            left_ref[...], right_ref[...], NT, preferred_element_type=jnp.float32
        )
        total = product if total is None else total + product
    half = outs[0].shape[0]
    for index, out_ref in enumerate(outs):
        out_ref[...] = total[index * half : (index + 1) * half].astype(out_ref.dtype)


def rows_out(distances, lefts, rights, spans, chunk_rows):
    width, rows = rights[0].shape[0], len(distances) * chunk_rows
    first = distances[0] // len(distances)
    halves = [dtype for k in distances for dtype in half_types(k)]
    in_specs = [
        pl.BlockSpec(
            (rows, left[1]), lambda n, index=left[2]: (first, index), pipeline_mode=pl.Buffered(1)
        )
        for left in lefts
    ] + [
        pl.BlockSpec((256, columns), lambda n, index=index: (n, index)) for columns, index in spans
    ]
    depth = sum(left[1] for left in lefts)
    outs = pl.pallas_call(
        functools.partial(rows_out_kernel, len(lefts)),
        grid=(width // 256,),
        in_specs=in_specs,
        out_specs=[pl.BlockSpec((chunk_rows // 2, 256), lambda n: (0, n))] * len(halves),
        out_shape=[jax.ShapeDtypeStruct((chunk_rows // 2, width), dtype) for dtype in halves],
        compiler_params=pltpu.CompilerParams(vmem_limit_bytes=60 * 2**20),
        cost_estimate=cost(2 * rows * depth * width, depth * rows // 4, 4.07),
    )(*(left[0] for left in lefts), *rights)
    return {k: (outs[2 * i], outs[2 * i + 1]) for i, k in enumerate(distances)}


def resid_kernel(count, place_ref, *refs):
    inputs, lefts = refs[:2], (refs[2 : 2 + count], refs[2 + count : 2 + 2 * count])
    rights = refs[2 + 2 * count : 1 + 4 * count]
    norm_ref, hidden_ref, resid_ref, sums_ref = refs[1 + 4 * count :]
    half = sums_ref.shape[1] // 2
    blocks = pl.num_programs(0) // 2

    def block(x_ref, left_refs):
        for core, others in (
            (place_ref[1], rights[1:count]), (1 - place_ref[1], rights[count:])
        ):
            start = pl.multiple_of(core * half, half)
            total = lax.dot_general(
                left_refs[0][...], rights[0][pl.ds(start, half), :], NT,
                preferred_element_type=jnp.float32,
            )
            for left_ref, right_ref in zip(left_refs[1:], others):
                total = total + lax.dot_general(
                    left_ref[...], right_ref[...], NT, preferred_element_type=jnp.float32
                )
            sums_ref[:, pl.ds(start, half)] = total
        resid = x_ref[...].astype(jnp.float32) + sums_ref[...]
        hidden_ref[...] = (resid * rms_scale(resid) * norm_ref[...]).astype(jnp.bfloat16)

        @pl.when(pl.program_id(0) < resid_ref.shape[0])
        def _():
            resid_ref[pl.program_id(0)] = resid

    for sequence in range(2):

        @pl.when(pl.program_id(0) // blocks == sequence)
        def _():
            block(inputs[sequence], lefts[sequence])


def residual(place, inputs, heads, own, others, norm, chunk_rows):
    width, count = inputs[0].shape[1], len(heads[0])
    q_width = heads[0][0].shape[1]
    rows, block = 2 * SEQ, min(512, chunk_rows)
    here, there = placed(chunk_rows, block)
    blocks = SEQ // block
    fixed = lambda r, place: (0, 0)
    once = pl.Buffered(1)
    steps = (
        lambda r: jnp.minimum(r, blocks - 1),
        lambda r: jnp.maximum(r - blocks, 0),
    )
    return pl.pallas_call(
        functools.partial(resid_kernel, count),
        grid_spec=pltpu.PrefetchScalarGridSpec(
            num_scalar_prefetch=1,
            grid=(rows // block,),
            in_specs=[
                pl.BlockSpec((block, width), lambda r, place, step=step: here(step(r), place))
                for step in steps
            ]
            + [
                pl.BlockSpec((block, q_width), lambda r, place, step=step: there(step(r), place))
                for step in steps
                for _ in range(count)
            ]
            + [pl.BlockSpec((width, q_width), fixed, pipeline_mode=once)]
            + [pl.BlockSpec(piece.shape, fixed, pipeline_mode=once) for piece in others]
            + [pl.BlockSpec((1, width), fixed)],
            out_specs=[
                pl.BlockSpec((block, width), here),
                pl.BlockSpec((chunk_rows // block, block, width), lambda r, place: (0, 0, 0)),
            ],
            scratch_shapes=[pltpu.VMEM((block, width), jnp.float32)],
        ),
        out_shape=[
            jax.ShapeDtypeStruct((rows, width), jnp.bfloat16),
            jax.ShapeDtypeStruct((chunk_rows // block, block, width), jnp.float32),
        ],
        compiler_params=pltpu.CompilerParams(vmem_limit_bytes=60 * 2**20),
        cost_estimate=cost(2 * rows * width * width, rows * width * 8, 0.46),
    )(place, *inputs, *heads[0], *heads[1], own, *others, norm[None, :])


def input_kernel(count, core_ref, *refs):
    lefts, rights = refs[:count], refs[count : 3 * count - 1]
    x_ref, grad_ref, norm_ref, out_ref, gains_ref, sums_ref = refs[3 * count - 1 :]
    used = lefts[0].shape[1]
    step, steps = pl.program_id(0), pl.num_programs(0)

    def block(others):
        own = rights[0][:, rights[0].shape[1] - used :]
        total = lax.dot_general(lefts[0][...], own, NT, preferred_element_type=jnp.float32)
        for left_ref, right_ref in zip(lefts[1:], others):
            total = total + lax.dot_general(
                left_ref[...], right_ref[...], NT, preferred_element_type=jnp.float32
            )
        sums_ref[:, pl.ds(pl.multiple_of(step * 256, 256), 256)] = total

    for half in range(2):

        @pl.when(step // (steps // 2) == (core_ref[0] if half == 0 else 1 - core_ref[0]))
        def _():
            block(rights[1 + half * (count - 1) : 1 + (half + 1) * (count - 1)])

    @pl.when(step == steps - 1)
    def _():
        gains_ref[...] = jnp.zeros_like(gains_ref)
        for at in range(0, sums_ref.shape[0], 64):
            rows = slice(at, at + 64)
            grads = sums_ref[rows, :]
            inputs = x_ref[rows, :].astype(jnp.float32)
            inverse = rms_scale(inputs)
            normed = inputs * inverse
            gains_ref[...] += jnp.sum((grads * normed).reshape(-1, 8, grads.shape[1]), axis=0)
            out_ref[rows, :] = grad_ref[rows, :] + norm_back(
                grads * norm_ref[...], normed, inverse
            )


def input_back(core, grads, own, others, inputs, grad_resid, norm):
    rows, width = inputs.shape
    count, used = len(grads), grads[0].shape[1]
    steps = width // 256
    whole = lambda n, core: (0, 0)
    near = lambda n, core: (jnp.clip(n - core[0] * (steps // 2), 0, steps // 2 - 1), 0)
    other = lambda n, core: (jnp.clip(n - (1 - core[0]) * (steps // 2), 0, steps // 2 - 1), 0)
    once = pl.Buffered(1)
    return pl.pallas_call(
        functools.partial(input_kernel, count),
        grid_spec=pltpu.PrefetchScalarGridSpec(
            num_scalar_prefetch=1,
            grid=(steps,),
            in_specs=[pl.BlockSpec((rows, used), whole, pipeline_mode=once)] * count
            + [pl.BlockSpec((256, own.shape[1]), lambda n, core: (n, 0))]
            + [pl.BlockSpec((256, used), near)] * (count - 1)
            + [pl.BlockSpec((256, used), other)] * (count - 1)
            + [pl.BlockSpec((rows, width), whole, pipeline_mode=once)] * 2
            + [pl.BlockSpec((1, width), whole)],
            out_specs=[pl.BlockSpec((rows, width), whole), pl.BlockSpec((8, width), whole)],
            scratch_shapes=[pltpu.VMEM((rows, width), jnp.float32)],
        ),
        out_shape=[
            jax.ShapeDtypeStruct((rows, width), jnp.float32),
            jax.ShapeDtypeStruct((8, width), jnp.float32),
        ],
        compiler_params=pltpu.CompilerParams(vmem_limit_bytes=60 * 2**20),
        cost_estimate=cost(2 * rows * used * width * count, rows * width * 20, 0.28),
    )(core, *grads, own, *others, inputs, grad_resid, norm[None, :])


def attention_weights_kernel(inner_ref, beside_ref, *refs):
    out_ref = refs[-1]
    q_width = refs[-2].shape[1]
    total = jnp.zeros((out_ref.shape[0], q_width), jnp.float32)
    pieces, at = [], 0
    chunk_rows = refs[0].shape[0]
    for ref in refs[:-1]:
        if ref.shape[0] < SEQ:
            pieces.append(ref)
            continue
        at = 0
        for piece in pieces:
            rows = piece.shape[0]
            start = (at // chunk_rows ^ inner_ref[0]) * chunk_rows + at % chunk_rows
            total = total + lax.dot_general(
                piece[...], ref[pl.ds(pl.multiple_of(start, rows), rows), :], TN,
                preferred_element_type=jnp.float32,
            )
            at += rows
        pieces = []
    out_ref[:, :q_width] = total.astype(jnp.bfloat16)
    out_ref[:, q_width:] = beside_ref[...]


def out_weights(inner, beside, pieces, attended):
    width, q_width = pieces[0][0].shape[1], attended[0].shape[1]
    whole = lambda n, inner: (0, 0)
    columns = q_width + beside.shape[1]
    in_specs = [pl.BlockSpec((256, beside.shape[1]), lambda n, inner: (n, 0))]
    for rows in range(2):
        in_specs += [pl.BlockSpec((piece.shape[0], 256), lambda n, inner: (0, n)) for piece in pieces[rows]]
        in_specs.append(pl.BlockSpec((SEQ, q_width), whole))
    return pl.pallas_call(
        attention_weights_kernel,
        grid_spec=pltpu.PrefetchScalarGridSpec(
            num_scalar_prefetch=1,
            grid=(width // 256,),
            in_specs=in_specs,
            out_specs=pl.BlockSpec((256, columns), lambda n, inner: (n, 0)),
        ),
        out_shape=jax.ShapeDtypeStruct((width, columns), jnp.bfloat16),
        compiler_params=pltpu.CompilerParams(vmem_limit_bytes=60 * 2**20),
        cost_estimate=cost(4 * SEQ * q_width * width, SEQ * width * 4, 0.35),
    )(inner, beside, *pieces[0], attended[0], *pieces[1], attended[1])


def projection_weights_kernel(norm_ref, *refs):
    inputs, inverses, grads, out_ref = refs[:2], refs[2:4], refs[4:-1], refs[-1]
    total = jnp.zeros(out_ref.shape, jnp.float32)
    chunk_rows = grads[0].shape[0]
    for k, grad_ref in enumerate(grads):
        at = k * chunk_rows
        rows = slice(at % SEQ, at % SEQ + chunk_rows)
        inverse = inverses[at // SEQ][rows, :]
        normed = inputs[at // SEQ][rows, :].astype(jnp.float32) * jnp.concatenate([inverse] * 2, axis=1)
        total = total + lax.dot_general(
            (normed * norm_ref[...]).astype(jnp.bfloat16), grad_ref[...], TN,
            preferred_element_type=jnp.float32,
        )
    out_ref[...] = total.astype(jnp.bfloat16)


def projection_weights(inputs, inverse, norm, grads):
    width, columns = inputs[0].shape[1], grads[0].shape[1]
    whole = lambda n: (0, 0)
    column = lambda n: (0, n)
    return pl.pallas_call(
        projection_weights_kernel,
        grid=(width // 256,),
        in_specs=[pl.BlockSpec((1, 256), column)]
        + [pl.BlockSpec((SEQ, 256), column)] * 2
        + [pl.BlockSpec((SEQ, 128), whole)] * 2
        + [pl.BlockSpec(part.shape, whole) for part in grads],
        out_specs=pl.BlockSpec((256, columns), lambda n: (n, 0)),
        out_shape=jax.ShapeDtypeStruct((width, columns), jnp.bfloat16),
        compiler_params=pltpu.CompilerParams(vmem_limit_bytes=60 * 2**20),
        cost_estimate=cost(4 * SEQ * columns * width, SEQ * width * 4, 0.43),
    )(norm[None, :], *inputs, *inverse, *grads)


def shift(values, distance, count, axis="tensor"):
    return lax.ppermute(values, axis, [(i, i ^ distance) for i in range(count)])


def gather_kernel(src_ref, own_ref, other_ref, send_sems, recv_sems, local_sem):
    rows = src_ref.shape[0]
    half = rows // 2
    x_top, x_bottom = own_ref.at[pl.ds(rows, half)], own_ref.at[pl.ds(rows + half, half)]
    y_top, y_bottom = other_ref.at[pl.ds(0, half)], other_ref.at[pl.ds(half, half)]
    far_top, far_bottom = other_ref.at[pl.ds(rows, half)], other_ref.at[pl.ds(rows + half, half)]
    top, bottom = src_ref.at[pl.ds(0, half)], src_ref.at[pl.ds(half, half)]
    greet([1, 2])

    def copy(index, from_ref, to_ref, distance):
        return pltpu.make_async_remote_copy(
            src_ref=from_ref, dst_ref=to_ref, send_sem=send_sems.at[index],
            recv_sem=recv_sems.at[index], **remote(distance),
        )

    first = [
        copy(0, bottom, x_bottom, 1), copy(1, top, y_top, 2),
        copy(2, top, x_top, 1), copy(3, bottom, y_bottom, 2),
    ]
    for sent in first:
        sent.start()
    local = pltpu.make_async_copy(src_ref, own_ref.at[pl.ds(0, rows)], local_sem.at[0])
    local.start()
    first[1].wait_recv()
    relay_top = copy(4, y_top, far_top, 1)
    relay_top.start()
    first[0].wait_recv()
    relay_bottom = copy(5, x_bottom, far_bottom, 2)
    relay_bottom.start()
    first[2].wait_recv()
    first[3].wait_recv()
    relay_top.wait_recv()
    relay_bottom.wait_recv()
    for sent in first + [relay_top, relay_bottom]:
        sent.wait_send()
    local.wait()


def gather_rows(values, count):
    if count != 4:
        near = gather_near(values, count)
        return [jnp.concatenate(near[i : i + count // 2], axis=0) for i in (0, count // 2)]
    place = pl.BlockSpec(memory_space=pl.ANY)
    rows, width = values.shape
    wide = jax.ShapeDtypeStruct((2 * rows, width), values.dtype)
    return pl.pallas_call(
        gather_kernel,
        in_specs=[place],
        out_specs=[place] * 2,
        out_shape=[wide, wide],
        scratch_shapes=[
            pltpu.SemaphoreType.DMA((6,)), pltpu.SemaphoreType.DMA((6,)),
            pltpu.SemaphoreType.DMA((1,)),
        ],
        compiler_params=pltpu.CompilerParams(collective_id=1, has_side_effects=True),
        cost_estimate=pl.CostEstimate(
            flops=0, bytes_accessed=values.size * 12, transcendentals=0,
            remote_bytes_transferred=values.size * 6,
        ),
    )(values)


def gather_near(values, count):
    if count == 4:
        return [values, shift(values, 1, count), shift(values, 2, count)]
    whole = lax.all_gather(values, "tensor", axis=0)
    mine = lax.axis_index("tensor")
    return [lax.dynamic_index_in_dim(whole, mine ^ k, 0, False) for k in range(count)]


def gather_far(near, count):
    if count != 4:
        return []
    half = near[0].shape[0] // 2
    return [shift(near[2][:half], 1, count), shift(near[1][half:], 2, count)]


def gather_chunks(values, count):
    near = gather_near(values, count)
    far = gather_far(near, count)
    return near + [jnp.concatenate(far, axis=0)] if far else near


def exchange(parts, distances, count):
    return [part if k == 0 else shift(part, k, count) for k, part in zip(distances, parts)]


def column_piece(weights, columns, core):
    half = weights.shape[0] // 2
    return lax.dynamic_slice(
        weights, (core[0] * half, columns[0]), (half, columns[1] - columns[0])
    )


def sum_first(parts, count):
    if count != 4:
        return None
    return shift(parts[3][0], 1, count), shift(parts[3][1], 2, count)


def sum_adds(parts, first):
    far_top, far_bottom = first
    return (
        (parts[2][0] + far_top.astype(jnp.float32)).astype(jnp.bfloat16),
        (parts[1][1] + far_bottom.astype(jnp.float32)).astype(jnp.bfloat16),
    )


def sum_rest(parts, near, adds, count):
    if count != 4:
        mine = lax.axis_index("tensor")
        half, width = parts[0][0].shape
        stacked = jnp.zeros((count, 2 * half, width), jnp.bfloat16)
        for k in range(count):
            term = jnp.concatenate([side.astype(jnp.bfloat16) for side in parts[k]], axis=0)
            stacked = lax.dynamic_update_index_in_dim(stacked, term, mine ^ k, 0)
        total = lax.psum_scatter(
            stacked.reshape(-1, width), "tensor", scatter_dimension=0, tiled=True
        ).astype(jnp.float32)
        none = jnp.zeros((half, width), jnp.bfloat16)
        return [[total[:half], none, none], [total[half:], none, none]]
    x_top, y_bottom = near
    y_top, x_bottom = shift(adds[0], 2, count), shift(adds[1], 1, count)
    return [[parts[0][0], x_top, y_top], [parts[0][1], x_bottom, y_bottom]]


def sum_near(parts, count):
    if count != 4:
        return ()
    return shift(parts[1][0], 1, count), shift(parts[2][1], 2, count)


def added(own_ref, x_ref, y_ref):
    return own_ref[...] + x_ref[...].astype(jnp.float32) + y_ref[...].astype(jnp.float32)


def own_rows_call(kernel, sums, twos, ones, out_shapes, gains):
    half, width = sums[0][0].shape
    block = min(64, half)
    term = pl.BlockSpec((block, width), lambda i: (i, 0))
    both = pl.BlockSpec((2, block, width), lambda i: (0, i, 0))
    out_specs = [both] * len(out_shapes)
    if gains:
        out_specs.append(pl.BlockSpec((8, width), lambda i: (0, 0)))
        out_shapes = out_shapes + [jax.ShapeDtypeStruct((8, width), jnp.float32)]
    return pl.pallas_call(
        kernel,
        grid=(half // block,),
        in_specs=[term] * 6 + [both] * len(twos) + [pl.BlockSpec((1, width), lambda i: (0, 0))] * len(ones),
        out_specs=out_specs,
        out_shape=out_shapes,
        compiler_params=pltpu.CompilerParams(vmem_limit_bytes=60 * 2**20),
        cost_estimate=cost(half * width * 10, half * width * 10, 1.0),
    )(*sums[0], *sums[1], *twos, *ones)


def resid_back_kernel(*refs):
    dy_ref, resid_ref, norm_ref, grad_ref, low_ref, gains_ref = refs[6:]

    @pl.when(pl.program_id(0) == 0)
    def _():
        gains_ref[...] = jnp.zeros_like(gains_ref)

    for side in range(2):
        grads = added(*refs[3 * side : 3 * side + 3])
        resid = resid_ref[side]
        inverse = rms_scale(resid)
        normed = resid * inverse
        gains_ref[...] += jnp.sum((grads * normed).reshape(-1, 8, grads.shape[1]), axis=0)
        total = dy_ref[side].astype(jnp.float32) + norm_back(grads * norm_ref[...], normed, inverse)
        grad_ref[side] = total
        low_ref[side] = total.astype(jnp.bfloat16)


def output_kernel(*refs):
    resid_ref, out_ref = refs[6:]
    for side in range(2):
        out_ref[side] = (resid_ref[side] + added(*refs[3 * side : 3 * side + 3])).astype(jnp.bfloat16)


def total_everywhere(values, sizes):
    for axis, size in sizes.items():
        distance = 1
        while distance < size:
            values = values + shift(values, distance, size, axis)
            distance *= 2
    return values


def after(value, *others):
    return lax.optimization_barrier((value, others))[0]


def pad_columns(values, width):
    return jnp.pad(values, ((0, 0), (0, width - values.shape[1])))


def gather_weights(*parts):
    return lax.all_gather(jnp.concatenate(parts, axis=1), "dp", axis=0, tiled=True)


def scatter_weights(grads):
    return lax.psum_scatter(grads, "dp", scatter_dimension=0, tiled=True)


def per_device(
    sizes,
    tokens,
    segments,
    positions,
    w_query,
    w_key,
    w_value,
    w_out,
    w_gate,
    w_up,
    w_down,
    norm_attn,
    norm_mlp,
    query_gain,
    key_gain,
    out_grad,
):
    count = sizes["tensor"]
    chunk_rows = tokens.shape[0]
    q_width, key_width = w_query.shape[1], w_key.shape[1]
    kv_width = -(-key_width // 128) * 128
    units = w_gate.shape[1] // 2
    mine = lax.axis_index("tensor").astype(jnp.int32).reshape(1)

    half, width = chunk_rows // 2, tokens.shape[1]
    inner_count = count // 2
    inner, flip = mine % inner_count, mine // inner_count
    core = lax.axis_index("dp").astype(jnp.int32).reshape(1) % 2

    def own_first(values):
        pair = values.reshape(2, SEQ)
        return jnp.where(flip == 0, pair, pair[::-1])

    w_attn = gather_weights(
        w_out, w_query, pad_columns(w_key, kv_width), pad_columns(w_value, kv_width)
    )
    rows_in = gather_rows(tokens, count)
    w_mlp = [
        gather_weights(w_gate[:, part], w_up[:, part], w_down[:, part])
        for part in (slice(0, units), slice(units, 2 * units))
    ]
    segments, positions = own_first(segments), own_first(positions)
    out_near = gather_near(column_piece(after(w_attn, rows_in), (0, q_width), core), count)
    inv_rows, queries, key_sides, value_sides, raw = [], [], [], [], []
    tables = rotary_tables(positions.reshape(-1))
    attended, inv_total, heads = [], [], []
    for sequence in range(2):
        rows = rows_in[sequence]
        if sequence == 1:
            rows = after(rows, attended, out_near)
            out_near = after(out_near, attended)
            out_far = gather_far(out_near, count)
            out_others = out_near[1:] + ([jnp.concatenate(out_far, axis=0)] if out_far else [])
            out_others = out_others + [shift(part, 1, sizes["dp"], "dp") for part in out_others]
        results = project(
            inner, sequence, rows, chunk_rows, norm_attn, w_attn, tables, query_gain, key_gain, q_width, kv_width
        )
        for kept, result in zip((inv_rows, queries, key_sides, value_sides, raw), results):
            kept.append(result)
        result, inverse = attend(
            queries[sequence], key_sides[sequence], value_sides[sequence], segments[sequence]
        )
        attended.append(result)
        inv_total.append(inverse)
        heads.append(gather_chunks(result, count))
    grad_near = gather_near(after(out_grad, heads), count)
    crossed = [
        heads[sequence][:inner_count] + heads[1 - sequence][inner_count:] for sequence in range(2)
    ]
    rows_two, resid = residual(
        jnp.concatenate([inner, core]), rows_in, crossed, w_attn, out_others, norm_mlp, chunk_rows
    )
    resid = resid.reshape(2, half, width)
    grad_near = after(grad_near, rows_two)
    grad_far = gather_far(grad_near, count)
    act_a, factors = hidden_forward(rows_two, w_mlp[0])
    grad_rows = jnp.concatenate(grad_near + after(grad_far, act_a), axis=0)

    grads_a = hidden_backward(grad_rows, factors, w_mlp[0])
    grad_a = contract_rows(rows_two, grads_a).astype(jnp.bfloat16)
    half_columns = column_piece(after(w_attn, grads_a), (q_width, w_attn.shape[1]), core)
    in_near = [shift(half_columns, k, count) for k in range(1, count - 1)]
    if count == 4:
        far_halves = gather_far([half_columns, *in_near], count)
        in_far = [jnp.concatenate(far_halves, axis=0)]
    else:
        far_halves = in_far = [shift(half_columns, count - 1, count)]
    act, grads_b = hidden_units(after(rows_two, grad_a), grad_rows, w_mlp[1], act_a)
    in_others = in_near + in_far
    in_others = in_others + [shift(part, 1, sizes["dp"], "dp") for part in in_others]
    spans = [(2 * units, 0), (2 * units, 0)]

    def two_parts(distances, grads):
        lefts = [(grads, 2 * units, 0), (grads_b, 2 * units, 0)]
        return rows_out(distances, lefts, w_mlp, spans, chunk_rows)

    grad_b = contract_rows(after(rows_two, in_near), grads_b).astype(jnp.bfloat16)
    two = two_parts(list(range(inner_count, count)), after(grads_a, grad_b, far_halves))
    two_first = sum_first(two, count)
    for k in range(1, inner_count):
        two.update(two_parts([k], after(grads_a, two[count - 1])))
    two_near = sum_near(two, count)
    two_adds = sum_adds(two, two_first) if count == 4 else ()
    two.update(two_parts([0], after(grads_a, two[1], two_adds)))
    two_rest = sum_rest(two, two_near, two_adds, count)
    distances = list(range(count))
    out_act = after(act, two[0])
    out = rows_out(
        distances, [(out_act, units, 0), (out_act, units, 1)], w_mlp, [(units, 2), (units, 2)], chunk_rows
    )
    out_first = sum_first(out, count)
    grad_resid, branch_low, gain_mlp = own_rows_call(
        resid_back_kernel,
        after(two_rest, out[0]),
        [out_grad.reshape(2, half, width), resid],
        [norm_mlp[None, :]],
        [
            jax.ShapeDtypeStruct((2, half, width), jnp.float32),
            jax.ShapeDtypeStruct((2, half, width), jnp.bfloat16),
        ],
        True,
    )
    branch_low = branch_low.reshape(chunk_rows, width)
    heads_out = grad_heads(core, branch_low, w_attn, out_others, q_width, count)
    heads_in = exchange(heads_out, distances, count)
    scattered_a = scatter_weights(grad_a)
    scattered_b = scatter_weights(after(grad_b, scattered_a, two[count - 1]))
    grad_down = contract_rows(
        after(grad_rows, heads_out[0], scattered_b, out_first), act
    ).astype(jnp.bfloat16)
    tops = bottoms = relays = []
    if count == 4:
        top, bottom = after((branch_low[:half], branch_low[half:]), heads_in, grad_down)
        tops = [shift(top, 1, count), shift(top, 2, count)]
    sums, raw_grads = [], []
    for sequence in range(2):
        pieces = heads_in[sequence * inner_count : (sequence + 1) * inner_count]
        if sequence == 0:
            pieces = after(pieces, heads_in, grad_down)
        else:
            pieces = after(pieces, tops, raw_grads)
            if count == 4:
                bottom = after(bottom, tops, raw_grads)
                bottoms = [shift(bottom, 1, count), shift(bottom, 2, count)]
        results = attend_back(
            inner, sequence, queries[sequence], key_sides[sequence], value_sides[sequence],
            segments[sequence], attended[sequence], inv_total[sequence], pieces, raw[sequence], tables,
            query_gain, key_gain,
        )
        raw_grads += results[:inner_count]
        sums.append(results[inner_count:])
    raw_in = exchange(raw_grads, distances, count)
    if count == 4:
        near_bottom, near_top = after((bottoms[0], tops[1]), bottoms, raw_grads)
        relays = [shift(near_top, 1, count), shift(near_bottom, 2, count)]
        branch = (
            [branch_low, tops[0], bottoms[0]],
            [tops[1], bottoms[1], *relays],
        )
    else:
        branch_near = gather_near(branch_low, count)
        branch = (branch_near[:inner_count], branch_near[inner_count:])
    scattered_down = scatter_weights(after(grad_down, scattered_b, heads_in))
    grad_qkv = projection_weights(after(rows_in, raw_grads, bottoms), inv_rows, norm_attn, raw_grads)
    grad_w_gate = jnp.concatenate(
        [scattered_a[:, :units], scattered_b[:, :units]], axis=1
    ).astype(jnp.float32)
    grad_w_up = jnp.concatenate(
        [scattered_a[:, units:], scattered_b[:, units:]], axis=1
    ).astype(jnp.float32)
    grad_attn = out_weights(inner, grad_qkv, after(branch, raw_grads, grad_w_gate, grad_w_up, in_others), attended)

    out_adds = sum_adds(out, after(out_first, grad_attn)) if count == 4 else ()
    scattered_attn = scatter_weights(
        after(
            grad_attn, scattered_down, raw_in[1:-1],
        )
    )

    grad_w_down = scattered_down.astype(jnp.float32)
    grad_tokens, gain_attn = input_back(
        core, after(raw_in, grad_w_down, out_adds), w_attn, in_others, tokens, grad_resid.reshape(chunk_rows, width), norm_attn
    )
    out_near = sum_near(after(out, raw_in), count)
    out_rest = sum_rest(out, out_near, after(out_adds, raw_in), count)
    gains = [
        jnp.sum(gain_attn, axis=0),
        jnp.sum(gain_mlp, axis=0),
        jnp.sum((sums[0][0] + sums[1][0]).reshape(-1, 64), axis=0),
        jnp.sum((sums[0][1] + sums[1][1]).reshape(-1, 64), axis=0),
    ]
    gains = jnp.concatenate(gains).reshape(-1, 128)
    gains = total_everywhere(gains, sizes).reshape(-1)
    (output,) = own_rows_call(
        output_kernel, after(out_rest, gains), [resid], [], [jax.ShapeDtypeStruct((2, half, width), jnp.bfloat16)],
        False,
    )
    distances = list(range(count))
    key_at = 2 * q_width
    value_at = key_at + kv_width
    return (
        output.reshape(chunk_rows, width),
        grad_tokens.reshape(chunk_rows, width),
        scattered_attn[:, q_width:key_at].astype(jnp.float32),
        scattered_attn[:, key_at : key_at + key_width].astype(jnp.float32),
        scattered_attn[:, value_at : value_at + key_width].astype(jnp.float32),
        scattered_attn[:, :q_width].astype(jnp.float32),
        grad_w_gate,
        grad_w_up,
        grad_w_down,
        gains[:width],
        gains[width : 2 * width],
        gains[2 * width : 2 * width + 64],
        gains[2 * width + 64 : 2 * width + 128],
    )


def solution(mesh):
    return jax.shard_map(
        functools.partial(per_device, dict(mesh.shape)),
        mesh=mesh,
        in_specs=(
            P(("dp", "tensor"), None),
            P("dp"),
            P("dp"),
            P("dp", "tensor"),
            P("dp", "tensor"),
            P("dp", "tensor"),
            P("dp", "tensor"),
            P("dp", "tensor"),
            P("dp", "tensor"),
            P("dp", "tensor"),
            P(),
            P(),
            P(),
            P(),
            P(("dp", "tensor"), None),
        ),
        out_specs=(
            P(("dp", "tensor"), None),
            P(("dp", "tensor"), None),
            P("dp", "tensor"),
            P("dp", "tensor"),
            P("dp", "tensor"),
            P("dp", "tensor"),
            P("dp", "tensor"),
            P("dp", "tensor"),
            P("dp", "tensor"),
            P(),
            P(),
            P(),
            P(),
        ),
        check_vma=False,
    )
```
